32 devices in a mesh: az: 16 (over z, x, core), rad: 2 (over y).
Axes of the slice: x: 2, y: 2, z: 4, core: 2. Of those that a mesh axis runs over, the one named last changes fastest.
Arguments:
- pressure: float32 [2, 256, 192, 128], P(None, 'az', 'rad'), may hold values from -6 to 6
- source: float32 [2, 256, 192, 128], P(None, 'az', 'rad'), may hold values from -6 to 6
- diagonal: float32 [2, 256, 192, 128], P(None, 'az', 'rad'), may hold values from 0.5 to 8
- rot_offset: int32 [1], replicated, may hold values from 0 to 255
Outputs:
- corrected: float32 [2, 256, 192, 128], P(None, 'az', 'rad')
The draws below stay inside these ranges and needn't reach their ends.
All inputs are finite; a program needn't handle non-finite values.
Results may differ from the reference program's by a relative error of at most 0.00002.
Values sent between devices are 32-bit elements; how exact they have to be, the bound alone decides.
No kernel may reach another device: no remote copies, remote signals or barrier semaphores. Data moves between devices by JAX's collectives and lax.ppermute only.
A program may use at most 64 MiB of HBM per device.

```python
import math
import jax
import jax.numpy as jnp

CZ = 128
STEPS = 2
SWEEPS = 4
NA = 256
NR = 192


def block_scale(stream_key, shape, pieces, least, high):
    def one(axis_at, shards_of):
        draws = jax.random.uniform(jax.random.fold_in(jax.random.fold_in(stream_key, 6), axis_at), (shards_of,), jnp.float32, least / len(pieces), high / len(pieces))
        return jnp.repeat(jnp.exp(draws), shape[axis_at] // shards_of).reshape((-1,) + (1,) * (len(shape) - axis_at - 1))

    loudness = one(*pieces[0])
    for cut in pieces[1:]:
        loudness = loudness * one(*cut)
    return loudness


def bell_draw(own_key, shape, deviation, reach, shards=(), held_as=jnp.bfloat16):
    result = deviation * jax.random.normal(own_key, shape, jnp.float32)
    if shards:
        result = result * block_scale(own_key, shape, shards, -0.22, 0.18)
    return jnp.clip(result, -reach, reach).astype(held_as)


def setup_inputs(seed: int = 0) -> dict:
    keys = jax.random.split(jax.random.key(seed), 5)
    return {
        "pressure": bell_draw(keys[0], (2, NA, NR, CZ), 1.0, 6.0, ((1, 16), (2, 2)), jnp.float32),
        "source": bell_draw(keys[1], (2, NA, NR, CZ), 1.0, 6.0, ((1, 16), (2, 2)), jnp.float32),
        "diagonal": jnp.clip(jnp.exp(math.log(8.0) - 2.7725887 * jax.random.uniform(keys[2], (2, NA, NR, CZ), jnp.float32) ** block_scale(keys[2], (2, NA, NR, CZ), ((1, 16), (2, 2)), -0.2, 0.2)), 0.5, 8.0),
        "rot_offset": jax.random.randint(keys[3], (1,), 0, NA).astype(jnp.int32),
    }


OMEGA = 0.8


def relax_once(pressure, low_ghost, high_ghost, source, diagonal):
    stacked = jnp.concatenate([low_ghost[:, :, None, :], pressure, high_ghost[:, :, None, :]], axis=2)
    radial = stacked[:, :, 2:, :] + stacked[:, :, :-2, :]
    beside_all = jnp.roll(pressure, 1, axis=1) + jnp.roll(pressure, -1, axis=1)
    axial_pad = jnp.pad(pressure, ((0, 0), (0, 0), (0, 0), (1, 1)))
    axial_sum = axial_pad[..., 2:] + axial_pad[..., :-2]
    center = 6.0 + diagonal
    misfit = source - (center * pressure - (radial + beside_all + axial_sum))
    return pressure + OMEGA * misfit / center


def reference(pressure, source, diagonal, rot_offset):
    cycle_length = pressure.shape[1]
    radial_cells = pressure.shape[2]
    azimuth_ids = jnp.arange(cycle_length, dtype=jnp.int32)
    for time_step in range(STEPS):
        offset = (rot_offset[0] * (time_step + 1)) % cycle_length
        rotor_edge = pressure[0, :, radial_cells - 1, :]
        stator_edge = pressure[1, :, 0, :]
        to_stator = jnp.take(rotor_edge, ((azimuth_ids - offset) % cycle_length).astype(jnp.int32), axis=0)
        to_rotor = jnp.take(stator_edge, ((azimuth_ids + offset) % cycle_length).astype(jnp.int32), axis=0)
        for sweep_number in range(SWEEPS):
            low_ghost = jnp.stack([pressure[0, :, 0, :], to_stator])
            high_ghost = jnp.stack([to_rotor, pressure[1, :, radial_cells - 1, :]])
            pressure = relax_once(pressure, low_ghost, high_ghost, source, diagonal)
    return pressure
```

```python
import functools

import jax
import jax.numpy as jnp
from jax import lax
from jax.experimental import pallas as pl
from jax.experimental.pallas import tpu as pltpu
from jax.sharding import PartitionSpec as P

STEPS = 2
SWEEPS = 4
OMEGA = 0.8
TILE = 8
HALO = SWEEPS


def sweep_column(before, here, after, weight, shift, low_phys, high_phys, low_value, high_value):
    rows, lanes = here.shape
    row = lax.broadcasted_iota(jnp.int32, here.shape, 0)
    lane = lax.broadcasted_iota(jnp.int32, here.shape, 1)
    low_fix = jnp.logical_and(row == TILE - 1, low_phys)
    high_fix = jnp.logical_and(row == rows - TILE, high_phys)
    edged = jnp.where(low_fix, low_value, jnp.where(high_fix, high_value, here))
    radial = pltpu.roll(edged, 1, 0) + pltpu.roll(edged, rows - 1, 0)
    axial = jnp.where(lane == 0, 0.0, pltpu.roll(here, 1, 1)) + jnp.where(
        lane == lanes - 1, 0.0, pltpu.roll(here, lanes - 1, 1)
    )
    nbr = (before + after) + (radial + axial)
    return (1.0 - OMEGA) * here + shift + weight * nbr


def run_sweeps(rad_ref, ghost_ref, field, weight, shift, out_ref):
    _, columns, rows, _ = field.shape
    at_low = rad_ref[0] == 0
    at_high = jnp.logical_not(at_low)
    for sweep in range(1, SWEEPS + 1):
        for annulus in range(2):

            def body(j, before, annulus=annulus, sweep=sweep):
                here = field[annulus, j]
                after = field[annulus, j + 1]
                ghost = ghost_ref[pl.ds(j, 1), :]
                low_value = here[TILE : TILE + 1] if annulus == 0 else ghost
                high_value = ghost if annulus == 0 else here[rows - TILE - 1 : rows - TILE]
                new = sweep_column(
                    before,
                    here,
                    after,
                    weight[annulus, j],
                    shift[annulus, j],
                    at_low,
                    at_high,
                    low_value,
                    high_value,
                )
                if sweep == SWEEPS:
                    out_ref[annulus, j - HALO] = new[TILE : rows - TILE]
                else:
                    field[annulus, j] = new
                return here

            lax.fori_loop(sweep, columns - sweep, body, field[annulus, sweep - 1])


def place(target, own, left, right, cut, cut_left, cut_right, width):
    _, columns, rows, _ = target.shape
    inner = pl.ds(TILE, rows - 2 * TILE)
    for first, block, cut_block in (
        (HALO - width, left, cut_left),
        (HALO, own, cut),
        (columns - HALO, right, cut_right),
    ):
        span = pl.ds(first, block.shape[1])
        target[:, span, inner, :] = block
        target[:, span, pl.ds(0, TILE), :] = cut_block
        target[:, span, pl.ds(rows - TILE, TILE), :] = cut_block


def first_kernel(
    rad_ref,
    ghost_ref,
    p_ref,
    s_ref,
    d_ref,
    left_ref,
    right_ref,
    cut_ref,
    cut_left_ref,
    cut_right_ref,
    out_ref,
    weight,
    shift,
    field,
):
    h, n = HALO, HALO - 1
    place(
        field,
        p_ref[...],
        left_ref[:, :h],
        right_ref[:, :h],
        cut_ref[0],
        cut_left_ref[:, :h],
        cut_right_ref[:, :h],
        h,
    )
    for target, source, at, k in ((shift, s_ref, h, 1), (weight, d_ref, h + n, 2)):
        place(
            target,
            source[...],
            left_ref[:, at : at + n],
            right_ref[:, at : at + n],
            cut_ref[k],
            cut_left_ref[:, at : at + n],
            cut_right_ref[:, at : at + n],
            n,
        )

    def body(j, carry):
        for annulus in range(2):
            w = OMEGA / (6.0 + weight[annulus, j])
            weight[annulus, j] = w
            shift[annulus, j] = w * shift[annulus, j]
        return carry

    lax.fori_loop(1, field.shape[1] - 1, body, 0)
    run_sweeps(rad_ref, ghost_ref, field, weight, shift, out_ref)


def later_kernel(
    rad_ref,
    ghost_ref,
    p_ref,
    weight,
    shift,
    left_ref,
    right_ref,
    cut_ref,
    cut_left_ref,
    cut_right_ref,
    out_ref,
    field,
):
    place(
        field,
        p_ref[...],
        left_ref[...],
        right_ref[...],
        cut_ref[...],
        cut_left_ref[...],
        cut_right_ref[...],
        HALO,
    )
    run_sweeps(rad_ref, ghost_ref, field, weight, shift, out_ref)


def ring(size, step):
    return [(i, (i + step) % size) for i in range(size)]


def diagonal_pairs(size, step):
    return [(2 * i + r, 2 * ((i + step) % size) + 1 - r) for i in range(size) for r in range(2)]


def facing_pairs(size, turn, k):
    pairs = []
    for i in range(size):
        pairs.append((2 * ((i - turn + k) % size) + 1, 2 * i))
        pairs.append((2 * ((i + turn + k) % size), 2 * i + 1))
    return pairs


def far_pairs(size, turn):
    return [(2 * i + r, 2 * ((i + (2 * r - 1) * turn) % size) + r) for i in range(size) for r in range(2)]


def ghost_window(edge, offset, radial_index):
    size = lax.axis_size("az")
    cells = edge.shape[0]
    turn = (offset + cells // 2) // cells
    rest = offset - turn * cells
    turn = turn % size
    near = min(size, 16)

    def far(t):
        return lambda e: lax.ppermute(e, ("az", "rad"), far_pairs(size, t * near))

    def branch(t):
        return lambda e: tuple(
            lax.ppermute(e, ("az", "rad"), facing_pairs(size, t, k)) for k in (-1, 0, 1)
        )

    if size > near:
        edge = lax.switch(turn // near, [far(t) for t in range(-(-size // near))], edge)
    blocks = lax.switch(turn % near, [branch(t) for t in range(near)], edge)
    start = cells - HALO + jnp.where(radial_index == 0, -rest, rest)
    return lax.dynamic_slice_in_dim(
        jnp.concatenate(blocks, axis=0), start, cells + 2 * HALO, 0
    )


def per_device(pressure, source, diagonal, rot_offset):
    _, cells, radial_cells, lanes = pressure.shape
    size = lax.axis_size("az")
    radial_index = lax.axis_index("rad")
    rad = radial_index.astype(jnp.int32).reshape(1)
    h, n = HALO, HALO - 1
    rows = radial_cells + 2 * TILE
    extended = jax.ShapeDtypeStruct((2, cells + 2 * h, rows, lanes), jnp.float32)
    own = jax.ShapeDtypeStruct(pressure.shape, jnp.float32)
    vmem = pl.BlockSpec(memory_space=pltpu.VMEM)
    smem = pl.BlockSpec(memory_space=pltpu.SMEM)
    params = pltpu.CompilerParams(vmem_limit_bytes=40 << 20)

    def cut_tile(x):
        return jnp.where(radial_index == 0, x[:, :, radial_cells - TILE :], x[:, :, :TILE])

    def interface(p, step):
        edge = jnp.where(radial_index == 0, p[1, :, 0, :], p[0, :, radial_cells - 1, :])
        offset = rot_offset[0] * step % (cells * size)
        return ghost_window(edge, offset, radial_index)

    def exchange(last, first, cut, cut_last, cut_first):
        left = lax.ppermute(last, "az", ring(size, 1))
        right = lax.ppermute(first, "az", ring(size, -1))
        facing = lax.ppermute(cut, "rad", [(0, 1), (1, 0)])
        corner_left = lax.ppermute(cut_last, ("az", "rad"), diagonal_pairs(size, 1))
        corner_right = lax.ppermute(cut_first, ("az", "rad"), diagonal_pairs(size, -1))
        return left, right, facing, corner_left, corner_right

    def ends(p, s, d):
        last = jnp.concatenate([p[:, cells - h :], s[:, cells - n :], d[:, cells - n :]], axis=1)
        first = jnp.concatenate([p[:, :h], s[:, :n], d[:, :n]], axis=1)
        return last, first

    cuts = [cut_tile(x) for x in (pressure, source, diagonal)]
    moved = exchange(*ends(pressure, source, diagonal), jnp.stack(cuts), *ends(*cuts))
    ghost = interface(pressure, 1)
    pressure, weight, shift = pl.pallas_call(
        first_kernel,
        out_shape=(own, extended, extended),
        in_specs=[smem] + [vmem] * 9,
        out_specs=[vmem] * 3,
        scratch_shapes=[pltpu.VMEM(extended.shape, jnp.float32)],
        compiler_params=params,
        name="first_step",
    )(rad, ghost, pressure, source, diagonal, *moved)
    for step in range(2, STEPS + 1):
        cut = cut_tile(pressure)
        moved = exchange(
            pressure[:, cells - h :], pressure[:, :h], cut, cut[:, cells - h :], cut[:, :h]
        )
        ghost = interface(pressure, step)
        pressure = pl.pallas_call(
            later_kernel,
            out_shape=own,
            in_specs=[smem] + [vmem] * 9,
            out_specs=vmem,
            scratch_shapes=[pltpu.VMEM(extended.shape, jnp.float32)],
            compiler_params=params,
            name="later_step",
        )(rad, ghost, pressure, weight, shift, *moved)
    return pressure


def solution(mesh):
    placed = (
        P(None, "az", "rad", None),
        P(None, "az", "rad", None),
        P(None, "az", "rad", None),
        P(),
    )
    return jax.shard_map(
        per_device,
        mesh=mesh,
        in_specs=placed,
        out_specs=P(None, "az", "rad", None),
        check_vma=False,
    )
```

```python
import jax
import jax.numpy as jnp
from jax import lax
from jax.experimental import pallas as pl
from jax.experimental.pallas import tpu as pltpu
from jax.sharding import PartitionSpec as P

STEPS = 2
SWEEPS = 4
OMEGA = 0.8
TILE = 8
OWN = 2 * TILE
SLOTS = SWEEPS + 2


class Side:
    def __init__(self, low, radial_cells):
        end = OWN + radial_cells
        self.low = low
        self.own = slice(OWN, end)
        self.first = OWN if low else TILE
        self.count = radial_cells + TILE
        self.rows = slice(self.first, self.first + self.count)
        self.cut = slice(end, end + SWEEPS) if low else slice(OWN - SWEEPS, OWN)
        self.tile = slice(end, end + TILE) if low else slice(TILE, OWN)
        self.ghost = OWN - 1 if low else end
        self.edge = OWN if low else end - 1
        self.spare = self.count - 1 if low else 0
        self.facing = 1 if low else 0


def shifted(s, by):
    return slice(s.start + by, s.stop + by)


def axial_sum(x):
    lane = lax.broadcasted_iota(jnp.int32, x.shape, 1)
    last = x.shape[1] - 1
    return jnp.where(lane == 0, 0.0, pltpu.roll(x, 1, 1)) + jnp.where(
        lane == last, 0.0, pltpu.roll(x, last, 1)
    )


def relaxed(column, side, beside, weight, shift):
    here = column[side.rows]
    radial = column[shifted(side.rows, -1)] + column[shifted(side.rows, 1)]
    nbr = beside + radial + axial_sum(here)
    kept = (1.0 - OMEGA) * here
    if shift is not None:
        kept = kept + shift
    return kept + weight * nbr


def mirror(column, side):
    column[side.ghost : side.ghost + 1] = column[side.edge : side.edge + 1]


def on_each_side(rad_ref, radial_cells, body):
    @pl.when(rad_ref[0] == 0)
    def _():
        body(Side(True, radial_cells))

    @pl.when(rad_ref[0] != 0)
    def _():
        body(Side(False, radial_cells))


def copy_all(copies):
    for c in copies:
        c.start()
    for c in copies:
        c.wait()


def trajectories(side, field, other, weight, shift, messages):
    bufs = (field, other)
    for edge, message in enumerate(messages):

        def at(distance, n, edge=edge):
            return distance - 1 if edge == 0 else n - distance

        for k in range(2):
            facing = k == side.facing
            for sweep in range(SWEEPS):
                src, dst = bufs[sweep % 2], bufs[1 - sweep % 2]
                top = src.at[edge, k, at(1, SWEEPS)]
                message[k, sweep] = top[side.rows]
                for j in range(1, SWEEPS - sweep):
                    here = src.at[edge, k, at(j, SWEEPS)]
                    beside = src[edge, k, at(j + 1, SWEEPS), side.rows]
                    if j > 1:
                        beside = beside + src[edge, k, at(j - 1, SWEEPS), side.rows]
                    i = at(j, SWEEPS - 1)
                    new = relaxed(here, side, beside, weight[edge, k, i], shift[edge, k, i])
                    out = dst.at[edge, k, at(j, SWEEPS)]
                    out[side.rows] = new
                    if facing:
                        out[side.ghost : side.ghost + 1] = jnp.zeros((1, new.shape[1]), jnp.float32)
                    else:
                        mirror(out, side)
            if message.shape[1] == SWEEPS:
                continue
            message[k, SWEEPS] = weight[edge, k, at(1, SWEEPS - 1)]
            message[k, SWEEPS + 1] = weight[edge, k, at(2, SWEEPS - 1)]
            if facing:
                row = side.edge - side.first
                message[k, SWEEPS + 1, side.spare : side.spare + 1] = weight[
                    edge, k, at(3, SWEEPS - 1), row : row + 1
                ]


def level_ghosts(side, field):
    for edge in range(2):
        for k in range(2):
            for i in range(SWEEPS):
                column = field.at[edge, k, i]
                if k == side.facing:
                    column[side.ghost : side.ghost + 1] = jnp.zeros(
                        (1, column.shape[1]), jnp.float32
                    )
                else:
                    mirror(column, side)


def first_edges(rad_ref, p_ref, s_ref, d_ref, cut_ref, last, first, field, other, weight, shift, sems):
    cells, radial_cells = p_ref.shape[1:3]

    def body(side):
        own = pl.ds(side.own.start - side.first, radial_cells)
        copies = []
        for edge in range(2):
            for n, source, target, rows in (
                (SWEEPS, p_ref, field, pl.ds(OWN, radial_cells)),
                (SWEEPS - 1, s_ref, shift, own),
                (SWEEPS - 1, d_ref, weight, own),
            ):
                span = pl.ds(0 if edge == 0 else cells - n, n)
                copies.append(
                    pltpu.make_async_copy(
                        source.at[:, span], target.at[edge, :, :, rows, :], sems.at[len(copies)]
                    )
                )
        copy_all(copies)
        cut = slice(side.cut.start - side.first, side.cut.stop - side.first)
        for edge in range(2):
            for at, n, target, rows in (
                (0, SWEEPS, field, side.cut),
                (1, SWEEPS - 1, shift, cut),
                (2, SWEEPS - 1, weight, cut),
            ):
                span = slice(0, n) if edge == 0 else slice(cells - n, cells)
                target[edge, :, :, rows, :] = cut_ref[at, :, span]
        for edge in range(2):
            for k in range(2):
                for i in range(SWEEPS - 1):
                    w = OMEGA / (6.0 + weight[edge, k, i])
                    weight[edge, k, i] = w
                    shift[edge, k, i] = w * shift[edge, k, i]
        level_ghosts(side, field)
        trajectories(side, field, other, weight, shift, (first, last))

    on_each_side(rad_ref, radial_cells, body)


def later_edges(rad_ref, p_ref, w_ref, b_ref, cut_ref, last, first, field, other, weight, shift, sems):
    cells, radial_cells = p_ref.shape[1:3]

    def body(side):
        copies = []
        for edge in range(2):
            for n, source, target in (
                (SWEEPS, p_ref, field.at[edge, :, :, pl.ds(OWN, radial_cells), :]),
                (SWEEPS - 1, b_ref, shift.at[edge]),
                (SWEEPS - 1, w_ref, weight.at[edge]),
            ):
                span = pl.ds(0 if edge == 0 else cells - n, n)
                copies.append(
                    pltpu.make_async_copy(source.at[:, span], target, sems.at[len(copies)])
                )
        copy_all(copies)
        for edge in range(2):
            span = slice(0, SWEEPS) if edge == 0 else slice(cells - SWEEPS, cells)
            field[edge, :, :, side.cut, :] = cut_ref[0, :, span]
        level_ghosts(side, field)
        trajectories(side, field, other, weight, shift, (first, last))

    on_each_side(rad_ref, radial_cells, body)


def correct(side, cells, ghost_ref, left_ref, right_ref, left_w, right_w, field, other, near, near2, weight, shift, out_ref):
    facing = side.facing
    sides = ((left_ref, left_w, 0, 1, -1), (right_ref, right_w, cells + 1, cells, 1))
    lanes = field.shape[-1]
    zero = jnp.zeros((1, lanes), jnp.float32)

    def ghost_at(column):
        g = column - 1 + SWEEPS
        return ghost_ref[g : g + 1]

    for buf in (field, other):
        for j in range(1, cells + 1):
            buf[facing, j, side.ghost : side.ghost + 1] = ghost_at(j)
    for j in range(1, cells + 1):
        mirror(field.at[1 - facing, j], side)
    for e, (message, weights, column, _, step) in enumerate(sides):
        for k in range(2):
            field[k, column, side.rows] = message[k, 0]
            for buf in (near, near2):
                for i in range(3):
                    buf[e, k, i] = jnp.zeros(buf.shape[3:], jnp.float32)
                    if k == facing and i < 2:
                        buf[e, k, i, side.ghost : side.ghost + 1] = ghost_at(column + i * step)
        w3 = weights[facing, SWEEPS + 1, side.spare : side.spare + 1]
        near2[e, facing, 2, side.edge : side.edge + 1] = w3 * ghost_at(column + 2 * step)

    fields, nears = (field, other), (near, near2)
    for sweep in range(SWEEPS):
        src, dst = fields[sweep % 2], fields[1 - sweep % 2]
        nsrc, ndst = nears[sweep % 2], nears[1 - sweep % 2]
        final = sweep == SWEEPS - 1

        def body(j, carry, src=src, dst=dst, final=final):
            for k in range(2):
                beside = src[k, j - 1, side.rows] + src[k, j + 1, side.rows]
                new = relaxed(src.at[k, j], side, beside, weight[k, j - 1], shift[k, j - 1])
                if final:
                    first = side.own.start - side.first
                    out_ref[k, j - 1] = new[first : first + side.own.stop - side.own.start]
                else:
                    dst[k, j, side.rows] = new
                    if k != facing:
                        at = side.edge - side.first
                        dst[k, j, side.ghost : side.ghost + 1] = new[at : at + 1]
            return carry

        lax.fori_loop(1, cells + 1, body, 0, unroll=2)
        if final:
            break
        for e, (message, weights, column, inner, _) in enumerate(sides):
            for k in range(2):
                beside = src[k, inner, side.rows] + nsrc[e, k, 1, side.rows]
                new = relaxed(nsrc.at[e, k, 0], side, beside, weights[k, SWEEPS], None)
                ndst[e, k, 0, side.rows] = new
                dst[k, column, side.rows] = message[k, sweep + 1] + new
                if k != facing:
                    mirror(ndst.at[e, k, 0], side)
                if sweep < SWEEPS - 2:
                    beside = nsrc[e, k, 0, side.rows] + nsrc[e, k, 2, side.rows]
                    new = relaxed(nsrc.at[e, k, 1], side, beside, weights[k, SWEEPS + 1], None)
                    ndst[e, k, 1, side.rows] = new
                    if k != facing:
                        mirror(ndst.at[e, k, 1], side)


def first_correct(
    rad_ref, p_ref, s_ref, d_ref, cut_ref, left_ref, right_ref, ghost_ref,
    out_ref, w_ref, b_ref, field, other, near, near2, weight, shift, sems,
):
    cells, radial_cells = p_ref.shape[1:3]

    def body(side):
        own = pl.ds(side.own.start - side.first, radial_cells)
        copy_all(
            [
                pltpu.make_async_copy(
                    p_ref, field.at[:, pl.ds(1, cells), pl.ds(OWN, radial_cells), :], sems.at[0]
                ),
                pltpu.make_async_copy(s_ref, shift.at[:, :, own, :], sems.at[1]),
                pltpu.make_async_copy(d_ref, weight.at[:, :, own, :], sems.at[2]),
            ]
        )
        cut = slice(side.cut.start - side.first, side.cut.stop - side.first)
        field[:, 1 : cells + 1, side.cut, :] = cut_ref[0]
        shift[:, :, cut, :] = cut_ref[1]
        weight[:, :, cut, :] = cut_ref[2]

        def invert(j, carry):
            for k in range(2):
                w = OMEGA / (6.0 + weight[k, j])
                weight[k, j] = w
                shift[k, j] = w * shift[k, j]
            return carry

        lax.fori_loop(0, cells, invert, 0)
        keep = [
            pltpu.make_async_copy(weight, w_ref, sems.at[0]),
            pltpu.make_async_copy(shift, b_ref, sems.at[1]),
        ]
        for c in keep:
            c.start()
        correct(
            side, cells, ghost_ref, left_ref, right_ref, left_ref, right_ref, field, other, near, near2, weight, shift, out_ref
        )
        for c in keep:
            c.wait()

    on_each_side(rad_ref, radial_cells, body)


def later_correct(
    rad_ref, p_ref, w_ref, b_ref, cut_ref, left_ref, right_ref, ghost_ref, left_w, right_w,
    out_ref, field, other, near, near2, weight, shift, sems,
):
    cells, radial_cells = p_ref.shape[1:3]

    def body(side):
        copy_all(
            [
                pltpu.make_async_copy(
                    p_ref, field.at[:, pl.ds(1, cells), pl.ds(OWN, radial_cells), :], sems.at[0]
                ),
                pltpu.make_async_copy(w_ref, weight, sems.at[1]),
                pltpu.make_async_copy(b_ref, shift, sems.at[2]),
            ]
        )
        field[:, 1 : cells + 1, side.cut, :] = cut_ref[0]
        correct(
            side, cells, ghost_ref, left_ref, right_ref, left_w, right_w, field, other, near, near2, weight, shift, out_ref
        )

    on_each_side(rad_ref, radial_cells, body)


def ring(size, step):
    return [(i, (i + step) % size) for i in range(size)]


def facing_pairs(size, turn, k):
    pairs = []
    for i in range(size):
        pairs.append((2 * ((i - turn + k) % size) + 1, 2 * i))
        pairs.append((2 * ((i + turn + k) % size), 2 * i + 1))
    return pairs


def far_pairs(size, turn):
    return [(2 * i + r, 2 * ((i + (2 * r - 1) * turn) % size) + r) for i in range(size) for r in range(2)]


def ghost_window(edge, offset, radial_index):
    size = lax.axis_size("az")
    cells = edge.shape[0]
    turn = (offset + cells // 2) // cells
    rest = offset - turn * cells
    turn = turn % size
    near = min(size, 16)

    def far(t):
        return lambda e: lax.ppermute(e, ("az", "rad"), far_pairs(size, t * near))

    def branch(t):
        return lambda e: tuple(
            lax.ppermute(e, ("az", "rad"), facing_pairs(size, t, k)) for k in (-1, 0, 1)
        )

    if size > near:
        edge = lax.switch(turn // near, [far(t) for t in range(-(-size // near))], edge)
    blocks = lax.switch(turn % near, [branch(t) for t in range(near)], edge)
    start = cells - SWEEPS + jnp.where(radial_index == 0, -rest, rest)
    return lax.dynamic_slice_in_dim(
        jnp.concatenate(blocks, axis=0), start, cells + 2 * SWEEPS, 0
    )


def per_device(pressure, source, diagonal, rot_offset):
    _, cells, radial_cells, lanes = pressure.shape
    size = lax.axis_size("az")
    radial_index = lax.axis_index("rad")
    rad = radial_index.astype(jnp.int32).reshape(1)
    rows, span = radial_cells + 4 * TILE, radial_cells + TILE
    f32 = jnp.float32
    own = jax.ShapeDtypeStruct(pressure.shape, f32)
    kept = jax.ShapeDtypeStruct((2, cells, span, lanes), f32)
    vmem = pl.BlockSpec(memory_space=pltpu.VMEM)
    smem = pl.BlockSpec(memory_space=pltpu.SMEM)
    hbm = pl.BlockSpec(memory_space=pl.ANY)
    params = pltpu.CompilerParams(vmem_limit_bytes=40 << 20)
    edge_scratch = [
        pltpu.VMEM((2, 2, SWEEPS, rows, lanes), f32),
        pltpu.VMEM((2, 2, SWEEPS, rows, lanes), f32),
        pltpu.VMEM((2, 2, SWEEPS - 1, span, lanes), f32),
        pltpu.VMEM((2, 2, SWEEPS - 1, span, lanes), f32),
        pltpu.SemaphoreType.DMA((6,)),
    ]
    correct_scratch = [
        pltpu.VMEM((2, cells + 2, rows, lanes), f32),
        pltpu.VMEM((2, cells + 2, rows, lanes), f32),
        pltpu.VMEM((2, 2, 3, rows, lanes), f32),
        pltpu.VMEM((2, 2, 3, rows, lanes), f32),
        pltpu.VMEM(kept.shape, f32),
        pltpu.VMEM(kept.shape, f32),
        pltpu.SemaphoreType.DMA((3,)),
    ]

    def call(kernel, name, out_shape, in_specs, out_specs, scratch, *operands):
        return pl.pallas_call(
            kernel,
            out_shape=out_shape,
            in_specs=in_specs,
            out_specs=out_specs,
            scratch_shapes=scratch,
            compiler_params=params,
            name=name,
        )(*operands)

    def swap_cut(arrays):
        cuts = [
            jnp.where(radial_index == 0, x[:, :, radial_cells - SWEEPS :], x[:, :, :SWEEPS])
            for x in arrays
        ]
        return lax.ppermute(jnp.stack(cuts), "rad", [(0, 1), (1, 0)])

    def exchange(last, first):
        left = lax.ppermute(last, "az", ring(size, 1))
        right = lax.ppermute(first, "az", ring(size, -1))
        return left, right

    def interface(edge, step):
        offset = rot_offset[0] * step % (cells * size)
        return ghost_window(edge, offset, radial_index)

    fields = (pressure, source, diagonal)
    for step in range(1, STEPS + 1):
        edge = jnp.where(
            radial_index == 0, pressure[1, :, 0, :], pressure[0, :, radial_cells - 1, :]
        )
        cut = swap_cut(fields if step == 1 else (pressure,))
        slots = SLOTS if step == 1 else SWEEPS
        message = jax.ShapeDtypeStruct((2, slots, span, lanes), f32)
        last, first = call(
            first_edges if step == 1 else later_edges,
            "edges",
            (message, message),
            [smem] + [hbm] * 3 + [vmem],
            [vmem] * 2,
            edge_scratch,
            rad,
            *fields,
            cut,
        )
        edge, last, first = lax.optimization_barrier((edge, last, first))
        left, right = exchange(last, first)
        ghost = interface(edge, step)
        operands = (rad, *fields, cut, left, right, ghost)
        in_specs = [smem] + [hbm] * 3 + [vmem] * 4
        if step == 1:
            weights = (left, right)
            pressure, weight, shift = call(
                first_correct,
                "correct",
                (own, kept, kept),
                in_specs,
                [vmem, hbm, hbm],
                correct_scratch,
                *operands,
            )
        else:
            pressure = call(
                later_correct,
                "correct",
                own,
                in_specs + [vmem] * 2,
                vmem,
                correct_scratch,
                *operands,
                *weights,
            )
        fields = (pressure, weight, shift)
    return pressure


def solution(mesh):
    placed = (
        P(None, "az", "rad", None),
        P(None, "az", "rad", None),
        P(None, "az", "rad", None),
        P(),
    )
    return jax.shard_map(
        per_device,
        mesh=mesh,
        in_specs=placed,
        out_specs=P(None, "az", "rad", None),
        check_vma=False,
    )
```

```python
import functools

import jax
import jax.numpy as jnp
from jax import lax
from jax.experimental import pallas as pl
from jax.experimental.pallas import tpu as pltpu
from jax.sharding import PartitionSpec as P

STEPS = 2
SWEEPS = 4
OMEGA = 0.8
TILE = 8
OWN = 2 * TILE
SLOTS = SWEEPS + 2


class Side:
    def __init__(self, low, radial_cells):
        end = OWN + radial_cells
        self.low = low
        self.own = slice(OWN, end)
        self.first = OWN if low else TILE
        self.count = radial_cells + TILE
        self.rows = slice(self.first, self.first + self.count)
        self.cut = slice(end, end + SWEEPS) if low else slice(OWN - SWEEPS, OWN)
        self.tile = slice(end, end + TILE) if low else slice(TILE, OWN)
        self.ghost = OWN - 1 if low else end
        self.edge = OWN if low else end - 1
        self.spare = self.count - 1 if low else 0
        self.facing = 1 if low else 0


def shifted(s, by):
    return slice(s.start + by, s.stop + by)


def axial_sum(x):
    lane = lax.broadcasted_iota(jnp.int32, x.shape, 1)
    last = x.shape[1] - 1
    return jnp.where(lane == 0, 0.0, pltpu.roll(x, 1, 1)) + jnp.where(
        lane == last, 0.0, pltpu.roll(x, last, 1)
    )


def relaxed(column, side, beside, weight, shift):
    here = column[side.rows]
    radial = column[shifted(side.rows, -1)] + column[shifted(side.rows, 1)]
    nbr = beside + radial + axial_sum(here)
    kept = (1.0 - OMEGA) * here
    if shift is not None:
        kept = kept + shift
    return kept + weight * nbr


def mirror(column, side):
    column[side.ghost : side.ghost + 1] = column[side.edge : side.edge + 1]


def on_each_side(rad_ref, radial_cells, body):
    @pl.when(rad_ref[0] == 0)
    def _():
        body(Side(True, radial_cells))

    @pl.when(rad_ref[0] != 0)
    def _():
        body(Side(False, radial_cells))


def copy_all(copies):
    for c in copies:
        c.start()
    for c in copies:
        c.wait()


def trajectories(side, field, other, weight, shift, messages):
    bufs = (field, other)
    for edge, message in enumerate(messages):

        def at(distance, n, edge=edge):
            return distance - 1 if edge == 0 else n - distance

        for k in range(2):
            facing = k == side.facing
            for sweep in range(SWEEPS):
                src, dst = bufs[sweep % 2], bufs[1 - sweep % 2]
                top = src.at[edge, k, at(1, SWEEPS)]
                message[k, sweep] = top[side.rows]
                for j in range(1, SWEEPS - sweep):
                    here = src.at[edge, k, at(j, SWEEPS)]
                    beside = src[edge, k, at(j + 1, SWEEPS), side.rows]
                    if j > 1:
                        beside = beside + src[edge, k, at(j - 1, SWEEPS), side.rows]
                    i = at(j, SWEEPS - 1)
                    new = relaxed(here, side, beside, weight[edge, k, i], shift[edge, k, i])
                    out = dst.at[edge, k, at(j, SWEEPS)]
                    out[side.rows] = new
                    if facing:
                        out[side.ghost : side.ghost + 1] = jnp.zeros((1, new.shape[1]), jnp.float32)
                    else:
                        mirror(out, side)
            if message.shape[1] == SWEEPS:
                continue
            message[k, SWEEPS] = weight[edge, k, at(1, SWEEPS - 1)]
            message[k, SWEEPS + 1] = weight[edge, k, at(2, SWEEPS - 1)]
            if facing:
                row = side.edge - side.first
                message[k, SWEEPS + 1, side.spare : side.spare + 1] = weight[
                    edge, k, at(3, SWEEPS - 1), row : row + 1
                ]


def level_ghosts(side, field):
    for edge in range(2):
        for k in range(2):
            for i in range(SWEEPS):
                column = field.at[edge, k, i]
                if k == side.facing:
                    column[side.ghost : side.ghost + 1] = jnp.zeros(
                        (1, column.shape[1]), jnp.float32
                    )
                else:
                    mirror(column, side)


def edges(known, rad_ref, p_ref, b_ref, w_ref, cut_ref, ghost_ref, last, first, *scratch):
    field, other, weight, shift, sems = scratch
    cells, radial_cells = p_ref.shape[1:3]
    n = SWEEPS - 1

    def body(side):
        inner = pl.ds(OWN, radial_cells)
        own = pl.ds(0, side.count) if known else pl.ds(OWN - side.first, radial_cells)
        copies = []
        for source, target, count, rows in (
            (p_ref, field, SWEEPS, inner),
            (b_ref, shift, n, own),
            (w_ref, weight, n, own),
        ):
            for edge in range(2):
                span = pl.ds(0 if edge == 0 else cells - count, count)
                copies.append(
                    pltpu.make_async_copy(
                        source.at[:, span], target.at[edge, :, :, rows, :], sems.at[len(copies)]
                    )
                )
        copy_all(copies)
        cut = shifted(side.cut, -side.first)
        for edge in range(2):
            for at, count, target, rows in (
                (0, SWEEPS, field, side.cut),
                (1, n, shift, cut),
                (2, n, weight, cut),
            )[: 1 if known else 3]:
                span = slice(0, count) if edge == 0 else slice(cells - count, cells)
                target[edge, :, :, rows, :] = cut_ref[at, :, span]
        if not known:
            for edge in range(2):
                for k in range(2):
                    for i in range(n):
                        w = OMEGA / (6.0 + weight[edge, k, i])
                        weight[edge, k, i] = w
                        shift[edge, k, i] = w * shift[edge, k, i]
        level_ghosts(side, field)
        trajectories(side, field, other, weight, shift, (first, last))
        for edge, message in enumerate((first, last)):
            for j in range(3):
                g = j if edge == 0 else cells - 1 - j
                message[side.facing, j, side.spare : side.spare + 1] = ghost_ref[g : g + 1]

    on_each_side(rad_ref, radial_cells, body)


def interior(known, rad_ref, p_ref, b_ref, w_ref, cut_ref, ghost_ref, *rest):
    if known:
        out_ref, stash, levels, last, weight, shift, sems = rest
    else:
        out_ref, stash, b_out, w_out, levels, last, weight, shift, sems = rest
    cells, radial_cells = p_ref.shape[1:3]

    def body(side):
        own = pl.ds(0, side.count) if known else pl.ds(OWN - side.first, radial_cells)
        copy_all(
            [
                pltpu.make_async_copy(
                    p_ref, levels.at[0, :, :, pl.ds(OWN, radial_cells), :], sems.at[0]
                ),
                pltpu.make_async_copy(b_ref, shift.at[:, :, own, :], sems.at[1]),
                pltpu.make_async_copy(w_ref, weight.at[:, :, own, :], sems.at[2]),
            ]
        )
        levels[0, :, :, side.cut, :] = cut_ref[0]
        pending = []
        if not known:
            cut = shifted(side.cut, -side.first)
            shift[:, :, cut, :] = cut_ref[1]
            weight[:, :, cut, :] = cut_ref[2]

            def invert(j, carry):
                for k in range(2):
                    w = OMEGA / (6.0 + weight[k, j])
                    weight[k, j] = w
                    shift[k, j] = w * shift[k, j]
                return carry

            lax.fori_loop(0, cells, invert, 0)
            pending += [
                pltpu.make_async_copy(shift, b_out, sems.at[1]),
                pltpu.make_async_copy(weight, w_out, sems.at[2]),
            ]
            for c in pending:
                c.start()
        for j in range(cells):
            mirror(levels.at[0, 1 - side.facing, j], side)
            for n in range(SWEEPS):
                levels[n, side.facing, j, side.ghost : side.ghost + 1] = ghost_ref[j : j + 1]
        for n in range(SWEEPS):
            final = n == SWEEPS - 1

            def step(j, carry, n=n, final=final):
                for k in range(2):
                    beside = levels[n, k, j - 1, side.rows] + levels[n, k, j + 1, side.rows]
                    new = relaxed(levels.at[n, k, j], side, beside, weight[k, j], shift[k, j])
                    if final:
                        at = OWN - side.first
                        last[k, j - SWEEPS] = new[at : at + radial_cells]
                    else:
                        levels[n + 1, k, j, side.rows] = new
                        if k != side.facing:
                            at = side.edge - side.first
                            levels[n + 1, k, j, side.ghost : side.ghost + 1] = new[at : at + 1]
                return carry

            lax.fori_loop(n + 1, cells - 1 - n, step, 0, unroll=2)
            if not final:
                for e, at in enumerate((n + 1, cells - 3 - n)):
                    pending.append(
                        pltpu.make_async_copy(
                            levels.at[n + 1, :, pl.ds(at, 2)],
                            stash.at[e, n],
                            sems.at[3 + 2 * n + e],
                        )
                    )
                    pending[-1].start()
        inner = pltpu.make_async_copy(
            last, out_ref.at[:, pl.ds(SWEEPS, cells - 2 * SWEEPS)], sems.at[0]
        )
        inner.start()
        pending.append(inner)
        for c in pending:
            c.wait()

    on_each_side(rad_ref, radial_cells, body)


def finish(known, rad_ref, p_ref, b_ref, w_ref, stash, cut_ref, ghost_ref, left_ref, right_ref, *rest):
    if known:
        left_w, right_w, _, out_ref, *rest = rest
    else:
        _, out_ref, *rest = rest
    levels, last, near, near2, weight, shift, moved, moved_w, sems = rest
    cells, radial_cells = p_ref.shape[1:3]
    width = SWEEPS + 2

    def at(e, distance):
        return distance if e == 0 else width - 1 - distance

    def body(side):
        facing = side.facing
        copies = []

        def fetch(source, target):
            copies.append(pltpu.make_async_copy(source, target, sems.at[len(copies)]))

        for e, message in enumerate((left_ref, right_ref)):
            fetch(message, moved.at[e])
            if known:
                fetch((left_w, right_w)[e].at[:, pl.ds(SWEEPS, 2)], moved_w.at[e])
            ends = pl.ds(0 if e == 0 else cells - SWEEPS, SWEEPS)
            fetch(b_ref.at[:, ends], shift.at[e])
            fetch(w_ref.at[:, ends], weight.at[e])
            fetch(
                p_ref.at[:, pl.ds(0 if e == 0 else cells - 2, 2)],
                levels.at[0, e, :, pl.ds(min(at(e, 1), at(e, 2)), 2), pl.ds(OWN, radial_cells), :],
            )
            for n in range(1, SWEEPS):
                fetch(
                    stash.at[e, n - 1],
                    levels.at[n, e, :, pl.ds(min(at(e, n + 1), at(e, n + 2)), 2)],
                )
        copy_all(copies)

        def weights(e, k, i):
            return moved_w[e, k, i] if known else moved[e, k, SWEEPS + i]

        lanes = levels.shape[-1]
        for e in range(2):
            for d in range(1, 3):
                column = d - 1 if e == 0 else cells - d
                for k in range(2):
                    target = levels.at[0, e, k, at(e, d)]
                    target[side.cut, :] = cut_ref[0, k, column]
                    if k != facing:
                        mirror(target, side)
            for d in range(1, SWEEPS):
                column = d - 1 if e == 0 else cells - d
                for n in range(SWEEPS):
                    if n >= d or (n == 0 and d < 3):
                        levels[n, e, facing, at(e, d), side.ghost : side.ghost + 1] = ghost_ref[
                            column : column + 1
                        ]
            beyond = [moved[e, facing, j, side.spare : side.spare + 1] for j in range(3)]
            for k in range(2):
                levels[0, e, k, at(e, 0), side.rows] = moved[e, k, 0]
                for buf in (near, near2):
                    for i in range(3):
                        buf[e, k, i] = jnp.zeros(buf.shape[3:], jnp.float32)
                        if k == facing and i < 2:
                            buf[e, k, i, side.ghost : side.ghost + 1] = beyond[i]
            w3 = (moved_w if known else moved)[
                e, facing, 1 if known else SWEEPS + 1, side.spare : side.spare + 1
            ]
            near2[e, facing, 2, side.edge : side.edge + 1] = w3 * beyond[2]
        nears = (near, near2)
        for n in range(SWEEPS):
            final = n == SWEEPS - 1
            src, dst = nears[n % 2], nears[1 - n % 2]
            for e in range(2):
                for k in range(2):
                    for d in range(1, n + 2):
                        i = d - 1 if e == 0 else SWEEPS - d
                        beside = (
                            levels[n, e, k, at(e, d - 1), side.rows]
                            + levels[n, e, k, at(e, d + 1), side.rows]
                        )
                        new = relaxed(
                            levels.at[n, e, k, at(e, d)],
                            side,
                            beside,
                            weight[e, k, i],
                            shift[e, k, i],
                        )
                        if final:
                            first = OWN - side.first
                            last[e, k, i] = new[first : first + radial_cells]
                        else:
                            levels[n + 1, e, k, at(e, d), side.rows] = new
                            if k != facing:
                                mirror(levels.at[n + 1, e, k, at(e, d)], side)
                    if final:
                        continue
                    beside = levels[n, e, k, at(e, 1), side.rows] + src[e, k, 1, side.rows]
                    new = relaxed(src.at[e, k, 0], side, beside, weights(e, k, 0), None)
                    dst[e, k, 0, side.rows] = new
                    levels[n + 1, e, k, at(e, 0), side.rows] = moved[e, k, n + 1] + new
                    if k != facing:
                        mirror(dst.at[e, k, 0], side)
                    if n < SWEEPS - 2:
                        beside = src[e, k, 0, side.rows] + src[e, k, 2, side.rows]
                        new = relaxed(src.at[e, k, 1], side, beside, weights(e, k, 1), None)
                        dst[e, k, 1, side.rows] = new
                        if k != facing:
                            mirror(dst.at[e, k, 1], side)
        copy_all(
            [
                pltpu.make_async_copy(
                    last.at[e],
                    out_ref.at[:, pl.ds(0 if e == 0 else cells - SWEEPS, SWEEPS)],
                    sems.at[e],
                )
                for e in range(2)
            ]
        )

    on_each_side(rad_ref, radial_cells, body)


def ring(size, step):
    return [(i, (i + step) % size) for i in range(size)]


def facing_pairs(size, turn, k):
    pairs = []
    for i in range(size):
        pairs.append((2 * ((i - turn - 1 + k) % size) + 1, 2 * i))
        pairs.append((2 * ((i + turn + k) % size), 2 * i + 1))
    return pairs


def far_pairs(size, turn):
    return [(2 * i + r, 2 * ((i + (2 * r - 1) * turn) % size) + r) for i in range(size) for r in range(2)]


def facing_cells(edge, offset, radial_index):
    size = lax.axis_size("az")
    cells = edge.shape[0]
    turn, rest = offset // cells, offset % cells
    near = min(size, 16)

    def far(t):
        return lambda e: lax.ppermute(e, ("az", "rad"), far_pairs(size, t * near))

    def branch(t):
        return lambda e: tuple(
            lax.ppermute(e, ("az", "rad"), facing_pairs(size, t, k)) for k in range(2)
        )

    if size > near:
        edge = lax.switch(turn // near, [far(t) for t in range(-(-size // near))], edge)
    blocks = lax.switch(turn % near, [branch(t) for t in range(near)], edge)
    start = jnp.where(radial_index == 0, cells - rest, rest)
    return lax.dynamic_slice_in_dim(jnp.concatenate(blocks, axis=0), start, cells, 0)


def per_device(pressure, source, diagonal, rot_offset):
    _, cells, radial_cells, lanes = pressure.shape
    size = lax.axis_size("az")
    radial_index = lax.axis_index("rad")
    rad = radial_index.astype(jnp.int32).reshape(1)
    rows, span = radial_cells + 4 * TILE, radial_cells + TILE

    def array(*shape):
        return jax.ShapeDtypeStruct(shape, jnp.float32)

    def scratch(*shape):
        return pltpu.VMEM(shape, jnp.float32)

    own = array(*pressure.shape)
    kept = array(2, cells, span, lanes)
    stash = array(2, SWEEPS - 1, 2, 2, rows, lanes)
    vmem = pl.BlockSpec(memory_space=pltpu.VMEM)
    smem = pl.BlockSpec(memory_space=pltpu.SMEM)
    hbm = pl.BlockSpec(memory_space=pltpu.HBM)

    def call(kernel, known, out_shape, in_specs, out_specs, scratch_shapes, operands, cells_done, **more):
        work = 2 * cells_done * span * lanes
        return pl.pallas_call(
            functools.partial(kernel, known),
            out_shape=out_shape,
            in_specs=in_specs,
            out_specs=out_specs,
            scratch_shapes=scratch_shapes,
            compiler_params=pltpu.CompilerParams(vmem_limit_bytes=40 << 20),
            cost_estimate=pl.CostEstimate(
                flops=12 * work, bytes_accessed=8 * work, transcendentals=0
            ),
            name=kernel.__name__,
            **more,
        )(*operands)

    def swap_cut(arrays):
        cuts = [
            jnp.where(radial_index == 0, x[:, :, radial_cells - SWEEPS :], x[:, :, :SWEEPS])
            for x in arrays
        ]
        return jnp.stack(cuts)

    fields = (pressure, source, diagonal)
    for step in range(1, STEPS + 1):
        known = step > 1
        p = fields[0]
        edge = jnp.where(radial_index == 0, p[1, :, 0, :], p[0, :, radial_cells - 1, :])
        cut = swap_cut(fields[:1] if known else fields)
        edge, cut = lax.optimization_barrier((edge, cut))
        cut = lax.ppermute(cut, "rad", [(0, 1), (1, 0)])
        offset = rot_offset[0] * step % (cells * size)
        ghost = facing_cells(edge, offset, radial_index)
        operands = (rad, *fields, cut, ghost)
        specs = [smem] + [hbm] * 3 + [vmem] * 2
        message = array(2, SWEEPS if known else SLOTS, span, lanes)
        last, first = call(
            edges,
            known,
            (message, message),
            specs,
            [vmem] * 2,
            [
                scratch(2, 2, SWEEPS, rows, lanes),
                scratch(2, 2, SWEEPS, rows, lanes),
                scratch(2, 2, SWEEPS - 1, span, lanes),
                scratch(2, 2, SWEEPS - 1, span, lanes),
                pltpu.SemaphoreType.DMA((6,)),
            ],
            operands,
            12,
        )
        left = lax.ppermute(last, "az", ring(size, 1))
        right = lax.ppermute(first, "az", ring(size, -1))
        inner, saved, *made = call(
            interior,
            known,
            (own, stash) if known else (own, stash, kept, kept),
            specs,
            [hbm] * (2 if known else 4),
            [
                scratch(SWEEPS, 2, cells, rows, lanes),
                scratch(2, cells - 2 * SWEEPS, radial_cells, lanes),
                scratch(*kept.shape),
                scratch(*kept.shape),
                pltpu.SemaphoreType.DMA((9,)),
            ],
            operands,
            44,
        )
        if not known:
            shift, weight = made
            beyond = (left, right)
        operands = (rad, p, shift, weight, saved, cut, ghost, left, right)
        specs = [smem] + [hbm] * 4 + [vmem] * 2 + [hbm] * 2
        if known:
            operands += beyond
            specs += [hbm] * 2
        pressure = call(
            finish,
            known,
            own,
            specs + [hbm],
            hbm,
            [
                scratch(SWEEPS, 2, 2, SWEEPS + 2, rows, lanes),
                scratch(2, 2, SWEEPS, radial_cells, lanes),
                scratch(2, 2, 3, rows, lanes),
                scratch(2, 2, 3, rows, lanes),
                scratch(2, 2, SWEEPS, span, lanes),
                scratch(2, 2, SWEEPS, span, lanes),
                scratch(2, *message.shape),
                scratch(2, 2, 2, span, lanes),
                pltpu.SemaphoreType.DMA((16,)),
            ],
            (*operands, inner),
            26,
            input_output_aliases={len(operands): 0},
        )
        fields = (pressure, shift, weight)
    return pressure


def solution(mesh):
    placed = (
        P(None, "az", "rad", None),
        P(None, "az", "rad", None),
        P(None, "az", "rad", None),
        P(),
    )
    return jax.shard_map(
        per_device,
        mesh=mesh,
        in_specs=placed,
        out_specs=P(None, "az", "rad", None),
        check_vma=False,
    )
```

```python
import functools

import jax
import jax.numpy as jnp
from jax import lax
from jax.experimental import pallas as pl
from jax.experimental.pallas import tpu as pltpu
from jax.sharding import PartitionSpec as P

STEPS = 2
SWEEPS = 4
OMEGA = 0.8
TILE = 8
OWN = 2 * TILE
SLOTS = SWEEPS + 2


class Side:
    def __init__(self, low, radial_cells):
        end = OWN + radial_cells
        self.low = low
        self.own = slice(OWN, end)
        self.first = OWN if low else TILE
        self.count = radial_cells + TILE
        self.rows = slice(self.first, self.first + self.count)
        self.cut = slice(end, end + SWEEPS) if low else slice(OWN - SWEEPS, OWN)
        self.tile = slice(end, end + TILE) if low else slice(TILE, OWN)
        self.ghost = OWN - 1 if low else end
        self.edge = OWN if low else end - 1
        self.spare = self.count - 1 if low else 0
        self.facing = 1 if low else 0
        self.sent = slice(radial_cells - SWEEPS, radial_cells) if low else slice(0, SWEEPS)
        self.sent_tile = radial_cells - TILE if low else 0
        self.edge_tile = 0 if low else radial_cells - TILE


def shifted(s, by):
    return slice(s.start + by, s.stop + by)


def axial_sum(x):
    lane = lax.broadcasted_iota(jnp.int32, x.shape, 1)
    last = x.shape[1] - 1
    return jnp.where(lane == 0, 0.0, pltpu.roll(x, 1, 1)) + jnp.where(
        lane == last, 0.0, pltpu.roll(x, last, 1)
    )


def relaxed(column, side, beside, weight, shift):
    here = column[side.rows]
    radial = column[shifted(side.rows, -1)] + column[shifted(side.rows, 1)]
    nbr = beside + radial + axial_sum(here)
    kept = (1.0 - OMEGA) * here
    if shift is not None:
        kept = kept + shift
    return kept + weight * nbr


def mirror(column, side):
    column[side.ghost : side.ghost + 1] = column[side.edge : side.edge + 1]


def on_each_side(rad_ref, radial_cells, body):
    @pl.when(rad_ref[0] == 0)
    def _():
        body(Side(True, radial_cells))

    @pl.when(rad_ref[0] != 0)
    def _():
        body(Side(False, radial_cells))


def copy_all(copies):
    for c in copies:
        c.start()
    for c in copies:
        c.wait()


def trajectories(side, field, other, weight, shift, messages):
    bufs = (field, other)
    for edge, message in enumerate(messages):

        def at(distance, n, edge=edge):
            return distance - 1 if edge == 0 else n - distance

        for k in range(2):
            facing = k == side.facing
            for sweep in range(SWEEPS):
                src, dst = bufs[sweep % 2], bufs[1 - sweep % 2]
                top = src.at[edge, k, at(1, SWEEPS)]
                message[k, sweep] = top[side.rows]
                for j in range(1, SWEEPS - sweep):
                    here = src.at[edge, k, at(j, SWEEPS)]
                    beside = src[edge, k, at(j + 1, SWEEPS), side.rows]
                    if j > 1:
                        beside = beside + src[edge, k, at(j - 1, SWEEPS), side.rows]
                    i = at(j, SWEEPS - 1)
                    new = relaxed(here, side, beside, weight[edge, k, i], shift[edge, k, i])
                    out = dst.at[edge, k, at(j, SWEEPS)]
                    out[side.rows] = new
                    if facing:
                        out[side.ghost : side.ghost + 1] = jnp.zeros((1, new.shape[1]), jnp.float32)
                    else:
                        mirror(out, side)
            if message.shape[1] == SWEEPS:
                continue
            message[k, SWEEPS] = weight[edge, k, at(1, SWEEPS - 1)]
            message[k, SWEEPS + 1] = weight[edge, k, at(2, SWEEPS - 1)]
            if facing:
                row = side.edge - side.first
                message[k, SWEEPS + 1, side.spare : side.spare + 1] = weight[
                    edge, k, at(3, SWEEPS - 1), row : row + 1
                ]


def level_ghosts(side, field):
    for edge in range(2):
        for k in range(2):
            for i in range(SWEEPS):
                column = field.at[edge, k, i]
                if k == side.facing:
                    column[side.ghost : side.ghost + 1] = jnp.zeros(
                        (1, column.shape[1]), jnp.float32
                    )
                else:
                    mirror(column, side)


def pack(rad_ref, p_ref, s_ref, d_ref, cut_ref, edge_ref, tiles, edge_tiles, sems):
    radial_cells = p_ref.shape[2]

    def body(side):
        rows = pl.ds(side.sent_tile, TILE)
        copies = [
            pltpu.make_async_copy(x.at[:, :, rows, :], tiles.at[i], sems.at[i])
            for i, x in enumerate((p_ref, s_ref, d_ref))
        ]
        rows = pl.ds(side.edge_tile, TILE)
        copies.append(
            pltpu.make_async_copy(p_ref.at[side.facing, :, rows, :], edge_tiles, sems.at[3])
        )
        copy_all(copies)
        cut_ref[...] = tiles[:, :, :, shifted(side.sent, -side.sent_tile), :]
        at = side.edge - OWN - side.edge_tile
        for j in range(edge_ref.shape[0]):
            edge_ref[j : j + 1] = edge_tiles[j, at : at + 1]

    on_each_side(rad_ref, radial_cells, body)


def edges(known, rad_ref, p_ref, b_ref, w_ref, cut_ref, near_ref, far_ref, last, first, ghost_ref, *scratch):
    field, other, weight, shift, wide, sems = scratch
    cells, radial_cells = p_ref.shape[1:3]
    n = SWEEPS - 1

    def body(side):
        inner = pl.ds(OWN, radial_cells)
        own = pl.ds(0, side.count) if known else pl.ds(OWN - side.first, radial_cells)
        copies = []
        for source, target, count, rows in (
            (p_ref, field, SWEEPS, inner),
            (b_ref, shift, n, own),
            (w_ref, weight, n, own),
        ):
            for edge in range(2):
                span = pl.ds(0 if edge == 0 else cells - count, count)
                copies.append(
                    pltpu.make_async_copy(
                        source.at[:, span], target.at[edge, :, :, rows, :], sems.at[len(copies)]
                    )
                )
        copy_all(copies)
        cut = shifted(side.cut, -side.first)
        for edge in range(2):
            for at, count, target, rows in (
                (0, SWEEPS, field, side.cut),
                (1, n, shift, cut),
                (2, n, weight, cut),
            )[: 1 if known else 3]:
                span = slice(0, count) if edge == 0 else slice(cells - count, cells)
                target[edge, :, :, rows, :] = cut_ref[at, :, span]
        if not known:
            for edge in range(2):
                for k in range(2):
                    for i in range(n):
                        w = OMEGA / (6.0 + weight[edge, k, i])
                        weight[edge, k, i] = w
                        shift[edge, k, i] = w * shift[edge, k, i]
        level_ghosts(side, field)
        trajectories(side, field, other, weight, shift, (first, last))
        wide[:cells] = near_ref[...]
        wide[cells:] = far_ref[...]
        ghost_ref[...] = wide[pl.ds(rad_ref[1], cells), :]
        for edge, message in enumerate((first, last)):
            for j in range(3):
                g = j if edge == 0 else cells - 1 - j
                message[side.facing, j, side.spare : side.spare + 1] = ghost_ref[g : g + 1]

    on_each_side(rad_ref, radial_cells, body)


def interior(known, rad_ref, p_ref, b_ref, w_ref, cut_ref, ghost_ref, *rest):
    if known:
        out_ref, stash, levels, last, weight, shift, sems = rest
    else:
        out_ref, stash, cut_out, edge_out, b_out, w_out, *rest = rest
        levels, last, weight, shift, sems = rest
    cells, radial_cells = p_ref.shape[1:3]

    def body(side):
        own = pl.ds(0, side.count) if known else pl.ds(OWN - side.first, radial_cells)
        copy_all(
            [
                pltpu.make_async_copy(
                    p_ref, levels.at[0, :, :, pl.ds(OWN, radial_cells), :], sems.at[0]
                ),
                pltpu.make_async_copy(b_ref, shift.at[:, :, own, :], sems.at[1]),
                pltpu.make_async_copy(w_ref, weight.at[:, :, own, :], sems.at[2]),
            ]
        )
        levels[0, :, :, side.cut, :] = cut_ref[0]
        pending = []
        if not known:
            cut = shifted(side.cut, -side.first)
            shift[:, :, cut, :] = cut_ref[1]
            weight[:, :, cut, :] = cut_ref[2]

            def invert(j, carry):
                for k in range(2):
                    w = OMEGA / (6.0 + weight[k, j])
                    weight[k, j] = w
                    shift[k, j] = w * shift[k, j]
                return carry

            lax.fori_loop(0, cells, invert, 0)
            pending += [
                pltpu.make_async_copy(shift, b_out, sems.at[1]),
                pltpu.make_async_copy(weight, w_out, sems.at[2]),
            ]
            for c in pending:
                c.start()
        for j in range(cells):
            mirror(levels.at[0, 1 - side.facing, j], side)
            for n in range(SWEEPS):
                levels[n, side.facing, j, side.ghost : side.ghost + 1] = ghost_ref[j : j + 1]
        for n in range(SWEEPS):
            final = n == SWEEPS - 1

            def step(j, carry, n=n, final=final):
                for k in range(2):
                    beside = levels[n, k, j - 1, side.rows] + levels[n, k, j + 1, side.rows]
                    new = relaxed(levels.at[n, k, j], side, beside, weight[k, j], shift[k, j])
                    if final:
                        at = OWN - side.first
                        last[k, j - SWEEPS] = new[at : at + radial_cells]
                    else:
                        levels[n + 1, k, j, side.rows] = new
                        if k != side.facing:
                            at = side.edge - side.first
                            levels[n + 1, k, j, side.ghost : side.ghost + 1] = new[at : at + 1]
                return carry

            lax.fori_loop(n + 1, cells - 1 - n, step, 0, unroll=2)
            if not final:
                for e, at in enumerate((n + 1, cells - 3 - n)):
                    pending.append(
                        pltpu.make_async_copy(
                            levels.at[n + 1, :, pl.ds(at, 2)],
                            stash.at[e, n],
                            sems.at[3 + 2 * n + e],
                        )
                    )
                    pending[-1].start()
        inner = pltpu.make_async_copy(
            last, out_ref.at[:, pl.ds(SWEEPS, cells - 2 * SWEEPS)], sems.at[0]
        )
        inner.start()
        pending.append(inner)
        if not known:
            cut_out[...] = last[:, :, side.sent, :]
            at = side.edge - OWN
            for j in range(cells - 2 * SWEEPS):
                edge_out[j : j + 1] = last[side.facing, j, at : at + 1]
        for c in pending:
            c.wait()

    on_each_side(rad_ref, radial_cells, body)


def finish(known, rad_ref, p_ref, b_ref, w_ref, stash, cut_ref, ghost_ref, left_ref, right_ref, *rest):
    if known:
        left_w, right_w, _, out_ref, *rest = rest
    else:
        cut_in, edge_in, _, out_ref, cut_out, edge_out, *rest = rest
    levels, last, near, near2, weight, shift, moved, moved_w, sems = rest
    cells, radial_cells = p_ref.shape[1:3]
    width = SWEEPS + 2

    def at(e, distance):
        return distance if e == 0 else width - 1 - distance

    def body(side):
        facing = side.facing
        copies = []

        def fetch(source, target):
            copies.append(pltpu.make_async_copy(source, target, sems.at[len(copies)]))

        for e, message in enumerate((left_ref, right_ref)):
            fetch(message, moved.at[e])
            if known:
                fetch((left_w, right_w)[e].at[:, pl.ds(SWEEPS, 2)], moved_w.at[e])
            ends = pl.ds(0 if e == 0 else cells - SWEEPS, SWEEPS)
            fetch(b_ref.at[:, ends], shift.at[e])
            fetch(w_ref.at[:, ends], weight.at[e])
            fetch(
                p_ref.at[:, pl.ds(0 if e == 0 else cells - 2, 2)],
                levels.at[0, e, :, pl.ds(min(at(e, 1), at(e, 2)), 2), pl.ds(OWN, radial_cells), :],
            )
            for n in range(1, SWEEPS):
                fetch(
                    stash.at[e, n - 1],
                    levels.at[n, e, :, pl.ds(min(at(e, n + 1), at(e, n + 2)), 2)],
                )
        copy_all(copies)

        def weights(e, k, i):
            return moved_w[e, k, i] if known else moved[e, k, SWEEPS + i]

        lanes = levels.shape[-1]
        for e in range(2):
            for d in range(1, 3):
                column = d - 1 if e == 0 else cells - d
                for k in range(2):
                    target = levels.at[0, e, k, at(e, d)]
                    target[side.cut, :] = cut_ref[0, k, column]
                    if k != facing:
                        mirror(target, side)
            for d in range(1, SWEEPS):
                column = d - 1 if e == 0 else cells - d
                for n in range(SWEEPS):
                    if n >= d or (n == 0 and d < 3):
                        levels[n, e, facing, at(e, d), side.ghost : side.ghost + 1] = ghost_ref[
                            column : column + 1
                        ]
            beyond = [moved[e, facing, j, side.spare : side.spare + 1] for j in range(3)]
            for k in range(2):
                levels[0, e, k, at(e, 0), side.rows] = moved[e, k, 0]
                for buf in (near, near2):
                    for i in range(3):
                        buf[e, k, i] = jnp.zeros(buf.shape[3:], jnp.float32)
                        if k == facing and i < 2:
                            buf[e, k, i, side.ghost : side.ghost + 1] = beyond[i]
            w3 = (moved_w if known else moved)[
                e, facing, 1 if known else SWEEPS + 1, side.spare : side.spare + 1
            ]
            near2[e, facing, 2, side.edge : side.edge + 1] = w3 * beyond[2]
        nears = (near, near2)
        for n in range(SWEEPS):
            final = n == SWEEPS - 1
            src, dst = nears[n % 2], nears[1 - n % 2]
            for e in range(2):
                for k in range(2):
                    for d in range(1, n + 2):
                        i = d - 1 if e == 0 else SWEEPS - d
                        beside = (
                            levels[n, e, k, at(e, d - 1), side.rows]
                            + levels[n, e, k, at(e, d + 1), side.rows]
                        )
                        new = relaxed(
                            levels.at[n, e, k, at(e, d)],
                            side,
                            beside,
                            weight[e, k, i],
                            shift[e, k, i],
                        )
                        if final:
                            first = OWN - side.first
                            last[e, k, i] = new[first : first + radial_cells]
                        else:
                            levels[n + 1, e, k, at(e, d), side.rows] = new
                            if k != facing:
                                mirror(levels.at[n + 1, e, k, at(e, d)], side)
                    if final:
                        continue
                    beside = levels[n, e, k, at(e, 1), side.rows] + src[e, k, 1, side.rows]
                    new = relaxed(src.at[e, k, 0], side, beside, weights(e, k, 0), None)
                    dst[e, k, 0, side.rows] = new
                    levels[n + 1, e, k, at(e, 0), side.rows] = moved[e, k, n + 1] + new
                    if k != facing:
                        mirror(dst.at[e, k, 0], side)
                    if n < SWEEPS - 2:
                        beside = src[e, k, 0, side.rows] + src[e, k, 2, side.rows]
                        new = relaxed(src.at[e, k, 1], side, beside, weights(e, k, 1), None)
                        dst[e, k, 1, side.rows] = new
                        if k != facing:
                            mirror(dst.at[e, k, 1], side)
        copies = [
            pltpu.make_async_copy(
                last.at[e],
                out_ref.at[:, pl.ds(0 if e == 0 else cells - SWEEPS, SWEEPS)],
                sems.at[e],
            )
            for e in range(2)
        ]
        for c in copies:
            c.start()
        if not known:
            row = side.edge - OWN
            cut_out[0, :, SWEEPS : cells - SWEEPS] = cut_in[...]
            edge_out[SWEEPS : cells - SWEEPS] = edge_in[...]
            for e, first in enumerate((0, cells - SWEEPS)):
                cut_out[0, :, first : first + SWEEPS] = last[e, :, :, side.sent, :]
                for i in range(SWEEPS):
                    edge_out[first + i : first + i + 1] = last[e, facing, i, row : row + 1]
        for c in copies:
            c.wait()

    on_each_side(rad_ref, radial_cells, body)


def ring(size, step):
    return [(i, (i + step) % size) for i in range(size)]


def facing_pairs(size, turn, k):
    pairs = []
    for i in range(size):
        pairs.append((2 * ((i - turn - 1 + k) % size) + 1, 2 * i))
        pairs.append((2 * ((i + turn + k) % size), 2 * i + 1))
    return pairs


def far_pairs(size, turn):
    return [(2 * i + r, 2 * ((i + (2 * r - 1) * turn) % size) + r) for i in range(size) for r in range(2)]


def facing_cells(edge, offset, radial_index):
    size = lax.axis_size("az")
    cells = edge.shape[0]
    turn, rest = offset // cells, offset % cells
    near = min(size, 16)

    def far(t):
        return lambda e: lax.ppermute(e, ("az", "rad"), far_pairs(size, t * near))

    def branch(t):
        return lambda e: tuple(
            lax.ppermute(e, ("az", "rad"), facing_pairs(size, t, k)) for k in range(2)
        )

    if size > near:
        edge = lax.switch(turn // near, [far(t) for t in range(-(-size // near))], edge)
    blocks = lax.switch(turn % near, [branch(t) for t in range(near)], edge)
    return blocks, jnp.where(radial_index == 0, cells - rest, rest)


def per_device(pressure, source, diagonal, rot_offset):
    _, cells, radial_cells, lanes = pressure.shape
    size = lax.axis_size("az")
    radial_index = lax.axis_index("rad")
    rad = radial_index.astype(jnp.int32).reshape(1)
    rows, span = radial_cells + 4 * TILE, radial_cells + TILE

    def array(*shape):
        return jax.ShapeDtypeStruct(shape, jnp.float32)

    def scratch(*shape):
        return pltpu.VMEM(shape, jnp.float32)

    def pinned(x):
        return pltpu.with_memory_space_constraint(x, pltpu.HBM)

    own = pltpu.HBM(pressure.shape, jnp.float32)
    kept = array(2, cells, span, lanes)
    stash = array(2, SWEEPS - 1, 2, 2, rows, lanes)
    cells_in = cells - 2 * SWEEPS
    vmem = pl.BlockSpec(memory_space=pltpu.VMEM)
    smem = pl.BlockSpec(memory_space=pltpu.SMEM)
    hbm = pl.BlockSpec(memory_space=pltpu.HBM)
    anywhere = pl.BlockSpec(memory_space=pl.ANY)

    def call(kernel, out_shape, in_specs, out_specs, scratch_shapes, operands, columns, mib, **more):
        work = 2 * columns * span * lanes
        return pl.pallas_call(
            kernel,
            out_shape=out_shape,
            in_specs=in_specs,
            out_specs=out_specs,
            scratch_shapes=scratch_shapes,
            compiler_params=pltpu.CompilerParams(vmem_limit_bytes=mib << 20),
            cost_estimate=pl.CostEstimate(
                flops=12 * work, bytes_accessed=8 * work, transcendentals=0
            ),
            **more,
        )(*operands)

    fields = tuple(pinned(x) for x in (pressure, source, diagonal))
    cut, edge = call(
        pack,
        (array(3, 2, cells, SWEEPS, lanes), array(cells, lanes)),
        [smem] + [hbm] * 3,
        [vmem] * 2,
        [
            scratch(3, 2, cells, TILE, lanes),
            scratch(cells, TILE, lanes),
            pltpu.SemaphoreType.DMA((4,)),
        ],
        (rad, *fields),
        1,
        4,
        name="pack",
    )
    for step in range(1, STEPS + 1):
        known = step > 1
        cut = lax.ppermute(cut, "rad", [(0, 1), (1, 0)])
        offset = rot_offset[0] * step % (cells * size)
        blocks, start = facing_cells(edge, offset, radial_index)
        place = jnp.stack([radial_index, start]).astype(jnp.int32)
        big = [hbm] + [anywhere if known else hbm] * 2
        message = array(2, SWEEPS if known else SLOTS, span, lanes)
        last, first, ghost = call(
            functools.partial(edges, known),
            (message, message, array(cells, lanes)),
            [smem, *big, vmem, vmem, vmem],
            [vmem] * 3,
            [
                scratch(2, 2, SWEEPS, rows, lanes),
                scratch(2, 2, SWEEPS, rows, lanes),
                scratch(2, 2, SWEEPS - 1, span, lanes),
                scratch(2, 2, SWEEPS - 1, span, lanes),
                scratch(2 * cells, lanes),
                pltpu.SemaphoreType.DMA((6,)),
            ],
            (place, *fields, cut, *blocks),
            12,
            8,
            name="edges",
        )
        left = lax.ppermute(last, "az", ring(size, 1))
        right = lax.ppermute(first, "az", ring(size, -1))
        outs = (own, stash)
        if not known:
            outs += (array(2, cells_in, SWEEPS, lanes), array(cells_in, lanes), kept, kept)
        inner, saved, *made = call(
            functools.partial(interior, known),
            outs,
            [smem, *big, vmem, vmem],
            [hbm, anywhere] + ([] if known else [vmem, vmem, anywhere, anywhere]),
            [
                scratch(SWEEPS, 2, cells, rows, lanes),
                scratch(2, cells_in, radial_cells, lanes),
                scratch(*kept.shape),
                scratch(*kept.shape),
                pltpu.SemaphoreType.DMA((9,)),
            ],
            (rad, *fields, cut, ghost),
            44,
            16,
            name="interior",
        )
        if not known:
            *inner_ends, shift, weight = made
            beyond = (left, right)
        operands = (rad, fields[0], shift, weight, saved, cut, ghost, left, right)
        specs = [smem, hbm] + [anywhere] * 3 + [vmem] * 2 + [anywhere] * 2
        if known:
            operands += beyond
            specs += [anywhere] * 2
            outs, out_specs = own, hbm
        else:
            operands += tuple(inner_ends)
            specs += [vmem] * 2
            outs = (own, array(1, 2, cells, SWEEPS, lanes), array(cells, lanes))
            out_specs = [hbm, vmem, vmem]
        pressure = call(
            functools.partial(finish, known),
            outs,
            specs + [hbm],
            out_specs,
            [
                scratch(SWEEPS, 2, 2, SWEEPS + 2, rows, lanes),
                scratch(2, 2, SWEEPS, radial_cells, lanes),
                scratch(2, 2, 3, rows, lanes),
                scratch(2, 2, 3, rows, lanes),
                scratch(2, 2, SWEEPS, span, lanes),
                scratch(2, 2, SWEEPS, span, lanes),
                scratch(2, *message.shape),
                scratch(2, 2, 2, span, lanes),
                pltpu.SemaphoreType.DMA((16,)),
            ],
            (*operands, inner),
            26,
            16,
            input_output_aliases={len(operands): 0},
            name="finish",
        )
        if not known:
            pressure, cut, edge = pressure
            fields = (pinned(pressure), shift, weight)
    return pressure


def solution(mesh):
    placed = (
        P(None, "az", "rad", None),
        P(None, "az", "rad", None),
        P(None, "az", "rad", None),
        P(),
    )
    return jax.shard_map(
        per_device,
        mesh=mesh,
        in_specs=placed,
        out_specs=P(None, "az", "rad", None),
        check_vma=False,
    )
```

```python
import functools

import jax
import jax.numpy as jnp
from jax import lax
from jax.experimental import pallas as pl
from jax.experimental.pallas import tpu as pltpu
from jax.sharding import PartitionSpec as P

STEPS = 2
SWEEPS = 4
OMEGA = 0.8
TILE = 8
OWN = 2 * TILE
SLOTS = SWEEPS + 2


class Side:
    def __init__(self, low, radial_cells):
        end = OWN + radial_cells
        self.low = low
        self.own = slice(OWN, end)
        self.first = OWN if low else TILE
        self.count = radial_cells + TILE
        self.rows = slice(self.first, self.first + self.count)
        self.cut = slice(end, end + SWEEPS) if low else slice(OWN - SWEEPS, OWN)
        self.tile = slice(end, end + TILE) if low else slice(TILE, OWN)
        self.ghost = OWN - 1 if low else end
        self.edge = OWN if low else end - 1
        self.spare = self.count - TILE + SWEEPS if low else 0
        self.facing = 1 if low else 0
        self.sent = slice(radial_cells - SWEEPS, radial_cells) if low else slice(0, SWEEPS)
        self.sent_tile = radial_cells - TILE if low else 0
        self.edge_tile = 0 if low else radial_cells - TILE


def shifted(s, by):
    return slice(s.start + by, s.stop + by)


def axial_sum(x):
    lane = lax.broadcasted_iota(jnp.int32, x.shape, 1)
    last = x.shape[1] - 1
    return jnp.where(lane == 0, 0.0, pltpu.roll(x, 1, 1)) + jnp.where(
        lane == last, 0.0, pltpu.roll(x, last, 1)
    )


def relaxed(column, side, beside, weight, shift):
    here = column[side.rows]
    radial = column[shifted(side.rows, -1)] + column[shifted(side.rows, 1)]
    nbr = beside + radial + axial_sum(here)
    kept = (1.0 - OMEGA) * here
    if shift is not None:
        kept = kept + shift
    return kept + weight * nbr


def mirror(column, side):
    column[side.ghost : side.ghost + 1] = column[side.edge : side.edge + 1]


def on_each_side(rad_ref, radial_cells, body):
    @pl.when(rad_ref[0] == 0)
    def _():
        body(Side(True, radial_cells))

    @pl.when(rad_ref[0] != 0)
    def _():
        body(Side(False, radial_cells))


def copy_all(copies):
    for c in copies:
        c.start()
    for c in copies:
        c.wait()


def end_columns(edge, cells, count):
    return slice(0, count) if edge == 0 else slice(cells - count, cells)


def spare_rows(side):
    return [(slot, side.spare + i) for slot in range(SWEEPS) for i in range(TILE - SWEEPS)]


def close(column, side, facing):
    row = slice(side.ghost, side.ghost + 1)
    if facing:
        column[row] = jnp.zeros((1, column.shape[1]), jnp.float32)
    else:
        column[row] = column[side.edge : side.edge + 1]


def trajectories(side, field, other, weight, shift, messages):
    bufs = (field, other)
    for edge, message in enumerate(messages):

        def at(distance, n, edge=edge):
            return distance - 1 if edge == 0 else n - distance

        for k in range(2):
            facing = k == side.facing
            for i in range(SWEEPS):
                close(field.at[edge, k, i], side, facing)
            for sweep in range(SWEEPS):
                src, dst = bufs[sweep % 2], bufs[1 - sweep % 2]
                top = src.at[edge, k, at(1, SWEEPS)]
                message[k, sweep] = top[side.rows]
                for j in range(1, SWEEPS - sweep):
                    here = src.at[edge, k, at(j, SWEEPS)]
                    beside = src[edge, k, at(j + 1, SWEEPS), side.rows]
                    if j > 1:
                        beside = beside + src[edge, k, at(j - 1, SWEEPS), side.rows]
                    i = at(j, SWEEPS - 1)
                    out = dst.at[edge, k, at(j, SWEEPS)]
                    out[side.rows] = relaxed(here, side, beside, weight(edge, k, i), shift(edge, k, i))
                    close(out, side, facing)
            if message.shape[1] == SWEEPS:
                continue
            for i in range(2):
                message[k, SWEEPS + i] = weight(edge, k, at(1 + i, SWEEPS - 1))
            if facing:
                row = side.edge - side.first
                message[k, SWEEPS + 1, side.spare : side.spare + 1] = weight(
                    edge, k, at(3, SWEEPS - 1)
                )[row : row + 1]


def pack(rad_ref, p_ref, s_ref, d_ref, cut_ref, edge_ref, p_ends, s_ends, d_ends, tiles, edge_tiles, sems):
    cells, radial_cells = p_ref.shape[1:3]

    def body(side):
        copies = []

        def fetch(source, target):
            copies.append(pltpu.make_async_copy(source, target, sems.at[len(copies)]))

        rows = pl.ds(side.sent_tile, TILE)
        for i, x in enumerate((p_ref, s_ref, d_ref)):
            fetch(x.at[:, :, rows, :], tiles.at[i])
        fetch(p_ref.at[side.facing, :, pl.ds(side.edge_tile, TILE), :], edge_tiles)
        for source, target in ((p_ref, p_ends), (s_ref, s_ends), (d_ref, d_ends)):
            count = target.shape[2]
            for edge in range(2):
                span = pl.ds(end_columns(edge, cells, count).start, count)
                fetch(source.at[:, span], target.at[edge])
        copy_all(copies)
        cut_ref[...] = tiles[:, :, :, shifted(side.sent, -side.sent_tile), :]
        at = side.edge - OWN - side.edge_tile
        for j in range(cells):
            edge_ref[j : j + 1] = edge_tiles[j, at : at + 1]

    on_each_side(rad_ref, radial_cells, body)


def fill_ends(field, side, p_column, cut_ref, cells, radial_cells):
    for edge in range(2):
        columns = end_columns(edge, cells, SWEEPS)
        for k in range(2):
            for i in range(SWEEPS):
                field[edge, k, i, side.own] = p_column(edge, k, i)
                field[edge, k, i, side.cut] = cut_ref[0, k, columns.start + i]


def send_block(side, block_ref, messages):
    for message in messages:
        for i, (slot, row) in enumerate(spare_rows(side)):
            message[side.facing, slot, row : row + 1] = block_ref[i : i + 1]


def first_edges(
    rad_ref, p_ends, s_ends, d_ends, cut_ref, block_ref, last, first, field, other, weight, shift
):
    radial_cells = p_ends.shape[3]
    cells = cut_ref.shape[2]
    n = SWEEPS - 1

    def body(side):
        own = shifted(side.own, -side.first)
        cut = shifted(side.cut, -side.first)
        fill_ends(field, side, lambda e, k, i: p_ends[e, k, i], cut_ref, cells, radial_cells)
        for edge in range(2):
            columns = end_columns(edge, cells, n)
            for k in range(2):
                for i in range(n):
                    for rows, s, d in (
                        (own, s_ends[edge, k, i], d_ends[edge, k, i]),
                        (cut, cut_ref[1, k, columns.start + i], cut_ref[2, k, columns.start + i]),
                    ):
                        w = OMEGA / (6.0 + d)
                        weight[edge, k, i, rows] = w
                        shift[edge, k, i, rows] = w * s
        trajectories(
            side,
            field,
            other,
            lambda e, k, i: weight[e, k, i],
            lambda e, k, i: shift[e, k, i],
            (first, last),
        )
        send_block(side, block_ref, (first, last))

    on_each_side(rad_ref, radial_cells, body)


def later_edges(rad_ref, p_ref, b_ref, w_ref, cut_ref, block_ref, last, first, field, other):
    cells, radial_cells = p_ref.shape[1:3]

    def body(side):
        fill_ends(
            field,
            side,
            lambda e, k, i: p_ref[k, end_columns(e, cells, SWEEPS).start + i],
            cut_ref,
            cells,
            radial_cells,
        )
        trajectories(
            side,
            field,
            other,
            lambda e, k, i: w_ref[k, end_columns(e, cells, SWEEPS - 1).start + i],
            lambda e, k, i: b_ref[k, end_columns(e, cells, SWEEPS - 1).start + i],
            (first, last),
        )
        send_block(side, block_ref, (first, last))

    on_each_side(rad_ref, radial_cells, body)


def inner_sweeps(side, levels, weight, shift, last, out_ref, stash, tile_out, sems):
    cells = levels.shape[2]
    radial_cells = side.own.stop - side.own.start
    for j in range(cells):
        for k in range(2):
            close(levels.at[0, k, j], side, k == side.facing)
        for n in range(1, SWEEPS):
            close(levels.at[n, side.facing, j], side, True)
    at = side.edge - side.first
    for n in range(SWEEPS):
        final = n == SWEEPS - 1

        def step(j, carry, n=n, final=final):
            for k in range(2):
                beside = levels[n, k, j - 1, side.rows] + levels[n, k, j + 1, side.rows]
                new = relaxed(levels.at[n, k, j], side, beside, weight[k, j], shift[k, j])
                if final:
                    last[k, j - SWEEPS] = new[shifted(side.own, -side.first)]
                else:
                    levels[n + 1, k, j, side.rows] = new
                    if k != side.facing:
                        levels[n + 1, k, j, side.ghost : side.ghost + 1] = new[at : at + 1]
            return carry

        lax.fori_loop(n + 1, cells - 1 - n, step, 0, unroll=2)
        if not final:
            for e, first in enumerate((n + 1, cells - 3 - n)):
                for k in range(2):
                    for i in range(2):
                        stash[e, n, k, i] = levels[n + 1, k, first + i]
    inner = pltpu.make_async_copy(
        last, out_ref.at[:, pl.ds(SWEEPS, cells - 2 * SWEEPS)], sems.at[0]
    )
    inner.start()
    tile_out[...] = last[side.facing, :, side.edge_tile : side.edge_tile + TILE, :]
    return inner


def first_interior(
    rad_ref, p_ref, s_ref, d_ref, cut_ref, out_ref, stash, tile_out, cut_out, b_out, w_out, levels, last, sems
):
    cells, radial_cells = p_ref.shape[1:3]

    def body(side):
        own = pl.ds(OWN - side.first, radial_cells)
        copy_all(
            [
                pltpu.make_async_copy(
                    p_ref, levels.at[0, :, :, pl.ds(OWN, radial_cells), :], sems.at[0]
                ),
                pltpu.make_async_copy(s_ref, b_out.at[:, :, own, :], sems.at[1]),
                pltpu.make_async_copy(d_ref, w_out.at[:, :, own, :], sems.at[2]),
            ]
        )
        cut = shifted(side.cut, -side.first)
        levels[0, :, :, side.cut, :] = cut_ref[0]
        b_out[:, :, cut, :] = cut_ref[1]
        w_out[:, :, cut, :] = cut_ref[2]

        def invert(j, carry):
            for k in range(2):
                w = OMEGA / (6.0 + w_out[k, j])
                w_out[k, j] = w
                b_out[k, j] = w * b_out[k, j]
            return carry

        lax.fori_loop(0, cells, invert, 0)
        inner = inner_sweeps(side, levels, w_out, b_out, last, out_ref, stash, tile_out, sems)
        cut_out[...] = last[:, :, side.sent, :]
        inner.wait()

    on_each_side(rad_ref, radial_cells, body)


def later_interior(
    rad_ref, p_ref, b_ref, w_ref, cut_ref, out_ref, stash, tile_out, levels, last, sems
):
    cells, radial_cells = p_ref.shape[1:3]

    def body(side):
        levels[0, :, :, side.own, :] = p_ref[...]
        levels[0, :, :, side.cut, :] = cut_ref[0]
        inner_sweeps(side, levels, w_ref, b_ref, last, out_ref, stash, tile_out, sems).wait()

    on_each_side(rad_ref, radial_cells, body)


def ghost_response(side, rad_ref, w_ref, block_ref, messages, weights, wide, source):
    facing = side.facing
    cells = w_ref.shape[1]
    reach = SWEEPS - 1
    tile = slice(side.edge_tile + OWN - side.first, side.edge_tile + OWN - side.first + TILE)
    at = side.edge - OWN - side.edge_tile
    rows = spare_rows(side)
    for i, (slot, row) in enumerate(rows):
        wide[i : i + 1] = messages[0][facing, slot, row : row + 1]
        wide[2 * cells + i : 2 * cells + i + 1] = messages[1][facing, slot, row : row + 1]
    wide[cells : 2 * cells] = block_ref[...]
    source[...] = jnp.zeros(source.shape, jnp.float32)
    for c in range(cells + 2 * reach):
        source[c, at : at + 1] = wide[pl.ds(rad_ref[1] + c, 1), :]
    row = lax.broadcasted_iota(jnp.int32, source.shape[1:], 0)
    weight = [w_ref[facing, j, tile] for j in range(cells)]
    for e in range(2):
        far = weights[e][facing, SWEEPS + 1, side.spare : side.spare + 1]
        beyond = [
            weights[e][facing, SWEEPS, tile],
            weights[e][facing, SWEEPS + 1, tile],
            jnp.where(row == at, far, 0.0),
        ]
        weight = beyond[::-1] + weight if e == 0 else weight + beyond
    given = [source[c] for c in range(cells + 2 * reach)]
    response = [w * g for w, g in zip(weight, given)]
    for n in range(1, SWEEPS):
        old = response
        response = list(old)
        for c in range(n, len(old) - n):
            x = old[c]
            radial = jnp.where(row == 0, 0.0, pltpu.roll(x, 1, 0)) + jnp.where(
                row == TILE - 1, 0.0, pltpu.roll(x, TILE - 1, 0)
            )
            nbr = (old[c - 1] + old[c + 1]) + (radial + axial_sum(x)) + given[c]
            response[c] = (1.0 - OMEGA) * x + weight[c] * nbr
    return response[reach : reach + cells]


def finish(known, rad_ref, p_ref, b_ref, w_ref, stash, cut_ref, block_ref, tile_in, left_ref, right_ref, *rest):
    if known:
        left_w, right_w, _, out_ref, *rest = rest
        weights = (left_w, right_w)
    else:
        cut_in, _, out_ref, cut_out, edge_out, *rest = rest
        weights = (left_ref, right_ref)
    levels, last, inner_tiles, near, near2, wide, source, sems = rest
    messages = (left_ref, right_ref)
    cells, radial_cells = w_ref.shape[1], out_ref.shape[2]

    def column(e, d):
        return d - 1 if e == 0 else cells - d

    def body(side):
        facing = side.facing

        def at(n, e, k, d):
            if n == 0 or d <= n:
                return levels.at[n, e, k, d]
            return stash.at[e, n - 1, k, d - n - 1 if e == 0 else n + 2 - d]

        for e in range(2):
            for k in range(2):
                for d in range(1, 3):
                    target = levels.at[0, e, k, d]
                    if known:
                        target[side.own] = p_ref[k, column(e, d)]
                    else:
                        target[side.own] = p_ref[e, k, d - 1 if e == 0 else SWEEPS - d]
                    target[side.cut] = cut_ref[0, k, column(e, d)]
                    close(target, side, k == facing)
                levels[0, e, k, 0, side.rows] = messages[e][k, 0]
                for buf in (near, near2):
                    buf[e, k] = jnp.zeros(buf.shape[2:], jnp.float32)
        nears = (near, near2)
        for n in range(SWEEPS):
            final = n == SWEEPS - 1
            src, dst = nears[n % 2], nears[1 - n % 2]
            for e in range(2):
                for k in range(2):
                    for d in range(1, n + 2):
                        j = column(e, d)
                        beside = at(n, e, k, d - 1)[side.rows] + at(n, e, k, d + 1)[side.rows]
                        new = relaxed(at(n, e, k, d), side, beside, w_ref[k, j], b_ref[k, j])
                        if final:
                            i = d - 1 if e == 0 else SWEEPS - d
                            last[e, k, i] = new[shifted(side.own, -side.first)]
                        else:
                            levels[n + 1, e, k, d, side.rows] = new
                            close(levels.at[n + 1, e, k, d], side, k == facing)
                    if final:
                        continue
                    beside = at(n, e, k, 1)[side.rows]
                    if n > 0:
                        beside = beside + src[e, k, 1, side.rows]
                        new = relaxed(src.at[e, k, 0], side, beside, weights[e][k, SWEEPS], None)
                    else:
                        new = weights[e][k, SWEEPS] * beside
                    dst[e, k, 0, side.rows] = new
                    levels[n + 1, e, k, 0, side.rows] = messages[e][k, n + 1] + new
                    close(dst.at[e, k, 0], side, k == facing)
                    if n == 1:
                        dst[e, k, 1, side.rows] = (
                            weights[e][k, SWEEPS + 1] * src[e, k, 0, side.rows]
                        )
        response = ghost_response(
            side, rad_ref, w_ref, block_ref, messages, weights, wide, source
        )
        tile = slice(side.edge_tile, side.edge_tile + TILE)
        for e in range(2):
            for i in range(SWEEPS):
                j = end_columns(e, cells, SWEEPS).start + i
                last[e, facing, i, tile] += response[j]
        for i in range(cells - 2 * SWEEPS):
            inner_tiles[i] = tile_in[i] + response[SWEEPS + i]
        copies = [
            pltpu.make_async_copy(
                last.at[e],
                out_ref.at[:, pl.ds(end_columns(e, cells, SWEEPS).start, SWEEPS)],
                sems.at[e],
            )
            for e in range(2)
        ]
        copies.append(
            pltpu.make_async_copy(
                inner_tiles,
                out_ref.at[
                    facing, pl.ds(SWEEPS, cells - 2 * SWEEPS), pl.ds(side.edge_tile, TILE), :
                ],
                sems.at[2],
            )
        )
        for c in copies:
            c.start()
        if not known:
            row = side.edge - OWN
            cut_out[0, :, SWEEPS : cells - SWEEPS] = cut_in[...]
            for i in range(cells - 2 * SWEEPS):
                j = SWEEPS + i
                r = row - side.edge_tile
                edge_out[j : j + 1] = inner_tiles[i, r : r + 1]
            for e in range(2):
                first = end_columns(e, cells, SWEEPS).start
                cut_out[0, :, first : first + SWEEPS] = last[e, :, :, side.sent, :]
                for i in range(SWEEPS):
                    edge_out[first + i : first + i + 1] = last[e, facing, i, row : row + 1]
        for c in copies:
            c.wait()

    on_each_side(rad_ref, radial_cells, body)


def ring(size, step):
    return [(i, (i + step) % size) for i in range(size)]


def facing_pairs(size, turn):
    pairs = []
    for i in range(size):
        pairs.append((2 * ((i - turn) % size) + 1, 2 * i))
        pairs.append((2 * ((i + turn) % size), 2 * i + 1))
    return pairs


def far_pairs(size, turn):
    return [(2 * i + r, 2 * ((i + (2 * r - 1) * turn) % size) + r) for i in range(size) for r in range(2)]


def facing_block(edge, offset, radial_index):
    size = lax.axis_size("az")
    cells = edge.shape[0]
    turn = (offset + cells // 2) // cells
    rest = offset - turn * cells
    turn = turn % size
    near = min(size, 16)

    def far(t):
        return lambda e: lax.ppermute(e, ("az", "rad"), far_pairs(size, t * near))

    def branch(t):
        return lambda e: lax.ppermute(e, ("az", "rad"), facing_pairs(size, t))

    if size > near:
        edge = lax.switch(turn // near, [far(t) for t in range(-(-size // near))], edge)
    block = lax.switch(turn % near, [branch(t) for t in range(near)], edge)
    return block, cells - (SWEEPS - 1) + jnp.where(radial_index == 0, -rest, rest)


def per_device(pressure, source, diagonal, rot_offset):
    _, cells, radial_cells, lanes = pressure.shape
    size = lax.axis_size("az")
    radial_index = lax.axis_index("rad")
    rad = radial_index.astype(jnp.int32).reshape(1)
    rows, span = radial_cells + 4 * TILE, radial_cells + TILE

    def array(*shape):
        return jax.ShapeDtypeStruct(shape, jnp.float32)

    def scratch(*shape):
        return pltpu.VMEM(shape, jnp.float32)

    def pinned(x):
        return pltpu.with_memory_space_constraint(x, pltpu.HBM)

    own = array(*pressure.shape)
    kept = array(2, cells, span, lanes)
    stash = array(2, SWEEPS - 1, 2, 2, rows, lanes)
    cells_in = cells - 2 * SWEEPS
    tiles = array(cells_in, TILE, lanes)
    vmem = pl.BlockSpec(memory_space=pltpu.VMEM)
    smem = pl.BlockSpec(memory_space=pltpu.SMEM)
    hbm = pl.BlockSpec(memory_space=pltpu.HBM)
    anywhere = pl.BlockSpec(memory_space=pl.ANY)
    columns = scratch(2, 2, SWEEPS, rows, lanes)
    three = scratch(2, 2, SWEEPS - 1, span, lanes)

    def call(kernel, out_shape, in_specs, out_specs, scratch_shapes, operands, work_columns, **more):
        work = 2 * work_columns * span * lanes
        return pl.pallas_call(
            kernel,
            out_shape=out_shape,
            in_specs=in_specs,
            out_specs=out_specs,
            scratch_shapes=scratch_shapes,
            compiler_params=pltpu.CompilerParams(vmem_limit_bytes=28 << 20),
            cost_estimate=pl.CostEstimate(
                flops=12 * work, bytes_accessed=8 * work, transcendentals=0
            ),
            **more,
        )(*operands)

    fields = tuple(pinned(x) for x in (pressure, source, diagonal))
    cut, edge, *ends = call(
        pack,
        (
            array(3, 2, cells, SWEEPS, lanes),
            array(cells, lanes),
            array(2, 2, SWEEPS, radial_cells, lanes),
            array(2, 2, SWEEPS - 1, radial_cells, lanes),
            array(2, 2, SWEEPS - 1, radial_cells, lanes),
        ),
        [smem] + [hbm] * 3,
        [vmem] * 2 + [anywhere] * 3,
        [
            scratch(3, 2, cells, TILE, lanes),
            scratch(cells, TILE, lanes),
            pltpu.SemaphoreType.DMA((10,)),
        ],
        (rad, *fields),
        1,
        name="pack",
    )
    for step in range(1, STEPS + 1):
        known = step > 1
        cut = lax.ppermute(cut, "rad", [(0, 1), (1, 0)])
        offset = rot_offset[0] * step % (cells * size)
        block, start = facing_block(edge, offset, radial_index)
        place = jnp.stack([radial_index, start]).astype(jnp.int32)
        message = array(2, SWEEPS if known else SLOTS, span, lanes)
        last, first = call(
            later_edges if known else first_edges,
            (message, message),
            [smem] + [vmem] * 5,
            [vmem] * 2,
            [columns] * 2 + ([] if known else [three] * 2),
            (rad, *(fields if known else ends), cut, block),
            12,
            name="edges",
        )
        left = lax.ppermute(last, "az", ring(size, 1))
        right = lax.ppermute(first, "az", ring(size, -1))
        outs = (own, stash, tiles)
        if not known:
            outs += (array(2, cells_in, SWEEPS, lanes), kept, kept)
        inner, saved, inner_tiles, *made = call(
            later_interior if known else first_interior,
            outs,
            [smem] + ([vmem] * 3 if known else [hbm] * 3) + [vmem],
            [anywhere] + [vmem] * (len(outs) - 1),
            [
                scratch(SWEEPS, 2, cells, rows, lanes),
                scratch(2, cells_in, radial_cells, lanes),
                pltpu.SemaphoreType.DMA((3,)),
            ],
            (rad, *fields, cut),
            44,
            name="interior",
        )
        if not known:
            inner_cut, shift, weight = made
            beyond = (left, right)
        operands = (
            place,
            fields[0] if known else ends[0],
            shift,
            weight,
            saved,
            cut,
            block,
            inner_tiles,
            left,
            right,
        )
        operands += beyond if known else (inner_cut,)
        outs = own if known else (own, array(1, 2, cells, SWEEPS, lanes), array(cells, lanes))
        pressure = call(
            functools.partial(finish, known),
            outs,
            [smem] + [vmem] * (len(operands) - 1) + [anywhere],
            anywhere if known else [anywhere, vmem, vmem],
            [
                scratch(SWEEPS, 2, 2, SWEEPS, rows, lanes),
                scratch(2, 2, SWEEPS, radial_cells, lanes),
                scratch(*tiles.shape),
                scratch(2, 2, 2, rows, lanes),
                scratch(2, 2, 2, rows, lanes),
                scratch(3 * cells, lanes),
                scratch(cells + 2 * (SWEEPS - 1), TILE, lanes),
                pltpu.SemaphoreType.DMA((3,)),
            ],
            (*operands, inner),
            26,
            input_output_aliases={len(operands): 0},
            name="finish",
        )
        if not known:
            pressure, cut, edge = pressure
            fields = (pressure, shift, weight)
    return pressure


def solution(mesh):
    placed = (
        P(None, "az", "rad", None),
        P(None, "az", "rad", None),
        P(None, "az", "rad", None),
        P(),
    )
    return jax.shard_map(
        per_device,
        mesh=mesh,
        in_specs=placed,
        out_specs=P(None, "az", "rad", None),
        check_vma=False,
    )
```

```python
import functools

import jax
import jax.numpy as jnp
from jax import lax
from jax.experimental import pallas as pl
from jax.experimental.pallas import tpu as pltpu
from jax.sharding import PartitionSpec as P

STEPS = 2
SWEEPS = 4
OMEGA = 0.8
TILE = 8
OWN = 2 * TILE
SLOTS = SWEEPS + 2


class Side:
    def __init__(self, low, radial_cells):
        end = OWN + radial_cells
        self.low = low
        self.own = slice(OWN, end)
        self.first = OWN if low else TILE
        self.count = radial_cells + TILE
        self.rows = slice(self.first, self.first + self.count)
        self.cut = slice(end, end + SWEEPS) if low else slice(OWN - SWEEPS, OWN)
        self.tile = slice(end, end + TILE) if low else slice(TILE, OWN)
        self.ghost = OWN - 1 if low else end
        self.edge = OWN if low else end - 1
        self.spare = self.count - TILE + SWEEPS if low else 0
        self.facing = 1 if low else 0
        self.sent = slice(radial_cells - SWEEPS, radial_cells) if low else slice(0, SWEEPS)
        self.sent_tile = radial_cells - TILE if low else 0
        self.edge_tile = 0 if low else radial_cells - TILE


def shifted(s, by):
    return slice(s.start + by, s.stop + by)


def axial_sum(x):
    lane = lax.broadcasted_iota(jnp.int32, x.shape, 1)
    last = x.shape[1] - 1
    return jnp.where(lane == 0, 0.0, pltpu.roll(x, 1, 1)) + jnp.where(
        lane == last, 0.0, pltpu.roll(x, last, 1)
    )


def relaxed(column, side, beside, weight, shift):
    here = column[side.rows]
    radial = column[shifted(side.rows, -1)] + column[shifted(side.rows, 1)]
    nbr = beside + radial + axial_sum(here)
    kept = (1.0 - OMEGA) * here
    if shift is not None:
        kept = kept + shift
    return kept + weight * nbr


def mirror(column, side):
    column[side.ghost : side.ghost + 1] = column[side.edge : side.edge + 1]


def on_each_side(radial_cells, body):
    low = lax.axis_index("rad") == 0

    @pl.when(low)
    def _():
        body(Side(True, radial_cells))

    @pl.when(jnp.logical_not(low))
    def _():
        body(Side(False, radial_cells))


def copy_all(copies):
    for c in copies:
        c.start()
    for c in copies:
        c.wait()


def end_columns(edge, cells, count):
    return slice(0, count) if edge == 0 else slice(cells - count, cells)


def spare_rows(side):
    return [(slot, side.spare + i) for slot in range(SWEEPS) for i in range(TILE - SWEEPS)]


def close(column, side, facing):
    row = slice(side.ghost, side.ghost + 1)
    if facing:
        column[row] = jnp.zeros((1, column.shape[1]), jnp.float32)
    else:
        column[row] = column[side.edge : side.edge + 1]


def trajectories(side, field, other, weight, shift, messages):
    bufs = (field, other)
    for edge, message in enumerate(messages):

        def at(distance, n, edge=edge):
            return distance - 1 if edge == 0 else n - distance

        for k in range(2):
            facing = k == side.facing
            for i in range(SWEEPS):
                close(field.at[edge, k, i], side, facing)
            for sweep in range(SWEEPS):
                src, dst = bufs[sweep % 2], bufs[1 - sweep % 2]
                top = src.at[edge, k, at(1, SWEEPS)]
                message[k, sweep] = top[side.rows]
                for j in range(1, SWEEPS - sweep):
                    here = src.at[edge, k, at(j, SWEEPS)]
                    beside = src[edge, k, at(j + 1, SWEEPS), side.rows]
                    if j > 1:
                        beside = beside + src[edge, k, at(j - 1, SWEEPS), side.rows]
                    i = at(j, SWEEPS - 1)
                    out = dst.at[edge, k, at(j, SWEEPS)]
                    out[side.rows] = relaxed(here, side, beside, weight(edge, k, i), shift(edge, k, i))
                    close(out, side, facing)
            if message.shape[1] == SWEEPS:
                continue
            for i in range(2):
                message[k, SWEEPS + i] = weight(edge, k, at(1 + i, SWEEPS - 1))
            if facing:
                row = side.edge - side.first
                message[k, SWEEPS + 1, side.spare : side.spare + 1] = weight(
                    edge, k, at(3, SWEEPS - 1)
                )[row : row + 1]


def pack(p_ref, s_ref, d_ref, cut_ref, edge_ref, p_ends, s_ends, d_ends, tiles, edge_tiles, sems):
    cells, radial_cells = p_ref.shape[1:3]

    def body(side):
        copies = []

        def fetch(source, target):
            copies.append(pltpu.make_async_copy(source, target, sems.at[len(copies)]))

        rows = pl.ds(side.sent_tile, TILE)
        for i, x in enumerate((p_ref, s_ref, d_ref)):
            fetch(x.at[:, :, rows, :], tiles.at[i])
        fetch(p_ref.at[side.facing, :, pl.ds(side.edge_tile, TILE), :], edge_tiles)
        for source, target in ((p_ref, p_ends), (s_ref, s_ends), (d_ref, d_ends)):
            count = target.shape[2]
            for edge in range(2):
                span = pl.ds(end_columns(edge, cells, count).start, count)
                fetch(source.at[:, span], target.at[edge])
        copy_all(copies)
        cut_ref[...] = tiles[:, :, :, shifted(side.sent, -side.sent_tile), :]
        at = side.edge - OWN - side.edge_tile
        for j in range(cells):
            edge_ref[j : j + 1] = edge_tiles[j, at : at + 1]

    on_each_side(radial_cells, body)


def fill_ends(field, side, p_column, cut_ref, cells, radial_cells):
    for edge in range(2):
        columns = end_columns(edge, cells, SWEEPS)
        for k in range(2):
            for i in range(SWEEPS):
                field[edge, k, i, side.own] = p_column(edge, k, i)
                field[edge, k, i, side.cut] = cut_ref[0, k, columns.start + i]


def send_block(side, arriving, block_ref, messages):
    arriving.wait()
    for message in messages:
        for i, (slot, row) in enumerate(spare_rows(side)):
            message[side.facing, slot, row : row + 1] = block_ref[i : i + 1]


def first_edges(
    p_ends, s_ends, d_ends, cut_ref, block_ref, last, first, block, sem, field, other, weight, shift
):
    radial_cells = p_ends.shape[3]
    cells = cut_ref.shape[2]
    n = SWEEPS - 1

    def body(side):
        arriving = pltpu.make_async_copy(block_ref, block, sem)
        arriving.start()
        own = shifted(side.own, -side.first)
        cut = shifted(side.cut, -side.first)
        fill_ends(field, side, lambda e, k, i: p_ends[e, k, i], cut_ref, cells, radial_cells)
        for edge in range(2):
            columns = end_columns(edge, cells, n)
            for k in range(2):
                for i in range(n):
                    for rows, s, d in (
                        (own, s_ends[edge, k, i], d_ends[edge, k, i]),
                        (cut, cut_ref[1, k, columns.start + i], cut_ref[2, k, columns.start + i]),
                    ):
                        w = OMEGA / (6.0 + d)
                        weight[edge, k, i, rows] = w
                        shift[edge, k, i, rows] = w * s
        trajectories(
            side,
            field,
            other,
            lambda e, k, i: weight[e, k, i],
            lambda e, k, i: shift[e, k, i],
            (first, last),
        )
        send_block(side, arriving, block, (first, last))

    on_each_side(radial_cells, body)


def later_edges(p_ref, b_ref, w_ref, cut_ref, block_ref, last, first, block, sem, field, other):
    cells, radial_cells = p_ref.shape[1:3]

    def body(side):
        arriving = pltpu.make_async_copy(block_ref, block, sem)
        arriving.start()
        fill_ends(
            field,
            side,
            lambda e, k, i: p_ref[k, end_columns(e, cells, SWEEPS).start + i],
            cut_ref,
            cells,
            radial_cells,
        )
        trajectories(
            side,
            field,
            other,
            lambda e, k, i: w_ref[k, end_columns(e, cells, SWEEPS - 1).start + i],
            lambda e, k, i: b_ref[k, end_columns(e, cells, SWEEPS - 1).start + i],
            (first, last),
        )
        send_block(side, arriving, block, (first, last))

    on_each_side(radial_cells, body)


def inner_sweeps(side, levels, weight, shift, last, out_ref, stash, tile_out, sems):
    cells = levels.shape[2]
    radial_cells = side.own.stop - side.own.start
    for j in range(cells):
        for k in range(2):
            close(levels.at[0, k, j], side, k == side.facing)
        for n in range(1, SWEEPS):
            close(levels.at[n, side.facing, j], side, True)
    at = side.edge - side.first
    for n in range(SWEEPS):
        final = n == SWEEPS - 1

        def step(j, carry, n=n, final=final):
            for k in range(2):
                beside = levels[n, k, j - 1, side.rows] + levels[n, k, j + 1, side.rows]
                new = relaxed(levels.at[n, k, j], side, beside, weight[k, j], shift[k, j])
                if final:
                    last[k, j - SWEEPS] = new[shifted(side.own, -side.first)]
                else:
                    levels[n + 1, k, j, side.rows] = new
                    if k != side.facing:
                        levels[n + 1, k, j, side.ghost : side.ghost + 1] = new[at : at + 1]
            return carry

        lax.fori_loop(n + 1, cells - 1 - n, step, 0, unroll=2)
        if not final:
            for e, first in enumerate((n + 1, cells - 3 - n)):
                for k in range(2):
                    for i in range(2):
                        stash[e, n, k, i] = levels[n + 1, k, first + i]
    inner = pltpu.make_async_copy(
        last, out_ref.at[:, pl.ds(SWEEPS, cells - 2 * SWEEPS)], sems.at[0]
    )
    inner.start()
    tile_out[...] = last[side.facing, :, side.edge_tile : side.edge_tile + TILE, :]
    return inner


def first_interior(
    p_ref, s_ref, d_ref, cut_ref, out_ref, stash, tile_out, cut_out, b_out, w_out, levels, last, sems
):
    cells, radial_cells = p_ref.shape[1:3]

    def body(side):
        own = pl.ds(OWN - side.first, radial_cells)
        copy_all(
            [
                pltpu.make_async_copy(
                    p_ref, levels.at[0, :, :, pl.ds(OWN, radial_cells), :], sems.at[0]
                ),
                pltpu.make_async_copy(s_ref, b_out.at[:, :, own, :], sems.at[1]),
                pltpu.make_async_copy(d_ref, w_out.at[:, :, own, :], sems.at[2]),
            ]
        )
        cut = shifted(side.cut, -side.first)
        levels[0, :, :, side.cut, :] = cut_ref[0]
        b_out[:, :, cut, :] = cut_ref[1]
        w_out[:, :, cut, :] = cut_ref[2]

        def invert(j, carry):
            for k in range(2):
                w = OMEGA / (6.0 + w_out[k, j])
                w_out[k, j] = w
                b_out[k, j] = w * b_out[k, j]
            return carry

        lax.fori_loop(0, cells, invert, 0)
        inner = inner_sweeps(side, levels, w_out, b_out, last, out_ref, stash, tile_out, sems)
        cut_out[...] = last[:, :, side.sent, :]
        inner.wait()

    on_each_side(radial_cells, body)


def later_interior(
    p_ref, b_ref, w_ref, cut_ref, out_ref, stash, tile_out, levels, last, sems
):
    cells, radial_cells = p_ref.shape[1:3]

    def body(side):
        levels[0, :, :, side.own, :] = p_ref[...]
        levels[0, :, :, side.cut, :] = cut_ref[0]
        inner_sweeps(side, levels, w_ref, b_ref, last, out_ref, stash, tile_out, sems).wait()

    on_each_side(radial_cells, body)


def ghost_response(side, start_ref, w_ref, block_ref, messages, weights, wide, source):
    facing = side.facing
    cells = w_ref.shape[1]
    reach = SWEEPS - 1
    tile = slice(side.edge_tile + OWN - side.first, side.edge_tile + OWN - side.first + TILE)
    at = side.edge - OWN - side.edge_tile
    rows = spare_rows(side)
    for i, (slot, row) in enumerate(rows):
        wide[i : i + 1] = messages[0][facing, slot, row : row + 1]
        wide[2 * cells + i : 2 * cells + i + 1] = messages[1][facing, slot, row : row + 1]
    wide[cells : 2 * cells] = block_ref[...]
    source[...] = jnp.zeros(source.shape, jnp.float32)
    for c in range(cells + 2 * reach):
        source[c, at : at + 1] = wide[pl.ds(start_ref[0] + c, 1), :]
    row = lax.broadcasted_iota(jnp.int32, source.shape[1:], 0)
    weight = [w_ref[facing, j, tile] for j in range(cells)]
    for e in range(2):
        far = weights[e][facing, SWEEPS + 1, side.spare : side.spare + 1]
        beyond = [
            weights[e][facing, SWEEPS, tile],
            weights[e][facing, SWEEPS + 1, tile],
            jnp.where(row == at, far, 0.0),
        ]
        weight = beyond[::-1] + weight if e == 0 else weight + beyond
    given = [source[c] for c in range(cells + 2 * reach)]
    response = [w * g for w, g in zip(weight, given)]
    for n in range(1, SWEEPS):
        old = response
        response = list(old)
        for c in range(n, len(old) - n):
            x = old[c]
            radial = jnp.where(row == 0, 0.0, pltpu.roll(x, 1, 0)) + jnp.where(
                row == TILE - 1, 0.0, pltpu.roll(x, TILE - 1, 0)
            )
            nbr = (old[c - 1] + old[c + 1]) + (radial + axial_sum(x)) + given[c]
            response[c] = (1.0 - OMEGA) * x + weight[c] * nbr
    return response[reach : reach + cells]


def finish(known, start_ref, p_ref, b_ref, w_ref, stash, cut_ref, block_ref, tile_in, left_ref, right_ref, *rest):
    if known:
        left_w, right_w, _, out_ref, *rest = rest
        weights = (left_w, right_w)
    else:
        cut_in, _, out_ref, cut_out, edge_out, *rest = rest
        weights = (left_ref, right_ref)
    levels, last, inner_tiles, near, near2, wide, source, sems = rest
    messages = (left_ref, right_ref)
    cells, radial_cells = w_ref.shape[1], out_ref.shape[2]

    def column(e, d):
        return d - 1 if e == 0 else cells - d

    def body(side):
        facing = side.facing

        def at(n, e, k, d):
            if n == 0 or d <= n:
                return levels.at[n, e, k, d]
            return stash.at[e, n - 1, k, d - n - 1 if e == 0 else n + 2 - d]

        for e in range(2):
            for k in range(2):
                for d in range(1, 3):
                    target = levels.at[0, e, k, d]
                    if known:
                        target[side.own] = p_ref[k, column(e, d)]
                    else:
                        target[side.own] = p_ref[e, k, d - 1 if e == 0 else SWEEPS - d]
                    target[side.cut] = cut_ref[0, k, column(e, d)]
                    close(target, side, k == facing)
                levels[0, e, k, 0, side.rows] = messages[e][k, 0]
                for buf in (near, near2):
                    buf[e, k] = jnp.zeros(buf.shape[2:], jnp.float32)
        nears = (near, near2)
        for n in range(SWEEPS):
            final = n == SWEEPS - 1
            src, dst = nears[n % 2], nears[1 - n % 2]
            for e in range(2):
                for k in range(2):
                    for d in range(1, n + 2):
                        j = column(e, d)
                        beside = at(n, e, k, d - 1)[side.rows] + at(n, e, k, d + 1)[side.rows]
                        new = relaxed(at(n, e, k, d), side, beside, w_ref[k, j], b_ref[k, j])
                        if final:
                            i = d - 1 if e == 0 else SWEEPS - d
                            last[e, k, i] = new[shifted(side.own, -side.first)]
                        else:
                            levels[n + 1, e, k, d, side.rows] = new
                            close(levels.at[n + 1, e, k, d], side, k == facing)
                    if final:
                        continue
                    beside = at(n, e, k, 1)[side.rows]
                    if n > 0:
                        beside = beside + src[e, k, 1, side.rows]
                        new = relaxed(src.at[e, k, 0], side, beside, weights[e][k, SWEEPS], None)
                    else:
                        new = weights[e][k, SWEEPS] * beside
                    dst[e, k, 0, side.rows] = new
                    levels[n + 1, e, k, 0, side.rows] = messages[e][k, n + 1] + new
                    close(dst.at[e, k, 0], side, k == facing)
                    if n == 1:
                        dst[e, k, 1, side.rows] = (
                            weights[e][k, SWEEPS + 1] * src[e, k, 0, side.rows]
                        )
        response = ghost_response(
            side, start_ref, w_ref, block_ref, messages, weights, wide, source
        )
        tile = slice(side.edge_tile, side.edge_tile + TILE)
        for e in range(2):
            for i in range(SWEEPS):
                j = end_columns(e, cells, SWEEPS).start + i
                last[e, facing, i, tile] += response[j]
        for i in range(cells - 2 * SWEEPS):
            inner_tiles[i] = tile_in[i] + response[SWEEPS + i]
        copies = [
            pltpu.make_async_copy(
                last.at[e],
                out_ref.at[:, pl.ds(end_columns(e, cells, SWEEPS).start, SWEEPS)],
                sems.at[e],
            )
            for e in range(2)
        ]
        copies.append(
            pltpu.make_async_copy(
                inner_tiles,
                out_ref.at[
                    facing, pl.ds(SWEEPS, cells - 2 * SWEEPS), pl.ds(side.edge_tile, TILE), :
                ],
                sems.at[2],
            )
        )
        for c in copies:
            c.start()
        if not known:
            row = side.edge - OWN
            cut_out[0, :, SWEEPS : cells - SWEEPS] = cut_in[...]
            for i in range(cells - 2 * SWEEPS):
                j = SWEEPS + i
                r = row - side.edge_tile
                edge_out[j : j + 1] = inner_tiles[i, r : r + 1]
            for e in range(2):
                first = end_columns(e, cells, SWEEPS).start
                cut_out[0, :, first : first + SWEEPS] = last[e, :, :, side.sent, :]
                for i in range(SWEEPS):
                    edge_out[first + i : first + i + 1] = last[e, facing, i, row : row + 1]
        for c in copies:
            c.wait()

    on_each_side(radial_cells, body)


def ring(size, step):
    return [(i, (i + step) % size) for i in range(size)]


def facing_pairs(size, turn):
    pairs = []
    for i in range(size):
        pairs.append((2 * ((i - turn) % size) + 1, 2 * i))
        pairs.append((2 * ((i + turn) % size), 2 * i + 1))
    return pairs


def far_pairs(size, turn):
    return [(2 * i + r, 2 * ((i + (2 * r - 1) * turn) % size) + r) for i in range(size) for r in range(2)]


def facing_block(edge, offset, radial_index):
    size = lax.axis_size("az")
    cells = edge.shape[0]
    turn = (offset + cells // 2) // cells
    rest = offset - turn * cells
    turn = turn % size
    near = min(size, 16)

    def far(t):
        return lambda e: lax.ppermute(e, ("az", "rad"), far_pairs(size, t * near))

    def branch(t):
        return lambda e: lax.ppermute(e, ("az", "rad"), facing_pairs(size, t))

    if size > near:
        edge = lax.switch(turn // near, [far(t) for t in range(-(-size // near))], edge)
    block = lax.switch(turn % near, [branch(t) for t in range(near)], edge)
    return block, cells - (SWEEPS - 1) + jnp.where(radial_index == 0, -rest, rest)


def per_device(pressure, source, diagonal, rot_offset):
    _, cells, radial_cells, lanes = pressure.shape
    size = lax.axis_size("az")
    radial_index = lax.axis_index("rad")
    rows, span = radial_cells + 4 * TILE, radial_cells + TILE

    def array(*shape):
        return jax.ShapeDtypeStruct(shape, jnp.float32)

    def scratch(*shape):
        return pltpu.VMEM(shape, jnp.float32)

    def pinned(x):
        return pltpu.with_memory_space_constraint(x, pltpu.HBM)

    kept = array(2, cells, span, lanes)
    stash = array(2, SWEEPS - 1, 2, 2, rows, lanes)
    cells_in = cells - 2 * SWEEPS
    tiles = array(cells_in, TILE, lanes)
    vmem = pl.BlockSpec(memory_space=pltpu.VMEM)
    smem = pl.BlockSpec(memory_space=pltpu.SMEM)
    hbm = pl.BlockSpec(memory_space=pltpu.HBM)
    anywhere = pl.BlockSpec(memory_space=pl.ANY)
    columns = scratch(2, 2, SWEEPS, rows, lanes)
    three = scratch(2, 2, SWEEPS - 1, span, lanes)

    def call(kernel, out_shape, in_specs, out_specs, scratch_shapes, operands, work_columns, **more):
        work = 2 * work_columns * span * lanes
        return pl.pallas_call(
            kernel,
            out_shape=out_shape,
            in_specs=in_specs,
            out_specs=out_specs,
            scratch_shapes=scratch_shapes,
            compiler_params=pltpu.CompilerParams(vmem_limit_bytes=28 << 20),
            cost_estimate=pl.CostEstimate(
                flops=12 * work, bytes_accessed=8 * work, transcendentals=0
            ),
            **more,
        )(*operands)

    fields = tuple(pinned(x) for x in (pressure, source, diagonal))
    cut, edge, *ends = call(
        pack,
        (
            array(3, 2, cells, SWEEPS, lanes),
            array(cells, lanes),
            array(2, 2, SWEEPS, radial_cells, lanes),
            array(2, 2, SWEEPS - 1, radial_cells, lanes),
            array(2, 2, SWEEPS - 1, radial_cells, lanes),
        ),
        [hbm] * 3,
        [vmem] * 2 + [anywhere] * 3,
        [
            scratch(3, 2, cells, TILE, lanes),
            scratch(cells, TILE, lanes),
            pltpu.SemaphoreType.DMA((10,)),
        ],
        fields,
        1,
        name="pack",
    )
    for step in range(1, STEPS + 1):
        known = step > 1
        cut = lax.ppermute(cut, "rad", [(0, 1), (1, 0)])
        offset = rot_offset[0] * step % (cells * size)
        block, start = facing_block(edge, offset, radial_index)
        place = start.astype(jnp.int32).reshape(1)
        message = array(2, SWEEPS if known else SLOTS, span, lanes)
        last, first = call(
            later_edges if known else first_edges,
            (message, message),
            [vmem] * 4 + [anywhere],
            [vmem] * 2,
            [scratch(cells, lanes), pltpu.SemaphoreType.DMA, columns, columns]
            + ([] if known else [three] * 2),
            (*(fields if known else ends), cut, block),
            12,
            name="edges",
        )
        left = lax.ppermute(last, "az", ring(size, 1))
        right = lax.ppermute(first, "az", ring(size, -1))
        result = array(*pressure.shape) if known else pltpu.VMEM(pressure.shape, jnp.float32)
        outs = (result, stash, tiles)
        if not known:
            outs += (array(2, cells_in, SWEEPS, lanes), kept, kept)
        inner, saved, inner_tiles, *made = call(
            later_interior if known else first_interior,
            outs,
            ([vmem] * 3 if known else [hbm] * 3) + [vmem],
            [anywhere] + [vmem] * (len(outs) - 1),
            [
                scratch(SWEEPS, 2, cells, rows, lanes),
                scratch(2, cells_in, radial_cells, lanes),
                pltpu.SemaphoreType.DMA((3,)),
            ],
            (*fields, cut),
            44,
            name="interior",
        )
        if not known:
            inner_cut, shift, weight = made
            beyond = (left, right)
        operands = (
            place,
            fields[0] if known else ends[0],
            shift,
            weight,
            saved,
            cut,
            block,
            inner_tiles,
            left,
            right,
        )
        operands += beyond if known else (inner_cut,)
        outs = result if known else (result, array(1, 2, cells, SWEEPS, lanes), array(cells, lanes))
        pressure = call(
            functools.partial(finish, known),
            outs,
            [smem] + [vmem] * (len(operands) - 1) + [anywhere],
            anywhere if known else [anywhere, vmem, vmem],
            [
                scratch(SWEEPS, 2, 2, SWEEPS, rows, lanes),
                scratch(2, 2, SWEEPS, radial_cells, lanes),
                scratch(*tiles.shape),
                scratch(2, 2, 2, rows, lanes),
                scratch(2, 2, 2, rows, lanes),
                scratch(3 * cells, lanes),
                scratch(cells + 2 * (SWEEPS - 1), TILE, lanes),
                pltpu.SemaphoreType.DMA((3,)),
            ],
            (*operands, inner),
            26,
            input_output_aliases={len(operands): 0},
            name="finish",
        )
        if not known:
            pressure, cut, edge = pressure
            fields = (
                pltpu.with_memory_space_constraint(pressure, pltpu.VMEM),
                shift,
                weight,
            )
    return pressure


def solution(mesh):
    placed = (
        P(None, "az", "rad", None),
        P(None, "az", "rad", None),
        P(None, "az", "rad", None),
        P(),
    )
    return jax.shard_map(
        per_device,
        mesh=mesh,
        in_specs=placed,
        out_specs=P(None, "az", "rad", None),
        check_vma=False,
    )
```

```python
import functools

import jax
import jax.numpy as jnp
from jax import lax
from jax.experimental import pallas as pl
from jax.experimental.pallas import tpu as pltpu
from jax.sharding import PartitionSpec as P

STEPS = 2
SWEEPS = 4
OMEGA = 0.8
TILE = 8
OWN = 2 * TILE
SLOTS = SWEEPS + 2


class Side:
    def __init__(self, low, radial_cells):
        end = OWN + radial_cells
        self.low = low
        self.own = slice(OWN, end)
        self.first = OWN if low else TILE
        self.count = radial_cells + TILE
        self.rows = slice(self.first, self.first + self.count)
        self.cut = slice(end, end + SWEEPS) if low else slice(OWN - SWEEPS, OWN)
        self.tile = slice(end, end + TILE) if low else slice(TILE, OWN)
        self.ghost = OWN - 1 if low else end
        self.edge = OWN if low else end - 1
        self.spare = self.count - TILE + SWEEPS if low else 0
        self.facing = 1 if low else 0
        self.sent = slice(radial_cells - SWEEPS, radial_cells) if low else slice(0, SWEEPS)
        self.sent_tile = radial_cells - TILE if low else 0
        self.edge_tile = 0 if low else radial_cells - TILE


def shifted(s, by):
    return slice(s.start + by, s.stop + by)


def axial_sum(x):
    lane = lax.broadcasted_iota(jnp.int32, x.shape, 1)
    last = x.shape[1] - 1
    return jnp.where(lane == 0, 0.0, pltpu.roll(x, 1, 1)) + jnp.where(
        lane == last, 0.0, pltpu.roll(x, last, 1)
    )


def relaxed(column, side, beside, weight, shift):
    here = column[side.rows]
    radial = column[shifted(side.rows, -1)] + column[shifted(side.rows, 1)]
    nbr = beside + radial + axial_sum(here)
    kept = (1.0 - OMEGA) * here
    if shift is not None:
        kept = kept + shift
    return kept + weight * nbr


def mirror(column, side):
    column[side.ghost : side.ghost + 1] = column[side.edge : side.edge + 1]


def on_each_side(radial_cells, body):
    low = lax.axis_index("rad") == 0

    @pl.when(low)
    def _():
        body(Side(True, radial_cells))

    @pl.when(jnp.logical_not(low))
    def _():
        body(Side(False, radial_cells))


def copy_all(copies):
    for c in copies:
        c.start()
    for c in copies:
        c.wait()


def end_columns(edge, cells, count):
    return slice(0, count) if edge == 0 else slice(cells - count, cells)


def spare_rows(side):
    return [(slot, side.spare + i) for slot in range(SWEEPS) for i in range(TILE - SWEEPS)]


def close(column, side, facing):
    row = slice(side.ghost, side.ghost + 1)
    if facing:
        column[row] = jnp.zeros((1, column.shape[1]), jnp.float32)
    else:
        column[row] = column[side.edge : side.edge + 1]


def trajectories(side, field, other, weight, shift, messages):
    bufs = (field, other)
    for edge, message in enumerate(messages):

        def at(distance, n, edge=edge):
            return distance - 1 if edge == 0 else n - distance

        for k in range(2):
            facing = k == side.facing
            for i in range(SWEEPS):
                close(field.at[edge, k, i], side, facing)
            for sweep in range(SWEEPS):
                src, dst = bufs[sweep % 2], bufs[1 - sweep % 2]
                top = src.at[edge, k, at(1, SWEEPS)]
                message[k, sweep] = top[side.rows]
                for j in range(1, SWEEPS - sweep):
                    here = src.at[edge, k, at(j, SWEEPS)]
                    beside = src[edge, k, at(j + 1, SWEEPS), side.rows]
                    if j > 1:
                        beside = beside + src[edge, k, at(j - 1, SWEEPS), side.rows]
                    i = at(j, SWEEPS - 1)
                    out = dst.at[edge, k, at(j, SWEEPS)]
                    out[side.rows] = relaxed(here, side, beside, weight(edge, k, i), shift(edge, k, i))
                    close(out, side, facing)
            if message.shape[1] == SWEEPS:
                continue
            for i in range(2):
                message[k, SWEEPS + i] = weight(edge, k, at(1 + i, SWEEPS - 1))
            if facing:
                row = side.edge - side.first
                message[k, SWEEPS + 1, side.spare : side.spare + 1] = weight(
                    edge, k, at(3, SWEEPS - 1)
                )[row : row + 1]


def pack(p_ref, s_ref, d_ref, cut_ref, edge_ref, p_ends, s_ends, d_ends, tiles, edge_tiles, sems):
    cells, radial_cells = p_ref.shape[1:3]

    def body(side):
        copies = []

        def fetch(source, target):
            copies.append(pltpu.make_async_copy(source, target, sems.at[len(copies)]))

        rows = pl.ds(side.sent_tile, TILE)
        for i, x in enumerate((p_ref, s_ref, d_ref)):
            fetch(x.at[:, :, rows, :], tiles.at[i])
        fetch(p_ref.at[side.facing, :, pl.ds(side.edge_tile, TILE), :], edge_tiles)
        for source, target in ((p_ref, p_ends), (s_ref, s_ends), (d_ref, d_ends)):
            count = target.shape[2]
            for edge in range(2):
                span = pl.ds(end_columns(edge, cells, count).start, count)
                fetch(source.at[:, span], target.at[edge])
        copy_all(copies)
        cut_ref[...] = tiles[:, :, :, shifted(side.sent, -side.sent_tile), :]
        at = side.edge - OWN - side.edge_tile
        for j in range(cells):
            edge_ref[j : j + 1] = edge_tiles[j, at : at + 1]

    on_each_side(radial_cells, body)


def fill_ends(field, side, p_ends, cut_ref, cells):
    for edge in range(2):
        columns = end_columns(edge, cells, SWEEPS)
        for k in range(2):
            for i in range(SWEEPS):
                field[edge, k, i, side.own] = p_ends[edge, k, i]
                field[edge, k, i, side.cut] = cut_ref[0, k, columns.start + i]


def send_block(side, arriving, block_ref, messages):
    arriving.wait()
    for message in messages:
        for i, (slot, row) in enumerate(spare_rows(side)):
            message[side.facing, slot, row : row + 1] = block_ref[i : i + 1]


def first_edges(
    p_ends, s_ends, d_ends, cut_ref, block_ref, last, first, block, sem, field, other, weight, shift
):
    radial_cells = p_ends.shape[3]
    cells = cut_ref.shape[2]
    n = SWEEPS - 1

    def body(side):
        arriving = pltpu.make_async_copy(block_ref, block, sem)
        arriving.start()
        own = shifted(side.own, -side.first)
        cut = shifted(side.cut, -side.first)
        fill_ends(field, side, p_ends, cut_ref, cells)
        for edge in range(2):
            columns = end_columns(edge, cells, n)
            for k in range(2):
                for i in range(n):
                    for rows, s, d in (
                        (own, s_ends[edge, k, i], d_ends[edge, k, i]),
                        (cut, cut_ref[1, k, columns.start + i], cut_ref[2, k, columns.start + i]),
                    ):
                        w = OMEGA / (6.0 + d)
                        weight[edge, k, i, rows] = w
                        shift[edge, k, i, rows] = w * s
        trajectories(
            side,
            field,
            other,
            lambda e, k, i: weight[e, k, i],
            lambda e, k, i: shift[e, k, i],
            (first, last),
        )
        send_block(side, arriving, block, (first, last))

    on_each_side(radial_cells, body)


def later_edges(p_ends, b_ref, w_ref, cut_ref, block_ref, last, first, block, sem, field, other):
    cells, radial_cells = w_ref.shape[1], p_ends.shape[3]

    def body(side):
        arriving = pltpu.make_async_copy(block_ref, block, sem)
        arriving.start()
        fill_ends(field, side, p_ends, cut_ref, cells)
        trajectories(
            side,
            field,
            other,
            lambda e, k, i: w_ref[k, end_columns(e, cells, SWEEPS - 1).start + i],
            lambda e, k, i: b_ref[k, end_columns(e, cells, SWEEPS - 1).start + i],
            (first, last),
        )
        send_block(side, arriving, block, (first, last))

    on_each_side(radial_cells, body)


def inner_sweeps(side, levels, weight, shift, last, out_ref, stash, tile_out, sems):
    cells = levels.shape[2]
    radial_cells = side.own.stop - side.own.start
    for j in range(cells):
        for k in range(2):
            close(levels.at[0, k, j], side, k == side.facing)
        for n in range(1, SWEEPS):
            close(levels.at[n, side.facing, j], side, True)
    at = side.edge - side.first
    for e, first in enumerate((0, cells - 2)):
        for k in range(2):
            for i in range(2):
                stash[e, 0, k, i] = levels[0, k, first + i]
    for n in range(SWEEPS):
        final = n == SWEEPS - 1

        def step(j, carry, n=n, final=final):
            for k in range(2):
                beside = levels[n, k, j - 1, side.rows] + levels[n, k, j + 1, side.rows]
                new = relaxed(levels.at[n, k, j], side, beside, weight[k, j], shift[k, j])
                if final:
                    last[k, j - SWEEPS] = new[shifted(side.own, -side.first)]
                else:
                    levels[n + 1, k, j, side.rows] = new
                    if k != side.facing:
                        levels[n + 1, k, j, side.ghost : side.ghost + 1] = new[at : at + 1]
            return carry

        lax.fori_loop(n + 1, cells - 1 - n, step, 0, unroll=2)
        if not final:
            for e, first in enumerate((n + 1, cells - 3 - n)):
                for k in range(2):
                    for i in range(2):
                        stash[e, n + 1, k, i] = levels[n + 1, k, first + i]
    inner = pltpu.make_async_copy(
        last, out_ref.at[:, pl.ds(SWEEPS, cells - 2 * SWEEPS)], sems.at[0]
    )
    inner.start()
    tile_out[...] = last[side.facing, :, side.edge_tile : side.edge_tile + TILE, :]
    return inner


def first_interior(
    p_ref, s_ref, d_ref, cut_ref, out_ref, stash, tile_out, cut_out, b_out, w_out, levels, last, sems
):
    cells, radial_cells = p_ref.shape[1:3]

    def body(side):
        own = pl.ds(OWN - side.first, radial_cells)
        copy_all(
            [
                pltpu.make_async_copy(
                    p_ref, levels.at[0, :, :, pl.ds(OWN, radial_cells), :], sems.at[0]
                ),
                pltpu.make_async_copy(s_ref, b_out.at[:, :, own, :], sems.at[1]),
                pltpu.make_async_copy(d_ref, w_out.at[:, :, own, :], sems.at[2]),
            ]
        )
        cut = shifted(side.cut, -side.first)
        levels[0, :, :, side.cut, :] = cut_ref[0]
        b_out[:, :, cut, :] = cut_ref[1]
        w_out[:, :, cut, :] = cut_ref[2]

        def invert(j, carry):
            for k in range(2):
                w = OMEGA / (6.0 + w_out[k, j])
                w_out[k, j] = w
                b_out[k, j] = w * b_out[k, j]
            return carry

        lax.fori_loop(0, cells, invert, 0)
        inner = inner_sweeps(side, levels, w_out, b_out, last, out_ref, stash, tile_out, sems)
        cut_out[...] = last[:, :, side.sent, :]
        inner.wait()

    on_each_side(radial_cells, body)


def later_interior(
    p_ref, b_ref, w_ref, cut_ref, out_ref, stash, tile_out, levels, last, sems
):
    cells, radial_cells = p_ref.shape[1:3]

    def body(side):
        arriving = pltpu.make_async_copy(
            p_ref, levels.at[0, :, :, pl.ds(OWN, radial_cells), :], sems.at[0]
        )
        arriving.start()
        arriving.wait()
        levels[0, :, :, side.cut, :] = cut_ref[0]
        inner_sweeps(side, levels, w_ref, b_ref, last, out_ref, stash, tile_out, sems).wait()

    on_each_side(radial_cells, body)


def ghost_response(side, start_ref, w_ref, block_ref, messages, weights, wide, source):
    facing = side.facing
    cells = w_ref.shape[1]
    reach = SWEEPS - 1
    tile = slice(side.edge_tile + OWN - side.first, side.edge_tile + OWN - side.first + TILE)
    at = side.edge - OWN - side.edge_tile
    rows = spare_rows(side)
    for i, (slot, row) in enumerate(rows):
        wide[i : i + 1] = messages[0][facing, slot, row : row + 1]
        wide[2 * cells + i : 2 * cells + i + 1] = messages[1][facing, slot, row : row + 1]
    wide[cells : 2 * cells] = block_ref[...]
    source[...] = jnp.zeros(source.shape, jnp.float32)
    for c in range(cells + 2 * reach):
        source[c, at : at + 1] = wide[pl.ds(start_ref[0] + c, 1), :]
    row = lax.broadcasted_iota(jnp.int32, source.shape[1:], 0)
    weight = [w_ref[facing, j, tile] for j in range(cells)]
    for e in range(2):
        far = weights[e][facing, SWEEPS + 1, side.spare : side.spare + 1]
        beyond = [
            weights[e][facing, SWEEPS, tile],
            weights[e][facing, SWEEPS + 1, tile],
            jnp.where(row == at, far, 0.0),
        ]
        weight = beyond[::-1] + weight if e == 0 else weight + beyond
    given = [source[c] for c in range(cells + 2 * reach)]
    response = [w * g for w, g in zip(weight, given)]
    for n in range(1, SWEEPS):
        old = response
        response = list(old)
        for c in range(n, len(old) - n):
            x = old[c]
            radial = jnp.where(row == 0, 0.0, pltpu.roll(x, 1, 0)) + jnp.where(
                row == TILE - 1, 0.0, pltpu.roll(x, TILE - 1, 0)
            )
            nbr = (old[c - 1] + old[c + 1]) + (radial + axial_sum(x)) + given[c]
            response[c] = (1.0 - OMEGA) * x + weight[c] * nbr
    return response[reach : reach + cells]


def finish(known, start_ref, b_ref, w_ref, stash, block_ref, tile_in, left_ref, right_ref, *rest):
    if known:
        left_w, right_w, _, out_ref, *rest = rest
        weights = (left_w, right_w)
    else:
        cut_in, _, out_ref, cut_out, edge_out, ends_out, *rest = rest
        weights = (left_ref, right_ref)
    levels, last, inner_tiles, near, near2, wide, source, sems = rest
    messages = (left_ref, right_ref)
    cells, radial_cells = w_ref.shape[1], out_ref.shape[2]

    def column(e, d):
        return d - 1 if e == 0 else cells - d

    def body(side):
        facing = side.facing

        def at(n, e, k, d):
            if d <= n:
                return levels.at[n, e, k, d]
            return stash.at[e, n, k, d - n - 1 if e == 0 else n + 2 - d]

        for e in range(2):
            for k in range(2):
                levels[0, e, k, 0, side.rows] = messages[e][k, 0]
                for buf in (near, near2):
                    buf[e, k] = jnp.zeros(buf.shape[2:], jnp.float32)
        nears = (near, near2)

        def own_column(n, e, k, d):
            j = column(e, d)
            beside = at(n, e, k, d - 1)[side.rows] + at(n, e, k, d + 1)[side.rows]
            return relaxed(at(n, e, k, d), side, beside, w_ref[k, j], b_ref[k, j])

        for n in range(SWEEPS - 1):
            src, dst = nears[n % 2], nears[1 - n % 2]
            for e in range(2):
                for k in range(2):
                    for d in range(1, n + 2):
                        levels[n + 1, e, k, d, side.rows] = own_column(n, e, k, d)
                        close(levels.at[n + 1, e, k, d], side, k == facing)
                    beside = at(n, e, k, 1)[side.rows]
                    if n > 0:
                        beside = beside + src[e, k, 1, side.rows]
                        new = relaxed(src.at[e, k, 0], side, beside, weights[e][k, SWEEPS], None)
                    else:
                        new = weights[e][k, SWEEPS] * beside
                    dst[e, k, 0, side.rows] = new
                    levels[n + 1, e, k, 0, side.rows] = messages[e][k, n + 1] + new
                    close(dst.at[e, k, 0], side, k == facing)
                    if n == 1:
                        dst[e, k, 1, side.rows] = (
                            weights[e][k, SWEEPS + 1] * src[e, k, 0, side.rows]
                        )
        copies = []

        def store(source, target):
            copies.append(pltpu.make_async_copy(source, target, sems.at[len(copies)]))
            copies[-1].start()

        response = None
        tile = slice(side.edge_tile, side.edge_tile + TILE)
        for k in (1 - facing, facing):
            if k == facing:
                response = ghost_response(
                    side, start_ref, w_ref, block_ref, messages, weights, wide, source
                )
                for i in range(cells - 2 * SWEEPS):
                    inner_tiles[i] = tile_in[i] + response[SWEEPS + i]
                store(
                    inner_tiles,
                    out_ref.at[
                        k, pl.ds(SWEEPS, cells - 2 * SWEEPS), pl.ds(side.edge_tile, TILE), :
                    ],
                )
            for e in range(2):
                first = end_columns(e, cells, SWEEPS).start
                for d in range(1, SWEEPS + 1):
                    new = own_column(SWEEPS - 1, e, k, d)[shifted(side.own, -side.first)]
                    i = column(e, d) - first
                    last[e, k, i] = new
                    if k == facing:
                        last[e, k, i, tile] = new[tile] + response[first + i]
                store(last.at[e, k], out_ref.at[k, pl.ds(first, SWEEPS)])
        if not known:
            row = side.edge - OWN
            cut_out[0, :, SWEEPS : cells - SWEEPS] = cut_in[...]
            for i in range(cells - 2 * SWEEPS):
                j = SWEEPS + i
                r = row - side.edge_tile
                edge_out[j : j + 1] = inner_tiles[i, r : r + 1]
            for e in range(2):
                first = end_columns(e, cells, SWEEPS).start
                cut_out[0, :, first : first + SWEEPS] = last[e, :, :, side.sent, :]
                for i in range(SWEEPS):
                    edge_out[first + i : first + i + 1] = last[e, facing, i, row : row + 1]
            ends_out[...] = last[...]
        for c in copies:
            c.wait()

    on_each_side(radial_cells, body)


def ring(size, step):
    return [(i, (i + step) % size) for i in range(size)]


def facing_pairs(size, turn):
    pairs = []
    for i in range(size):
        pairs.append((2 * ((i - turn) % size) + 1, 2 * i))
        pairs.append((2 * ((i + turn) % size), 2 * i + 1))
    return pairs


def far_pairs(size, turn):
    return [(2 * i + r, 2 * ((i + (2 * r - 1) * turn) % size) + r) for i in range(size) for r in range(2)]


def facing_block(edge, offset, radial_index):
    size = lax.axis_size("az")
    cells = edge.shape[0]
    turn = (offset + cells // 2) // cells
    rest = offset - turn * cells
    turn = turn % size
    near = min(size, 16)

    def far(t):
        return lambda e: lax.ppermute(e, ("az", "rad"), far_pairs(size, t * near))

    def branch(t):
        return lambda e: lax.ppermute(e, ("az", "rad"), facing_pairs(size, t))

    if size > near:
        edge = lax.switch(turn // near, [far(t) for t in range(-(-size // near))], edge)
    block = lax.switch(turn % near, [branch(t) for t in range(near)], edge)
    return block, cells - (SWEEPS - 1) + jnp.where(radial_index == 0, -rest, rest)


def per_device(pressure, source, diagonal, rot_offset):
    _, cells, radial_cells, lanes = pressure.shape
    size = lax.axis_size("az")
    radial_index = lax.axis_index("rad")
    rows, span = radial_cells + 4 * TILE, radial_cells + TILE

    def array(*shape):
        return jax.ShapeDtypeStruct(shape, jnp.float32)

    def scratch(*shape):
        return pltpu.VMEM(shape, jnp.float32)

    def pinned(x):
        return pltpu.with_memory_space_constraint(x, pltpu.HBM)

    kept = array(2, cells, span, lanes)
    stash = array(2, SWEEPS, 2, 2, rows, lanes)
    cells_in = cells - 2 * SWEEPS
    tiles = array(cells_in, TILE, lanes)
    vmem = pl.BlockSpec(memory_space=pltpu.VMEM)
    smem = pl.BlockSpec(memory_space=pltpu.SMEM)
    hbm = pl.BlockSpec(memory_space=pltpu.HBM)
    anywhere = pl.BlockSpec(memory_space=pl.ANY)
    columns = scratch(2, 2, SWEEPS, rows, lanes)
    three = scratch(2, 2, SWEEPS - 1, span, lanes)

    def call(kernel, out_shape, in_specs, out_specs, scratch_shapes, operands, work_columns, **more):
        work = 2 * work_columns * span * lanes
        return pl.pallas_call(
            kernel,
            out_shape=out_shape,
            in_specs=in_specs,
            out_specs=out_specs,
            scratch_shapes=scratch_shapes,
            compiler_params=pltpu.CompilerParams(vmem_limit_bytes=28 << 20),
            cost_estimate=pl.CostEstimate(
                flops=12 * work, bytes_accessed=8 * work, transcendentals=0
            ),
            **more,
        )(*operands)

    fields = tuple(pinned(x) for x in (pressure, source, diagonal))
    cut, edge, *ends = call(
        pack,
        (
            array(3, 2, cells, SWEEPS, lanes),
            array(cells, lanes),
            array(2, 2, SWEEPS, radial_cells, lanes),
            array(2, 2, SWEEPS - 1, radial_cells, lanes),
            array(2, 2, SWEEPS - 1, radial_cells, lanes),
        ),
        [hbm] * 3,
        [vmem] * 2 + [anywhere] * 3,
        [
            scratch(3, 2, cells, TILE, lanes),
            scratch(cells, TILE, lanes),
            pltpu.SemaphoreType.DMA((10,)),
        ],
        fields,
        1,
        name="pack",
    )
    for step in range(1, STEPS + 1):
        known = step > 1
        cut = lax.ppermute(cut, "rad", [(0, 1), (1, 0)])
        offset = rot_offset[0] * step % (cells * size)
        block, start = facing_block(edge, offset, radial_index)
        place = start.astype(jnp.int32).reshape(1)
        message = array(2, SWEEPS if known else SLOTS, span, lanes)
        last, first = call(
            later_edges if known else first_edges,
            (message, message),
            [vmem] * 4 + [anywhere],
            [vmem] * 2,
            [scratch(cells, lanes), pltpu.SemaphoreType.DMA, columns, columns]
            + ([] if known else [three] * 2),
            (*ends, cut, block),
            12,
            name="edges",
        )
        left = lax.ppermute(last, "az", ring(size, 1))
        right = lax.ppermute(first, "az", ring(size, -1))
        result = pltpu.HBM(pressure.shape, jnp.float32)
        outs = (result, stash, tiles)
        if not known:
            outs += (array(2, cells_in, SWEEPS, lanes), kept, kept)
        inner, saved, inner_tiles, *made = call(
            later_interior if known else first_interior,
            outs,
            ([hbm] + [vmem] * 2 if known else [hbm] * 3) + [vmem],
            [hbm] + [vmem] * (len(outs) - 1),
            [
                scratch(SWEEPS, 2, cells, rows, lanes),
                scratch(2, cells_in, radial_cells, lanes),
                pltpu.SemaphoreType.DMA((3,)),
            ],
            (*fields, cut),
            44,
            name="interior",
        )
        if not known:
            inner_cut, shift, weight = made
            beyond = (left, right)
        operands = (
            place,
            shift,
            weight,
            saved,
            block,
            inner_tiles,
            left,
            right,
        )
        operands += beyond if known else (inner_cut,)
        outs = result
        if not known:
            outs = (
                result,
                array(1, 2, cells, SWEEPS, lanes),
                array(cells, lanes),
                array(2, 2, SWEEPS, radial_cells, lanes),
            )
        pressure = call(
            functools.partial(finish, known),
            outs,
            [smem] + [vmem] * (len(operands) - 1) + [hbm],
            hbm if known else [hbm] + [vmem] * 3,
            [
                scratch(SWEEPS, 2, 2, SWEEPS, rows, lanes),
                scratch(2, 2, SWEEPS, radial_cells, lanes),
                scratch(*tiles.shape),
                scratch(2, 2, 2, rows, lanes),
                scratch(2, 2, 2, rows, lanes),
                scratch(3 * cells, lanes),
                scratch(cells + 2 * (SWEEPS - 1), TILE, lanes),
                pltpu.SemaphoreType.DMA((5,)),
            ],
            (*operands, inner),
            26,
            input_output_aliases={len(operands): 0},
            name="finish",
        )
        if not known:
            pressure, cut, edge, ends_now = pressure
            fields = (pinned(pressure), shift, weight)
            ends = (ends_now, shift, weight)
    return pressure


def solution(mesh):
    placed = (
        P(None, "az", "rad", None),
        P(None, "az", "rad", None),
        P(None, "az", "rad", None),
        P(),
    )
    return jax.shard_map(
        per_device,
        mesh=mesh,
        in_specs=placed,
        out_specs=P(None, "az", "rad", None),
        check_vma=False,
    )
```

```python
import functools

import jax
import jax.numpy as jnp
from jax import lax
from jax.experimental import pallas as pl
from jax.experimental.pallas import tpu as pltpu
from jax.sharding import PartitionSpec as P

STEPS = 2
SWEEPS = 4
OMEGA = 0.8
TILE = 8
OWN = 2 * TILE
SLOTS = SWEEPS + 2


class Side:
    def __init__(self, low, radial_cells):
        end = OWN + radial_cells
        self.low = low
        self.own = slice(OWN, end)
        self.first = OWN if low else TILE
        self.count = radial_cells + TILE
        self.rows = slice(self.first, self.first + self.count)
        self.cut = slice(end, end + SWEEPS) if low else slice(OWN - SWEEPS, OWN)
        self.tile = slice(end, end + TILE) if low else slice(TILE, OWN)
        self.ghost = OWN - 1 if low else end
        self.edge = OWN if low else end - 1
        self.spare = self.count - TILE + SWEEPS if low else 0
        self.facing = 1 if low else 0
        self.sent = slice(radial_cells - SWEEPS, radial_cells) if low else slice(0, SWEEPS)
        self.sent_tile = radial_cells - TILE if low else 0
        self.edge_tile = 0 if low else radial_cells - TILE


def shifted(s, by):
    return slice(s.start + by, s.stop + by)


def axial_sum(x):
    lane = lax.broadcasted_iota(jnp.int32, x.shape, 1)
    last = x.shape[1] - 1
    return jnp.where(lane == 0, 0.0, pltpu.roll(x, 1, 1)) + jnp.where(
        lane == last, 0.0, pltpu.roll(x, last, 1)
    )


def relaxed(column, side, beside, weight, shift):
    here = column[side.rows]
    radial = column[shifted(side.rows, -1)] + column[shifted(side.rows, 1)]
    nbr = beside + radial + axial_sum(here)
    kept = (1.0 - OMEGA) * here
    if shift is not None:
        kept = kept + shift
    return kept + weight * nbr


def mirror(column, side):
    column[side.ghost : side.ghost + 1] = column[side.edge : side.edge + 1]


def on_each_side(radial_cells, body):
    low = lax.axis_index("rad") == 0

    @pl.when(low)
    def _():
        body(Side(True, radial_cells))

    @pl.when(jnp.logical_not(low))
    def _():
        body(Side(False, radial_cells))


def copy_all(copies):
    for c in copies:
        c.start()
    for c in copies:
        c.wait()


def end_columns(edge, cells, count):
    return slice(0, count) if edge == 0 else slice(cells - count, cells)


def spare_rows(side):
    return [(slot, side.spare + i) for slot in range(SWEEPS) for i in range(TILE - SWEEPS)]


def close(column, side, facing):
    row = slice(side.ghost, side.ghost + 1)
    if facing:
        column[row] = jnp.zeros((1, column.shape[1]), jnp.float32)
    else:
        column[row] = column[side.edge : side.edge + 1]


def trajectories(side, field, other, weight, shift, messages):
    bufs = (field, other)
    for edge, message in enumerate(messages):

        def at(distance, n, edge=edge):
            return distance - 1 if edge == 0 else n - distance

        for k in range(2):
            facing = k == side.facing
            for i in range(SWEEPS):
                close(field.at[edge, k, i], side, facing)
            for sweep in range(SWEEPS):
                src, dst = bufs[sweep % 2], bufs[1 - sweep % 2]
                top = src.at[edge, k, at(1, SWEEPS)]
                message[k, sweep] = top[side.rows]
                for j in range(1, SWEEPS - sweep):
                    here = src.at[edge, k, at(j, SWEEPS)]
                    beside = src[edge, k, at(j + 1, SWEEPS), side.rows]
                    if j > 1:
                        beside = beside + src[edge, k, at(j - 1, SWEEPS), side.rows]
                    i = at(j, SWEEPS - 1)
                    out = dst.at[edge, k, at(j, SWEEPS)]
                    out[side.rows] = relaxed(here, side, beside, weight(edge, k, i), shift(edge, k, i))
                    close(out, side, facing)
            if message.shape[1] == SWEEPS:
                continue
            for i in range(2):
                message[k, SWEEPS + i] = weight(edge, k, at(1 + i, SWEEPS - 1))
            if facing:
                row = side.edge - side.first
                message[k, SWEEPS + 1, side.spare : side.spare + 1] = weight(
                    edge, k, at(3, SWEEPS - 1)
                )[row : row + 1]


def pack(p_ref, s_ref, d_ref, cut_ref, edge_ref, p_ends, s_ends, d_ends, tiles, edge_tiles, sems):
    cells, radial_cells = p_ref.shape[1:3]

    def body(side):
        copies = []

        def fetch(source, target):
            copies.append(pltpu.make_async_copy(source, target, sems.at[len(copies)]))

        rows = pl.ds(side.sent_tile, TILE)
        for i, x in enumerate((p_ref, s_ref, d_ref)):
            fetch(x.at[:, :, rows, :], tiles.at[i])
        fetch(p_ref.at[side.facing, :, pl.ds(side.edge_tile, TILE), :], edge_tiles)
        for source, target in ((p_ref, p_ends), (s_ref, s_ends), (d_ref, d_ends)):
            count = target.shape[2]
            for edge in range(2):
                span = pl.ds(end_columns(edge, cells, count).start, count)
                fetch(source.at[:, span], target.at[edge])
        copy_all(copies)
        cut_ref[...] = tiles[:, :, :, shifted(side.sent, -side.sent_tile), :]
        at = side.edge - OWN - side.edge_tile
        for j in range(cells):
            edge_ref[j : j + 1] = edge_tiles[j, at : at + 1]

    on_each_side(radial_cells, body)


def fill_ends(field, side, p_ends, cut_ref, cells):
    for edge in range(2):
        columns = end_columns(edge, cells, SWEEPS)
        for k in range(2):
            for i in range(SWEEPS):
                field[edge, k, i, side.own] = p_ends[edge, k, i]
                field[edge, k, i, side.cut] = cut_ref[0, k, columns.start + i]


def send_block(side, arriving, block_ref, messages):
    arriving.wait()
    for message in messages:
        for i, (slot, row) in enumerate(spare_rows(side)):
            message[side.facing, slot, row : row + 1] = block_ref[i : i + 1]


def first_edges(
    p_ends, s_ends, d_ends, cut_ref, block_ref, last, first, block, sem, field, other, weight, shift
):
    radial_cells = p_ends.shape[3]
    cells = cut_ref.shape[2]
    n = SWEEPS - 1

    def body(side):
        arriving = pltpu.make_async_copy(block_ref, block, sem)
        arriving.start()
        own = shifted(side.own, -side.first)
        cut = shifted(side.cut, -side.first)
        fill_ends(field, side, p_ends, cut_ref, cells)
        for edge in range(2):
            columns = end_columns(edge, cells, n)
            for k in range(2):
                for i in range(n):
                    for rows, s, d in (
                        (own, s_ends[edge, k, i], d_ends[edge, k, i]),
                        (cut, cut_ref[1, k, columns.start + i], cut_ref[2, k, columns.start + i]),
                    ):
                        w = OMEGA / (6.0 + d)
                        weight[edge, k, i, rows] = w
                        shift[edge, k, i, rows] = w * s
        trajectories(
            side,
            field,
            other,
            lambda e, k, i: weight[e, k, i],
            lambda e, k, i: shift[e, k, i],
            (first, last),
        )
        send_block(side, arriving, block, (first, last))

    on_each_side(radial_cells, body)


def later_edges(p_ends, b_ends, w_ends, cut_ref, block_ref, last, first, block, sem, field, other):
    cells, radial_cells = cut_ref.shape[2], p_ends.shape[3]

    def body(side):
        arriving = pltpu.make_async_copy(block_ref, block, sem)
        arriving.start()
        fill_ends(field, side, p_ends, cut_ref, cells)
        trajectories(
            side,
            field,
            other,
            lambda e, k, i: w_ends[e, k, i + e],
            lambda e, k, i: b_ends[e, k, i + e],
            (first, last),
        )
        send_block(side, arriving, block, (first, last))

    on_each_side(radial_cells, body)


def inner_sweeps(side, levels, weight, shift, last, out_ref, stash, tile_out, w_tile, sems):
    cells = levels.shape[2]
    radial_cells = side.own.stop - side.own.start
    for j in range(cells):
        for k in range(2):
            close(levels.at[0, k, j], side, k == side.facing)
        for n in range(1, SWEEPS):
            close(levels.at[n, side.facing, j], side, True)
    at = side.edge - side.first
    for e, first in enumerate((0, cells - 2)):
        for k in range(2):
            for i in range(2):
                stash[e, 0, k, i] = levels[0, k, first + i]
    for n in range(SWEEPS):
        final = n == SWEEPS - 1

        def step(j, carry, n=n, final=final):
            for k in range(2):
                beside = levels[n, k, j - 1, side.rows] + levels[n, k, j + 1, side.rows]
                new = relaxed(levels.at[n, k, j], side, beside, weight[k, j], shift[k, j])
                if final:
                    last[k, j - SWEEPS] = new[shifted(side.own, -side.first)]
                else:
                    levels[n + 1, k, j, side.rows] = new
                    if k != side.facing:
                        levels[n + 1, k, j, side.ghost : side.ghost + 1] = new[at : at + 1]
            return carry

        lax.fori_loop(n + 1, cells - 1 - n, step, 0, unroll=2)
        if not final:
            for e, first in enumerate((n + 1, cells - 3 - n)):
                for k in range(2):
                    for i in range(2):
                        stash[e, n + 1, k, i] = levels[n + 1, k, first + i]
    inner = pltpu.make_async_copy(
        last, out_ref.at[:, pl.ds(SWEEPS, cells - 2 * SWEEPS)], sems.at[0]
    )
    inner.start()
    tile_out[...] = last[side.facing, :, side.edge_tile : side.edge_tile + TILE, :]
    first = side.edge_tile + OWN - side.first
    w_tile[...] = weight[side.facing, :, first : first + TILE, :]
    return inner


def first_interior(
    p_ref, s_ref, d_ref, cut_ref,
    out_ref, stash, tile_out, w_tile, cut_out, b_ends, w_ends, b_out, w_out,
    levels, last, shift, weight, sems,
):
    cells, radial_cells = p_ref.shape[1:3]

    def body(side):
        own = pl.ds(OWN - side.first, radial_cells)
        copy_all(
            [
                pltpu.make_async_copy(
                    p_ref, levels.at[0, :, :, pl.ds(OWN, radial_cells), :], sems.at[0]
                ),
                pltpu.make_async_copy(s_ref, shift.at[:, :, own, :], sems.at[1]),
                pltpu.make_async_copy(d_ref, weight.at[:, :, own, :], sems.at[2]),
            ]
        )
        cut = shifted(side.cut, -side.first)
        levels[0, :, :, side.cut, :] = cut_ref[0]
        shift[:, :, cut, :] = cut_ref[1]
        weight[:, :, cut, :] = cut_ref[2]

        def invert(j, carry):
            for k in range(2):
                w = OMEGA / (6.0 + weight[k, j])
                weight[k, j] = w
                shift[k, j] = w * shift[k, j]
            return carry

        lax.fori_loop(0, cells, invert, 0)
        pending = [
            pltpu.make_async_copy(shift, b_out, sems.at[1]),
            pltpu.make_async_copy(weight, w_out, sems.at[2]),
        ]
        for c in pending:
            c.start()
        for e in range(2):
            columns = end_columns(e, cells, SWEEPS)
            b_ends[e] = shift[:, columns]
            w_ends[e] = weight[:, columns]
        pending.append(
            inner_sweeps(
                side, levels, weight, shift, last, out_ref, stash, tile_out, w_tile, sems
            )
        )
        cut_out[...] = last[:, :, side.sent, :]
        for c in pending:
            c.wait()

    on_each_side(radial_cells, body)


def later_interior(
    p_ref, b_ref, w_ref, cut_ref, out_ref, stash, tile_out, w_tile, levels, last, shift, weight, sems
):
    cells, radial_cells = p_ref.shape[1:3]

    def body(side):
        copy_all(
            [
                pltpu.make_async_copy(
                    p_ref, levels.at[0, :, :, pl.ds(OWN, radial_cells), :], sems.at[0]
                ),
                pltpu.make_async_copy(b_ref, shift, sems.at[1]),
                pltpu.make_async_copy(w_ref, weight, sems.at[2]),
            ]
        )
        levels[0, :, :, side.cut, :] = cut_ref[0]
        inner_sweeps(
            side, levels, weight, shift, last, out_ref, stash, tile_out, w_tile, sems
        ).wait()

    on_each_side(radial_cells, body)


def ghost_response(side, start_ref, w_tile, block_ref, messages, weights, wide, source):
    facing = side.facing
    cells = w_tile.shape[0]
    reach = SWEEPS - 1
    tile = slice(side.edge_tile + OWN - side.first, side.edge_tile + OWN - side.first + TILE)
    at = side.edge - OWN - side.edge_tile
    rows = spare_rows(side)
    for i, (slot, row) in enumerate(rows):
        wide[i : i + 1] = messages[0][facing, slot, row : row + 1]
        wide[2 * cells + i : 2 * cells + i + 1] = messages[1][facing, slot, row : row + 1]
    wide[cells : 2 * cells] = block_ref[...]
    source[...] = jnp.zeros(source.shape, jnp.float32)
    for c in range(cells + 2 * reach):
        source[c, at : at + 1] = wide[pl.ds(start_ref[0] + c, 1), :]
    row = lax.broadcasted_iota(jnp.int32, source.shape[1:], 0)
    weight = [w_tile[j] for j in range(cells)]
    for e in range(2):
        far = weights[e][facing, SWEEPS + 1, side.spare : side.spare + 1]
        beyond = [
            weights[e][facing, SWEEPS, tile],
            weights[e][facing, SWEEPS + 1, tile],
            jnp.where(row == at, far, 0.0),
        ]
        weight = beyond[::-1] + weight if e == 0 else weight + beyond
    given = [source[c] for c in range(cells + 2 * reach)]
    response = [w * g for w, g in zip(weight, given)]
    for n in range(1, SWEEPS):
        old = response
        response = list(old)
        for c in range(n, len(old) - n):
            x = old[c]
            radial = jnp.where(row == 0, 0.0, pltpu.roll(x, 1, 0)) + jnp.where(
                row == TILE - 1, 0.0, pltpu.roll(x, TILE - 1, 0)
            )
            nbr = (old[c - 1] + old[c + 1]) + (radial + axial_sum(x)) + given[c]
            response[c] = (1.0 - OMEGA) * x + weight[c] * nbr
    return response[reach : reach + cells]


def finish(known, start_ref, b_ends, w_ends, w_tile, stash, block_ref, tile_in, left_ref, right_ref, *rest):
    if known:
        left_w, right_w, _, out_ref, *rest = rest
        weights = (left_w, right_w)
    else:
        cut_in, _, out_ref, cut_out, edge_out, ends_out, *rest = rest
        weights = (left_ref, right_ref)
    levels, last, inner_tiles, near, near2, wide, source, sems = rest
    messages = (left_ref, right_ref)
    cells, radial_cells = out_ref.shape[1:3]

    def column(e, d):
        return d - 1 if e == 0 else cells - d

    def body(side):
        facing = side.facing

        def at(n, e, k, d):
            if d <= n:
                return levels.at[n, e, k, d]
            return stash.at[e, n, k, d - n - 1 if e == 0 else n + 2 - d]

        for e in range(2):
            for k in range(2):
                levels[0, e, k, 0, side.rows] = messages[e][k, 0]
                for buf in (near, near2):
                    buf[e, k] = jnp.zeros(buf.shape[2:], jnp.float32)
        nears = (near, near2)

        def own_column(n, e, k, d):
            i = d - 1 if e == 0 else SWEEPS - d
            beside = at(n, e, k, d - 1)[side.rows] + at(n, e, k, d + 1)[side.rows]
            return relaxed(at(n, e, k, d), side, beside, w_ends[e, k, i], b_ends[e, k, i])

        for n in range(SWEEPS - 1):
            src, dst = nears[n % 2], nears[1 - n % 2]
            for e in range(2):
                for k in range(2):
                    for d in range(1, n + 2):
                        levels[n + 1, e, k, d, side.rows] = own_column(n, e, k, d)
                        close(levels.at[n + 1, e, k, d], side, k == facing)
                    beside = at(n, e, k, 1)[side.rows]
                    if n > 0:
                        beside = beside + src[e, k, 1, side.rows]
                        new = relaxed(src.at[e, k, 0], side, beside, weights[e][k, SWEEPS], None)
                    else:
                        new = weights[e][k, SWEEPS] * beside
                    dst[e, k, 0, side.rows] = new
                    levels[n + 1, e, k, 0, side.rows] = messages[e][k, n + 1] + new
                    close(dst.at[e, k, 0], side, k == facing)
                    if n == 1:
                        dst[e, k, 1, side.rows] = (
                            weights[e][k, SWEEPS + 1] * src[e, k, 0, side.rows]
                        )
        copies = []

        def store(source, target):
            copies.append(pltpu.make_async_copy(source, target, sems.at[len(copies)]))
            copies[-1].start()

        response = None
        tile = slice(side.edge_tile, side.edge_tile + TILE)
        for k in (1 - facing, facing):
            if k == facing:
                response = ghost_response(
                    side, start_ref, w_tile, block_ref, messages, weights, wide, source
                )
                for i in range(cells - 2 * SWEEPS):
                    inner_tiles[i] = tile_in[i] + response[SWEEPS + i]
                store(
                    inner_tiles,
                    out_ref.at[
                        k, pl.ds(SWEEPS, cells - 2 * SWEEPS), pl.ds(side.edge_tile, TILE), :
                    ],
                )
            for e in range(2):
                first = end_columns(e, cells, SWEEPS).start
                for d in range(1, SWEEPS + 1):
                    new = own_column(SWEEPS - 1, e, k, d)[shifted(side.own, -side.first)]
                    i = column(e, d) - first
                    last[e, k, i] = new
                    if k == facing:
                        last[e, k, i, tile] = new[tile] + response[first + i]
                store(last.at[e, k], out_ref.at[k, pl.ds(first, SWEEPS)])
        if not known:
            row = side.edge - OWN
            cut_out[0, :, SWEEPS : cells - SWEEPS] = cut_in[...]
            for i in range(cells - 2 * SWEEPS):
                j = SWEEPS + i
                r = row - side.edge_tile
                edge_out[j : j + 1] = inner_tiles[i, r : r + 1]
            for e in range(2):
                first = end_columns(e, cells, SWEEPS).start
                cut_out[0, :, first : first + SWEEPS] = last[e, :, :, side.sent, :]
                for i in range(SWEEPS):
                    edge_out[first + i : first + i + 1] = last[e, facing, i, row : row + 1]
            ends_out[...] = last[...]
        for c in copies:
            c.wait()

    on_each_side(radial_cells, body)


def ring(size, step):
    return [(i, (i + step) % size) for i in range(size)]


def facing_pairs(size, turn):
    pairs = []
    for i in range(size):
        pairs.append((2 * ((i - turn) % size) + 1, 2 * i))
        pairs.append((2 * ((i + turn) % size), 2 * i + 1))
    return pairs


def far_pairs(size, turn):
    return [(2 * i + r, 2 * ((i + (2 * r - 1) * turn) % size) + r) for i in range(size) for r in range(2)]


def facing_block(edge, offset, radial_index):
    size = lax.axis_size("az")
    cells = edge.shape[0]
    turn = (offset + cells // 2) // cells
    rest = offset - turn * cells
    turn = turn % size
    near = min(size, 16)

    def far(t):
        return lambda e: lax.ppermute(e, ("az", "rad"), far_pairs(size, t * near))

    def branch(t):
        return lambda e: lax.ppermute(e, ("az", "rad"), facing_pairs(size, t))

    if size > near:
        edge = lax.switch(turn // near, [far(t) for t in range(-(-size // near))], edge)
    block = lax.switch(turn % near, [branch(t) for t in range(near)], edge)
    return block, cells - (SWEEPS - 1) + jnp.where(radial_index == 0, -rest, rest)


def per_device(pressure, source, diagonal, rot_offset):
    _, cells, radial_cells, lanes = pressure.shape
    size = lax.axis_size("az")
    radial_index = lax.axis_index("rad")
    rows, span = radial_cells + 4 * TILE, radial_cells + TILE

    def array(*shape):
        return jax.ShapeDtypeStruct(shape, jnp.float32)

    def scratch(*shape):
        return pltpu.VMEM(shape, jnp.float32)

    def pinned(x):
        return pltpu.with_memory_space_constraint(x, pltpu.HBM)

    kept = pltpu.HBM((2, cells, span, lanes), jnp.float32)
    kept_ends = array(2, 2, SWEEPS, span, lanes)
    stash = array(2, SWEEPS, 2, 2, rows, lanes)
    cells_in = cells - 2 * SWEEPS
    tiles = array(cells_in, TILE, lanes)
    vmem = pl.BlockSpec(memory_space=pltpu.VMEM)
    smem = pl.BlockSpec(memory_space=pltpu.SMEM)
    hbm = pl.BlockSpec(memory_space=pltpu.HBM)
    anywhere = pl.BlockSpec(memory_space=pl.ANY)
    columns = scratch(2, 2, SWEEPS, rows, lanes)
    three = scratch(2, 2, SWEEPS - 1, span, lanes)

    def call(kernel, out_shape, in_specs, out_specs, scratch_shapes, operands, work_columns, **more):
        work = 2 * work_columns * span * lanes
        return pl.pallas_call(
            kernel,
            out_shape=out_shape,
            in_specs=in_specs,
            out_specs=out_specs,
            scratch_shapes=scratch_shapes,
            compiler_params=pltpu.CompilerParams(vmem_limit_bytes=28 << 20),
            cost_estimate=pl.CostEstimate(
                flops=12 * work, bytes_accessed=8 * work, transcendentals=0
            ),
            **more,
        )(*operands)

    fields = tuple(pinned(x) for x in (pressure, source, diagonal))
    cut, edge, *ends = call(
        pack,
        (
            array(3, 2, cells, SWEEPS, lanes),
            array(cells, lanes),
            array(2, 2, SWEEPS, radial_cells, lanes),
            array(2, 2, SWEEPS - 1, radial_cells, lanes),
            array(2, 2, SWEEPS - 1, radial_cells, lanes),
        ),
        [hbm] * 3,
        [vmem] * 2 + [anywhere] * 3,
        [
            scratch(3, 2, cells, TILE, lanes),
            scratch(cells, TILE, lanes),
            pltpu.SemaphoreType.DMA((10,)),
        ],
        fields,
        1,
        name="pack",
    )
    for step in range(1, STEPS + 1):
        known = step > 1
        cut = lax.ppermute(cut, "rad", [(0, 1), (1, 0)])
        offset = rot_offset[0] * step % (cells * size)
        block, start = facing_block(edge, offset, radial_index)
        place = start.astype(jnp.int32).reshape(1)
        message = array(2, SWEEPS if known else SLOTS, span, lanes)
        last, first = call(
            later_edges if known else first_edges,
            (message, message),
            [vmem] * 4 + [anywhere],
            [vmem] * 2,
            [scratch(cells, lanes), pltpu.SemaphoreType.DMA, columns, columns]
            + ([] if known else [three] * 2),
            (*ends, cut, block),
            12,
            name="edges",
        )
        left = lax.ppermute(last, "az", ring(size, 1))
        right = lax.ppermute(first, "az", ring(size, -1))
        result = pltpu.HBM(pressure.shape, jnp.float32)
        outs = (result, stash, tiles, array(cells, TILE, lanes))
        out_specs = [hbm] + [vmem] * 3
        if not known:
            outs += (array(2, cells_in, SWEEPS, lanes), kept_ends, kept_ends, kept, kept)
            out_specs += [vmem] * 3 + [hbm] * 2
        inner, saved, inner_tiles, w_tile, *made = call(
            later_interior if known else first_interior,
            outs,
            [hbm] * 3 + [vmem],
            out_specs,
            [
                scratch(SWEEPS, 2, cells, rows, lanes),
                scratch(2, cells_in, radial_cells, lanes),
                scratch(*kept.shape),
                scratch(*kept.shape),
                pltpu.SemaphoreType.DMA((3,)),
            ],
            (*fields, cut),
            44,
            name="interior",
        )
        if not known:
            inner_cut, b_ends, w_ends, shift, weight = made
            beyond = (left, right)
        operands = (
            place,
            b_ends,
            w_ends,
            w_tile,
            saved,
            block,
            inner_tiles,
            left,
            right,
        )
        operands += beyond if known else (inner_cut,)
        outs = result
        if not known:
            outs = (
                result,
                array(1, 2, cells, SWEEPS, lanes),
                array(cells, lanes),
                array(2, 2, SWEEPS, radial_cells, lanes),
            )
        pressure = call(
            functools.partial(finish, known),
            outs,
            [smem] + [vmem] * (len(operands) - 1) + [hbm],
            hbm if known else [hbm] + [vmem] * 3,
            [
                scratch(SWEEPS, 2, 2, SWEEPS, rows, lanes),
                scratch(2, 2, SWEEPS, radial_cells, lanes),
                scratch(*tiles.shape),
                scratch(2, 2, 2, rows, lanes),
                scratch(2, 2, 2, rows, lanes),
                scratch(3 * cells, lanes),
                scratch(cells + 2 * (SWEEPS - 1), TILE, lanes),
                pltpu.SemaphoreType.DMA((5,)),
            ],
            (*operands, inner),
            26,
            input_output_aliases={len(operands): 0},
            name="finish",
        )
        if not known:
            pressure, cut, edge, ends_now = pressure
            fields = tuple(pinned(x) for x in (pressure, shift, weight))
            ends = (ends_now, b_ends, w_ends)
    return pressure


def solution(mesh):
    placed = (
        P(None, "az", "rad", None),
        P(None, "az", "rad", None),
        P(None, "az", "rad", None),
        P(),
    )
    return jax.shard_map(
        per_device,
        mesh=mesh,
        in_specs=placed,
        out_specs=P(None, "az", "rad", None),
        check_vma=False,
    )
```

```python
import functools

import jax
import jax.numpy as jnp
from jax import lax
from jax.experimental import pallas as pl
from jax.experimental.pallas import tpu as pltpu
from jax.sharding import PartitionSpec as P

STEPS = 2
SWEEPS = 4
OMEGA = 0.8
TILE = 8
OWN = 2 * TILE
SLOTS = SWEEPS + 2


class Side:
    def __init__(self, low, radial_cells):
        end = OWN + radial_cells
        self.low = low
        self.own = slice(OWN, end)
        self.first = OWN if low else TILE
        self.count = radial_cells + TILE
        self.rows = slice(self.first, self.first + self.count)
        self.cut = slice(end, end + SWEEPS) if low else slice(OWN - SWEEPS, OWN)
        self.tile = slice(end, end + TILE) if low else slice(TILE, OWN)
        self.ghost = OWN - 1 if low else end
        self.edge = OWN if low else end - 1
        self.spare = self.count - TILE + SWEEPS if low else 0
        self.facing = 1 if low else 0
        self.sent = slice(radial_cells - SWEEPS, radial_cells) if low else slice(0, SWEEPS)
        self.sent_tile = radial_cells - TILE if low else 0
        self.edge_tile = 0 if low else radial_cells - TILE


def shifted(s, by):
    return slice(s.start + by, s.stop + by)


def axial_sum(x):
    lane = lax.broadcasted_iota(jnp.int32, x.shape, 1)
    last = x.shape[1] - 1
    return jnp.where(lane == 0, 0.0, pltpu.roll(x, 1, 1)) + jnp.where(
        lane == last, 0.0, pltpu.roll(x, last, 1)
    )


def neighbour_matrix(lanes):
    gap = lax.broadcasted_iota(jnp.int32, (lanes, lanes), 0) - lax.broadcasted_iota(
        jnp.int32, (lanes, lanes), 1
    )
    return jnp.where(jnp.abs(gap) == 1, 1.0, 0.0).astype(jnp.bfloat16)


def axial_product(x, matrix):
    high = x.astype(jnp.bfloat16)
    low = (x - high.astype(jnp.float32)).astype(jnp.bfloat16)
    return jnp.dot(high, matrix, preferred_element_type=jnp.float32) + jnp.dot(
        low, matrix, preferred_element_type=jnp.float32
    )


def relax_all(side, matrix, items):
    by_matrix = len(items) // 4 * 2
    axial = []
    if by_matrix:
        here = jnp.concatenate([item[0][side.rows] for item in items[:by_matrix]], axis=0)
        product = axial_product(here, matrix)
        axial = [product[i * side.count : (i + 1) * side.count] for i in range(by_matrix)]
    for i, (column, beside, weight, shift, take) in enumerate(items):
        here = column[side.rows]
        radial = column[shifted(side.rows, -1)] + column[shifted(side.rows, 1)]
        nbr = beside() + radial + (axial[i] if i < by_matrix else axial_sum(here))
        kept = (1.0 - OMEGA) * here
        if shift is not None:
            kept = kept + shift()
        take(kept + weight() * nbr)


def on_each_side(radial_cells, body):
    low = lax.axis_index("rad") == 0

    @pl.when(low)
    def _():
        body(Side(True, radial_cells))

    @pl.when(jnp.logical_not(low))
    def _():
        body(Side(False, radial_cells))


def copy_all(copies):
    for c in copies:
        c.start()
    for c in copies:
        c.wait()


def end_columns(edge, cells, count):
    return slice(0, count) if edge == 0 else slice(cells - count, cells)


def spare_rows(side):
    return [(slot, side.spare + i) for slot in range(SWEEPS) for i in range(TILE - SWEEPS)]


def close(column, side, facing):
    row = slice(side.ghost, side.ghost + 1)
    if facing:
        column[row] = jnp.zeros((1, column.shape[1]), jnp.float32)
    else:
        column[row] = column[side.edge : side.edge + 1]


def trajectories(side, field, other, weight, shift, messages):
    bufs = (field, other)
    matrix = neighbour_matrix(field.shape[-1])

    def at(edge, distance, n):
        return distance - 1 if edge == 0 else n - distance

    for edge in range(2):
        for k in range(2):
            for i in range(SWEEPS):
                close(field.at[edge, k, i], side, k == side.facing)
    for sweep in range(SWEEPS):
        src, dst = bufs[sweep % 2], bufs[1 - sweep % 2]
        items = []
        for edge, message in enumerate(messages):
            for k in range(2):
                message[k, sweep] = src[edge, k, at(edge, 1, SWEEPS), side.rows]
                for j in range(1, SWEEPS - sweep):
                    i = at(edge, j, SWEEPS - 1)

                    def beside(edge=edge, k=k, j=j):
                        total = src[edge, k, at(edge, j + 1, SWEEPS), side.rows]
                        if j > 1:
                            total = total + src[edge, k, at(edge, j - 1, SWEEPS), side.rows]
                        return total

                    def take(new, edge=edge, k=k, j=j):
                        out = dst.at[edge, k, at(edge, j, SWEEPS)]
                        out[side.rows] = new
                        close(out, side, k == side.facing)

                    items.append(
                        (
                            src.at[edge, k, at(edge, j, SWEEPS)],
                            beside,
                            functools.partial(weight, edge, k, i),
                            functools.partial(shift, edge, k, i),
                            take,
                        )
                    )
        relax_all(side, matrix, items)
    for edge, message in enumerate(messages):
        if message.shape[1] == SWEEPS:
            continue
        for k in range(2):
            for i in range(2):
                message[k, SWEEPS + i] = weight(edge, k, at(edge, 1 + i, SWEEPS - 1))
            if k == side.facing:
                row = side.edge - side.first
                message[k, SWEEPS + 1, side.spare : side.spare + 1] = weight(
                    edge, k, at(edge, 3, SWEEPS - 1)
                )[row : row + 1]


def pack(p_ref, s_ref, d_ref, cut_ref, edge_ref, p_ends, s_ends, d_ends, tiles, edge_tiles, sems):
    cells, radial_cells = p_ref.shape[1:3]

    def body(side):
        copies = []

        def fetch(source, target):
            copies.append(pltpu.make_async_copy(source, target, sems.at[len(copies)]))

        rows = pl.ds(side.sent_tile, TILE)
        for i, x in enumerate((p_ref, s_ref, d_ref)):
            fetch(x.at[:, :, rows, :], tiles.at[i])
        fetch(p_ref.at[side.facing, :, pl.ds(side.edge_tile, TILE), :], edge_tiles)
        for source, target in ((p_ref, p_ends), (s_ref, s_ends), (d_ref, d_ends)):
            count = target.shape[2]
            for edge in range(2):
                span = pl.ds(end_columns(edge, cells, count).start, count)
                fetch(source.at[:, span], target.at[edge])
        copy_all(copies)
        cut_ref[...] = tiles[:, :, :, shifted(side.sent, -side.sent_tile), :]
        at = side.edge - OWN - side.edge_tile
        for j in range(cells):
            edge_ref[j : j + 1] = edge_tiles[j, at : at + 1]

    on_each_side(radial_cells, body)


def fill_ends(field, side, p_ends, cut_ref, cells):
    for edge in range(2):
        columns = end_columns(edge, cells, SWEEPS)
        for k in range(2):
            for i in range(SWEEPS):
                field[edge, k, i, side.own] = p_ends[edge, k, i]
                field[edge, k, i, side.cut] = cut_ref[0, k, columns.start + i]


def send_block(side, arriving, block_ref, messages):
    arriving.wait()
    for message in messages:
        for i, (slot, row) in enumerate(spare_rows(side)):
            message[side.facing, slot, row : row + 1] = block_ref[i : i + 1]


def first_edges(
    p_ends, s_ends, d_ends, cut_ref, block_ref, last, first, block, sem, field, other, weight, shift
):
    radial_cells = p_ends.shape[3]
    cells = cut_ref.shape[2]
    n = SWEEPS - 1

    def body(side):
        arriving = pltpu.make_async_copy(block_ref, block, sem)
        arriving.start()
        own = shifted(side.own, -side.first)
        cut = shifted(side.cut, -side.first)
        fill_ends(field, side, p_ends, cut_ref, cells)
        for edge in range(2):
            columns = end_columns(edge, cells, n)
            for k in range(2):
                for i in range(n):
                    for rows, s, d in (
                        (own, s_ends[edge, k, i], d_ends[edge, k, i]),
                        (cut, cut_ref[1, k, columns.start + i], cut_ref[2, k, columns.start + i]),
                    ):
                        w = OMEGA / (6.0 + d)
                        weight[edge, k, i, rows] = w
                        shift[edge, k, i, rows] = w * s
        trajectories(
            side,
            field,
            other,
            lambda e, k, i: weight[e, k, i],
            lambda e, k, i: shift[e, k, i],
            (first, last),
        )
        send_block(side, arriving, block, (first, last))

    on_each_side(radial_cells, body)


def later_edges(p_ends, b_ends, w_ends, cut_ref, block_ref, last, first, block, sem, field, other):
    cells, radial_cells = cut_ref.shape[2], p_ends.shape[3]

    def body(side):
        arriving = pltpu.make_async_copy(block_ref, block, sem)
        arriving.start()
        fill_ends(field, side, p_ends, cut_ref, cells)
        trajectories(
            side,
            field,
            other,
            lambda e, k, i: w_ends[e, k, i + e],
            lambda e, k, i: b_ends[e, k, i + e],
            (first, last),
        )
        send_block(side, arriving, block, (first, last))

    on_each_side(radial_cells, body)


def inner_sweeps(side, levels, weight, shift, last, out_ref, stash, tile_out, w_tile, sems):
    cells = levels.shape[2]
    radial_cells = side.own.stop - side.own.start
    for j in range(cells):
        for k in range(2):
            close(levels.at[0, k, j], side, k == side.facing)
        for n in range(1, SWEEPS):
            close(levels.at[n, side.facing, j], side, True)
    at = side.edge - side.first
    for e, first in enumerate((0, cells - 2)):
        for k in range(2):
            for i in range(2):
                stash[e, 0, k, i] = levels[0, k, first + i]
    matrix = neighbour_matrix(levels.shape[-1])
    for n in range(SWEEPS):
        final = n == SWEEPS - 1

        def step(i, carry, n=n, final=final):
            items = []
            for k in (1, 0):
                for j in (n + 1 + 2 * i, n + 2 + 2 * i):

                    def beside(k=k, j=j):
                        return levels[n, k, j - 1, side.rows] + levels[n, k, j + 1, side.rows]

                    def take(new, k=k, j=j):
                        if final:
                            last[k, j - SWEEPS] = new[shifted(side.own, -side.first)]
                            return
                        levels[n + 1, k, j, side.rows] = new
                        if k != side.facing:
                            levels[n + 1, k, j, side.ghost : side.ghost + 1] = new[at : at + 1]

                    items.append(
                        (
                            levels.at[n, k, j],
                            beside,
                            functools.partial(lambda k, j: weight[k, j], k, j),
                            functools.partial(lambda k, j: shift[k, j], k, j),
                            take,
                        )
                    )
            relax_all(side, matrix, items)
            return carry

        lax.fori_loop(0, cells // 2 - 1 - n, step, 0, unroll=2 if n % 2 else 1)
        if not final:
            for e, first in enumerate((n + 1, cells - 3 - n)):
                for k in range(2):
                    for i in range(2):
                        stash[e, n + 1, k, i] = levels[n + 1, k, first + i]
    inner = pltpu.make_async_copy(
        last, out_ref.at[:, pl.ds(SWEEPS, cells - 2 * SWEEPS)], sems.at[0]
    )
    inner.start()
    tile_out[...] = last[side.facing, :, side.edge_tile : side.edge_tile + TILE, :]
    first = side.edge_tile + OWN - side.first
    w_tile[...] = weight[side.facing, :, first : first + TILE, :]
    return inner


def first_interior(
    p_ref, s_ref, d_ref, cut_ref,
    out_ref, stash, tile_out, w_tile, cut_out, b_ends, w_ends, b_out, w_out,
    levels, last, shift, weight, sems,
):
    cells, radial_cells = p_ref.shape[1:3]

    def body(side):
        own = pl.ds(OWN - side.first, radial_cells)
        copy_all(
            [
                pltpu.make_async_copy(
                    p_ref, levels.at[0, :, :, pl.ds(OWN, radial_cells), :], sems.at[0]
                ),
                pltpu.make_async_copy(s_ref, shift.at[:, :, own, :], sems.at[1]),
                pltpu.make_async_copy(d_ref, weight.at[:, :, own, :], sems.at[2]),
            ]
        )
        cut = shifted(side.cut, -side.first)
        levels[0, :, :, side.cut, :] = cut_ref[0]
        shift[:, :, cut, :] = cut_ref[1]
        weight[:, :, cut, :] = cut_ref[2]

        def invert(j, carry):
            for k in range(2):
                w = OMEGA / (6.0 + weight[k, j])
                weight[k, j] = w
                shift[k, j] = w * shift[k, j]
            return carry

        lax.fori_loop(0, cells, invert, 0)
        pending = [
            pltpu.make_async_copy(shift, b_out, sems.at[1]),
            pltpu.make_async_copy(weight, w_out, sems.at[2]),
        ]
        for c in pending:
            c.start()
        for e in range(2):
            columns = end_columns(e, cells, SWEEPS)
            b_ends[e] = shift[:, columns]
            w_ends[e] = weight[:, columns]
        pending.append(
            inner_sweeps(
                side, levels, weight, shift, last, out_ref, stash, tile_out, w_tile, sems
            )
        )
        cut_out[...] = last[:, :, side.sent, :]
        for c in pending:
            c.wait()

    on_each_side(radial_cells, body)


def later_interior(
    p_ref, b_ref, w_ref, cut_ref, out_ref, stash, tile_out, w_tile, levels, last, shift, weight, sems
):
    cells, radial_cells = p_ref.shape[1:3]

    def body(side):
        copy_all(
            [
                pltpu.make_async_copy(
                    p_ref, levels.at[0, :, :, pl.ds(OWN, radial_cells), :], sems.at[0]
                ),
                pltpu.make_async_copy(b_ref, shift, sems.at[1]),
                pltpu.make_async_copy(w_ref, weight, sems.at[2]),
            ]
        )
        levels[0, :, :, side.cut, :] = cut_ref[0]
        inner_sweeps(
            side, levels, weight, shift, last, out_ref, stash, tile_out, w_tile, sems
        ).wait()

    on_each_side(radial_cells, body)


def ghost_response(side, start_ref, w_tile, block_ref, messages, weights, wide, source):
    facing = side.facing
    cells = w_tile.shape[0]
    reach = SWEEPS - 1
    tile = slice(side.edge_tile + OWN - side.first, side.edge_tile + OWN - side.first + TILE)
    at = side.edge - OWN - side.edge_tile
    rows = spare_rows(side)
    for i, (slot, row) in enumerate(rows):
        wide[i : i + 1] = messages[0][facing, slot, row : row + 1]
        wide[2 * cells + i : 2 * cells + i + 1] = messages[1][facing, slot, row : row + 1]
    wide[cells : 2 * cells] = block_ref[...]
    source[...] = jnp.zeros(source.shape, jnp.float32)
    for c in range(cells + 2 * reach):
        source[c, at : at + 1] = wide[pl.ds(start_ref[0] + c, 1), :]
    row = lax.broadcasted_iota(jnp.int32, source.shape[1:], 0)
    weight = [w_tile[j] for j in range(cells)]
    for e in range(2):
        far = weights[e][facing, 1, side.spare : side.spare + 1]
        beyond = [
            weights[e][facing, 0, tile],
            weights[e][facing, 1, tile],
            jnp.where(row == at, far, 0.0),
        ]
        weight = beyond[::-1] + weight if e == 0 else weight + beyond
    given = [source[c] for c in range(cells + 2 * reach)]
    response = [w * g for w, g in zip(weight, given)]
    for n in range(1, SWEEPS):
        old = response
        response = list(old)
        for c in range(n, len(old) - n):
            x = old[c]
            radial = jnp.where(row == 0, 0.0, pltpu.roll(x, 1, 0)) + jnp.where(
                row == TILE - 1, 0.0, pltpu.roll(x, TILE - 1, 0)
            )
            nbr = (old[c - 1] + old[c + 1]) + (radial + axial_sum(x)) + given[c]
            response[c] = (1.0 - OMEGA) * x + weight[c] * nbr
    return response[reach : reach + cells]


def finish(known, start_ref, b_ends, w_ends, w_tile, stash, block_ref, tile_in, left_ref, right_ref, *rest):
    if known:
        beyond, _, out_ref, *rest = rest
        weights = (beyond.at[0], beyond.at[1])
    else:
        cut_in, _, out_ref, cut_out, edge_out, ends_out, beyond_out, *rest = rest
        weights = tuple(x.at[:, pl.ds(SWEEPS, 2)] for x in (left_ref, right_ref))
    levels, last, inner_tiles, near, near2, wide, source, sems = rest
    messages = (left_ref, right_ref)
    cells, radial_cells = out_ref.shape[1:3]

    def column(e, d):
        return d - 1 if e == 0 else cells - d

    def body(side):
        facing = side.facing

        def at(n, e, k, d):
            if d <= n:
                return levels.at[n, e, k, d]
            return stash.at[e, n, k, d - n - 1 if e == 0 else n + 2 - d]

        for e in range(2):
            for k in range(2):
                levels[0, e, k, 0, side.rows] = messages[e][k, 0]
                for buf in (near, near2):
                    buf[e, k] = jnp.zeros(buf.shape[2:], jnp.float32)
        nears = (near, near2)

        matrix = neighbour_matrix(levels.shape[-1])

        def own_column(n, e, k, d, take):
            i = d - 1 if e == 0 else SWEEPS - d
            return (
                at(n, e, k, d),
                lambda: at(n, e, k, d - 1)[side.rows] + at(n, e, k, d + 1)[side.rows],
                lambda: w_ends[e, k, i],
                lambda: b_ends[e, k, i],
                take,
            )

        for n in range(SWEEPS - 1):
            src, dst = nears[n % 2], nears[1 - n % 2]
            items = []
            for e in range(2):
                for k in range(2):
                    for d in range(1, n + 2):

                        def take(new, e=e, k=k, d=d):
                            levels[n + 1, e, k, d, side.rows] = new
                            close(levels.at[n + 1, e, k, d], side, k == facing)

                        items.append(own_column(n, e, k, d, take))

                    def take(new, e=e, k=k):
                        dst[e, k, 0, side.rows] = new
                        levels[n + 1, e, k, 0, side.rows] = messages[e][k, n + 1] + new
                        close(dst.at[e, k, 0], side, k == facing)

                    if n == 0:
                        take(weights[e][k, 0] * at(n, e, k, 1)[side.rows])
                        continue
                    items.append(
                        (
                            src.at[e, k, 0],
                            lambda e=e, k=k: at(n, e, k, 1)[side.rows] + src[e, k, 1, side.rows],
                            lambda e=e, k=k: weights[e][k, 0],
                            None,
                            take,
                        )
                    )
                    if n == 1:
                        dst[e, k, 1, side.rows] = weights[e][k, 1] * src[e, k, 0, side.rows]
            relax_all(side, matrix, items)
        copies = []

        def store(source, target):
            copies.append(pltpu.make_async_copy(source, target, sems.at[len(copies)]))
            copies[-1].start()

        response = None
        tile = slice(side.edge_tile, side.edge_tile + TILE)
        for k in (1 - facing, facing):
            if k == facing:
                response = ghost_response(
                    side, start_ref, w_tile, block_ref, messages, weights, wide, source
                )
                for i in range(cells - 2 * SWEEPS):
                    inner_tiles[i] = tile_in[i] + response[SWEEPS + i]
                store(
                    inner_tiles,
                    out_ref.at[
                        k, pl.ds(SWEEPS, cells - 2 * SWEEPS), pl.ds(side.edge_tile, TILE), :
                    ],
                )
            items = []
            for d in range(1, SWEEPS + 1):
                for e in range(2):
                    first = end_columns(e, cells, SWEEPS).start

                    def take(new, e=e, k=k, i=column(e, d) - first, first=first):
                        new = new[shifted(side.own, -side.first)]
                        last[e, k, i] = new
                        if k == facing:
                            last[e, k, i, tile] = new[tile] + response[first + i]

                    items.append(own_column(SWEEPS - 1, e, k, d, take))
            relax_all(side, matrix, items)
            for e in range(2):
                first = end_columns(e, cells, SWEEPS).start
                store(last.at[e, k], out_ref.at[k, pl.ds(first, SWEEPS)])
        if not known:
            row = side.edge - OWN
            cut_out[0, :, SWEEPS : cells - SWEEPS] = cut_in[...]
            for i in range(cells - 2 * SWEEPS):
                j = SWEEPS + i
                r = row - side.edge_tile
                edge_out[j : j + 1] = inner_tiles[i, r : r + 1]
            for e in range(2):
                first = end_columns(e, cells, SWEEPS).start
                cut_out[0, :, first : first + SWEEPS] = last[e, :, :, side.sent, :]
                for i in range(SWEEPS):
                    edge_out[first + i : first + i + 1] = last[e, facing, i, row : row + 1]
            ends_out[...] = last[...]
            for e in range(2):
                beyond_out[e] = weights[e][...]
        for c in copies:
            c.wait()

    on_each_side(radial_cells, body)


def ring(size, step):
    return [(i, (i + step) % size) for i in range(size)]


def facing_pairs(size, turn):
    pairs = []
    for i in range(size):
        pairs.append((2 * ((i - turn) % size) + 1, 2 * i))
        pairs.append((2 * ((i + turn) % size), 2 * i + 1))
    return pairs


def far_pairs(size, turn):
    return [(2 * i + r, 2 * ((i + (2 * r - 1) * turn) % size) + r) for i in range(size) for r in range(2)]


def facing_block(edge, offset, radial_index):
    size = lax.axis_size("az")
    cells = edge.shape[0]
    turn = (offset + cells // 2) // cells
    rest = offset - turn * cells
    turn = turn % size
    near = min(size, 16)

    def far(t):
        return lambda e: lax.ppermute(e, ("az", "rad"), far_pairs(size, t * near))

    def branch(t):
        return lambda e: lax.ppermute(e, ("az", "rad"), facing_pairs(size, t))

    if size > near:
        edge = lax.switch(turn // near, [far(t) for t in range(-(-size // near))], edge)
    block = lax.switch(turn % near, [branch(t) for t in range(near)], edge)
    return block, cells - (SWEEPS - 1) + jnp.where(radial_index == 0, -rest, rest)


def per_device(pressure, source, diagonal, rot_offset):
    _, cells, radial_cells, lanes = pressure.shape
    size = lax.axis_size("az")
    radial_index = lax.axis_index("rad")
    rows, span = radial_cells + 4 * TILE, radial_cells + TILE

    def array(*shape):
        return jax.ShapeDtypeStruct(shape, jnp.float32)

    def scratch(*shape):
        return pltpu.VMEM(shape, jnp.float32)

    def pinned(x):
        return pltpu.with_memory_space_constraint(x, pltpu.HBM)

    kept = pltpu.HBM((2, cells, span, lanes), jnp.float32)
    kept_ends = array(2, 2, SWEEPS, span, lanes)
    stash = array(2, SWEEPS, 2, 2, rows, lanes)
    cells_in = cells - 2 * SWEEPS
    tiles = array(cells_in, TILE, lanes)
    vmem = pl.BlockSpec(memory_space=pltpu.VMEM)
    smem = pl.BlockSpec(memory_space=pltpu.SMEM)
    hbm = pl.BlockSpec(memory_space=pltpu.HBM)
    anywhere = pl.BlockSpec(memory_space=pl.ANY)
    columns = scratch(2, 2, SWEEPS, rows, lanes)
    three = scratch(2, 2, SWEEPS - 1, span, lanes)

    def call(kernel, out_shape, in_specs, out_specs, scratch_shapes, operands, work_columns, **more):
        work = 2 * work_columns * span * lanes
        return pl.pallas_call(
            kernel,
            out_shape=out_shape,
            in_specs=in_specs,
            out_specs=out_specs,
            scratch_shapes=scratch_shapes,
            compiler_params=pltpu.CompilerParams(vmem_limit_bytes=28 << 20),
            cost_estimate=pl.CostEstimate(
                flops=12 * work, bytes_accessed=8 * work, transcendentals=0
            ),
            **more,
        )(*operands)

    fields = tuple(pinned(x) for x in (pressure, source, diagonal))
    cut, edge, *ends = call(
        pack,
        (
            array(3, 2, cells, SWEEPS, lanes),
            array(cells, lanes),
            array(2, 2, SWEEPS, radial_cells, lanes),
            array(2, 2, SWEEPS - 1, radial_cells, lanes),
            array(2, 2, SWEEPS - 1, radial_cells, lanes),
        ),
        [hbm] * 3,
        [vmem] * 2 + [anywhere] * 3,
        [
            scratch(3, 2, cells, TILE, lanes),
            scratch(cells, TILE, lanes),
            pltpu.SemaphoreType.DMA((10,)),
        ],
        fields,
        1,
        name="pack",
    )
    for step in range(1, STEPS + 1):
        known = step > 1
        cut = lax.ppermute(cut, "rad", [(0, 1), (1, 0)])
        offset = rot_offset[0] * step % (cells * size)
        block, start = facing_block(edge, offset, radial_index)
        place = start.astype(jnp.int32).reshape(1)
        message = array(2, SWEEPS if known else SLOTS, span, lanes)
        last, first = call(
            later_edges if known else first_edges,
            (message, message),
            [vmem] * 4 + [anywhere],
            [vmem] * 2,
            [scratch(cells, lanes), pltpu.SemaphoreType.DMA, columns, columns]
            + ([] if known else [three] * 2),
            (*ends, cut, block),
            12,
            name="edges",
        )
        left = lax.ppermute(last, "az", ring(size, 1))
        right = lax.ppermute(first, "az", ring(size, -1))
        result = pltpu.HBM(pressure.shape, jnp.float32)
        outs = (result, stash, tiles, array(cells, TILE, lanes))
        out_specs = [hbm] + [vmem] * 3
        if not known:
            outs += (array(2, cells_in, SWEEPS, lanes), kept_ends, kept_ends, kept, kept)
            out_specs += [vmem] * 3 + [hbm] * 2
        inner, saved, inner_tiles, w_tile, *made = call(
            later_interior if known else first_interior,
            outs,
            [hbm] * 3 + [vmem],
            out_specs,
            [
                scratch(SWEEPS, 2, cells, rows, lanes),
                scratch(2, cells_in, radial_cells, lanes),
                scratch(*kept.shape),
                scratch(*kept.shape),
                pltpu.SemaphoreType.DMA((3,)),
            ],
            (*fields, cut),
            44,
            name="interior",
        )
        if not known:
            inner_cut, b_ends, w_ends, shift, weight = made
        operands = (
            place,
            b_ends,
            w_ends,
            w_tile,
            saved,
            block,
            inner_tiles,
            left,
            right,
        )
        operands += (beyond,) if known else (inner_cut,)
        outs = result
        if not known:
            outs = (
                result,
                array(1, 2, cells, SWEEPS, lanes),
                array(cells, lanes),
                array(2, 2, SWEEPS, radial_cells, lanes),
                array(2, 2, 2, span, lanes),
            )
        pressure = call(
            functools.partial(finish, known),
            outs,
            [smem] + [vmem] * (len(operands) - 1) + [hbm],
            hbm if known else [hbm] + [vmem] * 4,
            [
                scratch(SWEEPS, 2, 2, SWEEPS, rows, lanes),
                scratch(2, 2, SWEEPS, radial_cells, lanes),
                scratch(*tiles.shape),
                scratch(2, 2, 2, rows, lanes),
                scratch(2, 2, 2, rows, lanes),
                scratch(3 * cells, lanes),
                scratch(cells + 2 * (SWEEPS - 1), TILE, lanes),
                pltpu.SemaphoreType.DMA((5,)),
            ],
            (*operands, inner),
            26,
            input_output_aliases={len(operands): 0},
            name="finish",
        )
        if not known:
            pressure, cut, edge, ends_now, beyond = pressure
            fields = tuple(pinned(x) for x in (pressure, shift, weight))
            ends = (ends_now, b_ends, w_ends)
    return pressure


def solution(mesh):
    placed = (
        P(None, "az", "rad", None),
        P(None, "az", "rad", None),
        P(None, "az", "rad", None),
        P(),
    )
    return jax.shard_map(
        per_device,
        mesh=mesh,
        in_specs=placed,
        out_specs=P(None, "az", "rad", None),
        check_vma=False,
    )
```

```python
import functools

import jax
import jax.numpy as jnp
from jax import lax
from jax.experimental import pallas as pl
from jax.experimental.pallas import tpu as pltpu
from jax.sharding import PartitionSpec as P

STEPS = 2
SWEEPS = 4
OMEGA = 0.8
TILE = 8
OWN = 2 * TILE
SLOTS = SWEEPS + 2


class Side:
    def __init__(self, low, radial_cells):
        end = OWN + radial_cells
        self.low = low
        self.own = slice(OWN, end)
        self.first = OWN if low else TILE
        self.count = radial_cells + TILE
        self.rows = slice(self.first, self.first + self.count)
        self.cut = slice(end, end + SWEEPS) if low else slice(OWN - SWEEPS, OWN)
        self.tile = slice(end, end + TILE) if low else slice(TILE, OWN)
        self.ghost = OWN - 1 if low else end
        self.edge = OWN if low else end - 1
        self.spare = self.count - TILE + SWEEPS if low else 0
        self.facing = 1 if low else 0
        self.sent = slice(radial_cells - SWEEPS, radial_cells) if low else slice(0, SWEEPS)
        self.sent_tile = radial_cells - TILE if low else 0
        self.edge_tile = 0 if low else radial_cells - TILE


def shifted(s, by):
    return slice(s.start + by, s.stop + by)


def axial_sum(x):
    lane = lax.broadcasted_iota(jnp.int32, x.shape, 1)
    last = x.shape[1] - 1
    return jnp.where(lane == 0, 0.0, pltpu.roll(x, 1, 1)) + jnp.where(
        lane == last, 0.0, pltpu.roll(x, last, 1)
    )


def neighbour_matrix(lanes):
    gap = lax.broadcasted_iota(jnp.int32, (lanes, lanes), 0) - lax.broadcasted_iota(
        jnp.int32, (lanes, lanes), 1
    )
    return jnp.where(jnp.abs(gap) == 1, 1.0, 0.0).astype(jnp.bfloat16)


def axial_product(x, matrix):
    high = x.astype(jnp.bfloat16)
    low = (x - high.astype(jnp.float32)).astype(jnp.bfloat16)
    return jnp.dot(high, matrix, preferred_element_type=jnp.float32) + jnp.dot(
        low, matrix, preferred_element_type=jnp.float32
    )


def relax_all(side, matrix, items):
    by_matrix = len(items) // 4 * 2
    axial = []
    if by_matrix:
        here = jnp.concatenate([item[0][side.rows] for item in items[:by_matrix]], axis=0)
        product = axial_product(here, matrix)
        axial = [product[i * side.count : (i + 1) * side.count] for i in range(by_matrix)]
    for i, (column, beside, weight, shift, take) in enumerate(items):
        here = column[side.rows]
        radial = column[shifted(side.rows, -1)] + column[shifted(side.rows, 1)]
        nbr = beside() + radial + (axial[i] if i < by_matrix else axial_sum(here))
        kept = (1.0 - OMEGA) * here
        if shift is not None:
            kept = kept + shift()
        take(kept + weight() * nbr)


def on_each_side(radial_cells, body):
    low = lax.axis_index("rad") == 0

    @pl.when(low)
    def _():
        body(Side(True, radial_cells))

    @pl.when(jnp.logical_not(low))
    def _():
        body(Side(False, radial_cells))


def copy_all(copies):
    for c in copies:
        c.start()
    for c in copies:
        c.wait()


def end_columns(edge, cells, count):
    return slice(0, count) if edge == 0 else slice(cells - count, cells)


def spare_rows(side):
    return [(slot, side.spare + i) for slot in range(SWEEPS) for i in range(TILE - SWEEPS)]


def close(column, side, facing):
    row = slice(side.ghost, side.ghost + 1)
    if facing:
        column[row] = jnp.zeros((1, column.shape[1]), jnp.float32)
    else:
        column[row] = column[side.edge : side.edge + 1]


def trajectories(side, field, other, weight, shift, messages):
    bufs = (field, other)
    matrix = neighbour_matrix(field.shape[-1])

    def at(edge, distance, n):
        return distance - 1 if edge == 0 else n - distance

    for edge in range(2):
        for k in range(2):
            for i in range(SWEEPS):
                close(field.at[edge, k, i], side, k == side.facing)
    for sweep in range(SWEEPS):
        src, dst = bufs[sweep % 2], bufs[1 - sweep % 2]
        items = []
        for edge, message in enumerate(messages):
            for k in range(2):
                message[k, sweep] = src[edge, k, at(edge, 1, SWEEPS), side.rows]
                for j in range(1, SWEEPS - sweep):
                    i = at(edge, j, SWEEPS - 1)

                    def beside(edge=edge, k=k, j=j):
                        total = src[edge, k, at(edge, j + 1, SWEEPS), side.rows]
                        if j > 1:
                            total = total + src[edge, k, at(edge, j - 1, SWEEPS), side.rows]
                        return total

                    def take(new, edge=edge, k=k, j=j):
                        out = dst.at[edge, k, at(edge, j, SWEEPS)]
                        out[side.rows] = new
                        close(out, side, k == side.facing)

                    items.append(
                        (
                            src.at[edge, k, at(edge, j, SWEEPS)],
                            beside,
                            functools.partial(weight, edge, k, i),
                            functools.partial(shift, edge, k, i),
                            take,
                        )
                    )
        relax_all(side, matrix, items)
    for edge, message in enumerate(messages):
        if message.shape[1] == SWEEPS:
            continue
        for k in range(2):
            for i in range(2):
                message[k, SWEEPS + i] = weight(edge, k, at(edge, 1 + i, SWEEPS - 1))
            if k == side.facing:
                row = side.edge - side.first
                message[k, SWEEPS + 1, side.spare : side.spare + 1] = weight(
                    edge, k, at(edge, 3, SWEEPS - 1)
                )[row : row + 1]


def pack(p_ref, s_ref, d_ref, cut_ref, edge_ref, p_ends, s_ends, d_ends, tiles, edge_tiles, sems):
    cells, radial_cells = p_ref.shape[1:3]

    def body(side):
        copies = []

        def fetch(source, target):
            copies.append(pltpu.make_async_copy(source, target, sems.at[len(copies)]))

        rows = pl.ds(side.sent_tile, TILE)
        for i, x in enumerate((p_ref, s_ref, d_ref)):
            fetch(x.at[:, :, rows, :], tiles.at[i])
        fetch(p_ref.at[side.facing, :, pl.ds(side.edge_tile, TILE), :], edge_tiles)
        for source, target in ((p_ref, p_ends), (s_ref, s_ends), (d_ref, d_ends)):
            count = target.shape[2]
            for edge in range(2):
                span = pl.ds(end_columns(edge, cells, count).start, count)
                fetch(source.at[:, span], target.at[edge])
        copy_all(copies)
        cut_ref[...] = tiles[:, :, :, shifted(side.sent, -side.sent_tile), :]
        at = side.edge - OWN - side.edge_tile
        for j in range(cells):
            edge_ref[j : j + 1] = edge_tiles[j, at : at + 1]

    on_each_side(radial_cells, body)


def fill_ends(field, side, p_ends, cut_ref, cells):
    for edge in range(2):
        columns = end_columns(edge, cells, SWEEPS)
        for k in range(2):
            for i in range(SWEEPS):
                field[edge, k, i, side.own] = p_ends[edge, k, i]
                field[edge, k, i, side.cut] = cut_ref[0, k, columns.start + i]


def send_block(side, arriving, block_ref, messages):
    arriving.wait()
    for message in messages:
        for i, (slot, row) in enumerate(spare_rows(side)):
            message[side.facing, slot, row : row + 1] = block_ref[i : i + 1]


def first_edges(
    p_ends, s_ends, d_ends, cut_ref, block_ref, last, first, block, sem, field, other, weight, shift
):
    radial_cells = p_ends.shape[3]
    cells = cut_ref.shape[2]
    n = SWEEPS - 1

    def body(side):
        arriving = pltpu.make_async_copy(block_ref, block, sem)
        arriving.start()
        own = shifted(side.own, -side.first)
        cut = shifted(side.cut, -side.first)
        fill_ends(field, side, p_ends, cut_ref, cells)
        for edge in range(2):
            columns = end_columns(edge, cells, n)
            for k in range(2):
                for i in range(n):
                    for rows, s, d in (
                        (own, s_ends[edge, k, i], d_ends[edge, k, i]),
                        (cut, cut_ref[1, k, columns.start + i], cut_ref[2, k, columns.start + i]),
                    ):
                        w = OMEGA / (6.0 + d)
                        weight[edge, k, i, rows] = w
                        shift[edge, k, i, rows] = w * s
        trajectories(
            side,
            field,
            other,
            lambda e, k, i: weight[e, k, i],
            lambda e, k, i: shift[e, k, i],
            (first, last),
        )
        send_block(side, arriving, block, (first, last))

    on_each_side(radial_cells, body)


def later_edges(p_ends, b_ends, w_ends, cut_ref, block_ref, last, first, block, sem, field, other):
    cells, radial_cells = cut_ref.shape[2], p_ends.shape[3]

    def body(side):
        arriving = pltpu.make_async_copy(block_ref, block, sem)
        arriving.start()
        fill_ends(field, side, p_ends, cut_ref, cells)
        trajectories(
            side,
            field,
            other,
            lambda e, k, i: w_ends[e, k, i + e],
            lambda e, k, i: b_ends[e, k, i + e],
            (first, last),
        )
        send_block(side, arriving, block, (first, last))

    on_each_side(radial_cells, body)


def inner_sweeps(side, levels, weight, shift, last, out_ref, stash, tile_out, w_tile, sems):
    cells = levels.shape[2]
    radial_cells = side.own.stop - side.own.start
    for j in range(cells):
        for k in range(2):
            close(levels.at[0, k, j], side, k == side.facing)
        for n in range(1, SWEEPS):
            close(levels.at[n, side.facing, j], side, True)
    at = side.edge - side.first
    for e, first in enumerate((0, cells - 2)):
        for k in range(2):
            for i in range(2):
                stash[e, 0, k, i] = levels[0, k, first + i]
    matrix = neighbour_matrix(levels.shape[-1])
    for n in range(SWEEPS):
        final = n == SWEEPS - 1

        def step(i, carry, n=n, final=final):
            items = []
            for k in (1, 0):
                for j in (n + 1 + 2 * i, n + 2 + 2 * i):

                    def beside(k=k, j=j):
                        return levels[n, k, j - 1, side.rows] + levels[n, k, j + 1, side.rows]

                    def take(new, k=k, j=j):
                        if final:
                            last[k, j - SWEEPS] = new[shifted(side.own, -side.first)]
                            return
                        levels[n + 1, k, j, side.rows] = new
                        if k != side.facing:
                            levels[n + 1, k, j, side.ghost : side.ghost + 1] = new[at : at + 1]

                    items.append(
                        (
                            levels.at[n, k, j],
                            beside,
                            functools.partial(lambda k, j: weight[k, j], k, j),
                            functools.partial(lambda k, j: shift[k, j], k, j),
                            take,
                        )
                    )
            relax_all(side, matrix, items)
            return carry

        lax.fori_loop(0, cells // 2 - 1 - n, step, 0, unroll=2 if n % 2 else 1)
        if not final:
            for e, first in enumerate((n + 1, cells - 3 - n)):
                for k in range(2):
                    for i in range(2):
                        stash[e, n + 1, k, i] = levels[n + 1, k, first + i]
    inner = pltpu.make_async_copy(
        last, out_ref.at[:, pl.ds(SWEEPS, cells - 2 * SWEEPS)], sems.at[0]
    )
    inner.start()
    tile_out[...] = last[side.facing, :, side.edge_tile : side.edge_tile + TILE, :]
    first = side.edge_tile + OWN - side.first
    w_tile[...] = weight[side.facing, :, first : first + TILE, :]
    return inner


def first_interior(
    p_ref, s_ref, d_ref, cut_ref,
    out_ref, stash, tile_out, w_tile, cut_out, b_ends, w_ends, b_out, w_out,
    levels, last, shift, weight, sems,
):
    cells, radial_cells = p_ref.shape[1:3]

    def body(side):
        own = pl.ds(OWN - side.first, radial_cells)
        copy_all(
            [
                pltpu.make_async_copy(
                    p_ref, levels.at[0, :, :, pl.ds(OWN, radial_cells), :], sems.at[0]
                ),
                pltpu.make_async_copy(s_ref, shift.at[:, :, own, :], sems.at[1]),
                pltpu.make_async_copy(d_ref, weight.at[:, :, own, :], sems.at[2]),
            ]
        )
        cut = shifted(side.cut, -side.first)
        levels[0, :, :, side.cut, :] = cut_ref[0]
        shift[:, :, cut, :] = cut_ref[1]
        weight[:, :, cut, :] = cut_ref[2]

        def invert(j, carry):
            for k in range(2):
                w = OMEGA / (6.0 + weight[k, j])
                weight[k, j] = w
                shift[k, j] = w * shift[k, j]
            return carry

        lax.fori_loop(0, cells, invert, 0)
        pending = [
            pltpu.make_async_copy(shift, b_out, sems.at[1]),
            pltpu.make_async_copy(weight, w_out, sems.at[2]),
        ]
        for c in pending:
            c.start()
        for e in range(2):
            columns = end_columns(e, cells, SWEEPS)
            b_ends[e] = shift[:, columns]
            w_ends[e] = weight[:, columns]
        pending.append(
            inner_sweeps(
                side, levels, weight, shift, last, out_ref, stash, tile_out, w_tile, sems
            )
        )
        cut_out[...] = last[:, :, side.sent, :]
        for c in pending:
            c.wait()

    on_each_side(radial_cells, body)


def later_interior(
    p_ref, b_ref, w_ref, cut_ref, out_ref, stash, tile_out, w_tile, levels, last, shift, weight, sems
):
    cells, radial_cells = p_ref.shape[1:3]

    def body(side):
        copy_all(
            [
                pltpu.make_async_copy(
                    p_ref, levels.at[0, :, :, pl.ds(OWN, radial_cells), :], sems.at[0]
                ),
                pltpu.make_async_copy(b_ref, shift, sems.at[1]),
                pltpu.make_async_copy(w_ref, weight, sems.at[2]),
            ]
        )
        levels[0, :, :, side.cut, :] = cut_ref[0]
        inner_sweeps(
            side, levels, weight, shift, last, out_ref, stash, tile_out, w_tile, sems
        ).wait()

    on_each_side(radial_cells, body)


def ghost_response(side, step, turn_ref, w_tile, block_ref, messages, weights, wide, source):
    facing = side.facing
    cells = w_tile.shape[0]
    reach = SWEEPS - 1
    tile = slice(side.edge_tile + OWN - side.first, side.edge_tile + OWN - side.first + TILE)
    at = side.edge - OWN - side.edge_tile
    rows = spare_rows(side)
    for i, (slot, row) in enumerate(rows):
        wide[i : i + 1] = messages[0][facing, slot, row : row + 1]
        wide[2 * cells + i : 2 * cells + i + 1] = messages[1][facing, slot, row : row + 1]
    wide[cells : 2 * cells] = block_ref[...]
    source[...] = jnp.zeros(source.shape, jnp.float32)
    offset = lax.rem(turn_ref[0] * step, cells * lax.axis_size("az"))
    rest = offset - lax.div(offset + cells // 2, cells) * cells
    start = cells - reach + (-rest if side.low else rest)
    for c in range(cells + 2 * reach):
        source[c, at : at + 1] = wide[pl.ds(start + c, 1), :]
    row = lax.broadcasted_iota(jnp.int32, source.shape[1:], 0)
    weight = [w_tile[j] for j in range(cells)]
    for e in range(2):
        far = weights[e][facing, 1, side.spare : side.spare + 1]
        beyond = [
            weights[e][facing, 0, tile],
            weights[e][facing, 1, tile],
            jnp.where(row == at, far, 0.0),
        ]
        weight = beyond[::-1] + weight if e == 0 else weight + beyond
    given = [source[c] for c in range(cells + 2 * reach)]
    response = [w * g for w, g in zip(weight, given)]
    for n in range(1, SWEEPS):
        old = response
        response = list(old)
        for c in range(n, len(old) - n):
            x = old[c]
            radial = jnp.where(row == 0, 0.0, pltpu.roll(x, 1, 0)) + jnp.where(
                row == TILE - 1, 0.0, pltpu.roll(x, TILE - 1, 0)
            )
            nbr = (old[c - 1] + old[c + 1]) + (radial + axial_sum(x)) + given[c]
            response[c] = (1.0 - OMEGA) * x + weight[c] * nbr
    return response[reach : reach + cells]


def finish(step, turn_ref, b_ends, w_ends, w_tile, stash, block_ref, tile_in, left_ref, right_ref, *rest):
    known = step > 1
    if known:
        beyond, _, out_ref, *rest = rest
        weights = (beyond.at[0], beyond.at[1])
    else:
        cut_in, _, out_ref, cut_out, edge_out, ends_out, beyond_out, *rest = rest
        weights = tuple(x.at[:, pl.ds(SWEEPS, 2)] for x in (left_ref, right_ref))
    levels, last, inner_tiles, near, near2, wide, source, sems = rest
    messages = (left_ref, right_ref)
    cells, radial_cells = out_ref.shape[1:3]

    def column(e, d):
        return d - 1 if e == 0 else cells - d

    def body(side):
        facing = side.facing

        def at(n, e, k, d):
            if d <= n:
                return levels.at[n, e, k, d]
            return stash.at[e, n, k, d - n - 1 if e == 0 else n + 2 - d]

        for e in range(2):
            for k in range(2):
                levels[0, e, k, 0, side.rows] = messages[e][k, 0]
                for buf in (near, near2):
                    buf[e, k] = jnp.zeros(buf.shape[2:], jnp.float32)
        nears = (near, near2)

        matrix = neighbour_matrix(levels.shape[-1])

        def own_column(n, e, k, d, take):
            i = d - 1 if e == 0 else SWEEPS - d
            return (
                at(n, e, k, d),
                lambda: at(n, e, k, d - 1)[side.rows] + at(n, e, k, d + 1)[side.rows],
                lambda: w_ends[e, k, i],
                lambda: b_ends[e, k, i],
                take,
            )

        for n in range(SWEEPS - 1):
            src, dst = nears[n % 2], nears[1 - n % 2]
            items = []
            for e in range(2):
                for k in range(2):
                    for d in range(1, n + 2):

                        def take(new, e=e, k=k, d=d):
                            levels[n + 1, e, k, d, side.rows] = new
                            close(levels.at[n + 1, e, k, d], side, k == facing)

                        items.append(own_column(n, e, k, d, take))

                    def take(new, e=e, k=k):
                        dst[e, k, 0, side.rows] = new
                        levels[n + 1, e, k, 0, side.rows] = messages[e][k, n + 1] + new
                        close(dst.at[e, k, 0], side, k == facing)

                    if n == 0:
                        take(weights[e][k, 0] * at(n, e, k, 1)[side.rows])
                        continue
                    items.append(
                        (
                            src.at[e, k, 0],
                            lambda e=e, k=k: at(n, e, k, 1)[side.rows] + src[e, k, 1, side.rows],
                            lambda e=e, k=k: weights[e][k, 0],
                            None,
                            take,
                        )
                    )
                    if n == 1:
                        dst[e, k, 1, side.rows] = weights[e][k, 1] * src[e, k, 0, side.rows]
            relax_all(side, matrix, items)
        copies = []

        def store(source, target):
            copies.append(pltpu.make_async_copy(source, target, sems.at[len(copies)]))
            copies[-1].start()

        response = None
        tile = slice(side.edge_tile, side.edge_tile + TILE)
        for k in (1 - facing, facing):
            if k == facing:
                response = ghost_response(
                    side, step, turn_ref, w_tile, block_ref, messages, weights, wide, source
                )
                for i in range(cells - 2 * SWEEPS):
                    inner_tiles[i] = tile_in[i] + response[SWEEPS + i]
                store(
                    inner_tiles,
                    out_ref.at[
                        k, pl.ds(SWEEPS, cells - 2 * SWEEPS), pl.ds(side.edge_tile, TILE), :
                    ],
                )
            items = []
            for d in range(1, SWEEPS + 1):
                for e in range(2):
                    first = end_columns(e, cells, SWEEPS).start

                    def take(new, e=e, k=k, i=column(e, d) - first, first=first):
                        new = new[shifted(side.own, -side.first)]
                        last[e, k, i] = new
                        if k == facing:
                            last[e, k, i, tile] = new[tile] + response[first + i]

                    items.append(own_column(SWEEPS - 1, e, k, d, take))
            relax_all(side, matrix, items)
            for e in range(2):
                first = end_columns(e, cells, SWEEPS).start
                store(last.at[e, k], out_ref.at[k, pl.ds(first, SWEEPS)])
        if not known:
            row = side.edge - OWN
            cut_out[0, :, SWEEPS : cells - SWEEPS] = cut_in[...]
            for i in range(cells - 2 * SWEEPS):
                j = SWEEPS + i
                r = row - side.edge_tile
                edge_out[j : j + 1] = inner_tiles[i, r : r + 1]
            for e in range(2):
                first = end_columns(e, cells, SWEEPS).start
                cut_out[0, :, first : first + SWEEPS] = last[e, :, :, side.sent, :]
                for i in range(SWEEPS):
                    edge_out[first + i : first + i + 1] = last[e, facing, i, row : row + 1]
            ends_out[...] = last[...]
            for e in range(2):
                beyond_out[e] = weights[e][...]
        for c in copies:
            c.wait()

    on_each_side(radial_cells, body)


def ring(size, step):
    return [(i, (i + step) % size) for i in range(size)]


def facing_pairs(size, turn):
    pairs = []
    for i in range(size):
        pairs.append((2 * ((i - turn) % size) + 1, 2 * i))
        pairs.append((2 * ((i + turn) % size), 2 * i + 1))
    return pairs


def far_pairs(size, turn):
    return [(2 * i + r, 2 * ((i + (2 * r - 1) * turn) % size) + r) for i in range(size) for r in range(2)]


def facing_block(edge, offset):
    size = lax.axis_size("az")
    cells = edge.shape[0]
    turn = (offset + cells // 2) // cells % size
    near = min(size, 16)

    def far(t):
        return lambda e: lax.ppermute(e, ("az", "rad"), far_pairs(size, t * near))

    def branch(t):
        return lambda e: lax.ppermute(e, ("az", "rad"), facing_pairs(size, t))

    if size > near:
        edge = lax.switch(turn // near, [far(t) for t in range(-(-size // near))], edge)
    return lax.switch(turn % near, [branch(t) for t in range(near)], edge)


def per_device(pressure, source, diagonal, rot_offset):
    _, cells, radial_cells, lanes = pressure.shape
    size = lax.axis_size("az")
    rows, span = radial_cells + 4 * TILE, radial_cells + TILE

    def array(*shape):
        return jax.ShapeDtypeStruct(shape, jnp.float32)

    def scratch(*shape):
        return pltpu.VMEM(shape, jnp.float32)

    def pinned(x):
        return pltpu.with_memory_space_constraint(x, pltpu.HBM)

    kept = pltpu.HBM((2, cells, span, lanes), jnp.float32)
    kept_ends = array(2, 2, SWEEPS, span, lanes)
    stash = array(2, SWEEPS, 2, 2, rows, lanes)
    cells_in = cells - 2 * SWEEPS
    tiles = array(cells_in, TILE, lanes)
    vmem = pl.BlockSpec(memory_space=pltpu.VMEM)
    smem = pl.BlockSpec(memory_space=pltpu.SMEM)
    hbm = pl.BlockSpec(memory_space=pltpu.HBM)
    anywhere = pl.BlockSpec(memory_space=pl.ANY)
    columns = scratch(2, 2, SWEEPS, rows, lanes)
    three = scratch(2, 2, SWEEPS - 1, span, lanes)

    def call(kernel, out_shape, in_specs, out_specs, scratch_shapes, operands, work_columns, **more):
        work = 2 * work_columns * span * lanes
        return pl.pallas_call(
            kernel,
            out_shape=out_shape,
            in_specs=in_specs,
            out_specs=out_specs,
            scratch_shapes=scratch_shapes,
            compiler_params=pltpu.CompilerParams(vmem_limit_bytes=28 << 20),
            cost_estimate=pl.CostEstimate(
                flops=12 * work, bytes_accessed=8 * work, transcendentals=0
            ),
            **more,
        )(*operands)

    fields = tuple(pinned(x) for x in (pressure, source, diagonal))
    cut, edge, *ends = call(
        pack,
        (
            array(3, 2, cells, SWEEPS, lanes),
            array(cells, lanes),
            array(2, 2, SWEEPS, radial_cells, lanes),
            array(2, 2, SWEEPS - 1, radial_cells, lanes),
            array(2, 2, SWEEPS - 1, radial_cells, lanes),
        ),
        [hbm] * 3,
        [vmem] * 2 + [anywhere] * 3,
        [
            scratch(3, 2, cells, TILE, lanes),
            scratch(cells, TILE, lanes),
            pltpu.SemaphoreType.DMA((10,)),
        ],
        fields,
        1,
        name="pack",
    )
    for step in range(1, STEPS + 1):
        known = step > 1
        cut = lax.ppermute(cut, "rad", [(0, 1), (1, 0)])
        offset = rot_offset[0] * step % (cells * size)
        block = facing_block(edge, offset)
        message = array(2, SWEEPS if known else SLOTS, span, lanes)
        last, first = call(
            later_edges if known else first_edges,
            (message, message),
            [vmem] * 4 + [anywhere],
            [vmem] * 2,
            [scratch(cells, lanes), pltpu.SemaphoreType.DMA, columns, columns]
            + ([] if known else [three] * 2),
            (*ends, cut, block),
            12,
            name="edges",
        )
        left = lax.ppermute(last, "az", ring(size, 1))
        right = lax.ppermute(first, "az", ring(size, -1))
        result = pltpu.HBM(pressure.shape, jnp.float32)
        outs = (result, stash, tiles, array(cells, TILE, lanes))
        out_specs = [hbm] + [vmem] * 3
        if not known:
            outs += (array(2, cells_in, SWEEPS, lanes), kept_ends, kept_ends, kept, kept)
            out_specs += [vmem] * 3 + [hbm] * 2
        inner, saved, inner_tiles, w_tile, *made = call(
            later_interior if known else first_interior,
            outs,
            [hbm] * 3 + [vmem],
            out_specs,
            [
                scratch(SWEEPS, 2, cells, rows, lanes),
                scratch(2, cells_in, radial_cells, lanes),
                scratch(*kept.shape),
                scratch(*kept.shape),
                pltpu.SemaphoreType.DMA((3,)),
            ],
            (*fields, cut),
            44,
            name="interior",
        )
        if not known:
            inner_cut, b_ends, w_ends, shift, weight = made
        operands = (
            rot_offset,
            b_ends,
            w_ends,
            w_tile,
            saved,
            block,
            inner_tiles,
            left,
            right,
        )
        operands += (beyond,) if known else (inner_cut,)
        outs = result
        if not known:
            outs = (
                result,
                array(1, 2, cells, SWEEPS, lanes),
                array(cells, lanes),
                array(2, 2, SWEEPS, radial_cells, lanes),
                array(2, 2, 2, span, lanes),
            )
        pressure = call(
            functools.partial(finish, step),
            outs,
            [smem] + [vmem] * (len(operands) - 1) + [hbm],
            hbm if known else [hbm] + [vmem] * 4,
            [
                scratch(SWEEPS, 2, 2, SWEEPS, rows, lanes),
                scratch(2, 2, SWEEPS, radial_cells, lanes),
                scratch(*tiles.shape),
                scratch(2, 2, 2, rows, lanes),
                scratch(2, 2, 2, rows, lanes),
                scratch(3 * cells, lanes),
                scratch(cells + 2 * (SWEEPS - 1), TILE, lanes),
                pltpu.SemaphoreType.DMA((5,)),
            ],
            (*operands, inner),
            26,
            input_output_aliases={len(operands): 0},
            name="finish",
        )
        if not known:
            pressure, cut, edge, ends_now, beyond = pressure
            fields = tuple(pinned(x) for x in (pressure, shift, weight))
            ends = (ends_now, b_ends, w_ends)
    return pressure


def solution(mesh):
    placed = (
        P(None, "az", "rad", None),
        P(None, "az", "rad", None),
        P(None, "az", "rad", None),
        P(),
    )
    return jax.shard_map(
        per_device,
        mesh=mesh,
        in_specs=placed,
        out_specs=P(None, "az", "rad", None),
        check_vma=False,
    )
```

```python
import functools

import jax
import jax.numpy as jnp
from jax import lax
from jax.experimental import pallas as pl
from jax.experimental.pallas import tpu as pltpu
from jax.sharding import PartitionSpec as P

STEPS = 2
SWEEPS = 4
OMEGA = 0.8
TILE = 8
OWN = 2 * TILE
EARLY = False
LEVELS = tuple(range(SWEEPS))
WEIGHTS = (SWEEPS, SWEEPS + 1)
FIRST_EARLY = (0, *WEIGHTS) if EARLY else ()
FIRST_LATE = LEVELS[1:] if EARLY else LEVELS + WEIGHTS


class Side:
    def __init__(self, low, radial_cells):
        end = OWN + radial_cells
        self.low = low
        self.own = slice(OWN, end)
        self.first = OWN if low else TILE
        self.count = radial_cells + TILE
        self.rows = slice(self.first, self.first + self.count)
        self.cut = slice(end, end + SWEEPS) if low else slice(OWN - SWEEPS, OWN)
        self.tile = slice(end, end + TILE) if low else slice(TILE, OWN)
        self.ghost = OWN - 1 if low else end
        self.edge = OWN if low else end - 1
        self.spare = self.count - 1 if low else 0
        self.inside = shifted(self.own, -self.first)
        self.facing = 1 if low else 0
        self.sent = slice(radial_cells - SWEEPS, radial_cells) if low else slice(0, SWEEPS)
        self.sent_tile = radial_cells - TILE if low else 0
        self.edge_tile = 0 if low else radial_cells - TILE

    def beyond(self, distance):
        return self.inside.stop - 1 + distance if self.low else self.inside.start - distance


def shifted(s, by):
    return slice(s.start + by, s.stop + by)


def axial_sum(x):
    lane = lax.broadcasted_iota(jnp.int32, x.shape, 1)
    last = x.shape[1] - 1
    return jnp.where(lane == 0, 0.0, pltpu.roll(x, 1, 1)) + jnp.where(
        lane == last, 0.0, pltpu.roll(x, last, 1)
    )


def neighbour_matrix(lanes):
    gap = lax.broadcasted_iota(jnp.int32, (lanes, lanes), 0) - lax.broadcasted_iota(
        jnp.int32, (lanes, lanes), 1
    )
    return jnp.where(jnp.abs(gap) == 1, 1.0, 0.0).astype(jnp.bfloat16)


def axial_product(x, matrix):
    high = x.astype(jnp.bfloat16)
    low = (x - high.astype(jnp.float32)).astype(jnp.bfloat16)
    return jnp.dot(high, matrix, preferred_element_type=jnp.float32) + jnp.dot(
        low, matrix, preferred_element_type=jnp.float32
    )


def relax_all(side, matrix, items):
    by_matrix = len(items) // 4 * 2
    axial = []
    if by_matrix:
        here = jnp.concatenate([item[0][side.rows] for item in items[:by_matrix]], axis=0)
        product = axial_product(here, matrix)
        axial = [product[i * side.count : (i + 1) * side.count] for i in range(by_matrix)]
    for i, (column, beside, weight, shift, take) in enumerate(items):
        here = column[side.rows]
        radial = column[shifted(side.rows, -1)] + column[shifted(side.rows, 1)]
        nbr = beside() + radial + (axial[i] if i < by_matrix else axial_sum(here))
        kept = (1.0 - OMEGA) * here
        if shift is not None:
            kept = kept + shift()
        take(kept + weight() * nbr)


def on_each_side(radial_cells, body):
    low = lax.axis_index("rad") == 0

    @pl.when(low)
    def _():
        body(Side(True, radial_cells))

    @pl.when(jnp.logical_not(low))
    def _():
        body(Side(False, radial_cells))


def copy_all(copies):
    for c in copies:
        c.start()
    for c in copies:
        c.wait()


def end_columns(edge, cells, count):
    return slice(0, count) if edge == 0 else slice(cells - count, cells)


def block_rows(cells):
    return cells // 2 + SWEEPS - 1


class Message:
    def __init__(self, slots, radial_cells, cells, weights):
        self.slots = slots
        self.radial_cells = radial_cells
        tail = []
        if 1 in slots:
            needed = [(n, SWEEPS - 1 - n) for n in LEVELS] + [(SWEEPS, 2)] * weights
            tail += [(slot, k, h) for slot, n in needed for k in range(2) for h in range(1, n + 1)]
            tail += [("block", i) for i in range(block_rows(cells))]
            tail += ["third"] * weights
        start = 2 * len(slots) * radial_cells
        self.tail = {what: start + i for i, what in enumerate(tail)}
        self.rows = start + -(-len(tail) // TILE) * TILE

    def block(self, slot, k):
        start = (2 * self.slots.index(slot) + k) * self.radial_cells
        return slice(start, start + self.radial_cells)

    def row(self, *what):
        at = self.tail[what if len(what) > 1 else what[0]]
        return slice(at, at + 1)

    def beyond(self, slot, k):
        return [w[2] for w in self.tail if w != "third" and w[:2] == (slot, k) and len(w) == 3]

    def put(self, ref, side, slot, k, value):
        if slot in self.slots:
            ref[self.block(slot, k)] = value[side.inside]
        for h in self.beyond(slot, k):
            at = side.beyond(h)
            ref[self.row(slot, k, h)] = value[at : at + 1]


def messages_of(step, radial_cells, cells):
    late = FIRST_LATE if step == 1 else LEVELS
    return (
        Message(FIRST_EARLY if step == 1 else (), radial_cells, cells, False),
        Message(late, radial_cells, cells, step == 1),
    )


def close(column, side, facing):
    row = slice(side.ghost, side.ghost + 1)
    if facing:
        column[row] = jnp.zeros((1, column.shape[1]), jnp.float32)
    else:
        column[row] = column[side.edge : side.edge + 1]


def trajectories(side, field, other, weight, shift, layout, messages, weights):
    bufs = (field, other)
    matrix = neighbour_matrix(field.shape[-1])

    def at(edge, distance, n):
        return distance - 1 if edge == 0 else n - distance

    for edge in range(2):
        for k in range(2):
            for i in range(SWEEPS):
                close(field.at[edge, k, i], side, k == side.facing)
    for sweep in range(SWEEPS):
        src, dst = bufs[sweep % 2], bufs[1 - sweep % 2]
        items = []
        for edge, message in enumerate(messages):
            for k in range(2):
                layout.put(
                    message, side, sweep, k, src[edge, k, at(edge, 1, SWEEPS), side.rows]
                )
                for j in range(1, SWEEPS - sweep):
                    i = at(edge, j, SWEEPS - 1)

                    def beside(edge=edge, k=k, j=j):
                        total = src[edge, k, at(edge, j + 1, SWEEPS), side.rows]
                        if j > 1:
                            total = total + src[edge, k, at(edge, j - 1, SWEEPS), side.rows]
                        return total

                    def take(new, edge=edge, k=k, j=j):
                        out = dst.at[edge, k, at(edge, j, SWEEPS)]
                        out[side.rows] = new
                        close(out, side, k == side.facing)

                    items.append(
                        (
                            src.at[edge, k, at(edge, j, SWEEPS)],
                            beside,
                            functools.partial(weight, edge, k, i),
                            functools.partial(shift, edge, k, i),
                            take,
                        )
                    )
        relax_all(side, matrix, items)
    if not weights:
        return
    for edge, message in enumerate(messages):
        for k in range(2):
            for i in range(2):
                layout.put(
                    message, side, SWEEPS + i, k, weight(edge, k, at(edge, 1 + i, SWEEPS - 1))
                )
        row = side.edge - side.first
        message[layout.row("third")] = weight(edge, side.facing, at(edge, 3, SWEEPS - 1))[
            row : row + 1
        ]


def pack(p_ref, s_ref, d_ref, cut_ref, edge_ref, p_ends, s_ends, d_ends, *rest):
    *early, tiles, edge_tiles, sems = rest
    cells, radial_cells = p_ref.shape[1:3]
    layout, _ = messages_of(1, radial_cells, cells)

    def body(side):
        copies = []

        def fetch(source, target):
            copies.append(pltpu.make_async_copy(source, target, sems.at[len(copies)]))

        rows = pl.ds(side.sent_tile, TILE)
        for i, x in enumerate((p_ref, s_ref, d_ref)):
            fetch(x.at[:, :, rows, :], tiles.at[i])
        fetch(p_ref.at[side.facing, :, pl.ds(side.edge_tile, TILE), :], edge_tiles)
        for source, target in ((p_ref, p_ends), (s_ref, s_ends), (d_ref, d_ends)):
            count = target.shape[2]
            for edge in range(2):
                span = pl.ds(end_columns(edge, cells, count).start, count)
                fetch(source.at[:, span], target.at[edge])
        copy_all(copies)
        for edge, message in enumerate(early[::-1]):
            for k in range(2):
                i = 0 if edge == 0 else SWEEPS - 1
                message[layout.block(0, k)] = p_ends[edge, k, i]
                for j in range(2):
                    i = j if edge == 0 else SWEEPS - 2 - j
                    message[layout.block(SWEEPS + j, k)] = OMEGA / (6.0 + d_ends[edge, k, i])
        cut_ref[...] = tiles[:, :, :, shifted(side.sent, -side.sent_tile), :]
        at = side.edge - OWN - side.edge_tile
        for j in range(cells):
            edge_ref[j : j + 1] = edge_tiles[j, at : at + 1]

    on_each_side(radial_cells, body)


def fill_ends(field, side, p_ends, cut_ref, cells):
    for edge in range(2):
        columns = end_columns(edge, cells, SWEEPS)
        for k in range(2):
            for i in range(SWEEPS):
                field[edge, k, i, side.own] = p_ends[edge, k, i]
                field[edge, k, i, side.cut] = cut_ref[0, k, columns.start + i]


def send_block(layout, arriving, block, messages):
    arriving.wait()
    cells = block.shape[0]
    count = block_rows(cells)
    for edge, message in enumerate(messages):
        for i in range(count):
            at = i if edge == 0 else cells - count + i
            message[layout.row("block", i)] = block[at : at + 1]


def first_edges(
    p_ends, s_ends, d_ends, cut_ref, block_ref, last, first, block, sem, field, other, weight, shift
):
    radial_cells = p_ends.shape[3]
    cells = cut_ref.shape[2]
    n = SWEEPS - 1
    _, layout = messages_of(1, radial_cells, cells)

    def body(side):
        arriving = pltpu.make_async_copy(block_ref, block, sem)
        arriving.start()
        own = shifted(side.own, -side.first)
        cut = shifted(side.cut, -side.first)
        fill_ends(field, side, p_ends, cut_ref, cells)
        for edge in range(2):
            columns = end_columns(edge, cells, n)
            for k in range(2):
                for i in range(n):
                    for rows, s, d in (
                        (own, s_ends[edge, k, i], d_ends[edge, k, i]),
                        (cut, cut_ref[1, k, columns.start + i], cut_ref[2, k, columns.start + i]),
                    ):
                        w = OMEGA / (6.0 + d)
                        weight[edge, k, i, rows] = w
                        shift[edge, k, i, rows] = w * s
        trajectories(
            side,
            field,
            other,
            lambda e, k, i: weight[e, k, i],
            lambda e, k, i: shift[e, k, i],
            layout,
            (first, last),
            True,
        )
        send_block(layout, arriving, block, (first, last))

    on_each_side(radial_cells, body)


def later_edges(p_ends, b_ends, w_ends, cut_ref, block_ref, last, first, block, sem, field, other):
    cells, radial_cells = cut_ref.shape[2], p_ends.shape[3]
    _, layout = messages_of(2, radial_cells, cells)

    def body(side):
        arriving = pltpu.make_async_copy(block_ref, block, sem)
        arriving.start()
        fill_ends(field, side, p_ends, cut_ref, cells)
        trajectories(
            side,
            field,
            other,
            lambda e, k, i: w_ends[e, k, i + e],
            lambda e, k, i: b_ends[e, k, i + e],
            layout,
            (first, last),
            False,
        )
        send_block(layout, arriving, block, (first, last))

    on_each_side(radial_cells, body)


def inner_sweeps(side, levels, weight, shift, last, out_ref, stash, tile_out, w_tile, sems):
    cells = levels.shape[2]
    radial_cells = side.own.stop - side.own.start
    for j in range(cells):
        for k in range(2):
            close(levels.at[0, k, j], side, k == side.facing)
        for n in range(1, SWEEPS):
            close(levels.at[n, side.facing, j], side, True)
    at = side.edge - side.first
    for e, first in enumerate((0, cells - 2)):
        for k in range(2):
            for i in range(2):
                stash[e, 0, k, i] = levels[0, k, first + i]
    matrix = neighbour_matrix(levels.shape[-1])
    for n in range(SWEEPS):
        final = n == SWEEPS - 1

        def step(i, carry, n=n, final=final):
            items = []
            for k in (1, 0):
                for j in (n + 1 + 2 * i, n + 2 + 2 * i):

                    def beside(k=k, j=j):
                        return levels[n, k, j - 1, side.rows] + levels[n, k, j + 1, side.rows]

                    def take(new, k=k, j=j):
                        if final:
                            last[k, j - SWEEPS] = new[shifted(side.own, -side.first)]
                            return
                        levels[n + 1, k, j, side.rows] = new
                        if k != side.facing:
                            levels[n + 1, k, j, side.ghost : side.ghost + 1] = new[at : at + 1]

                    items.append(
                        (
                            levels.at[n, k, j],
                            beside,
                            functools.partial(lambda k, j: weight[k, j], k, j),
                            functools.partial(lambda k, j: shift[k, j], k, j),
                            take,
                        )
                    )
            relax_all(side, matrix, items)
            return carry

        lax.fori_loop(0, cells // 2 - 1 - n, step, 0, unroll=2 if n % 2 else 1)
        if not final:
            for e, first in enumerate((n + 1, cells - 3 - n)):
                for k in range(2):
                    for i in range(2):
                        stash[e, n + 1, k, i] = levels[n + 1, k, first + i]
    inner = pltpu.make_async_copy(
        last, out_ref.at[:, pl.ds(SWEEPS, cells - 2 * SWEEPS)], sems.at[0]
    )
    inner.start()
    tile_out[...] = last[side.facing, :, side.edge_tile : side.edge_tile + TILE, :]
    first = side.edge_tile + OWN - side.first
    w_tile[...] = weight[side.facing, :, first : first + TILE, :]
    return inner


def first_interior(
    p_ref, s_ref, d_ref, cut_ref,
    out_ref, stash, tile_out, w_tile, cut_out, b_ends, w_ends, b_out, w_out,
    levels, last, shift, weight, sems,
):
    cells, radial_cells = p_ref.shape[1:3]

    def body(side):
        own = pl.ds(OWN - side.first, radial_cells)
        copy_all(
            [
                pltpu.make_async_copy(
                    p_ref, levels.at[0, :, :, pl.ds(OWN, radial_cells), :], sems.at[0]
                ),
                pltpu.make_async_copy(s_ref, shift.at[:, :, own, :], sems.at[1]),
                pltpu.make_async_copy(d_ref, weight.at[:, :, own, :], sems.at[2]),
            ]
        )
        cut = shifted(side.cut, -side.first)
        levels[0, :, :, side.cut, :] = cut_ref[0]
        shift[:, :, cut, :] = cut_ref[1]
        weight[:, :, cut, :] = cut_ref[2]

        def invert(j, carry):
            for k in range(2):
                w = OMEGA / (6.0 + weight[k, j])
                weight[k, j] = w
                shift[k, j] = w * shift[k, j]
            return carry

        lax.fori_loop(0, cells, invert, 0)
        pending = [
            pltpu.make_async_copy(shift, b_out, sems.at[1]),
            pltpu.make_async_copy(weight, w_out, sems.at[2]),
        ]
        for c in pending:
            c.start()
        for e in range(2):
            columns = end_columns(e, cells, SWEEPS)
            b_ends[e] = shift[:, columns]
            w_ends[e] = weight[:, columns]
        pending.append(
            inner_sweeps(
                side, levels, weight, shift, last, out_ref, stash, tile_out, w_tile, sems
            )
        )
        cut_out[...] = last[:, :, side.sent, :]
        for c in pending:
            c.wait()

    on_each_side(radial_cells, body)


def later_interior(
    p_ref, b_ref, w_ref, cut_ref, out_ref, stash, tile_out, w_tile, levels, last, shift, weight, sems
):
    cells, radial_cells = p_ref.shape[1:3]

    def body(side):
        copy_all(
            [
                pltpu.make_async_copy(
                    p_ref, levels.at[0, :, :, pl.ds(OWN, radial_cells), :], sems.at[0]
                ),
                pltpu.make_async_copy(b_ref, shift, sems.at[1]),
                pltpu.make_async_copy(w_ref, weight, sems.at[2]),
            ]
        )
        levels[0, :, :, side.cut, :] = cut_ref[0]
        inner_sweeps(
            side, levels, weight, shift, last, out_ref, stash, tile_out, w_tile, sems
        ).wait()

    on_each_side(radial_cells, body)


def ghost_response(side, step, turn_ref, w_tile, block_ref, layout, messages, weights, wide, source):
    facing = side.facing
    cells = w_tile.shape[0]
    reach = SWEEPS - 1
    tile = slice(side.edge_tile + OWN - side.first, side.edge_tile + OWN - side.first + TILE)
    at = side.edge - OWN - side.edge_tile
    count = block_rows(cells)
    for i in range(count):
        for message, to in zip(messages, (cells - count + i, 2 * cells + i)):
            wide[to : to + 1] = message[layout.row("block", i)]
    wide[cells : 2 * cells] = block_ref[...]
    source[...] = jnp.zeros(source.shape, jnp.float32)
    offset = lax.rem(turn_ref[0] * step, cells * lax.axis_size("az"))
    rest = offset - lax.div(offset + cells // 2, cells) * cells
    start = cells - reach + (-rest if side.low else rest)
    for c in range(cells + 2 * reach):
        source[c, at : at + 1] = wide[pl.ds(start + c, 1), :]
    row = lax.broadcasted_iota(jnp.int32, source.shape[1:], 0)
    weight = [w_tile[j] for j in range(cells)]
    for e in range(2):
        far = weights[e][facing, 1, side.spare : side.spare + 1]
        beyond = [
            weights[e][facing, 0, tile],
            weights[e][facing, 1, tile],
            jnp.where(row == at, far, 0.0),
        ]
        weight = beyond[::-1] + weight if e == 0 else weight + beyond
    given = [source[c] for c in range(cells + 2 * reach)]
    response = [w * g for w, g in zip(weight, given)]
    for n in range(1, SWEEPS):
        old = response
        response = list(old)
        for c in range(n, len(old) - n):
            x = old[c]
            radial = jnp.where(row == 0, 0.0, pltpu.roll(x, 1, 0)) + jnp.where(
                row == TILE - 1, 0.0, pltpu.roll(x, TILE - 1, 0)
            )
            nbr = (old[c - 1] + old[c + 1]) + (radial + axial_sum(x)) + given[c]
            response[c] = (1.0 - OMEGA) * x + weight[c] * nbr
    return response[reach : reach + cells]


def finish(step, turn_ref, b_ends, w_ends, w_tile, stash, block_ref, tile_in, left_ref, right_ref, *rest):
    known = step > 1
    if known:
        beyond, _, out_ref, *rest = rest
        early = ()
    else:
        early = rest[1:3] if EARLY else ()
        cut_in, rest = rest[0], rest[1 + len(early) :]
        _, out_ref, cut_out, edge_out, ends_out, beyond, *rest = rest
    weights = (beyond.at[0], beyond.at[1])
    levels, last, inner_tiles, near, near2, wide, source, sems = rest
    messages = (left_ref, right_ref)
    cells, radial_cells = out_ref.shape[1:3]
    early_layout, layout = messages_of(step, radial_cells, cells)

    def given(e, k, slot):
        if slot in layout.slots:
            return messages[e][layout.block(slot, k)]
        return early[e][early_layout.block(slot, k)]

    def column(e, d):
        return d - 1 if e == 0 else cells - d

    def body(side):
        facing = side.facing

        def at(n, e, k, d):
            if d <= n:
                return levels.at[n, e, k, d]
            return stash.at[e, n, k, d - n - 1 if e == 0 else n + 2 - d]

        def meet(e, k, n, response):
            target = levels.at[n, e, k, 0]
            value = given(e, k, n)
            target[side.own] = value if response is None else value + response[side.inside]
            for h in layout.beyond(n, k):
                at = side.beyond(h)
                value = messages[e][layout.row(n, k, h)]
                if response is not None:
                    value = value + response[at : at + 1]
                target[side.first + at : side.first + at + 1] = value

        for e in range(2):
            if not known:
                for k in range(2):
                    for i in range(2):
                        target = beyond.at[e, k, i]
                        target[side.inside] = given(e, k, SWEEPS + i)
                        for h in layout.beyond(SWEEPS + i, k):
                            row = side.beyond(h)
                            target[row : row + 1] = messages[e][layout.row(SWEEPS + i, k, h)]
                beyond[e, facing, 1, side.spare : side.spare + 1] = messages[e][
                    layout.row("third")
                ]
            for k in range(2):
                meet(e, k, 0, None)
                for buf in (near, near2):
                    buf[e, k] = jnp.zeros(buf.shape[2:], jnp.float32)
        nears = (near, near2)

        matrix = neighbour_matrix(levels.shape[-1])

        def own_column(n, e, k, d, take):
            i = d - 1 if e == 0 else SWEEPS - d
            return (
                at(n, e, k, d),
                lambda: at(n, e, k, d - 1)[side.rows] + at(n, e, k, d + 1)[side.rows],
                lambda: w_ends[e, k, i],
                lambda: b_ends[e, k, i],
                take,
            )

        for n in range(SWEEPS - 1):
            src, dst = nears[n % 2], nears[1 - n % 2]
            items = []
            for e in range(2):
                for k in range(2):
                    for d in range(1, n + 2):

                        def take(new, e=e, k=k, d=d):
                            levels[n + 1, e, k, d, side.rows] = new
                            close(levels.at[n + 1, e, k, d], side, k == facing)

                        items.append(own_column(n, e, k, d, take))

                    def take(new, e=e, k=k):
                        dst[e, k, 0, side.rows] = new
                        meet(e, k, n + 1, new)
                        close(dst.at[e, k, 0], side, k == facing)

                    if n == 0:
                        take(weights[e][k, 0] * at(n, e, k, 1)[side.rows])
                        continue
                    items.append(
                        (
                            src.at[e, k, 0],
                            lambda e=e, k=k: at(n, e, k, 1)[side.rows] + src[e, k, 1, side.rows],
                            lambda e=e, k=k: weights[e][k, 0],
                            None,
                            take,
                        )
                    )
                    if n == 1:
                        dst[e, k, 1, side.rows] = weights[e][k, 1] * src[e, k, 0, side.rows]
            relax_all(side, matrix, items)
        copies = []

        def store(source, target):
            copies.append(pltpu.make_async_copy(source, target, sems.at[len(copies)]))
            copies[-1].start()

        response = None
        tile = slice(side.edge_tile, side.edge_tile + TILE)
        for k in (1 - facing, facing):
            if k == facing:
                response = ghost_response(
                    side, step, turn_ref, w_tile, block_ref, layout, messages, weights, wide, source
                )
                for i in range(cells - 2 * SWEEPS):
                    inner_tiles[i] = tile_in[i] + response[SWEEPS + i]
                store(
                    inner_tiles,
                    out_ref.at[
                        k, pl.ds(SWEEPS, cells - 2 * SWEEPS), pl.ds(side.edge_tile, TILE), :
                    ],
                )
            items = []
            for d in range(1, SWEEPS + 1):
                for e in range(2):
                    first = end_columns(e, cells, SWEEPS).start

                    def take(new, e=e, k=k, i=column(e, d) - first, first=first):
                        new = new[shifted(side.own, -side.first)]
                        last[e, k, i] = new
                        if k == facing:
                            last[e, k, i, tile] = new[tile] + response[first + i]

                    items.append(own_column(SWEEPS - 1, e, k, d, take))
            relax_all(side, matrix, items)
            for e in range(2):
                first = end_columns(e, cells, SWEEPS).start
                store(last.at[e, k], out_ref.at[k, pl.ds(first, SWEEPS)])
        if not known:
            row = side.edge - OWN
            cut_out[0, :, SWEEPS : cells - SWEEPS] = cut_in[...]
            for i in range(cells - 2 * SWEEPS):
                j = SWEEPS + i
                r = row - side.edge_tile
                edge_out[j : j + 1] = inner_tiles[i, r : r + 1]
            for e in range(2):
                first = end_columns(e, cells, SWEEPS).start
                cut_out[0, :, first : first + SWEEPS] = last[e, :, :, side.sent, :]
                for i in range(SWEEPS):
                    edge_out[first + i : first + i + 1] = last[e, facing, i, row : row + 1]
            ends_out[...] = last[...]
        for c in copies:
            c.wait()

    on_each_side(radial_cells, body)


def ring(size, step):
    return [(i, (i + step) % size) for i in range(size)]


def facing_pairs(size, turn):
    pairs = []
    for i in range(size):
        pairs.append((2 * ((i - turn) % size) + 1, 2 * i))
        pairs.append((2 * ((i + turn) % size), 2 * i + 1))
    return pairs


def far_pairs(size, turn):
    return [(2 * i + r, 2 * ((i + (2 * r - 1) * turn) % size) + r) for i in range(size) for r in range(2)]


def facing_block(edge, offset):
    size = lax.axis_size("az")
    cells = edge.shape[0]
    turn = (offset + cells // 2) // cells % size
    near = min(size, 16)

    def far(t):
        return lambda e: lax.ppermute(e, ("az", "rad"), far_pairs(size, t * near))

    def branch(t):
        return lambda e: lax.ppermute(e, ("az", "rad"), facing_pairs(size, t))

    if size > near:
        edge = lax.switch(turn // near, [far(t) for t in range(-(-size // near))], edge)
    return lax.switch(turn % near, [branch(t) for t in range(near)], edge)


def per_device(pressure, source, diagonal, rot_offset):
    _, cells, radial_cells, lanes = pressure.shape
    size = lax.axis_size("az")
    rows, span = radial_cells + 4 * TILE, radial_cells + TILE

    def array(*shape):
        return jax.ShapeDtypeStruct(shape, jnp.float32)

    def scratch(*shape):
        return pltpu.VMEM(shape, jnp.float32)

    def pinned(x):
        return pltpu.with_memory_space_constraint(x, pltpu.HBM)

    kept = pltpu.HBM((2, cells, span, lanes), jnp.float32)
    kept_ends = array(2, 2, SWEEPS, span, lanes)
    stash = array(2, SWEEPS, 2, 2, rows, lanes)
    cells_in = cells - 2 * SWEEPS
    tiles = array(cells_in, TILE, lanes)
    vmem = pl.BlockSpec(memory_space=pltpu.VMEM)
    smem = pl.BlockSpec(memory_space=pltpu.SMEM)
    hbm = pl.BlockSpec(memory_space=pltpu.HBM)
    anywhere = pl.BlockSpec(memory_space=pl.ANY)
    columns = scratch(2, 2, SWEEPS, rows, lanes)
    three = scratch(2, 2, SWEEPS - 1, span, lanes)

    def call(kernel, out_shape, in_specs, out_specs, scratch_shapes, operands, work_columns, **more):
        work = 2 * work_columns * span * lanes
        return pl.pallas_call(
            kernel,
            out_shape=out_shape,
            in_specs=in_specs,
            out_specs=out_specs,
            scratch_shapes=scratch_shapes,
            compiler_params=pltpu.CompilerParams(vmem_limit_bytes=28 << 20),
            cost_estimate=pl.CostEstimate(
                flops=12 * work, bytes_accessed=8 * work, transcendentals=0
            ),
            **more,
        )(*operands)

    fields = tuple(pinned(x) for x in (pressure, source, diagonal))
    layout, _ = messages_of(1, radial_cells, cells)
    early_message = array(layout.rows, lanes)
    cut, edge, *ends = call(
        pack,
        (
            array(3, 2, cells, SWEEPS, lanes),
            array(cells, lanes),
            array(2, 2, SWEEPS, radial_cells, lanes),
            array(2, 2, SWEEPS - 1, radial_cells, lanes),
            array(2, 2, SWEEPS - 1, radial_cells, lanes),
            *([early_message] * 2 if EARLY else []),
        ),
        [hbm] * 3,
        [vmem] * (7 if EARLY else 5),
        [
            scratch(3, 2, cells, TILE, lanes),
            scratch(cells, TILE, lanes),
            pltpu.SemaphoreType.DMA((10,)),
        ],
        fields,
        1,
        name="pack",
    )
    early = []
    if EARLY:
        *ends, last, first = ends
        early = [
            lax.ppermute(last, "az", ring(size, 1)),
            lax.ppermute(first, "az", ring(size, -1)),
        ]
    for step in range(1, STEPS + 1):
        known = step > 1
        cut = lax.ppermute(cut, "rad", [(0, 1), (1, 0)])
        offset = rot_offset[0] * step % (cells * size)
        block = facing_block(edge, offset)
        _, layout = messages_of(step, radial_cells, cells)
        message = array(layout.rows, lanes)
        last, first = call(
            later_edges if known else first_edges,
            (message, message),
            [vmem] * 4 + [anywhere],
            [vmem] * 2,
            [scratch(cells, lanes), pltpu.SemaphoreType.DMA, columns, columns]
            + ([] if known else [three] * 2),
            (*ends, cut, block),
            12,
            name="edges",
        )
        left = lax.ppermute(last, "az", ring(size, 1))
        right = lax.ppermute(first, "az", ring(size, -1))
        result = pltpu.HBM(pressure.shape, jnp.float32)
        outs = (result, stash, tiles, array(cells, TILE, lanes))
        out_specs = [hbm] + [vmem] * 3
        if not known:
            outs += (array(2, cells_in, SWEEPS, lanes), kept_ends, kept_ends, kept, kept)
            out_specs += [vmem] * 3 + [hbm] * 2
        inner, saved, inner_tiles, w_tile, *made = call(
            later_interior if known else first_interior,
            outs,
            [hbm] * 3 + [vmem],
            out_specs,
            [
                scratch(SWEEPS, 2, cells, rows, lanes),
                scratch(2, cells_in, radial_cells, lanes),
                scratch(*kept.shape),
                scratch(*kept.shape),
                pltpu.SemaphoreType.DMA((3,)),
            ],
            (*fields, cut),
            44,
            name="interior",
        )
        if not known:
            inner_cut, b_ends, w_ends, shift, weight = made
        operands = (
            rot_offset,
            b_ends,
            w_ends,
            w_tile,
            saved,
            block,
            inner_tiles,
            left,
            right,
        )
        operands += (beyond,) if known else (inner_cut, *early)
        outs = result
        if not known:
            outs = (
                result,
                array(1, 2, cells, SWEEPS, lanes),
                array(cells, lanes),
                array(2, 2, SWEEPS, radial_cells, lanes),
                array(2, 2, 2, span, lanes),
            )
        pressure = call(
            functools.partial(finish, step),
            outs,
            [smem] + [vmem] * (len(operands) - 1) + [hbm],
            hbm if known else [hbm] + [vmem] * 4,
            [
                scratch(SWEEPS, 2, 2, SWEEPS, rows, lanes),
                scratch(2, 2, SWEEPS, radial_cells, lanes),
                scratch(*tiles.shape),
                scratch(2, 2, 2, rows, lanes),
                scratch(2, 2, 2, rows, lanes),
                scratch(3 * cells, lanes),
                scratch(cells + 2 * (SWEEPS - 1), TILE, lanes),
                pltpu.SemaphoreType.DMA((5,)),
            ],
            (*operands, inner),
            26,
            input_output_aliases={len(operands): 0},
            name="finish",
        )
        if not known:
            pressure, cut, edge, ends_now, beyond = pressure
            fields = tuple(pinned(x) for x in (pressure, shift, weight))
            ends = (ends_now, b_ends, w_ends)
    return pressure


def solution(mesh):
    placed = (
        P(None, "az", "rad", None),
        P(None, "az", "rad", None),
        P(None, "az", "rad", None),
        P(),
    )
    return jax.shard_map(
        per_device,
        mesh=mesh,
        in_specs=placed,
        out_specs=P(None, "az", "rad", None),
        check_vma=False,
    )
```

```python
import functools

import jax
import jax.numpy as jnp
from jax import lax
from jax.experimental import pallas as pl
from jax.experimental.pallas import tpu as pltpu
from jax.sharding import PartitionSpec as P

STEPS = 2
SWEEPS = 4
OMEGA = 0.8
TILE = 8
OWN = 2 * TILE
EARLY = True
LEVELS = tuple(range(SWEEPS))
WEIGHTS = (SWEEPS, SWEEPS + 1)
FIRST_EARLY = (0, *WEIGHTS) if EARLY else ()
FIRST_LATE = LEVELS[1:] if EARLY else LEVELS + WEIGHTS


class Side:
    def __init__(self, low, radial_cells):
        end = OWN + radial_cells
        self.low = low
        self.own = slice(OWN, end)
        self.first = OWN if low else TILE
        self.count = radial_cells + TILE
        self.rows = slice(self.first, self.first + self.count)
        self.cut = slice(end, end + SWEEPS) if low else slice(OWN - SWEEPS, OWN)
        self.tile = slice(end, end + TILE) if low else slice(TILE, OWN)
        self.ghost = OWN - 1 if low else end
        self.edge = OWN if low else end - 1
        self.spare = self.count - 1 if low else 0
        self.inside = shifted(self.own, -self.first)
        self.facing = 1 if low else 0
        self.sent = slice(radial_cells - SWEEPS, radial_cells) if low else slice(0, SWEEPS)
        self.sent_tile = radial_cells - TILE if low else 0
        self.edge_tile = 0 if low else radial_cells - TILE

    def beyond(self, distance):
        return self.inside.stop - 1 + distance if self.low else self.inside.start - distance


def shifted(s, by):
    return slice(s.start + by, s.stop + by)


def axial_sum(x):
    lane = lax.broadcasted_iota(jnp.int32, x.shape, 1)
    last = x.shape[1] - 1
    return jnp.where(lane == 0, 0.0, pltpu.roll(x, 1, 1)) + jnp.where(
        lane == last, 0.0, pltpu.roll(x, last, 1)
    )


def neighbour_matrix(lanes):
    gap = lax.broadcasted_iota(jnp.int32, (lanes, lanes), 0) - lax.broadcasted_iota(
        jnp.int32, (lanes, lanes), 1
    )
    return jnp.where(jnp.abs(gap) == 1, 1.0, 0.0).astype(jnp.bfloat16)


def axial_product(x, matrix):
    high = x.astype(jnp.bfloat16)
    low = (x - high.astype(jnp.float32)).astype(jnp.bfloat16)
    return jnp.dot(high, matrix, preferred_element_type=jnp.float32) + jnp.dot(
        low, matrix, preferred_element_type=jnp.float32
    )


def relax_all(side, matrix, items):
    by_matrix = len(items) // 4 * 2
    axial = []
    if by_matrix:
        here = jnp.concatenate([item[0][side.rows] for item in items[:by_matrix]], axis=0)
        product = axial_product(here, matrix)
        axial = [product[i * side.count : (i + 1) * side.count] for i in range(by_matrix)]
    for i, (column, beside, weight, shift, take) in enumerate(items):
        here = column[side.rows]
        radial = column[shifted(side.rows, -1)] + column[shifted(side.rows, 1)]
        nbr = beside() + radial + (axial[i] if i < by_matrix else axial_sum(here))
        kept = (1.0 - OMEGA) * here
        if shift is not None:
            kept = kept + shift()
        take(kept + weight() * nbr)


def on_each_side(radial_cells, body):
    low = lax.axis_index("rad") == 0

    @pl.when(low)
    def _():
        body(Side(True, radial_cells))

    @pl.when(jnp.logical_not(low))
    def _():
        body(Side(False, radial_cells))


def copy_all(copies):
    for c in copies:
        c.start()
    for c in copies:
        c.wait()


def end_columns(edge, cells, count):
    return slice(0, count) if edge == 0 else slice(cells - count, cells)


def block_rows(cells):
    return cells // 2 + SWEEPS - 1


class Message:
    def __init__(self, slots, radial_cells, cells, weights):
        self.slots = slots
        self.radial_cells = radial_cells
        tail = []
        if 1 in slots:
            needed = [(n, SWEEPS - 1 - n) for n in LEVELS] + [(SWEEPS, 2)] * weights
            tail += [(slot, k, h) for slot, n in needed for k in range(2) for h in range(1, n + 1)]
            tail += [("block", i) for i in range(block_rows(cells))]
            tail += ["third"] * weights
        start = 2 * len(slots) * radial_cells
        self.tail = {what: start + i for i, what in enumerate(tail)}
        self.rows = start + -(-len(tail) // TILE) * TILE

    def block(self, slot, k):
        start = (2 * self.slots.index(slot) + k) * self.radial_cells
        return slice(start, start + self.radial_cells)

    def row(self, *what):
        at = self.tail[what if len(what) > 1 else what[0]]
        return slice(at, at + 1)

    def beyond(self, slot, k):
        return [w[2] for w in self.tail if w != "third" and w[:2] == (slot, k) and len(w) == 3]

    def put(self, ref, side, slot, k, value):
        if slot in self.slots:
            ref[self.block(slot, k)] = value[side.inside]
        for h in self.beyond(slot, k):
            at = side.beyond(h)
            ref[self.row(slot, k, h)] = value[at : at + 1]


def messages_of(step, radial_cells, cells):
    late = FIRST_LATE if step == 1 else LEVELS
    return (
        Message(FIRST_EARLY if step == 1 else (), radial_cells, cells, False),
        Message(late, radial_cells, cells, step == 1),
    )


def close(column, side, facing):
    row = slice(side.ghost, side.ghost + 1)
    if facing:
        column[row] = jnp.zeros((1, column.shape[1]), jnp.float32)
    else:
        column[row] = column[side.edge : side.edge + 1]


def trajectories(side, field, other, weight, shift, layout, messages, weights):
    bufs = (field, other)
    matrix = neighbour_matrix(field.shape[-1])

    def at(edge, distance, n):
        return distance - 1 if edge == 0 else n - distance

    for edge in range(2):
        for k in range(2):
            for i in range(SWEEPS):
                close(field.at[edge, k, i], side, k == side.facing)
    for sweep in range(SWEEPS):
        src, dst = bufs[sweep % 2], bufs[1 - sweep % 2]
        items = []
        for edge, message in enumerate(messages):
            for k in range(2):
                layout.put(
                    message, side, sweep, k, src[edge, k, at(edge, 1, SWEEPS), side.rows]
                )
                for j in range(1, SWEEPS - sweep):
                    i = at(edge, j, SWEEPS - 1)

                    def beside(edge=edge, k=k, j=j):
                        total = src[edge, k, at(edge, j + 1, SWEEPS), side.rows]
                        if j > 1:
                            total = total + src[edge, k, at(edge, j - 1, SWEEPS), side.rows]
                        return total

                    def take(new, edge=edge, k=k, j=j):
                        out = dst.at[edge, k, at(edge, j, SWEEPS)]
                        out[side.rows] = new
                        close(out, side, k == side.facing)

                    items.append(
                        (
                            src.at[edge, k, at(edge, j, SWEEPS)],
                            beside,
                            functools.partial(weight, edge, k, i),
                            functools.partial(shift, edge, k, i),
                            take,
                        )
                    )
        relax_all(side, matrix, items)
    if not weights:
        return
    for edge, message in enumerate(messages):
        for k in range(2):
            for i in range(2):
                layout.put(
                    message, side, SWEEPS + i, k, weight(edge, k, at(edge, 1 + i, SWEEPS - 1))
                )
        row = side.edge - side.first
        message[layout.row("third")] = weight(edge, side.facing, at(edge, 3, SWEEPS - 1))[
            row : row + 1
        ]


def pack(p_ref, s_ref, d_ref, cut_ref, edge_ref, p_ends, s_ends, d_ends, *rest):
    *early, tiles, edge_tiles, sems = rest
    cells, radial_cells = p_ref.shape[1:3]
    layout, _ = messages_of(1, radial_cells, cells)

    def body(side):
        copies = []

        def fetch(source, target):
            copies.append(pltpu.make_async_copy(source, target, sems.at[len(copies)]))

        rows = pl.ds(side.sent_tile, TILE)
        for i, x in enumerate((p_ref, s_ref, d_ref)):
            fetch(x.at[:, :, rows, :], tiles.at[i])
        fetch(p_ref.at[side.facing, :, pl.ds(side.edge_tile, TILE), :], edge_tiles)
        for source, target in ((p_ref, p_ends), (s_ref, s_ends), (d_ref, d_ends)):
            count = target.shape[2]
            for edge in range(2):
                span = pl.ds(end_columns(edge, cells, count).start, count)
                fetch(source.at[:, span], target.at[edge])
        copy_all(copies)
        for edge, message in enumerate(early[::-1]):
            for k in range(2):
                i = 0 if edge == 0 else SWEEPS - 1
                message[layout.block(0, k)] = p_ends[edge, k, i]
                for j in range(2):
                    i = j if edge == 0 else SWEEPS - 2 - j
                    message[layout.block(SWEEPS + j, k)] = OMEGA / (6.0 + d_ends[edge, k, i])
        cut_ref[...] = tiles[:, :, :, shifted(side.sent, -side.sent_tile), :]
        at = side.edge - OWN - side.edge_tile
        for j in range(cells):
            edge_ref[j : j + 1] = edge_tiles[j, at : at + 1]

    on_each_side(radial_cells, body)


def fill_ends(field, side, p_ends, cut_ref, cells):
    for edge in range(2):
        columns = end_columns(edge, cells, SWEEPS)
        for k in range(2):
            for i in range(SWEEPS):
                field[edge, k, i, side.own] = p_ends[edge, k, i]
                field[edge, k, i, side.cut] = cut_ref[0, k, columns.start + i]


def send_block(layout, arriving, block, messages):
    arriving.wait()
    cells = block.shape[0]
    count = block_rows(cells)
    for edge, message in enumerate(messages):
        for i in range(count):
            at = i if edge == 0 else cells - count + i
            message[layout.row("block", i)] = block[at : at + 1]


def first_edges(
    p_ends, s_ends, d_ends, cut_ref, block_ref, last, first, block, sem, field, other, weight, shift
):
    radial_cells = p_ends.shape[3]
    cells = cut_ref.shape[2]
    n = SWEEPS - 1
    _, layout = messages_of(1, radial_cells, cells)

    def body(side):
        arriving = pltpu.make_async_copy(block_ref, block, sem)
        arriving.start()
        own = shifted(side.own, -side.first)
        cut = shifted(side.cut, -side.first)
        fill_ends(field, side, p_ends, cut_ref, cells)
        for edge in range(2):
            columns = end_columns(edge, cells, n)
            for k in range(2):
                for i in range(n):
                    for rows, s, d in (
                        (own, s_ends[edge, k, i], d_ends[edge, k, i]),
                        (cut, cut_ref[1, k, columns.start + i], cut_ref[2, k, columns.start + i]),
                    ):
                        w = OMEGA / (6.0 + d)
                        weight[edge, k, i, rows] = w
                        shift[edge, k, i, rows] = w * s
        trajectories(
            side,
            field,
            other,
            lambda e, k, i: weight[e, k, i],
            lambda e, k, i: shift[e, k, i],
            layout,
            (first, last),
            True,
        )
        send_block(layout, arriving, block, (first, last))

    on_each_side(radial_cells, body)


def later_edges(p_ends, b_ends, w_ends, cut_ref, block_ref, last, first, block, sem, field, other):
    cells, radial_cells = cut_ref.shape[2], p_ends.shape[3]
    _, layout = messages_of(2, radial_cells, cells)

    def body(side):
        arriving = pltpu.make_async_copy(block_ref, block, sem)
        arriving.start()
        fill_ends(field, side, p_ends, cut_ref, cells)
        trajectories(
            side,
            field,
            other,
            lambda e, k, i: w_ends[e, k, i + e],
            lambda e, k, i: b_ends[e, k, i + e],
            layout,
            (first, last),
            False,
        )
        send_block(layout, arriving, block, (first, last))

    on_each_side(radial_cells, body)


def inner_sweeps(side, levels, weight, shift, last, out_ref, stash, tile_out, w_tile, sems):
    cells = levels.shape[2]
    radial_cells = side.own.stop - side.own.start
    for j in range(cells):
        for k in range(2):
            close(levels.at[0, k, j], side, k == side.facing)
        for n in range(1, SWEEPS):
            close(levels.at[n, side.facing, j], side, True)
    at = side.edge - side.first
    for e, first in enumerate((0, cells - 2)):
        for k in range(2):
            for i in range(2):
                stash[e, 0, k, i] = levels[0, k, first + i]
    matrix = neighbour_matrix(levels.shape[-1])
    for n in range(SWEEPS):
        final = n == SWEEPS - 1

        def step(i, carry, n=n, final=final):
            items = []
            for k in (1, 0):
                for j in (n + 1 + 2 * i, n + 2 + 2 * i):

                    def beside(k=k, j=j):
                        return levels[n, k, j - 1, side.rows] + levels[n, k, j + 1, side.rows]

                    def take(new, k=k, j=j):
                        if final:
                            last[k, j - SWEEPS] = new[shifted(side.own, -side.first)]
                            return
                        levels[n + 1, k, j, side.rows] = new
                        if k != side.facing:
                            levels[n + 1, k, j, side.ghost : side.ghost + 1] = new[at : at + 1]

                    items.append(
                        (
                            levels.at[n, k, j],
                            beside,
                            functools.partial(lambda k, j: weight[k, j], k, j),
                            functools.partial(lambda k, j: shift[k, j], k, j),
                            take,
                        )
                    )
            relax_all(side, matrix, items)
            return carry

        lax.fori_loop(0, cells // 2 - 1 - n, step, 0, unroll=2 if n % 2 else 1)
        if not final:
            for e, first in enumerate((n + 1, cells - 3 - n)):
                for k in range(2):
                    for i in range(2):
                        stash[e, n + 1, k, i] = levels[n + 1, k, first + i]
    inner = pltpu.make_async_copy(
        last, out_ref.at[:, pl.ds(SWEEPS, cells - 2 * SWEEPS)], sems.at[0]
    )
    inner.start()
    tile_out[...] = last[side.facing, :, side.edge_tile : side.edge_tile + TILE, :]
    first = side.edge_tile + OWN - side.first
    w_tile[...] = weight[side.facing, :, first : first + TILE, :]
    return inner


def first_interior(
    p_ref, s_ref, d_ref, cut_ref,
    out_ref, stash, tile_out, w_tile, cut_out, b_ends, w_ends, b_out, w_out,
    levels, last, shift, weight, sems,
):
    cells, radial_cells = p_ref.shape[1:3]

    def body(side):
        own = pl.ds(OWN - side.first, radial_cells)
        copy_all(
            [
                pltpu.make_async_copy(
                    p_ref, levels.at[0, :, :, pl.ds(OWN, radial_cells), :], sems.at[0]
                ),
                pltpu.make_async_copy(s_ref, shift.at[:, :, own, :], sems.at[1]),
                pltpu.make_async_copy(d_ref, weight.at[:, :, own, :], sems.at[2]),
            ]
        )
        cut = shifted(side.cut, -side.first)
        levels[0, :, :, side.cut, :] = cut_ref[0]
        shift[:, :, cut, :] = cut_ref[1]
        weight[:, :, cut, :] = cut_ref[2]

        def invert(j, carry):
            for k in range(2):
                w = OMEGA / (6.0 + weight[k, j])
                weight[k, j] = w
                shift[k, j] = w * shift[k, j]
            return carry

        lax.fori_loop(0, cells, invert, 0)
        pending = [
            pltpu.make_async_copy(shift, b_out, sems.at[1]),
            pltpu.make_async_copy(weight, w_out, sems.at[2]),
        ]
        for c in pending:
            c.start()
        for e in range(2):
            columns = end_columns(e, cells, SWEEPS)
            b_ends[e] = shift[:, columns]
            w_ends[e] = weight[:, columns]
        pending.append(
            inner_sweeps(
                side, levels, weight, shift, last, out_ref, stash, tile_out, w_tile, sems
            )
        )
        cut_out[...] = last[:, :, side.sent, :]
        for c in pending:
            c.wait()

    on_each_side(radial_cells, body)


def later_interior(
    p_ref, b_ref, w_ref, cut_ref, out_ref, stash, tile_out, w_tile, levels, last, shift, weight, sems
):
    cells, radial_cells = p_ref.shape[1:3]

    def body(side):
        copy_all(
            [
                pltpu.make_async_copy(
                    p_ref, levels.at[0, :, :, pl.ds(OWN, radial_cells), :], sems.at[0]
                ),
                pltpu.make_async_copy(b_ref, shift, sems.at[1]),
                pltpu.make_async_copy(w_ref, weight, sems.at[2]),
            ]
        )
        levels[0, :, :, side.cut, :] = cut_ref[0]
        inner_sweeps(
            side, levels, weight, shift, last, out_ref, stash, tile_out, w_tile, sems
        ).wait()

    on_each_side(radial_cells, body)


def ghost_response(side, step, turn_ref, w_tile, block_ref, layout, messages, weights, wide, source):
    facing = side.facing
    cells = w_tile.shape[0]
    reach = SWEEPS - 1
    tile = slice(side.edge_tile + OWN - side.first, side.edge_tile + OWN - side.first + TILE)
    at = side.edge - OWN - side.edge_tile
    count = block_rows(cells)
    for i in range(count):
        for message, to in zip(messages, (cells - count + i, 2 * cells + i)):
            wide[to : to + 1] = message[layout.row("block", i)]
    wide[cells : 2 * cells] = block_ref[...]
    source[...] = jnp.zeros(source.shape, jnp.float32)
    offset = lax.rem(turn_ref[0] * step, cells * lax.axis_size("az"))
    rest = offset - lax.div(offset + cells // 2, cells) * cells
    start = cells - reach + (-rest if side.low else rest)
    for c in range(cells + 2 * reach):
        source[c, at : at + 1] = wide[pl.ds(start + c, 1), :]
    row = lax.broadcasted_iota(jnp.int32, source.shape[1:], 0)
    weight = [w_tile[j] for j in range(cells)]
    for e in range(2):
        far = weights[e][facing, 1, side.spare : side.spare + 1]
        beyond = [
            weights[e][facing, 0, tile],
            weights[e][facing, 1, tile],
            jnp.where(row == at, far, 0.0),
        ]
        weight = beyond[::-1] + weight if e == 0 else weight + beyond
    given = [source[c] for c in range(cells + 2 * reach)]
    response = [w * g for w, g in zip(weight, given)]
    for n in range(1, SWEEPS):
        old = response
        response = list(old)
        for c in range(n, len(old) - n):
            x = old[c]
            radial = jnp.where(row == 0, 0.0, pltpu.roll(x, 1, 0)) + jnp.where(
                row == TILE - 1, 0.0, pltpu.roll(x, TILE - 1, 0)
            )
            nbr = (old[c - 1] + old[c + 1]) + (radial + axial_sum(x)) + given[c]
            response[c] = (1.0 - OMEGA) * x + weight[c] * nbr
    return response[reach : reach + cells]


def finish(step, turn_ref, b_ends, w_ends, w_tile, stash, block_ref, tile_in, left_ref, right_ref, *rest):
    known = step > 1
    if known:
        beyond, _, out_ref, *rest = rest
        early = ()
    else:
        early = rest[1:3] if EARLY else ()
        cut_in, rest = rest[0], rest[1 + len(early) :]
        _, out_ref, cut_out, edge_out, ends_out, beyond, *rest = rest
    weights = (beyond.at[0], beyond.at[1])
    levels, last, inner_tiles, near, near2, wide, source, sems = rest
    messages = (left_ref, right_ref)
    cells, radial_cells = out_ref.shape[1:3]
    early_layout, layout = messages_of(step, radial_cells, cells)

    def given(e, k, slot):
        if slot in layout.slots:
            return messages[e][layout.block(slot, k)]
        return early[e][early_layout.block(slot, k)]

    def column(e, d):
        return d - 1 if e == 0 else cells - d

    def body(side):
        facing = side.facing

        def at(n, e, k, d):
            if d <= n:
                return levels.at[n, e, k, d]
            return stash.at[e, n, k, d - n - 1 if e == 0 else n + 2 - d]

        def meet(e, k, n, response):
            target = levels.at[n, e, k, 0]
            value = given(e, k, n)
            target[side.own] = value if response is None else value + response[side.inside]
            for h in layout.beyond(n, k):
                at = side.beyond(h)
                value = messages[e][layout.row(n, k, h)]
                if response is not None:
                    value = value + response[at : at + 1]
                target[side.first + at : side.first + at + 1] = value

        for e in range(2):
            if not known:
                for k in range(2):
                    for i in range(2):
                        target = beyond.at[e, k, i]
                        target[side.inside] = given(e, k, SWEEPS + i)
                        for h in layout.beyond(SWEEPS + i, k):
                            row = side.beyond(h)
                            target[row : row + 1] = messages[e][layout.row(SWEEPS + i, k, h)]
                beyond[e, facing, 1, side.spare : side.spare + 1] = messages[e][
                    layout.row("third")
                ]
            for k in range(2):
                meet(e, k, 0, None)
                for buf in (near, near2):
                    buf[e, k] = jnp.zeros(buf.shape[2:], jnp.float32)
        nears = (near, near2)

        matrix = neighbour_matrix(levels.shape[-1])

        def own_column(n, e, k, d, take):
            i = d - 1 if e == 0 else SWEEPS - d
            return (
                at(n, e, k, d),
                lambda: at(n, e, k, d - 1)[side.rows] + at(n, e, k, d + 1)[side.rows],
                lambda: w_ends[e, k, i],
                lambda: b_ends[e, k, i],
                take,
            )

        for n in range(SWEEPS - 1):
            src, dst = nears[n % 2], nears[1 - n % 2]
            items = []
            for e in range(2):
                for k in range(2):
                    for d in range(1, n + 2):

                        def take(new, e=e, k=k, d=d):
                            levels[n + 1, e, k, d, side.rows] = new
                            close(levels.at[n + 1, e, k, d], side, k == facing)

                        items.append(own_column(n, e, k, d, take))

                    def take(new, e=e, k=k):
                        dst[e, k, 0, side.rows] = new
                        meet(e, k, n + 1, new)
                        close(dst.at[e, k, 0], side, k == facing)

                    if n == 0:
                        take(weights[e][k, 0] * at(n, e, k, 1)[side.rows])
                        continue
                    items.append(
                        (
                            src.at[e, k, 0],
                            lambda e=e, k=k: at(n, e, k, 1)[side.rows] + src[e, k, 1, side.rows],
                            lambda e=e, k=k: weights[e][k, 0],
                            None,
                            take,
                        )
                    )
                    if n == 1:
                        dst[e, k, 1, side.rows] = weights[e][k, 1] * src[e, k, 0, side.rows]
            relax_all(side, matrix, items)
        copies = []

        def store(source, target):
            copies.append(pltpu.make_async_copy(source, target, sems.at[len(copies)]))
            copies[-1].start()

        response = None
        tile = slice(side.edge_tile, side.edge_tile + TILE)
        for k in (1 - facing, facing):
            if k == facing:
                response = ghost_response(
                    side, step, turn_ref, w_tile, block_ref, layout, messages, weights, wide, source
                )
                for i in range(cells - 2 * SWEEPS):
                    inner_tiles[i] = tile_in[i] + response[SWEEPS + i]
                store(
                    inner_tiles,
                    out_ref.at[
                        k, pl.ds(SWEEPS, cells - 2 * SWEEPS), pl.ds(side.edge_tile, TILE), :
                    ],
                )
            items = []
            for d in range(1, SWEEPS + 1):
                for e in range(2):
                    first = end_columns(e, cells, SWEEPS).start

                    def take(new, e=e, k=k, i=column(e, d) - first, first=first):
                        new = new[shifted(side.own, -side.first)]
                        last[e, k, i] = new
                        if k == facing:
                            last[e, k, i, tile] = new[tile] + response[first + i]

                    items.append(own_column(SWEEPS - 1, e, k, d, take))
            relax_all(side, matrix, items)
            for e in range(2):
                first = end_columns(e, cells, SWEEPS).start
                store(last.at[e, k], out_ref.at[k, pl.ds(first, SWEEPS)])
        if not known:
            row = side.edge - OWN
            cut_out[0, :, SWEEPS : cells - SWEEPS] = cut_in[...]
            for i in range(cells - 2 * SWEEPS):
                j = SWEEPS + i
                r = row - side.edge_tile
                edge_out[j : j + 1] = inner_tiles[i, r : r + 1]
            for e in range(2):
                first = end_columns(e, cells, SWEEPS).start
                cut_out[0, :, first : first + SWEEPS] = last[e, :, :, side.sent, :]
                for i in range(SWEEPS):
                    edge_out[first + i : first + i + 1] = last[e, facing, i, row : row + 1]
            ends_out[...] = last[...]
        for c in copies:
            c.wait()

    on_each_side(radial_cells, body)


def ring(size, step):
    return [(i, (i + step) % size) for i in range(size)]


def facing_pairs(size, turn):
    pairs = []
    for i in range(size):
        pairs.append((2 * ((i - turn) % size) + 1, 2 * i))
        pairs.append((2 * ((i + turn) % size), 2 * i + 1))
    return pairs


def far_pairs(size, turn):
    return [(2 * i + r, 2 * ((i + (2 * r - 1) * turn) % size) + r) for i in range(size) for r in range(2)]


def facing_block(edge, offset):
    size = lax.axis_size("az")
    cells = edge.shape[0]
    turn = (offset + cells // 2) // cells % size
    near = min(size, 16)

    def far(t):
        return lambda e: lax.ppermute(e, ("az", "rad"), far_pairs(size, t * near))

    def branch(t):
        return lambda e: lax.ppermute(e, ("az", "rad"), facing_pairs(size, t))

    if size > near:
        edge = lax.switch(turn // near, [far(t) for t in range(-(-size // near))], edge)
    return lax.switch(turn % near, [branch(t) for t in range(near)], edge)


def per_device(pressure, source, diagonal, rot_offset):
    _, cells, radial_cells, lanes = pressure.shape
    size = lax.axis_size("az")
    rows, span = radial_cells + 4 * TILE, radial_cells + TILE

    def array(*shape):
        return jax.ShapeDtypeStruct(shape, jnp.float32)

    def scratch(*shape):
        return pltpu.VMEM(shape, jnp.float32)

    def pinned(x):
        return pltpu.with_memory_space_constraint(x, pltpu.HBM)

    kept = pltpu.HBM((2, cells, span, lanes), jnp.float32)
    kept_ends = array(2, 2, SWEEPS, span, lanes)
    stash = array(2, SWEEPS, 2, 2, rows, lanes)
    cells_in = cells - 2 * SWEEPS
    tiles = array(cells_in, TILE, lanes)
    vmem = pl.BlockSpec(memory_space=pltpu.VMEM)
    smem = pl.BlockSpec(memory_space=pltpu.SMEM)
    hbm = pl.BlockSpec(memory_space=pltpu.HBM)
    anywhere = pl.BlockSpec(memory_space=pl.ANY)
    columns = scratch(2, 2, SWEEPS, rows, lanes)
    three = scratch(2, 2, SWEEPS - 1, span, lanes)

    def call(kernel, out_shape, in_specs, out_specs, scratch_shapes, operands, work_columns, **more):
        work = 2 * work_columns * span * lanes
        return pl.pallas_call(
            kernel,
            out_shape=out_shape,
            in_specs=in_specs,
            out_specs=out_specs,
            scratch_shapes=scratch_shapes,
            compiler_params=pltpu.CompilerParams(vmem_limit_bytes=28 << 20),
            cost_estimate=pl.CostEstimate(
                flops=12 * work, bytes_accessed=8 * work, transcendentals=0
            ),
            **more,
        )(*operands)

    fields = tuple(pinned(x) for x in (pressure, source, diagonal))
    layout, _ = messages_of(1, radial_cells, cells)
    early_message = array(layout.rows, lanes)
    cut, edge, *ends = call(
        pack,
        (
            array(3, 2, cells, SWEEPS, lanes),
            array(cells, lanes),
            array(2, 2, SWEEPS, radial_cells, lanes),
            array(2, 2, SWEEPS - 1, radial_cells, lanes),
            array(2, 2, SWEEPS - 1, radial_cells, lanes),
            *([early_message] * 2 if EARLY else []),
        ),
        [hbm] * 3,
        [vmem] * (7 if EARLY else 5),
        [
            scratch(3, 2, cells, TILE, lanes),
            scratch(cells, TILE, lanes),
            pltpu.SemaphoreType.DMA((10,)),
        ],
        fields,
        1,
        name="pack",
    )
    early = []
    if EARLY:
        *ends, last, first = ends
        early = [
            lax.ppermute(last, "az", ring(size, 1)),
            lax.ppermute(first, "az", ring(size, -1)),
        ]
    for step in range(1, STEPS + 1):
        known = step > 1
        cut = lax.ppermute(cut, "rad", [(0, 1), (1, 0)])
        offset = rot_offset[0] * step % (cells * size)
        block = facing_block(edge, offset)
        _, layout = messages_of(step, radial_cells, cells)
        message = array(layout.rows, lanes)
        last, first = call(
            later_edges if known else first_edges,
            (message, message),
            [vmem] * 4 + [anywhere],
            [vmem] * 2,
            [scratch(cells, lanes), pltpu.SemaphoreType.DMA, columns, columns]
            + ([] if known else [three] * 2),
            (*ends, cut, block),
            12,
            name="edges",
        )
        left = lax.ppermute(last, "az", ring(size, 1))
        right = lax.ppermute(first, "az", ring(size, -1))
        result = pltpu.HBM(pressure.shape, jnp.float32)
        outs = (result, stash, tiles, array(cells, TILE, lanes))
        out_specs = [hbm] + [vmem] * 3
        if not known:
            outs += (array(2, cells_in, SWEEPS, lanes), kept_ends, kept_ends, kept, kept)
            out_specs += [vmem] * 3 + [hbm] * 2
        inner, saved, inner_tiles, w_tile, *made = call(
            later_interior if known else first_interior,
            outs,
            [hbm] * 3 + [vmem],
            out_specs,
            [
                scratch(SWEEPS, 2, cells, rows, lanes),
                scratch(2, cells_in, radial_cells, lanes),
                scratch(*kept.shape),
                scratch(*kept.shape),
                pltpu.SemaphoreType.DMA((3,)),
            ],
            (*fields, cut),
            44,
            name="interior",
        )
        if not known:
            inner_cut, b_ends, w_ends, shift, weight = made
        operands = (
            rot_offset,
            b_ends,
            w_ends,
            w_tile,
            saved,
            block,
            inner_tiles,
            left,
            right,
        )
        operands += (beyond,) if known else (inner_cut, *early)
        outs = result
        if not known:
            outs = (
                result,
                array(1, 2, cells, SWEEPS, lanes),
                array(cells, lanes),
                array(2, 2, SWEEPS, radial_cells, lanes),
                array(2, 2, 2, span, lanes),
            )
        pressure = call(
            functools.partial(finish, step),
            outs,
            [smem] + [vmem] * (len(operands) - 1) + [hbm],
            hbm if known else [hbm] + [vmem] * 4,
            [
                scratch(SWEEPS, 2, 2, SWEEPS, rows, lanes),
                scratch(2, 2, SWEEPS, radial_cells, lanes),
                scratch(*tiles.shape),
                scratch(2, 2, 2, rows, lanes),
                scratch(2, 2, 2, rows, lanes),
                scratch(3 * cells, lanes),
                scratch(cells + 2 * (SWEEPS - 1), TILE, lanes),
                pltpu.SemaphoreType.DMA((5,)),
            ],
            (*operands, inner),
            26,
            input_output_aliases={len(operands): 0},
            name="finish",
        )
        if not known:
            pressure, cut, edge, ends_now, beyond = pressure
            fields = tuple(pinned(x) for x in (pressure, shift, weight))
            ends = (ends_now, b_ends, w_ends)
    return pressure


def solution(mesh):
    placed = (
        P(None, "az", "rad", None),
        P(None, "az", "rad", None),
        P(None, "az", "rad", None),
        P(),
    )
    return jax.shard_map(
        per_device,
        mesh=mesh,
        in_specs=placed,
        out_specs=P(None, "az", "rad", None),
        check_vma=False,
    )
```

```python
import functools

import jax
import jax.numpy as jnp
from jax import lax
from jax.experimental import pallas as pl
from jax.experimental.pallas import tpu as pltpu
from jax.sharding import PartitionSpec as P

STEPS = 2
SWEEPS = 4
OMEGA = 0.8
TILE = 8
OWN = 2 * TILE
LEVELS = tuple(range(SWEEPS))
WEIGHTS = (SWEEPS, SWEEPS + 1)


class Side:
    def __init__(self, low, radial_cells):
        end = OWN + radial_cells
        self.low = low
        self.own = slice(OWN, end)
        self.first = OWN if low else TILE
        self.count = radial_cells + TILE
        self.rows = slice(self.first, self.first + self.count)
        self.cut = slice(end, end + SWEEPS) if low else slice(OWN - SWEEPS, OWN)
        self.tile = slice(end, end + TILE) if low else slice(TILE, OWN)
        self.ghost = OWN - 1 if low else end
        self.edge = OWN if low else end - 1
        self.spare = self.count - 1 if low else 0
        self.inside = shifted(self.own, -self.first)
        self.facing = 1 if low else 0
        self.sent = slice(radial_cells - SWEEPS, radial_cells) if low else slice(0, SWEEPS)
        self.sent_tile = radial_cells - TILE if low else 0
        self.edge_tile = 0 if low else radial_cells - TILE

    def beyond(self, distance):
        return self.inside.stop - 1 + distance if self.low else self.inside.start - distance


def shifted(s, by):
    return slice(s.start + by, s.stop + by)


def axial_sum(x):
    lane = lax.broadcasted_iota(jnp.int32, x.shape, 1)
    last = x.shape[1] - 1
    return jnp.where(lane == 0, 0.0, pltpu.roll(x, 1, 1)) + jnp.where(
        lane == last, 0.0, pltpu.roll(x, last, 1)
    )


def neighbour_matrix(lanes):
    gap = lax.broadcasted_iota(jnp.int32, (lanes, lanes), 0) - lax.broadcasted_iota(
        jnp.int32, (lanes, lanes), 1
    )
    return jnp.where(jnp.abs(gap) == 1, 1.0, 0.0).astype(jnp.bfloat16)


def axial_product(x, matrix):
    high = x.astype(jnp.bfloat16)
    low = (x - high.astype(jnp.float32)).astype(jnp.bfloat16)
    return jnp.dot(high, matrix, preferred_element_type=jnp.float32) + jnp.dot(
        low, matrix, preferred_element_type=jnp.float32
    )


def relax_all(side, matrix, items):
    by_matrix = len(items) // 4 * 2
    axial = []
    if by_matrix:
        here = jnp.concatenate([item[0][side.rows] for item in items[:by_matrix]], axis=0)
        product = axial_product(here, matrix)
        axial = [product[i * side.count : (i + 1) * side.count] for i in range(by_matrix)]
    for i, (column, beside, weight, shift, take) in enumerate(items):
        here = column[side.rows]
        radial = column[shifted(side.rows, -1)] + column[shifted(side.rows, 1)]
        nbr = beside() + radial + (axial[i] if i < by_matrix else axial_sum(here))
        kept = (1.0 - OMEGA) * here
        if shift is not None:
            kept = kept + shift()
        take(kept + weight() * nbr)


def on_each_side(radial_cells, body):
    low = lax.axis_index("rad") == 0

    @pl.when(low)
    def _():
        body(Side(True, radial_cells))

    @pl.when(jnp.logical_not(low))
    def _():
        body(Side(False, radial_cells))


def copy_all(copies):
    for c in copies:
        c.start()
    for c in copies:
        c.wait()


def end_columns(edge, cells, count):
    return slice(0, count) if edge == 0 else slice(cells - count, cells)


def block_rows(cells):
    return cells // 2 + SWEEPS - 1


class Message:
    def __init__(self, slots, radial_cells, cells, weights):
        self.slots = slots
        self.radial_cells = radial_cells
        tail = []
        needed = [(n, SWEEPS - 1 - n) for n in LEVELS] + [(SWEEPS, 2)] * weights
        tail += [(slot, k, h) for slot, n in needed for k in range(2) for h in range(1, n + 1)]
        tail += [("block", i) for i in range(block_rows(cells))]
        tail += ["third"] * weights
        start = 2 * len(slots) * radial_cells
        self.tail = {what: start + i for i, what in enumerate(tail)}
        self.rows = start + -(-len(tail) // TILE) * TILE

    def block(self, slot, k):
        start = (2 * self.slots.index(slot) + k) * self.radial_cells
        return slice(start, start + self.radial_cells)

    def row(self, *what):
        at = self.tail[what if len(what) > 1 else what[0]]
        return slice(at, at + 1)

    def beyond(self, slot, k):
        return [w[2] for w in self.tail if w != "third" and w[:2] == (slot, k) and len(w) == 3]

    def put(self, ref, side, slot, k, value):
        ref[self.block(slot, k)] = value[side.inside]
        for h in self.beyond(slot, k):
            at = side.beyond(h)
            ref[self.row(slot, k, h)] = value[at : at + 1]


def message_of(step, radial_cells, cells):
    return Message(LEVELS + WEIGHTS if step == 1 else LEVELS, radial_cells, cells, step == 1)


def close(column, side, facing):
    row = slice(side.ghost, side.ghost + 1)
    if facing:
        column[row] = jnp.zeros((1, column.shape[1]), jnp.float32)
    else:
        column[row] = column[side.edge : side.edge + 1]


def trajectories(side, field, other, weight, shift, layout, messages, weights):
    bufs = (field, other)
    matrix = neighbour_matrix(field.shape[-1])

    def at(edge, distance, n):
        return distance - 1 if edge == 0 else n - distance

    for edge in range(2):
        for k in range(2):
            for i in range(SWEEPS):
                close(field.at[edge, k, i], side, k == side.facing)
    for sweep in range(SWEEPS):
        src, dst = bufs[sweep % 2], bufs[1 - sweep % 2]
        items = []
        for edge, message in enumerate(messages):
            for k in range(2):
                layout.put(
                    message, side, sweep, k, src[edge, k, at(edge, 1, SWEEPS), side.rows]
                )
                for j in range(1, SWEEPS - sweep):
                    i = at(edge, j, SWEEPS - 1)

                    def beside(edge=edge, k=k, j=j):
                        total = src[edge, k, at(edge, j + 1, SWEEPS), side.rows]
                        if j > 1:
                            total = total + src[edge, k, at(edge, j - 1, SWEEPS), side.rows]
                        return total

                    def take(new, edge=edge, k=k, j=j):
                        out = dst.at[edge, k, at(edge, j, SWEEPS)]
                        out[side.rows] = new
                        close(out, side, k == side.facing)

                    items.append(
                        (
                            src.at[edge, k, at(edge, j, SWEEPS)],
                            beside,
                            functools.partial(weight, edge, k, i),
                            functools.partial(shift, edge, k, i),
                            take,
                        )
                    )
        relax_all(side, matrix, items)
    if not weights:
        return
    for edge, message in enumerate(messages):
        for k in range(2):
            for i in range(2):
                layout.put(
                    message, side, SWEEPS + i, k, weight(edge, k, at(edge, 1 + i, SWEEPS - 1))
                )
        row = side.edge - side.first
        message[layout.row("third")] = weight(edge, side.facing, at(edge, 3, SWEEPS - 1))[
            row : row + 1
        ]


def pack(p_ref, s_ref, d_ref, cut_ref, edge_ref, p_ends, s_ends, d_ends, *rest):
    tiles, edge_tiles, sems = rest
    cells, radial_cells = p_ref.shape[1:3]

    def body(side):
        copies = []

        def fetch(source, target):
            copies.append(pltpu.make_async_copy(source, target, sems.at[len(copies)]))

        rows = pl.ds(side.sent_tile, TILE)
        for i, x in enumerate((p_ref, s_ref, d_ref)):
            fetch(x.at[:, :, rows, :], tiles.at[i])
        fetch(p_ref.at[side.facing, :, pl.ds(side.edge_tile, TILE), :], edge_tiles)
        for source, target in ((p_ref, p_ends), (s_ref, s_ends), (d_ref, d_ends)):
            count = target.shape[2]
            for edge in range(2):
                span = pl.ds(end_columns(edge, cells, count).start, count)
                fetch(source.at[:, span], target.at[edge])
        copy_all(copies)
        cut_ref[...] = tiles[:, :, :, shifted(side.sent, -side.sent_tile), :]
        at = side.edge - OWN - side.edge_tile
        for j in range(cells):
            edge_ref[j : j + 1] = edge_tiles[j, at : at + 1]

    on_each_side(radial_cells, body)


def fill_ends(field, side, p_ends, cut_ref, cells):
    for edge in range(2):
        columns = end_columns(edge, cells, SWEEPS)
        for k in range(2):
            for i in range(SWEEPS):
                field[edge, k, i, side.own] = p_ends[edge, k, i]
                field[edge, k, i, side.cut] = cut_ref[0, k, columns.start + i]


def send_block(layout, arriving, block, messages):
    arriving.wait()
    cells = block.shape[0]
    count = block_rows(cells)
    for edge, message in enumerate(messages):
        for i in range(count):
            at = i if edge == 0 else cells - count + i
            message[layout.row("block", i)] = block[at : at + 1]


def first_edges(
    p_ends, s_ends, d_ends, cut_ref, block_ref, last, first, block, sem, field, other, weight, shift
):
    radial_cells = p_ends.shape[3]
    cells = cut_ref.shape[2]
    n = SWEEPS - 1
    layout = message_of(1, radial_cells, cells)

    def body(side):
        arriving = pltpu.make_async_copy(block_ref, block, sem)
        arriving.start()
        own = shifted(side.own, -side.first)
        cut = shifted(side.cut, -side.first)
        fill_ends(field, side, p_ends, cut_ref, cells)
        for edge in range(2):
            columns = end_columns(edge, cells, n)
            for k in range(2):
                for i in range(n):
                    for rows, s, d in (
                        (own, s_ends[edge, k, i], d_ends[edge, k, i]),
                        (cut, cut_ref[1, k, columns.start + i], cut_ref[2, k, columns.start + i]),
                    ):
                        w = OMEGA / (6.0 + d)
                        weight[edge, k, i, rows] = w
                        shift[edge, k, i, rows] = w * s
        trajectories(
            side,
            field,
            other,
            lambda e, k, i: weight[e, k, i],
            lambda e, k, i: shift[e, k, i],
            layout,
            (first, last),
            True,
        )
        send_block(layout, arriving, block, (first, last))

    on_each_side(radial_cells, body)


def later_edges(p_ends, b_ends, w_ends, cut_ref, block_ref, last, first, block, sem, field, other):
    cells, radial_cells = cut_ref.shape[2], p_ends.shape[3]
    layout = message_of(2, radial_cells, cells)

    def body(side):
        arriving = pltpu.make_async_copy(block_ref, block, sem)
        arriving.start()
        fill_ends(field, side, p_ends, cut_ref, cells)
        trajectories(
            side,
            field,
            other,
            lambda e, k, i: w_ends[e, k, i + e],
            lambda e, k, i: b_ends[e, k, i + e],
            layout,
            (first, last),
            False,
        )
        send_block(layout, arriving, block, (first, last))

    on_each_side(radial_cells, body)


def inner_sweeps(side, levels, weight, shift, last, stash, tile_out, w_tile):
    cells = levels.shape[2]
    radial_cells = side.own.stop - side.own.start
    for j in range(cells):
        for k in range(2):
            close(levels.at[0, k, j], side, k == side.facing)
        for n in range(1, SWEEPS):
            close(levels.at[n, side.facing, j], side, True)
    at = side.edge - side.first
    for e, first in enumerate((0, cells - 2)):
        for k in range(2):
            for i in range(2):
                stash[e, 0, k, i] = levels[0, k, first + i]
    matrix = neighbour_matrix(levels.shape[-1])
    for n in range(SWEEPS):
        final = n == SWEEPS - 1

        def step(i, carry, n=n, final=final):
            items = []
            for k in (1, 0):
                for j in (n + 1 + 2 * i, n + 2 + 2 * i):

                    def beside(k=k, j=j):
                        return levels[n, k, j - 1, side.rows] + levels[n, k, j + 1, side.rows]

                    def take(new, k=k, j=j):
                        if final:
                            last[k, j - SWEEPS] = new[shifted(side.own, -side.first)]
                            return
                        levels[n + 1, k, j, side.rows] = new
                        if k != side.facing:
                            levels[n + 1, k, j, side.ghost : side.ghost + 1] = new[at : at + 1]

                    items.append(
                        (
                            levels.at[n, k, j],
                            beside,
                            functools.partial(lambda k, j: weight[k, j], k, j),
                            functools.partial(lambda k, j: shift[k, j], k, j),
                            take,
                        )
                    )
            relax_all(side, matrix, items)
            return carry

        lax.fori_loop(0, cells // 2 - 1 - n, step, 0, unroll=2 if n % 2 else 1)
        if not final:
            for e, first in enumerate((n + 1, cells - 3 - n)):
                for k in range(2):
                    for i in range(2):
                        stash[e, n + 1, k, i] = levels[n + 1, k, first + i]
    tile_out[...] = last[side.facing, :, side.edge_tile : side.edge_tile + TILE, :]
    first = side.edge_tile + OWN - side.first
    w_tile[...] = weight[side.facing, :, first : first + TILE, :]


def first_interior(
    p_ref, s_ref, d_ref, cut_ref,
    last, stash, tile_out, w_tile, cut_out, b_ends, w_ends, b_out, w_out,
    levels, shift, weight, sems,
):
    cells, radial_cells = p_ref.shape[1:3]

    def body(side):
        own = pl.ds(OWN - side.first, radial_cells)
        copy_all(
            [
                pltpu.make_async_copy(
                    p_ref, levels.at[0, :, :, pl.ds(OWN, radial_cells), :], sems.at[0]
                ),
                pltpu.make_async_copy(s_ref, shift.at[:, :, own, :], sems.at[1]),
                pltpu.make_async_copy(d_ref, weight.at[:, :, own, :], sems.at[2]),
            ]
        )
        cut = shifted(side.cut, -side.first)
        levels[0, :, :, side.cut, :] = cut_ref[0]
        shift[:, :, cut, :] = cut_ref[1]
        weight[:, :, cut, :] = cut_ref[2]

        def invert(j, carry):
            for k in range(2):
                w = OMEGA / (6.0 + weight[k, j])
                weight[k, j] = w
                shift[k, j] = w * shift[k, j]
            return carry

        lax.fori_loop(0, cells, invert, 0)
        pending = [
            pltpu.make_async_copy(shift, b_out, sems.at[1]),
            pltpu.make_async_copy(weight, w_out, sems.at[2]),
        ]
        for c in pending:
            c.start()
        for e in range(2):
            columns = end_columns(e, cells, SWEEPS)
            b_ends[e] = shift[:, columns]
            w_ends[e] = weight[:, columns]
        inner_sweeps(side, levels, weight, shift, last, stash, tile_out, w_tile)
        cut_out[...] = last[:, :, side.sent, :]
        for c in pending:
            c.wait()

    on_each_side(radial_cells, body)


def later_interior(
    inner_ref, tile_ref, p_ends, b_ref, w_ref, cut_ref,
    out_ref, stash, tile_out, w_tile,
    levels, last, shift, weight, sems,
):
    cells, radial_cells = out_ref.shape[1:3]
    inner = slice(SWEEPS, cells - SWEEPS)

    def body(side):
        copies = [
            pltpu.make_async_copy(b_ref, shift, sems.at[0]),
            pltpu.make_async_copy(w_ref, weight, sems.at[1]),
        ]
        for c in copies:
            c.start()
        start = OWN + side.edge_tile
        levels[0, :, inner, side.own, :] = inner_ref[...]
        levels[0, side.facing, inner, start : start + TILE, :] = tile_ref[...]
        for e in range(2):
            levels[0, :, end_columns(e, cells, SWEEPS), side.own, :] = p_ends[e]
        levels[0, :, :, side.cut, :] = cut_ref[0]
        for c in copies:
            c.wait()
        inner_sweeps(side, levels, weight, shift, last, stash, tile_out, w_tile)
        copy_all([pltpu.make_async_copy(last, out_ref.at[:, pl.ds(SWEEPS, cells - 2 * SWEEPS)], sems.at[0])])

    on_each_side(radial_cells, body)


def ghost_response(side, step, turn_ref, w_tile, block_ref, layout, messages, weights, wide, source):
    facing = side.facing
    cells = w_tile.shape[0]
    reach = SWEEPS - 1
    tile = slice(side.edge_tile + OWN - side.first, side.edge_tile + OWN - side.first + TILE)
    at = side.edge - OWN - side.edge_tile
    count = block_rows(cells)
    for i in range(count):
        for message, to in zip(messages, (cells - count + i, 2 * cells + i)):
            wide[to : to + 1] = message[layout.row("block", i)]
    wide[cells : 2 * cells] = block_ref[...]
    source[...] = jnp.zeros(source.shape, jnp.float32)
    offset = lax.rem(turn_ref[0] * step, cells * lax.axis_size("az"))
    rest = offset - lax.div(offset + cells // 2, cells) * cells
    start = cells - reach + (-rest if side.low else rest)
    for c in range(cells + 2 * reach):
        source[c, at : at + 1] = wide[pl.ds(start + c, 1), :]
    row = lax.broadcasted_iota(jnp.int32, source.shape[1:], 0)
    weight = [w_tile[j] for j in range(cells)]
    for e in range(2):
        far = weights[e][facing, 1, side.spare : side.spare + 1]
        beyond = [
            weights[e][facing, 0, tile],
            weights[e][facing, 1, tile],
            jnp.where(row == at, far, 0.0),
        ]
        weight = beyond[::-1] + weight if e == 0 else weight + beyond
    given = [source[c] for c in range(cells + 2 * reach)]
    response = [w * g for w, g in zip(weight, given)]
    for n in range(1, SWEEPS):
        old = response
        response = list(old)
        for c in range(n, len(old) - n):
            x = old[c]
            radial = jnp.where(row == 0, 0.0, pltpu.roll(x, 1, 0)) + jnp.where(
                row == TILE - 1, 0.0, pltpu.roll(x, TILE - 1, 0)
            )
            nbr = (old[c - 1] + old[c + 1]) + (radial + axial_sum(x)) + given[c]
            response[c] = (1.0 - OMEGA) * x + weight[c] * nbr
    return response[reach : reach + cells]


def finish(step, turn_ref, b_ends, w_ends, w_tile, stash, block_ref, tile_in, left_ref, right_ref, *rest):
    known = step > 1
    if known:
        beyond, _, out_ref, levels, last, inner_tiles, near, near2, wide, source, sems = rest
    else:
        cut_in, cut_out, edge_out, last, inner_tiles, beyond, *rest = rest
        levels, near, near2, wide, source = rest
    weights = (beyond.at[0], beyond.at[1])
    messages = (left_ref, right_ref)
    cells, radial_cells = block_ref.shape[0], last.shape[3]
    layout = message_of(step, radial_cells, cells)

    def given(e, k, slot):
        return messages[e][layout.block(slot, k)]

    def column(e, d):
        return d - 1 if e == 0 else cells - d

    def body(side):
        facing = side.facing

        def at(n, e, k, d):
            if d <= n:
                return levels.at[n, e, k, d]
            return stash.at[e, n, k, d - n - 1 if e == 0 else n + 2 - d]

        def meet(e, k, n, response):
            target = levels.at[n, e, k, 0]
            value = given(e, k, n)
            target[side.own] = value if response is None else value + response[side.inside]
            for h in layout.beyond(n, k):
                at = side.beyond(h)
                value = messages[e][layout.row(n, k, h)]
                if response is not None:
                    value = value + response[at : at + 1]
                target[side.first + at : side.first + at + 1] = value

        for e in range(2):
            if not known:
                for k in range(2):
                    for i in range(2):
                        target = beyond.at[e, k, i]
                        target[side.inside] = given(e, k, SWEEPS + i)
                        for h in layout.beyond(SWEEPS + i, k):
                            row = side.beyond(h)
                            target[row : row + 1] = messages[e][layout.row(SWEEPS + i, k, h)]
                beyond[e, facing, 1, side.spare : side.spare + 1] = messages[e][
                    layout.row("third")
                ]
            for k in range(2):
                meet(e, k, 0, None)
                for buf in (near, near2):
                    buf[e, k] = jnp.zeros(buf.shape[2:], jnp.float32)
        nears = (near, near2)

        matrix = neighbour_matrix(levels.shape[-1])

        def own_column(n, e, k, d, take):
            i = d - 1 if e == 0 else SWEEPS - d
            return (
                at(n, e, k, d),
                lambda: at(n, e, k, d - 1)[side.rows] + at(n, e, k, d + 1)[side.rows],
                lambda: w_ends[e, k, i],
                lambda: b_ends[e, k, i],
                take,
            )

        for n in range(SWEEPS - 1):
            src, dst = nears[n % 2], nears[1 - n % 2]
            items = []
            for e in range(2):
                for k in range(2):
                    for d in range(1, n + 2):

                        def take(new, e=e, k=k, d=d):
                            levels[n + 1, e, k, d, side.rows] = new
                            close(levels.at[n + 1, e, k, d], side, k == facing)

                        items.append(own_column(n, e, k, d, take))

                    def take(new, e=e, k=k):
                        dst[e, k, 0, side.rows] = new
                        meet(e, k, n + 1, new)
                        close(dst.at[e, k, 0], side, k == facing)

                    if n == 0:
                        take(weights[e][k, 0] * at(n, e, k, 1)[side.rows])
                        continue
                    items.append(
                        (
                            src.at[e, k, 0],
                            lambda e=e, k=k: at(n, e, k, 1)[side.rows] + src[e, k, 1, side.rows],
                            lambda e=e, k=k: weights[e][k, 0],
                            None,
                            take,
                        )
                    )
                    if n == 1:
                        dst[e, k, 1, side.rows] = weights[e][k, 1] * src[e, k, 0, side.rows]
            relax_all(side, matrix, items)
        copies = []

        def store(source, k, columns, rows):
            if known:
                target = out_ref.at[k, pl.ds(*columns), pl.ds(*rows), :]
                copies.append(pltpu.make_async_copy(source, target, sems.at[len(copies)]))
                copies[-1].start()

        response = None
        tile = slice(side.edge_tile, side.edge_tile + TILE)
        for k in (1 - facing, facing):
            if k == facing:
                response = ghost_response(
                    side, step, turn_ref, w_tile, block_ref, layout, messages, weights, wide, source
                )
                for i in range(cells - 2 * SWEEPS):
                    inner_tiles[i] = tile_in[i] + response[SWEEPS + i]
                columns = (SWEEPS, cells - 2 * SWEEPS)
                store(inner_tiles, k, columns, (side.edge_tile, TILE))
            items = []
            for d in range(1, SWEEPS + 1):
                for e in range(2):
                    first = end_columns(e, cells, SWEEPS).start

                    def take(new, e=e, k=k, i=column(e, d) - first, first=first):
                        new = new[shifted(side.own, -side.first)]
                        last[e, k, i] = new
                        if k == facing:
                            last[e, k, i, tile] = new[tile] + response[first + i]

                    items.append(own_column(SWEEPS - 1, e, k, d, take))
            relax_all(side, matrix, items)
            for e in range(2):
                first = end_columns(e, cells, SWEEPS).start
                store(last.at[e, k], k, (first, SWEEPS), (0, radial_cells))
        if not known:
            row = side.edge - OWN
            cut_out[0, :, SWEEPS : cells - SWEEPS] = cut_in[...]
            for i in range(cells - 2 * SWEEPS):
                j = SWEEPS + i
                r = row - side.edge_tile
                edge_out[j : j + 1] = inner_tiles[i, r : r + 1]
            for e in range(2):
                first = end_columns(e, cells, SWEEPS).start
                cut_out[0, :, first : first + SWEEPS] = last[e, :, :, side.sent, :]
                for i in range(SWEEPS):
                    edge_out[first + i : first + i + 1] = last[e, facing, i, row : row + 1]
        for c in copies:
            c.wait()

    on_each_side(radial_cells, body)


def ring(size, step):
    return [(i, (i + step) % size) for i in range(size)]


def facing_pairs(size, turn):
    pairs = []
    for i in range(size):
        pairs.append((2 * ((i - turn) % size) + 1, 2 * i))
        pairs.append((2 * ((i + turn) % size), 2 * i + 1))
    return pairs


def far_pairs(size, turn):
    return [(2 * i + r, 2 * ((i + (2 * r - 1) * turn) % size) + r) for i in range(size) for r in range(2)]


def facing_block(edge, offset):
    size = lax.axis_size("az")
    cells = edge.shape[0]
    turn = (offset + cells // 2) // cells % size
    near = min(size, 16)

    def far(t):
        return lambda e: lax.ppermute(e, ("az", "rad"), far_pairs(size, t * near))

    def branch(t):
        return lambda e: lax.ppermute(e, ("az", "rad"), facing_pairs(size, t))

    if size > near:
        edge = lax.switch(turn // near, [far(t) for t in range(-(-size // near))], edge)
    return lax.switch(turn % near, [branch(t) for t in range(near)], edge)


def per_device(pressure, source, diagonal, rot_offset):
    _, cells, radial_cells, lanes = pressure.shape
    size = lax.axis_size("az")
    rows, span = radial_cells + 4 * TILE, radial_cells + TILE

    def array(*shape):
        return jax.ShapeDtypeStruct(shape, jnp.float32)

    def scratch(*shape):
        return pltpu.VMEM(shape, jnp.float32)

    def pinned(x):
        return pltpu.with_memory_space_constraint(x, pltpu.HBM)

    kept = pltpu.HBM((2, cells, span, lanes), jnp.float32)
    kept_ends = array(2, 2, SWEEPS, span, lanes)
    stash = array(2, SWEEPS, 2, 2, rows, lanes)
    cells_in = cells - 2 * SWEEPS
    tiles = array(cells_in, TILE, lanes)
    vmem = pl.BlockSpec(memory_space=pltpu.VMEM)
    smem = pl.BlockSpec(memory_space=pltpu.SMEM)
    hbm = pl.BlockSpec(memory_space=pltpu.HBM)
    anywhere = pl.BlockSpec(memory_space=pl.ANY)
    columns = scratch(2, 2, SWEEPS, rows, lanes)
    three = scratch(2, 2, SWEEPS - 1, span, lanes)

    def call(kernel, out_shape, in_specs, out_specs, scratch_shapes, operands, work_columns, **more):
        work = 2 * work_columns * span * lanes
        return pl.pallas_call(
            kernel,
            out_shape=out_shape,
            in_specs=in_specs,
            out_specs=out_specs,
            scratch_shapes=scratch_shapes,
            compiler_params=pltpu.CompilerParams(vmem_limit_bytes=28 << 20),
            cost_estimate=pl.CostEstimate(
                flops=12 * work, bytes_accessed=8 * work, transcendentals=0
            ),
            **more,
        )(*operands)

    fields = tuple(pinned(x) for x in (pressure, source, diagonal))
    cut, edge, *ends = call(
        pack,
        (
            array(3, 2, cells, SWEEPS, lanes),
            array(cells, lanes),
            array(2, 2, SWEEPS, radial_cells, lanes),
            array(2, 2, SWEEPS - 1, radial_cells, lanes),
            array(2, 2, SWEEPS - 1, radial_cells, lanes),
        ),
        [hbm] * 3,
        [vmem] * 5,
        [
            scratch(3, 2, cells, TILE, lanes),
            scratch(cells, TILE, lanes),
            pltpu.SemaphoreType.DMA((10,)),
        ],
        fields,
        1,
        name="pack",
    )
    for step in range(1, STEPS + 1):
        known = step > 1
        cut = lax.ppermute(cut, "rad", [(0, 1), (1, 0)])
        offset = rot_offset[0] * step % (cells * size)
        block = facing_block(edge, offset)
        message = array(message_of(step, radial_cells, cells).rows, lanes)
        last, first = call(
            later_edges if known else first_edges,
            (message, message),
            [vmem] * 4 + [anywhere],
            [vmem] * 2,
            [scratch(cells, lanes), pltpu.SemaphoreType.DMA, columns, columns]
            + ([] if known else [three] * 2),
            (*ends, cut, block),
            12,
            name="edges",
        )
        left = lax.ppermute(last, "az", ring(size, 1))
        right = lax.ppermute(first, "az", ring(size, -1))
        result = pltpu.HBM(pressure.shape, jnp.float32)
        inner_shape = (2, cells_in, radial_cells, lanes)
        outs = (stash, tiles, array(cells, TILE, lanes))
        levels = scratch(SWEEPS, 2, cells, rows, lanes)
        whole = [scratch(*kept.shape), scratch(*kept.shape), pltpu.SemaphoreType.DMA((3,))]
        if not known:
            inner, saved, inner_tiles, w_tile, inner_cut, b_ends, w_ends, shift, weight = call(
                first_interior,
                (
                    array(*inner_shape),
                    *outs,
                    array(2, cells_in, SWEEPS, lanes),
                    *[kept_ends] * 2,
                    *[kept] * 2,
                ),
                [hbm] * 3 + [vmem],
                [vmem] * 7 + [hbm] * 2,
                [levels, *whole],
                (*fields, cut),
                44,
                name="interior",
            )
        else:
            done, saved, inner_tiles, w_tile = call(
                later_interior,
                (result, *outs),
                [vmem] * 3 + [hbm] * 2 + [vmem],
                [hbm] + [vmem] * 3,
                [levels, scratch(*inner_shape), *whole],
                (inner, fixed_tiles, ends[0], pinned(shift), pinned(weight), cut),
                44,
                name="interior",
            )
        operands = (
            rot_offset,
            b_ends,
            w_ends,
            w_tile,
            saved,
            block,
            inner_tiles,
            left,
            right,
        )
        last = (2, 2, SWEEPS, radial_cells, lanes)
        work = [
            scratch(2, 2, 2, rows, lanes),
            scratch(2, 2, 2, rows, lanes),
            scratch(3 * cells, lanes),
            scratch(cells + 2 * (SWEEPS - 1), TILE, lanes),
        ]
        levels = scratch(SWEEPS, 2, 2, SWEEPS, rows, lanes)
        if not known:
            operands += (inner_cut,)
            cut, edge, ends_now, fixed_tiles, beyond = call(
                functools.partial(finish, step),
                (
                    array(1, 2, cells, SWEEPS, lanes),
                    array(cells, lanes),
                    array(*last),
                    tiles,
                    array(2, 2, 2, span, lanes),
                ),
                [smem] + [vmem] * (len(operands) - 1),
                [vmem] * 5,
                [levels, *work],
                operands,
                26,
                name="finish",
            )
            ends = (ends_now, b_ends, w_ends)
        else:
            operands += (beyond,)
            pressure = call(
                functools.partial(finish, step),
                result,
                [smem] + [vmem] * (len(operands) - 1) + [hbm],
                hbm,
                [
                    levels,
                    scratch(*last),
                    scratch(*tiles.shape),
                    *work,
                    pltpu.SemaphoreType.DMA((5,)),
                ],
                (*operands, done),
                26,
                input_output_aliases={len(operands): 0},
                name="finish",
            )
    return pressure


def solution(mesh):
    placed = (
        P(None, "az", "rad", None),
        P(None, "az", "rad", None),
        P(None, "az", "rad", None),
        P(),
    )
    return jax.shard_map(
        per_device,
        mesh=mesh,
        in_specs=placed,
        out_specs=P(None, "az", "rad", None),
        check_vma=False,
    )
```

```python
import functools

import jax
import jax.numpy as jnp
from jax import lax
from jax.experimental import pallas as pl
from jax.experimental.pallas import tpu as pltpu
from jax.sharding import PartitionSpec as P

STEPS = 2
SWEEPS = 4
OMEGA = 0.8
TILE = 8
OWN = 2 * TILE
LEVELS = tuple(range(SWEEPS))
WEIGHTS = (SWEEPS, SWEEPS + 1)


class Side:
    def __init__(self, low, radial_cells):
        end = OWN + radial_cells
        self.low = low
        self.own = slice(OWN, end)
        self.first = OWN if low else TILE
        self.count = radial_cells + TILE
        self.rows = slice(self.first, self.first + self.count)
        self.cut = slice(end, end + SWEEPS) if low else slice(OWN - SWEEPS, OWN)
        self.tile = slice(end, end + TILE) if low else slice(TILE, OWN)
        self.ghost = OWN - 1 if low else end
        self.edge = OWN if low else end - 1
        self.spare = self.count - 1 if low else 0
        self.inside = shifted(self.own, -self.first)
        self.facing = 1 if low else 0
        self.sent = slice(radial_cells - SWEEPS, radial_cells) if low else slice(0, SWEEPS)
        self.sent_tile = radial_cells - TILE if low else 0
        self.edge_tile = 0 if low else radial_cells - TILE

    def beyond(self, distance):
        return self.inside.stop - 1 + distance if self.low else self.inside.start - distance


def shifted(s, by):
    return slice(s.start + by, s.stop + by)


def axial_sum(x):
    lane = lax.broadcasted_iota(jnp.int32, x.shape, 1)
    last = x.shape[1] - 1
    return jnp.where(lane == 0, 0.0, pltpu.roll(x, 1, 1)) + jnp.where(
        lane == last, 0.0, pltpu.roll(x, last, 1)
    )


def neighbour_matrix(lanes):
    gap = lax.broadcasted_iota(jnp.int32, (lanes, lanes), 0) - lax.broadcasted_iota(
        jnp.int32, (lanes, lanes), 1
    )
    return jnp.where(jnp.abs(gap) == 1, 1.0, 0.0).astype(jnp.bfloat16)


def axial_product(x, matrix):
    high = x.astype(jnp.bfloat16)
    low = (x - high.astype(jnp.float32)).astype(jnp.bfloat16)
    return jnp.dot(high, matrix, preferred_element_type=jnp.float32) + jnp.dot(
        low, matrix, preferred_element_type=jnp.float32
    )


def relax_all(side, matrix, items):
    by_matrix = len(items) // 4 * 2
    axial = []
    if by_matrix:
        here = jnp.concatenate([item[0][side.rows] for item in items[:by_matrix]], axis=0)
        product = axial_product(here, matrix)
        axial = [product[i * side.count : (i + 1) * side.count] for i in range(by_matrix)]
    for i, (column, beside, weight, shift, take) in enumerate(items):
        here = column[side.rows]
        radial = column[shifted(side.rows, -1)] + column[shifted(side.rows, 1)]
        nbr = beside() + radial + (axial[i] if i < by_matrix else axial_sum(here))
        kept = (1.0 - OMEGA) * here
        if shift is not None:
            kept = kept + shift()
        take(kept + weight() * nbr)


def on_each_side(radial_cells, body):
    low = lax.axis_index("rad") == 0

    @pl.when(low)
    def _():
        body(Side(True, radial_cells))

    @pl.when(jnp.logical_not(low))
    def _():
        body(Side(False, radial_cells))


def copy_all(copies):
    for c in copies:
        c.start()
    for c in copies:
        c.wait()


def end_columns(edge, cells, count):
    return slice(0, count) if edge == 0 else slice(cells - count, cells)


def block_rows(cells):
    return cells // 2 + SWEEPS - 1


class Message:
    def __init__(self, slots, radial_cells, cells, weights):
        self.slots = slots
        self.radial_cells = radial_cells
        tail = []
        needed = [(n, SWEEPS - 1 - n) for n in LEVELS] + [(SWEEPS, 2)] * weights
        tail += [(slot, k, h) for slot, n in needed for k in range(2) for h in range(1, n + 1)]
        tail += [("block", i) for i in range(block_rows(cells))]
        tail += ["third"] * weights
        start = 2 * len(slots) * radial_cells
        self.tail = {what: start + i for i, what in enumerate(tail)}
        self.rows = start + -(-len(tail) // TILE) * TILE

    def block(self, slot, k):
        start = (2 * self.slots.index(slot) + k) * self.radial_cells
        return slice(start, start + self.radial_cells)

    def row(self, *what):
        at = self.tail[what if len(what) > 1 else what[0]]
        return slice(at, at + 1)

    def beyond(self, slot, k):
        return [w[2] for w in self.tail if w != "third" and w[:2] == (slot, k) and len(w) == 3]

    def put(self, ref, side, slot, k, value):
        ref[self.block(slot, k)] = value[side.inside]
        for h in self.beyond(slot, k):
            at = side.beyond(h)
            ref[self.row(slot, k, h)] = value[at : at + 1]


def message_of(step, radial_cells, cells):
    return Message(LEVELS + WEIGHTS if step == 1 else LEVELS, radial_cells, cells, step == 1)


def close(column, side, facing):
    row = slice(side.ghost, side.ghost + 1)
    if facing:
        column[row] = jnp.zeros((1, column.shape[1]), jnp.float32)
    else:
        column[row] = column[side.edge : side.edge + 1]


def trajectories(side, field, other, weight, shift, layout, messages, weights):
    bufs = (field, other)
    matrix = neighbour_matrix(field.shape[-1])

    def at(edge, distance, n):
        return distance - 1 if edge == 0 else n - distance

    for edge in range(2):
        for k in range(2):
            for i in range(SWEEPS):
                close(field.at[edge, k, i], side, k == side.facing)
    for sweep in range(SWEEPS):
        src, dst = bufs[sweep % 2], bufs[1 - sweep % 2]
        items = []
        for edge, message in enumerate(messages):
            for k in range(2):
                layout.put(
                    message, side, sweep, k, src[edge, k, at(edge, 1, SWEEPS), side.rows]
                )
                for j in range(1, SWEEPS - sweep):
                    i = at(edge, j, SWEEPS - 1)

                    def beside(edge=edge, k=k, j=j):
                        total = src[edge, k, at(edge, j + 1, SWEEPS), side.rows]
                        if j > 1:
                            total = total + src[edge, k, at(edge, j - 1, SWEEPS), side.rows]
                        return total

                    def take(new, edge=edge, k=k, j=j):
                        out = dst.at[edge, k, at(edge, j, SWEEPS)]
                        out[side.rows] = new
                        close(out, side, k == side.facing)

                    items.append(
                        (
                            src.at[edge, k, at(edge, j, SWEEPS)],
                            beside,
                            functools.partial(weight, edge, k, i),
                            functools.partial(shift, edge, k, i),
                            take,
                        )
                    )
        relax_all(side, matrix, items)
    if not weights:
        return
    for edge, message in enumerate(messages):
        for k in range(2):
            for i in range(2):
                layout.put(
                    message, side, SWEEPS + i, k, weight(edge, k, at(edge, 1 + i, SWEEPS - 1))
                )
        row = side.edge - side.first
        message[layout.row("third")] = weight(edge, side.facing, at(edge, 3, SWEEPS - 1))[
            row : row + 1
        ]


def pack(p_ref, s_ref, d_ref, cut_ref, edge_ref, p_ends, s_ends, d_ends, *rest):
    tiles, edge_tiles, sems = rest
    cells, radial_cells = p_ref.shape[1:3]

    def body(side):
        copies = []

        def fetch(source, target):
            copies.append(pltpu.make_async_copy(source, target, sems.at[len(copies)]))

        rows = pl.ds(side.sent_tile, TILE)
        for i, x in enumerate((p_ref, s_ref, d_ref)):
            fetch(x.at[:, :, rows, :], tiles.at[i])
        fetch(p_ref.at[side.facing, :, pl.ds(side.edge_tile, TILE), :], edge_tiles)
        for source, target in ((p_ref, p_ends), (s_ref, s_ends), (d_ref, d_ends)):
            count = target.shape[2]
            for edge in range(2):
                span = pl.ds(end_columns(edge, cells, count).start, count)
                fetch(source.at[:, span], target.at[edge])
        copy_all(copies)
        cut_ref[...] = tiles[:, :, :, shifted(side.sent, -side.sent_tile), :]
        at = side.edge - OWN - side.edge_tile
        for j in range(cells):
            edge_ref[j : j + 1] = edge_tiles[j, at : at + 1]

    on_each_side(radial_cells, body)


def fill_ends(field, side, p_ends, cut_ref, cells):
    for edge in range(2):
        columns = end_columns(edge, cells, SWEEPS)
        for k in range(2):
            for i in range(SWEEPS):
                field[edge, k, i, side.own] = p_ends[edge, k, i]
                field[edge, k, i, side.cut] = cut_ref[0, k, columns.start + i]


def send_block(layout, arriving, block, messages):
    arriving.wait()
    cells = block.shape[0]
    count = block_rows(cells)
    for edge, message in enumerate(messages):
        for i in range(count):
            at = i if edge == 0 else cells - count + i
            message[layout.row("block", i)] = block[at : at + 1]


def first_edges(
    p_ends, s_ends, d_ends, cut_ref, block_ref, last, first, block, sem, field, other, weight, shift
):
    radial_cells = p_ends.shape[3]
    cells = cut_ref.shape[2]
    n = SWEEPS - 1
    layout = message_of(1, radial_cells, cells)

    def body(side):
        arriving = pltpu.make_async_copy(block_ref, block, sem)
        arriving.start()
        own = shifted(side.own, -side.first)
        cut = shifted(side.cut, -side.first)
        fill_ends(field, side, p_ends, cut_ref, cells)
        for edge in range(2):
            columns = end_columns(edge, cells, n)
            for k in range(2):
                for i in range(n):
                    for rows, s, d in (
                        (own, s_ends[edge, k, i], d_ends[edge, k, i]),
                        (cut, cut_ref[1, k, columns.start + i], cut_ref[2, k, columns.start + i]),
                    ):
                        w = OMEGA / (6.0 + d)
                        weight[edge, k, i, rows] = w
                        shift[edge, k, i, rows] = w * s
        trajectories(
            side,
            field,
            other,
            lambda e, k, i: weight[e, k, i],
            lambda e, k, i: shift[e, k, i],
            layout,
            (first, last),
            True,
        )
        send_block(layout, arriving, block, (first, last))

    on_each_side(radial_cells, body)


def later_edges(p_ends, b_ends, w_ends, cut_ref, block_ref, last, first, block, sem, field, other):
    cells, radial_cells = cut_ref.shape[2], p_ends.shape[3]
    layout = message_of(2, radial_cells, cells)

    def body(side):
        arriving = pltpu.make_async_copy(block_ref, block, sem)
        arriving.start()
        fill_ends(field, side, p_ends, cut_ref, cells)
        trajectories(
            side,
            field,
            other,
            lambda e, k, i: w_ends[e, k, i + e],
            lambda e, k, i: b_ends[e, k, i + e],
            layout,
            (first, last),
            False,
        )
        send_block(layout, arriving, block, (first, last))

    on_each_side(radial_cells, body)


def inner_sweeps(side, levels, weight, shift, last, stash, tile_out, w_tile):
    cells = levels.shape[2]
    radial_cells = side.own.stop - side.own.start
    for j in range(cells):
        for k in range(2):
            close(levels.at[0, k, j], side, k == side.facing)
        for n in range(1, SWEEPS):
            close(levels.at[n, side.facing, j], side, True)
    at = side.edge - side.first
    for e, first in enumerate((0, cells - 2)):
        for k in range(2):
            for i in range(2):
                stash[e, 0, k, i] = levels[0, k, first + i]
    matrix = neighbour_matrix(levels.shape[-1])
    for n in range(SWEEPS):
        final = n == SWEEPS - 1

        def step(i, carry, n=n, final=final):
            items = []
            for k in (1, 0):
                for j in (n + 1 + 2 * i, n + 2 + 2 * i):

                    def beside(k=k, j=j):
                        return levels[n, k, j - 1, side.rows] + levels[n, k, j + 1, side.rows]

                    def take(new, k=k, j=j):
                        if final:
                            last[k, j - SWEEPS] = new[shifted(side.own, -side.first)]
                            return
                        levels[n + 1, k, j, side.rows] = new
                        if k != side.facing:
                            levels[n + 1, k, j, side.ghost : side.ghost + 1] = new[at : at + 1]

                    items.append(
                        (
                            levels.at[n, k, j],
                            beside,
                            functools.partial(lambda k, j: weight[k, j], k, j),
                            functools.partial(lambda k, j: shift[k, j], k, j),
                            take,
                        )
                    )
            relax_all(side, matrix, items)
            return carry

        lax.fori_loop(0, cells // 2 - 1 - n, step, 0, unroll=2 if n % 2 else 1)
        if not final:
            for e, first in enumerate((n + 1, cells - 3 - n)):
                for k in range(2):
                    for i in range(2):
                        stash[e, n + 1, k, i] = levels[n + 1, k, first + i]
    tile_out[...] = last[side.facing, :, side.edge_tile : side.edge_tile + TILE, :]
    first = side.edge_tile + OWN - side.first
    w_tile[...] = weight[side.facing, :, first : first + TILE, :]


def first_interior(
    p_ref, s_ref, d_ref, cut_ref,
    stash, tile_out, w_tile, cut_out, b_ends, w_ends, inner_out, b_out, w_out,
    levels, last, shift, weight, sems,
):
    cells, radial_cells = p_ref.shape[1:3]

    def body(side):
        own = pl.ds(OWN - side.first, radial_cells)
        copy_all(
            [
                pltpu.make_async_copy(
                    p_ref, levels.at[0, :, :, pl.ds(OWN, radial_cells), :], sems.at[0]
                ),
                pltpu.make_async_copy(s_ref, shift.at[:, :, own, :], sems.at[1]),
                pltpu.make_async_copy(d_ref, weight.at[:, :, own, :], sems.at[2]),
            ]
        )
        cut = shifted(side.cut, -side.first)
        levels[0, :, :, side.cut, :] = cut_ref[0]
        shift[:, :, cut, :] = cut_ref[1]
        weight[:, :, cut, :] = cut_ref[2]

        def invert(j, carry):
            for k in range(2):
                w = OMEGA / (6.0 + weight[k, j])
                weight[k, j] = w
                shift[k, j] = w * shift[k, j]
            return carry

        lax.fori_loop(0, cells, invert, 0)
        pending = [
            pltpu.make_async_copy(shift, b_out, sems.at[1]),
            pltpu.make_async_copy(weight, w_out, sems.at[2]),
        ]
        for c in pending:
            c.start()
        for e in range(2):
            columns = end_columns(e, cells, SWEEPS)
            b_ends[e] = shift[:, columns]
            w_ends[e] = weight[:, columns]
        inner_sweeps(side, levels, weight, shift, last, stash, tile_out, w_tile)
        pending.append(pltpu.make_async_copy(last, inner_out, sems.at[0]))
        pending[-1].start()
        cut_out[...] = last[:, :, side.sent, :]
        for c in pending:
            c.wait()

    on_each_side(radial_cells, body)


def later_interior(
    inner_ref, tile_ref, p_ends, b_ref, w_ref, cut_ref,
    out_ref, stash, tile_out, w_tile,
    levels, last, shift, weight, sems,
):
    cells, radial_cells = out_ref.shape[1:3]
    inner = slice(SWEEPS, cells - SWEEPS)

    def body(side):
        copies = [
            pltpu.make_async_copy(b_ref, shift, sems.at[0]),
            pltpu.make_async_copy(w_ref, weight, sems.at[1]),
            pltpu.make_async_copy(
                inner_ref,
                levels.at[
                    0, :, pl.ds(SWEEPS, cells - 2 * SWEEPS), pl.ds(OWN, radial_cells), :
                ],
                sems.at[2],
            ),
        ]
        for c in copies:
            c.start()
        start = OWN + side.edge_tile
        for e in range(2):
            levels[0, :, end_columns(e, cells, SWEEPS), side.own, :] = p_ends[e]
        levels[0, :, :, side.cut, :] = cut_ref[0]
        for c in copies:
            c.wait()
        levels[0, side.facing, inner, start : start + TILE, :] = tile_ref[...]
        inner_sweeps(side, levels, weight, shift, last, stash, tile_out, w_tile)
        copy_all([pltpu.make_async_copy(last, out_ref.at[:, pl.ds(SWEEPS, cells - 2 * SWEEPS)], sems.at[0])])

    on_each_side(radial_cells, body)


def ghost_response(side, step, turn_ref, w_tile, block_ref, layout, messages, weights, wide, source):
    facing = side.facing
    cells = w_tile.shape[0]
    reach = SWEEPS - 1
    tile = slice(side.edge_tile + OWN - side.first, side.edge_tile + OWN - side.first + TILE)
    at = side.edge - OWN - side.edge_tile
    count = block_rows(cells)
    for i in range(count):
        for message, to in zip(messages, (cells - count + i, 2 * cells + i)):
            wide[to : to + 1] = message[layout.row("block", i)]
    wide[cells : 2 * cells] = block_ref[...]
    source[...] = jnp.zeros(source.shape, jnp.float32)
    offset = lax.rem(turn_ref[0] * step, cells * lax.axis_size("az"))
    rest = offset - lax.div(offset + cells // 2, cells) * cells
    start = cells - reach + (-rest if side.low else rest)
    for c in range(cells + 2 * reach):
        source[c, at : at + 1] = wide[pl.ds(start + c, 1), :]
    row = lax.broadcasted_iota(jnp.int32, source.shape[1:], 0)
    weight = [w_tile[j] for j in range(cells)]
    for e in range(2):
        far = weights[e][facing, 1, side.spare : side.spare + 1]
        beyond = [
            weights[e][facing, 0, tile],
            weights[e][facing, 1, tile],
            jnp.where(row == at, far, 0.0),
        ]
        weight = beyond[::-1] + weight if e == 0 else weight + beyond
    given = [source[c] for c in range(cells + 2 * reach)]
    response = [w * g for w, g in zip(weight, given)]
    for n in range(1, SWEEPS):
        old = response
        response = list(old)
        for c in range(n, len(old) - n):
            x = old[c]
            radial = jnp.where(row == 0, 0.0, pltpu.roll(x, 1, 0)) + jnp.where(
                row == TILE - 1, 0.0, pltpu.roll(x, TILE - 1, 0)
            )
            nbr = (old[c - 1] + old[c + 1]) + (radial + axial_sum(x)) + given[c]
            response[c] = (1.0 - OMEGA) * x + weight[c] * nbr
    return response[reach : reach + cells]


def finish(step, turn_ref, b_ends, w_ends, w_tile, stash, block_ref, tile_in, left_ref, right_ref, *rest):
    known = step > 1
    if known:
        beyond, _, out_ref, levels, last, inner_tiles, near, near2, wide, source, sems = rest
    else:
        cut_in, cut_out, edge_out, last, inner_tiles, beyond, *rest = rest
        levels, near, near2, wide, source = rest
    weights = (beyond.at[0], beyond.at[1])
    messages = (left_ref, right_ref)
    cells, radial_cells = block_ref.shape[0], last.shape[3]
    layout = message_of(step, radial_cells, cells)

    def given(e, k, slot):
        return messages[e][layout.block(slot, k)]

    def column(e, d):
        return d - 1 if e == 0 else cells - d

    def body(side):
        facing = side.facing

        def at(n, e, k, d):
            if d <= n:
                return levels.at[n, e, k, d]
            return stash.at[e, n, k, d - n - 1 if e == 0 else n + 2 - d]

        def meet(e, k, n, response):
            target = levels.at[n, e, k, 0]
            value = given(e, k, n)
            target[side.own] = value if response is None else value + response[side.inside]
            for h in layout.beyond(n, k):
                at = side.beyond(h)
                value = messages[e][layout.row(n, k, h)]
                if response is not None:
                    value = value + response[at : at + 1]
                target[side.first + at : side.first + at + 1] = value

        for e in range(2):
            if not known:
                for k in range(2):
                    for i in range(2):
                        target = beyond.at[e, k, i]
                        target[side.inside] = given(e, k, SWEEPS + i)
                        for h in layout.beyond(SWEEPS + i, k):
                            row = side.beyond(h)
                            target[row : row + 1] = messages[e][layout.row(SWEEPS + i, k, h)]
                beyond[e, facing, 1, side.spare : side.spare + 1] = messages[e][
                    layout.row("third")
                ]
            for k in range(2):
                meet(e, k, 0, None)
                for buf in (near, near2):
                    buf[e, k] = jnp.zeros(buf.shape[2:], jnp.float32)
        nears = (near, near2)

        matrix = neighbour_matrix(levels.shape[-1])

        def own_column(n, e, k, d, take):
            i = d - 1 if e == 0 else SWEEPS - d
            return (
                at(n, e, k, d),
                lambda: at(n, e, k, d - 1)[side.rows] + at(n, e, k, d + 1)[side.rows],
                lambda: w_ends[e, k, i],
                lambda: b_ends[e, k, i],
                take,
            )

        for n in range(SWEEPS - 1):
            src, dst = nears[n % 2], nears[1 - n % 2]
            items = []
            for e in range(2):
                for k in range(2):
                    for d in range(1, n + 2):

                        def take(new, e=e, k=k, d=d):
                            levels[n + 1, e, k, d, side.rows] = new
                            close(levels.at[n + 1, e, k, d], side, k == facing)

                        items.append(own_column(n, e, k, d, take))

                    def take(new, e=e, k=k):
                        dst[e, k, 0, side.rows] = new
                        meet(e, k, n + 1, new)
                        close(dst.at[e, k, 0], side, k == facing)

                    if n == 0:
                        take(weights[e][k, 0] * at(n, e, k, 1)[side.rows])
                        continue
                    items.append(
                        (
                            src.at[e, k, 0],
                            lambda e=e, k=k: at(n, e, k, 1)[side.rows] + src[e, k, 1, side.rows],
                            lambda e=e, k=k: weights[e][k, 0],
                            None,
                            take,
                        )
                    )
                    if n == 1:
                        dst[e, k, 1, side.rows] = weights[e][k, 1] * src[e, k, 0, side.rows]
            relax_all(side, matrix, items)
        copies = []

        def store(source, k, columns, rows):
            if known:
                target = out_ref.at[k, pl.ds(*columns), pl.ds(*rows), :]
                copies.append(pltpu.make_async_copy(source, target, sems.at[len(copies)]))
                copies[-1].start()

        response = None
        tile = slice(side.edge_tile, side.edge_tile + TILE)
        for k in (1 - facing, facing):
            if k == facing:
                response = ghost_response(
                    side, step, turn_ref, w_tile, block_ref, layout, messages, weights, wide, source
                )
                for i in range(cells - 2 * SWEEPS):
                    inner_tiles[i] = tile_in[i] + response[SWEEPS + i]
                columns = (SWEEPS, cells - 2 * SWEEPS)
                store(inner_tiles, k, columns, (side.edge_tile, TILE))
            items = []
            for d in range(1, SWEEPS + 1):
                for e in range(2):
                    first = end_columns(e, cells, SWEEPS).start

                    def take(new, e=e, k=k, i=column(e, d) - first, first=first):
                        new = new[shifted(side.own, -side.first)]
                        last[e, k, i] = new
                        if k == facing:
                            last[e, k, i, tile] = new[tile] + response[first + i]

                    items.append(own_column(SWEEPS - 1, e, k, d, take))
            relax_all(side, matrix, items)
            for e in range(2):
                first = end_columns(e, cells, SWEEPS).start
                store(last.at[e, k], k, (first, SWEEPS), (0, radial_cells))
        if not known:
            row = side.edge - OWN
            cut_out[0, :, SWEEPS : cells - SWEEPS] = cut_in[...]
            for i in range(cells - 2 * SWEEPS):
                j = SWEEPS + i
                r = row - side.edge_tile
                edge_out[j : j + 1] = inner_tiles[i, r : r + 1]
            for e in range(2):
                first = end_columns(e, cells, SWEEPS).start
                cut_out[0, :, first : first + SWEEPS] = last[e, :, :, side.sent, :]
                for i in range(SWEEPS):
                    edge_out[first + i : first + i + 1] = last[e, facing, i, row : row + 1]
        for c in copies:
            c.wait()

    on_each_side(radial_cells, body)


def ring(size, step):
    return [(i, (i + step) % size) for i in range(size)]


def facing_pairs(size, turn):
    pairs = []
    for i in range(size):
        pairs.append((2 * ((i - turn) % size) + 1, 2 * i))
        pairs.append((2 * ((i + turn) % size), 2 * i + 1))
    return pairs


def far_pairs(size, turn):
    return [(2 * i + r, 2 * ((i + (2 * r - 1) * turn) % size) + r) for i in range(size) for r in range(2)]


def facing_block(edge, offset):
    size = lax.axis_size("az")
    cells = edge.shape[0]
    turn = (offset + cells // 2) // cells % size
    near = min(size, 16)

    def far(t):
        return lambda e: lax.ppermute(e, ("az", "rad"), far_pairs(size, t * near))

    def branch(t):
        return lambda e: lax.ppermute(e, ("az", "rad"), facing_pairs(size, t))

    if size > near:
        edge = lax.switch(turn // near, [far(t) for t in range(-(-size // near))], edge)
    return lax.switch(turn % near, [branch(t) for t in range(near)], edge)


def per_device(pressure, source, diagonal, rot_offset):
    _, cells, radial_cells, lanes = pressure.shape
    size = lax.axis_size("az")
    rows, span = radial_cells + 4 * TILE, radial_cells + TILE

    def array(*shape):
        return jax.ShapeDtypeStruct(shape, jnp.float32)

    def scratch(*shape):
        return pltpu.VMEM(shape, jnp.float32)

    def pinned(x):
        return pltpu.with_memory_space_constraint(x, pltpu.HBM)

    kept = pltpu.HBM((2, cells, span, lanes), jnp.float32)
    kept_ends = array(2, 2, SWEEPS, span, lanes)
    stash = array(2, SWEEPS, 2, 2, rows, lanes)
    cells_in = cells - 2 * SWEEPS
    tiles = array(cells_in, TILE, lanes)
    vmem = pl.BlockSpec(memory_space=pltpu.VMEM)
    smem = pl.BlockSpec(memory_space=pltpu.SMEM)
    hbm = pl.BlockSpec(memory_space=pltpu.HBM)
    anywhere = pl.BlockSpec(memory_space=pl.ANY)
    columns = scratch(2, 2, SWEEPS, rows, lanes)
    three = scratch(2, 2, SWEEPS - 1, span, lanes)

    def call(kernel, out_shape, in_specs, out_specs, scratch_shapes, operands, work_columns, **more):
        work = 2 * work_columns * span * lanes
        return pl.pallas_call(
            kernel,
            out_shape=out_shape,
            in_specs=in_specs,
            out_specs=out_specs,
            scratch_shapes=scratch_shapes,
            compiler_params=pltpu.CompilerParams(vmem_limit_bytes=28 << 20),
            cost_estimate=pl.CostEstimate(
                flops=12 * work, bytes_accessed=8 * work, transcendentals=0
            ),
            **more,
        )(*operands)

    fields = tuple(pinned(x) for x in (pressure, source, diagonal))
    cut, edge, *ends = call(
        pack,
        (
            array(3, 2, cells, SWEEPS, lanes),
            array(cells, lanes),
            array(2, 2, SWEEPS, radial_cells, lanes),
            array(2, 2, SWEEPS - 1, radial_cells, lanes),
            array(2, 2, SWEEPS - 1, radial_cells, lanes),
        ),
        [hbm] * 3,
        [vmem] * 5,
        [
            scratch(3, 2, cells, TILE, lanes),
            scratch(cells, TILE, lanes),
            pltpu.SemaphoreType.DMA((10,)),
        ],
        fields,
        1,
        name="pack",
    )
    for step in range(1, STEPS + 1):
        known = step > 1
        cut = lax.ppermute(cut, "rad", [(0, 1), (1, 0)])
        offset = rot_offset[0] * step % (cells * size)
        block = facing_block(edge, offset)
        message = array(message_of(step, radial_cells, cells).rows, lanes)
        last, first = call(
            later_edges if known else first_edges,
            (message, message),
            [vmem] * 4 + [anywhere],
            [vmem] * 2,
            [scratch(cells, lanes), pltpu.SemaphoreType.DMA, columns, columns]
            + ([] if known else [three] * 2),
            (*ends, cut, block),
            12,
            name="edges",
        )
        left = lax.ppermute(last, "az", ring(size, 1))
        right = lax.ppermute(first, "az", ring(size, -1))
        result = pltpu.HBM(pressure.shape, jnp.float32)
        inner_shape = (2, cells_in, radial_cells, lanes)
        outs = (stash, tiles, array(cells, TILE, lanes))
        levels = scratch(SWEEPS, 2, cells, rows, lanes)
        whole = [scratch(*kept.shape), scratch(*kept.shape), pltpu.SemaphoreType.DMA((3,))]
        if not known:
            saved, inner_tiles, w_tile, inner_cut, b_ends, w_ends, inner, shift, weight = call(
                first_interior,
                (
                    *outs,
                    array(2, cells_in, SWEEPS, lanes),
                    *[kept_ends] * 2,
                    pltpu.HBM(inner_shape, jnp.float32),
                    *[kept] * 2,
                ),
                [hbm] * 3 + [vmem],
                [vmem] * 6 + [hbm] * 3,
                [levels, scratch(*inner_shape), *whole],
                (*fields, cut),
                44,
                name="interior",
            )
        else:
            done, saved, inner_tiles, w_tile = call(
                later_interior,
                (result, *outs),
                [hbm] + [vmem] * 2 + [hbm] * 2 + [vmem],
                [hbm] + [vmem] * 3,
                [levels, scratch(*inner_shape), *whole],
                (pinned(inner), fixed_tiles, ends[0], pinned(shift), pinned(weight), cut),
                44,
                name="interior",
            )
        operands = (
            rot_offset,
            b_ends,
            w_ends,
            w_tile,
            saved,
            block,
            inner_tiles,
            left,
            right,
        )
        last = (2, 2, SWEEPS, radial_cells, lanes)
        work = [
            scratch(2, 2, 2, rows, lanes),
            scratch(2, 2, 2, rows, lanes),
            scratch(3 * cells, lanes),
            scratch(cells + 2 * (SWEEPS - 1), TILE, lanes),
        ]
        levels = scratch(SWEEPS, 2, 2, SWEEPS, rows, lanes)
        if not known:
            operands += (inner_cut,)
            cut, edge, ends_now, fixed_tiles, beyond = call(
                functools.partial(finish, step),
                (
                    array(1, 2, cells, SWEEPS, lanes),
                    array(cells, lanes),
                    array(*last),
                    tiles,
                    array(2, 2, 2, span, lanes),
                ),
                [smem] + [vmem] * (len(operands) - 1),
                [vmem] * 5,
                [levels, *work],
                operands,
                26,
                name="finish",
            )
            ends = (ends_now, b_ends, w_ends)
        else:
            operands += (beyond,)
            pressure = call(
                functools.partial(finish, step),
                result,
                [smem] + [vmem] * (len(operands) - 1) + [hbm],
                hbm,
                [
                    levels,
                    scratch(*last),
                    scratch(*tiles.shape),
                    *work,
                    pltpu.SemaphoreType.DMA((5,)),
                ],
                (*operands, done),
                26,
                input_output_aliases={len(operands): 0},
                name="finish",
            )
    return pressure


def solution(mesh):
    placed = (
        P(None, "az", "rad", None),
        P(None, "az", "rad", None),
        P(None, "az", "rad", None),
        P(),
    )
    return jax.shard_map(
        per_device,
        mesh=mesh,
        in_specs=placed,
        out_specs=P(None, "az", "rad", None),
        check_vma=False,
    )
```

```python
import functools

import jax
import jax.numpy as jnp
from jax import lax
from jax.experimental import pallas as pl
from jax.experimental.pallas import tpu as pltpu
from jax.sharding import PartitionSpec as P

STEPS = 2
SWEEPS = 4
OMEGA = 0.8
TILE = 8
OWN = 2 * TILE
LEVELS = tuple(range(SWEEPS))
WEIGHTS = (SWEEPS, SWEEPS + 1)


class Side:
    def __init__(self, low, radial_cells):
        end = OWN + radial_cells
        self.low = low
        self.own = slice(OWN, end)
        self.first = OWN if low else TILE
        self.count = radial_cells + TILE
        self.rows = slice(self.first, self.first + self.count)
        self.cut = slice(end, end + SWEEPS) if low else slice(OWN - SWEEPS, OWN)
        self.tile = slice(end, end + TILE) if low else slice(TILE, OWN)
        self.ghost = OWN - 1 if low else end
        self.edge = OWN if low else end - 1
        self.spare = self.count - 1 if low else 0
        self.inside = shifted(self.own, -self.first)
        self.facing = 1 if low else 0
        self.sent = slice(radial_cells - SWEEPS, radial_cells) if low else slice(0, SWEEPS)
        self.sent_tile = radial_cells - TILE if low else 0
        self.edge_tile = 0 if low else radial_cells - TILE

    def beyond(self, distance):
        return self.inside.stop - 1 + distance if self.low else self.inside.start - distance


def shifted(s, by):
    return slice(s.start + by, s.stop + by)


def axial_sum(x):
    lane = lax.broadcasted_iota(jnp.int32, x.shape, 1)
    last = x.shape[1] - 1
    return jnp.where(lane == 0, 0.0, pltpu.roll(x, 1, 1)) + jnp.where(
        lane == last, 0.0, pltpu.roll(x, last, 1)
    )


def neighbour_matrix(lanes):
    gap = lax.broadcasted_iota(jnp.int32, (lanes, lanes), 0) - lax.broadcasted_iota(
        jnp.int32, (lanes, lanes), 1
    )
    return jnp.where(jnp.abs(gap) == 1, 1.0, 0.0).astype(jnp.bfloat16)


def axial_product(x, matrix):
    high = x.astype(jnp.bfloat16)
    low = (x - high.astype(jnp.float32)).astype(jnp.bfloat16)
    return jnp.dot(high, matrix, preferred_element_type=jnp.float32) + jnp.dot(
        low, matrix, preferred_element_type=jnp.float32
    )


def relax_all(side, matrix, items, share=1 / 2):
    by_matrix = int(len(items) * share) // 2 * 2
    axial = []
    if by_matrix:
        here = jnp.concatenate([item[0][side.rows] for item in items[:by_matrix]], axis=0)
        product = axial_product(here, matrix)
        axial = [product[i * side.count : (i + 1) * side.count] for i in range(by_matrix)]
    for i, (column, beside, weight, shift, take) in enumerate(items):
        here = column[side.rows]
        radial = column[shifted(side.rows, -1)] + column[shifted(side.rows, 1)]
        nbr = beside() + radial + (axial[i] if i < by_matrix else axial_sum(here))
        kept = (1.0 - OMEGA) * here
        if shift is not None:
            kept = kept + shift()
        take(kept + weight() * nbr)


def on_each_side(radial_cells, body):
    low = lax.axis_index("rad") == 0

    @pl.when(low)
    def _():
        body(Side(True, radial_cells))

    @pl.when(jnp.logical_not(low))
    def _():
        body(Side(False, radial_cells))


def copy_all(copies):
    for c in copies:
        c.start()
    for c in copies:
        c.wait()


def end_columns(edge, cells, count):
    return slice(0, count) if edge == 0 else slice(cells - count, cells)


def block_rows(cells):
    return cells // 2 + SWEEPS - 1


class Message:
    def __init__(self, slots, radial_cells, cells, weights):
        self.slots = slots
        self.radial_cells = radial_cells
        tail = []
        needed = [(n, SWEEPS - 1 - n) for n in LEVELS] + [(SWEEPS, 2)] * weights
        tail += [(slot, k, h) for slot, n in needed for k in range(2) for h in range(1, n + 1)]
        tail += [("block", i) for i in range(block_rows(cells))]
        tail += ["third"] * weights
        start = 2 * len(slots) * radial_cells
        self.tail = {what: start + i for i, what in enumerate(tail)}
        self.rows = start + -(-len(tail) // TILE) * TILE

    def block(self, slot, k):
        start = (2 * self.slots.index(slot) + k) * self.radial_cells
        return slice(start, start + self.radial_cells)

    def row(self, *what):
        at = self.tail[what if len(what) > 1 else what[0]]
        return slice(at, at + 1)

    def beyond(self, slot, k):
        return [w[2] for w in self.tail if w != "third" and w[:2] == (slot, k) and len(w) == 3]

    def put(self, ref, side, slot, k, value):
        ref[self.block(slot, k)] = value[side.inside]
        for h in self.beyond(slot, k):
            at = side.beyond(h)
            ref[self.row(slot, k, h)] = value[at : at + 1]


def message_of(step, radial_cells, cells):
    return Message(LEVELS + WEIGHTS if step == 1 else LEVELS, radial_cells, cells, step == 1)


def close(column, side, facing):
    row = slice(side.ghost, side.ghost + 1)
    if facing:
        column[row] = jnp.zeros((1, column.shape[1]), jnp.float32)
    else:
        column[row] = column[side.edge : side.edge + 1]


def trajectories(side, field, other, weight, shift, layout, messages, weights):
    bufs = (field, other)
    matrix = neighbour_matrix(field.shape[-1])

    def at(edge, distance, n):
        return distance - 1 if edge == 0 else n - distance

    for edge in range(2):
        for k in range(2):
            for i in range(SWEEPS):
                close(field.at[edge, k, i], side, k == side.facing)
    for sweep in range(SWEEPS):
        src, dst = bufs[sweep % 2], bufs[1 - sweep % 2]
        items = []
        for edge, message in enumerate(messages):
            for k in range(2):
                layout.put(
                    message, side, sweep, k, src[edge, k, at(edge, 1, SWEEPS), side.rows]
                )
                for j in range(1, SWEEPS - sweep):
                    i = at(edge, j, SWEEPS - 1)

                    def beside(edge=edge, k=k, j=j):
                        total = src[edge, k, at(edge, j + 1, SWEEPS), side.rows]
                        if j > 1:
                            total = total + src[edge, k, at(edge, j - 1, SWEEPS), side.rows]
                        return total

                    def take(new, edge=edge, k=k, j=j):
                        out = dst.at[edge, k, at(edge, j, SWEEPS)]
                        out[side.rows] = new
                        close(out, side, k == side.facing)

                    items.append(
                        (
                            src.at[edge, k, at(edge, j, SWEEPS)],
                            beside,
                            functools.partial(weight, edge, k, i),
                            functools.partial(shift, edge, k, i),
                            take,
                        )
                    )
        relax_all(side, matrix, items, 3 / 4)
    if not weights:
        return
    for edge, message in enumerate(messages):
        for k in range(2):
            for i in range(2):
                layout.put(
                    message, side, SWEEPS + i, k, weight(edge, k, at(edge, 1 + i, SWEEPS - 1))
                )
        row = side.edge - side.first
        message[layout.row("third")] = weight(edge, side.facing, at(edge, 3, SWEEPS - 1))[
            row : row + 1
        ]


def pack(p_ref, s_ref, d_ref, cut_ref, edge_ref, p_ends, s_ends, d_ends, *rest):
    tiles, edge_tiles, sems = rest
    cells, radial_cells = p_ref.shape[1:3]

    def body(side):
        copies = []

        def fetch(source, target):
            copies.append(pltpu.make_async_copy(source, target, sems.at[len(copies)]))

        rows = pl.ds(side.sent_tile, TILE)
        for i, x in enumerate((p_ref, s_ref, d_ref)):
            fetch(x.at[:, :, rows, :], tiles.at[i])
        fetch(p_ref.at[side.facing, :, pl.ds(side.edge_tile, TILE), :], edge_tiles)
        for source, target in ((p_ref, p_ends), (s_ref, s_ends), (d_ref, d_ends)):
            count = target.shape[2]
            for edge in range(2):
                span = pl.ds(end_columns(edge, cells, count).start, count)
                fetch(source.at[:, span], target.at[edge])
        for c in copies:
            c.start()
        for c in copies[:4]:
            c.wait()
        cut_ref[...] = tiles[:, :, :, shifted(side.sent, -side.sent_tile), :]
        at = side.edge - OWN - side.edge_tile
        for j in range(cells):
            edge_ref[j : j + 1] = edge_tiles[j, at : at + 1]
        for c in copies[4:]:
            c.wait()

    on_each_side(radial_cells, body)


def fill_ends(field, side, p_ends, cut_ref, cells):
    for edge in range(2):
        columns = end_columns(edge, cells, SWEEPS)
        for k in range(2):
            for i in range(SWEEPS):
                field[edge, k, i, side.own] = p_ends[edge, k, i]
                field[edge, k, i, side.cut] = cut_ref[0, k, columns.start + i]


def send_block(layout, arriving, block, messages):
    arriving.wait()
    cells = block.shape[0]
    count = block_rows(cells)
    for edge, message in enumerate(messages):
        for i in range(count):
            at = i if edge == 0 else cells - count + i
            message[layout.row("block", i)] = block[at : at + 1]


def first_edges(
    p_ends, s_ends, d_ends, cut_ref, block_ref, last, first, block, sem, field, other, weight, shift
):
    radial_cells = p_ends.shape[3]
    cells = cut_ref.shape[2]
    n = SWEEPS - 1
    layout = message_of(1, radial_cells, cells)

    def body(side):
        arriving = pltpu.make_async_copy(block_ref, block, sem)
        arriving.start()
        own = shifted(side.own, -side.first)
        cut = shifted(side.cut, -side.first)
        fill_ends(field, side, p_ends, cut_ref, cells)
        for edge in range(2):
            columns = end_columns(edge, cells, n)
            for k in range(2):
                for i in range(n):
                    for rows, s, d in (
                        (own, s_ends[edge, k, i], d_ends[edge, k, i]),
                        (cut, cut_ref[1, k, columns.start + i], cut_ref[2, k, columns.start + i]),
                    ):
                        w = OMEGA / (6.0 + d)
                        weight[edge, k, i, rows] = w
                        shift[edge, k, i, rows] = w * s
        trajectories(
            side,
            field,
            other,
            lambda e, k, i: weight[e, k, i],
            lambda e, k, i: shift[e, k, i],
            layout,
            (first, last),
            True,
        )
        send_block(layout, arriving, block, (first, last))

    on_each_side(radial_cells, body)


def later_edges(p_ends, b_ends, w_ends, cut_ref, block_ref, last, first, block, sem, field, other):
    cells, radial_cells = cut_ref.shape[2], p_ends.shape[3]
    layout = message_of(2, radial_cells, cells)

    def body(side):
        arriving = pltpu.make_async_copy(block_ref, block, sem)
        arriving.start()
        fill_ends(field, side, p_ends, cut_ref, cells)
        trajectories(
            side,
            field,
            other,
            lambda e, k, i: w_ends[e, k, i + e],
            lambda e, k, i: b_ends[e, k, i + e],
            layout,
            (first, last),
            False,
        )
        send_block(layout, arriving, block, (first, last))

    on_each_side(radial_cells, body)


def inner_sweeps(side, levels, weight, shift, last, stash, tile_out, w_tile):
    cells = levels.shape[2]
    radial_cells = side.own.stop - side.own.start
    for j in range(cells):
        for k in range(2):
            close(levels.at[0, k, j], side, k == side.facing)
        for n in range(1, SWEEPS):
            close(levels.at[n, side.facing, j], side, True)
    at = side.edge - side.first
    for e, first in enumerate((0, cells - 2)):
        for k in range(2):
            for i in range(2):
                stash[e, 0, k, i] = levels[0, k, first + i]
    matrix = neighbour_matrix(levels.shape[-1])
    for n in range(SWEEPS):
        final = n == SWEEPS - 1

        def step(i, carry, n=n, final=final):
            items = []
            for k in (1, 0):
                for j in (n + 1 + 2 * i, n + 2 + 2 * i):

                    def beside(k=k, j=j):
                        return levels[n, k, j - 1, side.rows] + levels[n, k, j + 1, side.rows]

                    def take(new, k=k, j=j):
                        if final:
                            last[k, j - SWEEPS] = new[shifted(side.own, -side.first)]
                            return
                        levels[n + 1, k, j, side.rows] = new
                        if k != side.facing:
                            levels[n + 1, k, j, side.ghost : side.ghost + 1] = new[at : at + 1]

                    items.append(
                        (
                            levels.at[n, k, j],
                            beside,
                            functools.partial(lambda k, j: weight[k, j], k, j),
                            functools.partial(lambda k, j: shift[k, j], k, j),
                            take,
                        )
                    )
            relax_all(side, matrix, items)
            return carry

        lax.fori_loop(0, cells // 2 - 1 - n, step, 0, unroll=2 if n % 2 else 1)
        if not final:
            for e, first in enumerate((n + 1, cells - 3 - n)):
                for k in range(2):
                    for i in range(2):
                        stash[e, n + 1, k, i] = levels[n + 1, k, first + i]
    tile_out[...] = last[side.facing, :, side.edge_tile : side.edge_tile + TILE, :]
    first = side.edge_tile + OWN - side.first
    w_tile[...] = weight[side.facing, :, first : first + TILE, :]


def first_interior(
    p_ref, s_ref, d_ref, cut_ref,
    stash, tile_out, w_tile, cut_out, b_ends, w_ends, inner_out, b_out, w_out,
    levels, last, shift, weight, sems,
):
    cells, radial_cells = p_ref.shape[1:3]

    def body(side):
        own = pl.ds(OWN - side.first, radial_cells)
        copy_all(
            [
                pltpu.make_async_copy(
                    p_ref, levels.at[0, :, :, pl.ds(OWN, radial_cells), :], sems.at[0]
                ),
                pltpu.make_async_copy(s_ref, shift.at[:, :, own, :], sems.at[1]),
                pltpu.make_async_copy(d_ref, weight.at[:, :, own, :], sems.at[2]),
            ]
        )
        cut = shifted(side.cut, -side.first)
        levels[0, :, :, side.cut, :] = cut_ref[0]
        shift[:, :, cut, :] = cut_ref[1]
        weight[:, :, cut, :] = cut_ref[2]

        def invert(j, carry):
            for k in range(2):
                w = OMEGA / (6.0 + weight[k, j])
                weight[k, j] = w
                shift[k, j] = w * shift[k, j]
            return carry

        lax.fori_loop(0, cells, invert, 0)
        pending = [
            pltpu.make_async_copy(shift, b_out, sems.at[1]),
            pltpu.make_async_copy(weight, w_out, sems.at[2]),
        ]
        for c in pending:
            c.start()
        for e in range(2):
            columns = end_columns(e, cells, SWEEPS)
            b_ends[e] = shift[:, columns]
            w_ends[e] = weight[:, columns]
        inner_sweeps(side, levels, weight, shift, last, stash, tile_out, w_tile)
        pending.append(pltpu.make_async_copy(last, inner_out, sems.at[0]))
        pending[-1].start()
        cut_out[...] = last[:, :, side.sent, :]
        for c in pending:
            c.wait()

    on_each_side(radial_cells, body)


def later_interior(
    inner_ref, tile_ref, p_ends, b_ref, w_ref, cut_ref,
    out_ref, stash, tile_out, w_tile,
    levels, last, shift, weight, sems,
):
    cells, radial_cells = out_ref.shape[1:3]
    inner = slice(SWEEPS, cells - SWEEPS)

    def body(side):
        copies = [
            pltpu.make_async_copy(b_ref, shift, sems.at[0]),
            pltpu.make_async_copy(w_ref, weight, sems.at[1]),
            pltpu.make_async_copy(
                inner_ref,
                levels.at[
                    0, :, pl.ds(SWEEPS, cells - 2 * SWEEPS), pl.ds(OWN, radial_cells), :
                ],
                sems.at[2],
            ),
        ]
        for c in copies:
            c.start()
        start = OWN + side.edge_tile
        for e in range(2):
            levels[0, :, end_columns(e, cells, SWEEPS), side.own, :] = p_ends[e]
        levels[0, :, :, side.cut, :] = cut_ref[0]
        for c in copies:
            c.wait()
        levels[0, side.facing, inner, start : start + TILE, :] = tile_ref[...]
        inner_sweeps(side, levels, weight, shift, last, stash, tile_out, w_tile)
        copy_all([pltpu.make_async_copy(last, out_ref.at[:, pl.ds(SWEEPS, cells - 2 * SWEEPS)], sems.at[0])])

    on_each_side(radial_cells, body)


def ghost_response(side, step, turn_ref, w_tile, block_ref, layout, messages, weights, wide, source):
    facing = side.facing
    cells = w_tile.shape[0]
    reach = SWEEPS - 1
    tile = slice(side.edge_tile + OWN - side.first, side.edge_tile + OWN - side.first + TILE)
    at = side.edge - OWN - side.edge_tile
    count = block_rows(cells)
    for i in range(count):
        for message, to in zip(messages, (cells - count + i, 2 * cells + i)):
            wide[to : to + 1] = message[layout.row("block", i)]
    wide[cells : 2 * cells] = block_ref[...]
    source[...] = jnp.zeros(source.shape, jnp.float32)
    offset = lax.rem(turn_ref[0] * step, cells * lax.axis_size("az"))
    rest = offset - lax.div(offset + cells // 2, cells) * cells
    start = cells - reach + (-rest if side.low else rest)
    for c in range(cells + 2 * reach):
        source[c, at : at + 1] = wide[pl.ds(start + c, 1), :]
    row = lax.broadcasted_iota(jnp.int32, source.shape[1:], 0)
    weight = [w_tile[j] for j in range(cells)]
    for e in range(2):
        far = weights[e][facing, 1, side.spare : side.spare + 1]
        beyond = [
            weights[e][facing, 0, tile],
            weights[e][facing, 1, tile],
            jnp.where(row == at, far, 0.0),
        ]
        weight = beyond[::-1] + weight if e == 0 else weight + beyond
    given = [source[c] for c in range(cells + 2 * reach)]
    response = [w * g for w, g in zip(weight, given)]
    for n in range(1, SWEEPS):
        old = response
        response = list(old)
        for c in range(n, len(old) - n):
            x = old[c]
            radial = jnp.where(row == 0, 0.0, pltpu.roll(x, 1, 0)) + jnp.where(
                row == TILE - 1, 0.0, pltpu.roll(x, TILE - 1, 0)
            )
            nbr = (old[c - 1] + old[c + 1]) + (radial + axial_sum(x)) + given[c]
            response[c] = (1.0 - OMEGA) * x + weight[c] * nbr
    return response[reach : reach + cells]


def finish(step, turn_ref, b_ends, w_ends, w_tile, stash, block_ref, tile_in, left_ref, right_ref, *rest):
    known = step > 1
    if known:
        beyond, _, out_ref, levels, last, inner_tiles, near, near2, wide, source, sems = rest
    else:
        cut_in, cut_out, edge_out, last, inner_tiles, beyond, *rest = rest
        levels, near, near2, wide, source = rest
    weights = (beyond.at[0], beyond.at[1])
    messages = (left_ref, right_ref)
    cells, radial_cells = block_ref.shape[0], last.shape[3]
    layout = message_of(step, radial_cells, cells)

    def given(e, k, slot):
        return messages[e][layout.block(slot, k)]

    def column(e, d):
        return d - 1 if e == 0 else cells - d

    def body(side):
        facing = side.facing

        def at(n, e, k, d):
            if d <= n:
                return levels.at[n, e, k, d]
            return stash.at[e, n, k, d - n - 1 if e == 0 else n + 2 - d]

        def meet(e, k, n, response):
            target = levels.at[n, e, k, 0]
            value = given(e, k, n)
            target[side.own] = value if response is None else value + response[side.inside]
            for h in layout.beyond(n, k):
                at = side.beyond(h)
                value = messages[e][layout.row(n, k, h)]
                if response is not None:
                    value = value + response[at : at + 1]
                target[side.first + at : side.first + at + 1] = value

        for e in range(2):
            if not known:
                for k in range(2):
                    for i in range(2):
                        target = beyond.at[e, k, i]
                        target[side.inside] = given(e, k, SWEEPS + i)
                        for h in layout.beyond(SWEEPS + i, k):
                            row = side.beyond(h)
                            target[row : row + 1] = messages[e][layout.row(SWEEPS + i, k, h)]
                beyond[e, facing, 1, side.spare : side.spare + 1] = messages[e][
                    layout.row("third")
                ]
            for k in range(2):
                meet(e, k, 0, None)
                for buf in (near, near2):
                    buf[e, k] = jnp.zeros(buf.shape[2:], jnp.float32)
        nears = (near, near2)

        matrix = neighbour_matrix(levels.shape[-1])

        def own_column(n, e, k, d, take):
            i = d - 1 if e == 0 else SWEEPS - d
            return (
                at(n, e, k, d),
                lambda: at(n, e, k, d - 1)[side.rows] + at(n, e, k, d + 1)[side.rows],
                lambda: w_ends[e, k, i],
                lambda: b_ends[e, k, i],
                take,
            )

        for n in range(SWEEPS - 1):
            src, dst = nears[n % 2], nears[1 - n % 2]
            items = []
            for e in range(2):
                for k in range(2):
                    for d in range(1, n + 2):

                        def take(new, e=e, k=k, d=d):
                            levels[n + 1, e, k, d, side.rows] = new
                            close(levels.at[n + 1, e, k, d], side, k == facing)

                        items.append(own_column(n, e, k, d, take))

                    def take(new, e=e, k=k):
                        dst[e, k, 0, side.rows] = new
                        meet(e, k, n + 1, new)
                        close(dst.at[e, k, 0], side, k == facing)

                    if n == 0:
                        take(weights[e][k, 0] * at(n, e, k, 1)[side.rows])
                        continue
                    items.append(
                        (
                            src.at[e, k, 0],
                            lambda e=e, k=k: at(n, e, k, 1)[side.rows] + src[e, k, 1, side.rows],
                            lambda e=e, k=k: weights[e][k, 0],
                            None,
                            take,
                        )
                    )
                    if n == 1:
                        dst[e, k, 1, side.rows] = weights[e][k, 1] * src[e, k, 0, side.rows]
            relax_all(side, matrix, items)
        copies = []

        def store(source, k, columns, rows):
            if known:
                target = out_ref.at[k, pl.ds(*columns), pl.ds(*rows), :]
                copies.append(pltpu.make_async_copy(source, target, sems.at[len(copies)]))
                copies[-1].start()

        response = None
        tile = slice(side.edge_tile, side.edge_tile + TILE)
        for k in (1 - facing, facing):
            if k == facing:
                response = ghost_response(
                    side, step, turn_ref, w_tile, block_ref, layout, messages, weights, wide, source
                )
                for i in range(cells - 2 * SWEEPS):
                    inner_tiles[i] = tile_in[i] + response[SWEEPS + i]
                columns = (SWEEPS, cells - 2 * SWEEPS)
                store(inner_tiles, k, columns, (side.edge_tile, TILE))
            items = []
            for d in range(1, SWEEPS + 1):
                for e in range(2):
                    first = end_columns(e, cells, SWEEPS).start

                    def take(new, e=e, k=k, i=column(e, d) - first, first=first):
                        new = new[shifted(side.own, -side.first)]
                        last[e, k, i] = new
                        if k == facing:
                            last[e, k, i, tile] = new[tile] + response[first + i]

                    items.append(own_column(SWEEPS - 1, e, k, d, take))
            relax_all(side, matrix, items)
            for e in range(2):
                first = end_columns(e, cells, SWEEPS).start
                store(last.at[e, k], k, (first, SWEEPS), (0, radial_cells))
        if not known:
            row = side.edge - OWN
            cut_out[0, :, SWEEPS : cells - SWEEPS] = cut_in[...]
            for i in range(cells - 2 * SWEEPS):
                j = SWEEPS + i
                r = row - side.edge_tile
                edge_out[j : j + 1] = inner_tiles[i, r : r + 1]
            for e in range(2):
                first = end_columns(e, cells, SWEEPS).start
                cut_out[0, :, first : first + SWEEPS] = last[e, :, :, side.sent, :]
                for i in range(SWEEPS):
                    edge_out[first + i : first + i + 1] = last[e, facing, i, row : row + 1]
        for c in copies:
            c.wait()

    on_each_side(radial_cells, body)


def ring(size, step):
    return [(i, (i + step) % size) for i in range(size)]


def facing_pairs(size, turn):
    pairs = []
    for i in range(size):
        pairs.append((2 * ((i - turn) % size) + 1, 2 * i))
        pairs.append((2 * ((i + turn) % size), 2 * i + 1))
    return pairs


def far_pairs(size, turn):
    return [(2 * i + r, 2 * ((i + (2 * r - 1) * turn) % size) + r) for i in range(size) for r in range(2)]


def facing_block(edge, offset):
    size = lax.axis_size("az")
    cells = edge.shape[0]
    turn = (offset + cells // 2) // cells % size
    near = min(size, 16)

    def far(t):
        return lambda e: lax.ppermute(e, ("az", "rad"), far_pairs(size, t * near))

    def branch(t):
        return lambda e: lax.ppermute(e, ("az", "rad"), facing_pairs(size, t))

    if size > near:
        edge = lax.switch(turn // near, [far(t) for t in range(-(-size // near))], edge)
    return lax.switch(turn % near, [branch(t) for t in range(near)], edge)


def per_device(pressure, source, diagonal, rot_offset):
    _, cells, radial_cells, lanes = pressure.shape
    size = lax.axis_size("az")
    rows, span = radial_cells + 4 * TILE, radial_cells + TILE

    def array(*shape):
        return jax.ShapeDtypeStruct(shape, jnp.float32)

    def scratch(*shape):
        return pltpu.VMEM(shape, jnp.float32)

    def pinned(x):
        return pltpu.with_memory_space_constraint(x, pltpu.HBM)

    kept = pltpu.HBM((2, cells, span, lanes), jnp.float32)
    kept_ends = array(2, 2, SWEEPS, span, lanes)
    stash = array(2, SWEEPS, 2, 2, rows, lanes)
    cells_in = cells - 2 * SWEEPS
    tiles = array(cells_in, TILE, lanes)
    vmem = pl.BlockSpec(memory_space=pltpu.VMEM)
    smem = pl.BlockSpec(memory_space=pltpu.SMEM)
    hbm = pl.BlockSpec(memory_space=pltpu.HBM)
    anywhere = pl.BlockSpec(memory_space=pl.ANY)
    columns = scratch(2, 2, SWEEPS, rows, lanes)
    three = scratch(2, 2, SWEEPS - 1, span, lanes)

    def call(kernel, out_shape, in_specs, out_specs, scratch_shapes, operands, work_columns, **more):
        work = 2 * work_columns * span * lanes
        return pl.pallas_call(
            kernel,
            out_shape=out_shape,
            in_specs=in_specs,
            out_specs=out_specs,
            scratch_shapes=scratch_shapes,
            compiler_params=pltpu.CompilerParams(vmem_limit_bytes=28 << 20),
            cost_estimate=pl.CostEstimate(
                flops=12 * work, bytes_accessed=8 * work, transcendentals=0
            ),
            **more,
        )(*operands)

    fields = tuple(pinned(x) for x in (pressure, source, diagonal))
    cut, edge, *ends = call(
        pack,
        (
            array(3, 2, cells, SWEEPS, lanes),
            array(cells, lanes),
            array(2, 2, SWEEPS, radial_cells, lanes),
            array(2, 2, SWEEPS - 1, radial_cells, lanes),
            array(2, 2, SWEEPS - 1, radial_cells, lanes),
        ),
        [hbm] * 3,
        [vmem] * 5,
        [
            scratch(3, 2, cells, TILE, lanes),
            scratch(cells, TILE, lanes),
            pltpu.SemaphoreType.DMA((10,)),
        ],
        fields,
        1,
        name="pack",
    )
    for step in range(1, STEPS + 1):
        known = step > 1
        cut = lax.ppermute(cut, "rad", [(0, 1), (1, 0)])
        offset = rot_offset[0] * step % (cells * size)
        block = facing_block(edge, offset)
        message = array(message_of(step, radial_cells, cells).rows, lanes)
        last, first = call(
            later_edges if known else first_edges,
            (message, message),
            [vmem] * 4 + [anywhere],
            [vmem] * 2,
            [scratch(cells, lanes), pltpu.SemaphoreType.DMA, columns, columns]
            + ([] if known else [three] * 2),
            (*ends, cut, block),
            12,
            name="edges",
        )
        left = lax.ppermute(last, "az", ring(size, 1))
        right = lax.ppermute(first, "az", ring(size, -1))
        result = pltpu.HBM(pressure.shape, jnp.float32)
        inner_shape = (2, cells_in, radial_cells, lanes)
        outs = (stash, tiles, array(cells, TILE, lanes))
        levels = scratch(SWEEPS, 2, cells, rows, lanes)
        whole = [scratch(*kept.shape), scratch(*kept.shape), pltpu.SemaphoreType.DMA((3,))]
        if not known:
            saved, inner_tiles, w_tile, inner_cut, b_ends, w_ends, inner, shift, weight = call(
                first_interior,
                (
                    *outs,
                    array(2, cells_in, SWEEPS, lanes),
                    *[kept_ends] * 2,
                    pltpu.HBM(inner_shape, jnp.float32),
                    *[kept] * 2,
                ),
                [hbm] * 3 + [vmem],
                [vmem] * 6 + [hbm] * 3,
                [levels, scratch(*inner_shape), *whole],
                (*fields, cut),
                44,
                name="interior",
            )
        else:
            done, saved, inner_tiles, w_tile = call(
                later_interior,
                (result, *outs),
                [hbm] + [vmem] * 2 + [hbm] * 2 + [vmem],
                [hbm] + [vmem] * 3,
                [levels, scratch(*inner_shape), *whole],
                (pinned(inner), fixed_tiles, ends[0], pinned(shift), pinned(weight), cut),
                44,
                name="interior",
            )
        operands = (
            rot_offset,
            b_ends,
            w_ends,
            w_tile,
            saved,
            block,
            inner_tiles,
            left,
            right,
        )
        last = (2, 2, SWEEPS, radial_cells, lanes)
        work = [
            scratch(2, 2, 2, rows, lanes),
            scratch(2, 2, 2, rows, lanes),
            scratch(3 * cells, lanes),
            scratch(cells + 2 * (SWEEPS - 1), TILE, lanes),
        ]
        levels = scratch(SWEEPS, 2, 2, SWEEPS, rows, lanes)
        if not known:
            operands += (inner_cut,)
            cut, edge, ends_now, fixed_tiles, beyond = call(
                functools.partial(finish, step),
                (
                    array(1, 2, cells, SWEEPS, lanes),
                    array(cells, lanes),
                    array(*last),
                    tiles,
                    array(2, 2, 2, span, lanes),
                ),
                [smem] + [vmem] * (len(operands) - 1),
                [vmem] * 5,
                [levels, *work],
                operands,
                26,
                name="finish",
            )
            ends = (ends_now, b_ends, w_ends)
        else:
            operands += (beyond,)
            pressure = call(
                functools.partial(finish, step),
                result,
                [smem] + [vmem] * (len(operands) - 1) + [hbm],
                hbm,
                [
                    levels,
                    scratch(*last),
                    scratch(*tiles.shape),
                    *work,
                    pltpu.SemaphoreType.DMA((5,)),
                ],
                (*operands, done),
                26,
                input_output_aliases={len(operands): 0},
                name="finish",
            )
    return pressure


def solution(mesh):
    placed = (
        P(None, "az", "rad", None),
        P(None, "az", "rad", None),
        P(None, "az", "rad", None),
        P(),
    )
    return jax.shard_map(
        per_device,
        mesh=mesh,
        in_specs=placed,
        out_specs=P(None, "az", "rad", None),
        check_vma=False,
    )
```

```python
import functools

import jax
import jax.numpy as jnp
from jax import lax
from jax.experimental import pallas as pl
from jax.experimental.pallas import tpu as pltpu
from jax.sharding import PartitionSpec as P

STEPS = 2
SWEEPS = 4
OMEGA = 0.8
TILE = 8
OWN = 2 * TILE
LEVELS = tuple(range(SWEEPS))
WEIGHTS = (SWEEPS, SWEEPS + 1)


class Side:
    def __init__(self, low, radial_cells):
        end = OWN + radial_cells
        self.low = low
        self.own = slice(OWN, end)
        self.first = OWN if low else TILE
        self.count = radial_cells + TILE
        self.rows = slice(self.first, self.first + self.count)
        self.cut = slice(end, end + SWEEPS) if low else slice(OWN - SWEEPS, OWN)
        self.tile = slice(end, end + TILE) if low else slice(TILE, OWN)
        self.ghost = OWN - 1 if low else end
        self.edge = OWN if low else end - 1
        self.spare = self.count - 1 if low else 0
        self.inside = shifted(self.own, -self.first)
        self.facing = 1 if low else 0
        self.sent = slice(radial_cells - SWEEPS, radial_cells) if low else slice(0, SWEEPS)
        self.sent_tile = radial_cells - TILE if low else 0
        self.edge_tile = 0 if low else radial_cells - TILE

    def beyond(self, distance):
        return self.inside.stop - 1 + distance if self.low else self.inside.start - distance


def shifted(s, by):
    return slice(s.start + by, s.stop + by)


def axial_sum(x):
    lane = lax.broadcasted_iota(jnp.int32, x.shape, 1)
    last = x.shape[1] - 1
    return jnp.where(lane == 0, 0.0, pltpu.roll(x, 1, 1)) + jnp.where(
        lane == last, 0.0, pltpu.roll(x, last, 1)
    )


def neighbour_matrix(lanes):
    gap = lax.broadcasted_iota(jnp.int32, (lanes, lanes), 0) - lax.broadcasted_iota(
        jnp.int32, (lanes, lanes), 1
    )
    return jnp.where(jnp.abs(gap) == 1, 1.0, 0.0).astype(jnp.bfloat16)


def axial_product(x, matrix):
    high = x.astype(jnp.bfloat16)
    low = (x - high.astype(jnp.float32)).astype(jnp.bfloat16)
    return jnp.dot(high, matrix, preferred_element_type=jnp.float32) + jnp.dot(
        low, matrix, preferred_element_type=jnp.float32
    )


def relax_all(side, matrix, items, share=1 / 2):
    by_matrix = int(len(items) * share) // 2 * 2
    axial = []
    if by_matrix:
        here = jnp.concatenate([item[0][side.rows] for item in items[:by_matrix]], axis=0)
        product = axial_product(here, matrix)
        axial = [product[i * side.count : (i + 1) * side.count] for i in range(by_matrix)]
    for i, (column, beside, weight, shift, take) in enumerate(items):
        here = column[side.rows]
        radial = column[shifted(side.rows, -1)] + column[shifted(side.rows, 1)]
        nbr = beside() + radial + (axial[i] if i < by_matrix else axial_sum(here))
        kept = (1.0 - OMEGA) * here
        if shift is not None:
            kept = kept + shift()
        take(kept + weight() * nbr)


def on_each_side(radial_cells, body):
    low = lax.axis_index("rad") == 0

    @pl.when(low)
    def _():
        body(Side(True, radial_cells))

    @pl.when(jnp.logical_not(low))
    def _():
        body(Side(False, radial_cells))


def copy_all(copies):
    for c in copies:
        c.start()
    for c in copies:
        c.wait()


def end_columns(edge, cells, count):
    return slice(0, count) if edge == 0 else slice(cells - count, cells)


def block_rows(cells):
    return cells // 2 + SWEEPS - 1


class Message:
    def __init__(self, slots, radial_cells, cells, weights):
        self.slots = slots
        self.radial_cells = radial_cells
        tail = []
        needed = [(n, SWEEPS - 1 - n) for n in LEVELS] + [(SWEEPS, 2)] * weights
        tail += [(slot, k, h) for slot, n in needed for k in range(2) for h in range(1, n + 1)]
        tail += [("block", i) for i in range(block_rows(cells))]
        tail += ["third"] * weights
        start = 2 * len(slots) * radial_cells
        self.tail = {what: start + i for i, what in enumerate(tail)}
        self.rows = start + -(-len(tail) // TILE) * TILE

    def block(self, slot, k):
        start = (2 * self.slots.index(slot) + k) * self.radial_cells
        return slice(start, start + self.radial_cells)

    def row(self, *what):
        at = self.tail[what if len(what) > 1 else what[0]]
        return slice(at, at + 1)

    def beyond(self, slot, k):
        return [w[2] for w in self.tail if w != "third" and w[:2] == (slot, k) and len(w) == 3]

    def put(self, ref, side, slot, k, value):
        ref[self.block(slot, k)] = value[side.inside]
        for h in self.beyond(slot, k):
            at = side.beyond(h)
            ref[self.row(slot, k, h)] = value[at : at + 1]


def message_of(step, radial_cells, cells):
    return Message(LEVELS + WEIGHTS if step == 1 else LEVELS, radial_cells, cells, step == 1)


def close(column, side, facing):
    row = slice(side.ghost, side.ghost + 1)
    if facing:
        column[row] = jnp.zeros((1, column.shape[1]), jnp.float32)
    else:
        column[row] = column[side.edge : side.edge + 1]


def trajectories(side, field, other, weight, shift, layout, messages, weights):
    bufs = (field, other)
    matrix = neighbour_matrix(field.shape[-1])

    def at(edge, distance, n):
        return distance - 1 if edge == 0 else n - distance

    for edge in range(2):
        for k in range(2):
            for i in range(SWEEPS):
                close(field.at[edge, k, i], side, k == side.facing)
    for sweep in range(SWEEPS):
        src, dst = bufs[sweep % 2], bufs[1 - sweep % 2]
        items = []
        for edge, message in enumerate(messages):
            for k in range(2):
                layout.put(
                    message, side, sweep, k, src[edge, k, at(edge, 1, SWEEPS), side.rows]
                )
                for j in range(1, SWEEPS - sweep):
                    i = at(edge, j, SWEEPS - 1)

                    def beside(edge=edge, k=k, j=j):
                        total = src[edge, k, at(edge, j + 1, SWEEPS), side.rows]
                        if j > 1:
                            total = total + src[edge, k, at(edge, j - 1, SWEEPS), side.rows]
                        return total

                    def take(new, edge=edge, k=k, j=j):
                        out = dst.at[edge, k, at(edge, j, SWEEPS)]
                        out[side.rows] = new
                        close(out, side, k == side.facing)

                    items.append(
                        (
                            src.at[edge, k, at(edge, j, SWEEPS)],
                            beside,
                            functools.partial(weight, edge, k, i),
                            functools.partial(shift, edge, k, i),
                            take,
                        )
                    )
        relax_all(side, matrix, items, 3 / 4)
    if not weights:
        return
    for edge, message in enumerate(messages):
        for k in range(2):
            for i in range(2):
                layout.put(
                    message, side, SWEEPS + i, k, weight(edge, k, at(edge, 1 + i, SWEEPS - 1))
                )
        row = side.edge - side.first
        message[layout.row("third")] = weight(edge, side.facing, at(edge, 3, SWEEPS - 1))[
            row : row + 1
        ]


def pack(p_ref, s_ref, d_ref, cut_ref, edge_ref, p_ends, s_ends, d_ends, *rest):
    tiles, edge_tiles, sems = rest
    cells, radial_cells = p_ref.shape[1:3]

    def body(side):
        copies = []

        def fetch(source, target):
            copies.append(pltpu.make_async_copy(source, target, sems.at[len(copies)]))

        rows = pl.ds(side.sent_tile, TILE)
        for i, x in enumerate((p_ref, s_ref, d_ref)):
            fetch(x.at[:, :, rows, :], tiles.at[i])
        fetch(p_ref.at[side.facing, :, pl.ds(side.edge_tile, TILE), :], edge_tiles)
        for source, target in ((p_ref, p_ends), (s_ref, s_ends), (d_ref, d_ends)):
            count = target.shape[2]
            for edge in range(2):
                span = pl.ds(end_columns(edge, cells, count).start, count)
                fetch(source.at[:, span], target.at[edge])
        for c in copies:
            c.start()
        for c in copies[:4]:
            c.wait()
        cut_ref[...] = tiles[:, :, :, shifted(side.sent, -side.sent_tile), :]
        at = side.edge - OWN - side.edge_tile
        for j in range(cells):
            edge_ref[j : j + 1] = edge_tiles[j, at : at + 1]
        for c in copies[4:]:
            c.wait()

    on_each_side(radial_cells, body)


def fill_ends(field, side, p_ends, cut_ref, cells):
    for edge in range(2):
        columns = end_columns(edge, cells, SWEEPS)
        for k in range(2):
            for i in range(SWEEPS):
                field[edge, k, i, side.own] = p_ends[edge, k, i]
                field[edge, k, i, side.cut] = cut_ref[0, k, columns.start + i]


def send_block(layout, arriving, block, messages):
    arriving.wait()
    cells = block.shape[0]
    count = block_rows(cells)
    for edge, message in enumerate(messages):
        for i in range(count):
            at = i if edge == 0 else cells - count + i
            message[layout.row("block", i)] = block[at : at + 1]


def first_edges(
    p_ends, s_ends, d_ends, cut_ref, block_ref, last, first, block, sem, field, other, weight, shift
):
    radial_cells = p_ends.shape[3]
    cells = cut_ref.shape[2]
    n = SWEEPS - 1
    layout = message_of(1, radial_cells, cells)

    def body(side):
        arriving = pltpu.make_async_copy(block_ref, block, sem)
        arriving.start()
        own = shifted(side.own, -side.first)
        cut = shifted(side.cut, -side.first)
        fill_ends(field, side, p_ends, cut_ref, cells)
        for edge in range(2):
            columns = end_columns(edge, cells, n)
            for k in range(2):
                for i in range(n):
                    for rows, s, d in (
                        (own, s_ends[edge, k, i], d_ends[edge, k, i]),
                        (cut, cut_ref[1, k, columns.start + i], cut_ref[2, k, columns.start + i]),
                    ):
                        w = OMEGA / (6.0 + d)
                        weight[edge, k, i, rows] = w
                        shift[edge, k, i, rows] = w * s
        trajectories(
            side,
            field,
            other,
            lambda e, k, i: weight[e, k, i],
            lambda e, k, i: shift[e, k, i],
            layout,
            (first, last),
            True,
        )
        send_block(layout, arriving, block, (first, last))

    on_each_side(radial_cells, body)


def later_edges(p_ends, b_ends, w_ends, cut_ref, block_ref, last, first, block, sem, field, other):
    cells, radial_cells = cut_ref.shape[2], p_ends.shape[3]
    layout = message_of(2, radial_cells, cells)

    def body(side):
        arriving = pltpu.make_async_copy(block_ref, block, sem)
        arriving.start()
        fill_ends(field, side, p_ends, cut_ref, cells)
        trajectories(
            side,
            field,
            other,
            lambda e, k, i: w_ends[e, k, i + e],
            lambda e, k, i: b_ends[e, k, i + e],
            layout,
            (first, last),
            False,
        )
        send_block(layout, arriving, block, (first, last))

    on_each_side(radial_cells, body)


def inner_sweeps(side, levels, weight, shift, last, stash, tile_out, w_tile):
    cells = levels.shape[2]
    radial_cells = side.own.stop - side.own.start
    for j in range(cells):
        for k in range(2):
            close(levels.at[0, k, j], side, k == side.facing)
        for n in range(1, SWEEPS):
            close(levels.at[n, side.facing, j], side, True)
    at = side.edge - side.first
    for e, first in enumerate((0, cells - 2)):
        for k in range(2):
            for i in range(2):
                stash[e, 0, k, i] = levels[0, k, first + i]
    matrix = neighbour_matrix(levels.shape[-1])
    for n in range(SWEEPS):
        final = n == SWEEPS - 1

        def step(i, carry, n=n, final=final):
            items = []
            for k in (1, 0):
                for j in (n + 1 + 2 * i, n + 2 + 2 * i):

                    def beside(k=k, j=j):
                        return levels[n, k, j - 1, side.rows] + levels[n, k, j + 1, side.rows]

                    def take(new, k=k, j=j):
                        if final:
                            last[k, j - SWEEPS] = new[shifted(side.own, -side.first)]
                            return
                        levels[n + 1, k, j, side.rows] = new
                        if k != side.facing:
                            levels[n + 1, k, j, side.ghost : side.ghost + 1] = new[at : at + 1]

                    items.append(
                        (
                            levels.at[n, k, j],
                            beside,
                            functools.partial(lambda k, j: weight[k, j], k, j),
                            functools.partial(lambda k, j: shift[k, j], k, j),
                            take,
                        )
                    )
            relax_all(side, matrix, items)
            return carry

        lax.fori_loop(0, cells // 2 - 1 - n, step, 0, unroll=2 if n % 2 else 1)
        if not final:
            for e, first in enumerate((n + 1, cells - 3 - n)):
                for k in range(2):
                    for i in range(2):
                        stash[e, n + 1, k, i] = levels[n + 1, k, first + i]
    tile_out[...] = last[side.facing, :, side.edge_tile : side.edge_tile + TILE, :]
    first = side.edge_tile + OWN - side.first
    w_tile[...] = weight[side.facing, :, first : first + TILE, :]


def first_interior(
    p_ref, s_ref, d_ref, cut_ref,
    stash, tile_out, w_tile, cut_out, b_ends, w_ends, inner_out, b_out, w_out,
    levels, last, shift, weight, sems,
):
    cells, radial_cells = p_ref.shape[1:3]

    def body(side):
        own = pl.ds(OWN - side.first, radial_cells)
        copy_all(
            [
                pltpu.make_async_copy(
                    p_ref, levels.at[0, :, :, pl.ds(OWN, radial_cells), :], sems.at[0]
                ),
                pltpu.make_async_copy(s_ref, shift.at[:, :, own, :], sems.at[1]),
                pltpu.make_async_copy(d_ref, weight.at[:, :, own, :], sems.at[2]),
            ]
        )
        cut = shifted(side.cut, -side.first)
        levels[0, :, :, side.cut, :] = cut_ref[0]
        shift[:, :, cut, :] = cut_ref[1]
        weight[:, :, cut, :] = cut_ref[2]

        def invert(j, carry):
            for k in range(2):
                w = OMEGA / (6.0 + weight[k, j])
                weight[k, j] = w
                shift[k, j] = w * shift[k, j]
            return carry

        lax.fori_loop(0, cells, invert, 0)
        pending = [
            pltpu.make_async_copy(shift, b_out, sems.at[1]),
            pltpu.make_async_copy(weight, w_out, sems.at[2]),
        ]
        for c in pending:
            c.start()
        for e in range(2):
            columns = end_columns(e, cells, SWEEPS)
            b_ends[e] = shift[:, columns]
            w_ends[e] = weight[:, columns]
        inner_sweeps(side, levels, weight, shift, last, stash, tile_out, w_tile)
        pending.append(pltpu.make_async_copy(last, inner_out, sems.at[0]))
        pending[-1].start()
        cut_out[...] = last[:, :, side.sent, :]
        for c in pending:
            c.wait()

    on_each_side(radial_cells, body)


def later_interior(
    inner_ref, tile_ref, p_ends, b_ref, w_ref, cut_ref,
    out_ref, stash, tile_out, w_tile,
    levels, last, shift, weight, sems,
):
    cells, radial_cells = out_ref.shape[1:3]
    inner = slice(SWEEPS, cells - SWEEPS)

    def body(side):
        copies = [
            pltpu.make_async_copy(b_ref, shift, sems.at[0]),
            pltpu.make_async_copy(w_ref, weight, sems.at[1]),
            pltpu.make_async_copy(
                inner_ref,
                levels.at[
                    0, :, pl.ds(SWEEPS, cells - 2 * SWEEPS), pl.ds(OWN, radial_cells), :
                ],
                sems.at[2],
            ),
        ]
        for c in copies:
            c.start()
        start = OWN + side.edge_tile
        for e in range(2):
            levels[0, :, end_columns(e, cells, SWEEPS), side.own, :] = p_ends[e]
        levels[0, :, :, side.cut, :] = cut_ref[0]
        for c in copies:
            c.wait()
        levels[0, side.facing, inner, start : start + TILE, :] = tile_ref[...]
        inner_sweeps(side, levels, weight, shift, last, stash, tile_out, w_tile)
        copy_all([pltpu.make_async_copy(last, out_ref.at[:, pl.ds(SWEEPS, cells - 2 * SWEEPS)], sems.at[0])])

    on_each_side(radial_cells, body)


def ghost_response(side, step, turn_ref, w_tile, block_ref, layout, messages, weights, wide, source, matrix):
    facing = side.facing
    cells = w_tile.shape[0]
    reach = SWEEPS - 1
    tile = slice(side.edge_tile + OWN - side.first, side.edge_tile + OWN - side.first + TILE)
    at = side.edge - OWN - side.edge_tile
    count = block_rows(cells)
    for i in range(count):
        for message, to in zip(messages, (cells - count + i, 2 * cells + i)):
            wide[to : to + 1] = message[layout.row("block", i)]
    wide[cells : 2 * cells] = block_ref[...]
    source[...] = jnp.zeros(source.shape, jnp.float32)
    offset = lax.rem(turn_ref[0] * step, cells * lax.axis_size("az"))
    rest = offset - lax.div(offset + cells // 2, cells) * cells
    start = cells - reach + (-rest if side.low else rest)
    for c in range(cells + 2 * reach):
        source[c, at : at + 1] = wide[pl.ds(start + c, 1), :]
    row = lax.broadcasted_iota(jnp.int32, source.shape[1:], 0)
    weight = [w_tile[j] for j in range(cells)]
    for e in range(2):
        far = weights[e][facing, 1, side.spare : side.spare + 1]
        beyond = [
            weights[e][facing, 0, tile],
            weights[e][facing, 1, tile],
            jnp.where(row == at, far, 0.0),
        ]
        weight = beyond[::-1] + weight if e == 0 else weight + beyond
    given = [source[c] for c in range(cells + 2 * reach)]
    response = [w * g for w, g in zip(weight, given)]
    for n in range(1, SWEEPS):
        old = response
        response = list(old)
        axial = axial_product(jnp.concatenate(old, axis=0), matrix)
        for c in range(n, len(old) - n):
            x = old[c]
            radial = jnp.where(row == 0, 0.0, pltpu.roll(x, 1, 0)) + jnp.where(
                row == TILE - 1, 0.0, pltpu.roll(x, TILE - 1, 0)
            )
            along = axial[c * TILE : (c + 1) * TILE]
            nbr = (old[c - 1] + old[c + 1]) + (radial + along) + given[c]
            response[c] = (1.0 - OMEGA) * x + weight[c] * nbr
    return response[reach : reach + cells]


def finish(step, turn_ref, b_ends, w_ends, w_tile, stash, block_ref, tile_in, left_ref, right_ref, *rest):
    known = step > 1
    if known:
        beyond, _, out_ref, levels, last, inner_tiles, near, near2, wide, source, sems = rest
    else:
        cut_in, cut_out, edge_out, last, inner_tiles, beyond, *rest = rest
        levels, near, near2, wide, source = rest
    weights = (beyond.at[0], beyond.at[1])
    messages = (left_ref, right_ref)
    cells, radial_cells = block_ref.shape[0], last.shape[3]
    layout = message_of(step, radial_cells, cells)

    def given(e, k, slot):
        return messages[e][layout.block(slot, k)]

    def column(e, d):
        return d - 1 if e == 0 else cells - d

    def body(side):
        facing = side.facing

        def at(n, e, k, d):
            if d <= n:
                return levels.at[n, e, k, d]
            return stash.at[e, n, k, d - n - 1 if e == 0 else n + 2 - d]

        def meet(e, k, n, response):
            target = levels.at[n, e, k, 0]
            value = given(e, k, n)
            target[side.own] = value if response is None else value + response[side.inside]
            for h in layout.beyond(n, k):
                at = side.beyond(h)
                value = messages[e][layout.row(n, k, h)]
                if response is not None:
                    value = value + response[at : at + 1]
                target[side.first + at : side.first + at + 1] = value

        for e in range(2):
            if not known:
                for k in range(2):
                    for i in range(2):
                        target = beyond.at[e, k, i]
                        target[side.inside] = given(e, k, SWEEPS + i)
                        for h in layout.beyond(SWEEPS + i, k):
                            row = side.beyond(h)
                            target[row : row + 1] = messages[e][layout.row(SWEEPS + i, k, h)]
                beyond[e, facing, 1, side.spare : side.spare + 1] = messages[e][
                    layout.row("third")
                ]
            for k in range(2):
                meet(e, k, 0, None)
                for buf in (near, near2):
                    buf[e, k] = jnp.zeros(buf.shape[2:], jnp.float32)
        nears = (near, near2)

        matrix = neighbour_matrix(levels.shape[-1])

        def own_column(n, e, k, d, take):
            i = d - 1 if e == 0 else SWEEPS - d
            return (
                at(n, e, k, d),
                lambda: at(n, e, k, d - 1)[side.rows] + at(n, e, k, d + 1)[side.rows],
                lambda: w_ends[e, k, i],
                lambda: b_ends[e, k, i],
                take,
            )

        for n in range(SWEEPS - 1):
            src, dst = nears[n % 2], nears[1 - n % 2]
            items = []
            for e in range(2):
                for k in range(2):
                    for d in range(1, n + 2):

                        def take(new, e=e, k=k, d=d):
                            levels[n + 1, e, k, d, side.rows] = new
                            close(levels.at[n + 1, e, k, d], side, k == facing)

                        items.append(own_column(n, e, k, d, take))

                    def take(new, e=e, k=k):
                        dst[e, k, 0, side.rows] = new
                        meet(e, k, n + 1, new)
                        close(dst.at[e, k, 0], side, k == facing)

                    if n == 0:
                        take(weights[e][k, 0] * at(n, e, k, 1)[side.rows])
                        continue
                    items.append(
                        (
                            src.at[e, k, 0],
                            lambda e=e, k=k: at(n, e, k, 1)[side.rows] + src[e, k, 1, side.rows],
                            lambda e=e, k=k: weights[e][k, 0],
                            None,
                            take,
                        )
                    )
                    if n == 1:
                        dst[e, k, 1, side.rows] = weights[e][k, 1] * src[e, k, 0, side.rows]
            relax_all(side, matrix, items)
        copies = []

        def store(source, k, columns, rows):
            if known:
                target = out_ref.at[k, pl.ds(*columns), pl.ds(*rows), :]
                copies.append(pltpu.make_async_copy(source, target, sems.at[len(copies)]))
                copies[-1].start()

        response = None
        tile = slice(side.edge_tile, side.edge_tile + TILE)
        for k in (1 - facing, facing):
            if k == facing:
                response = ghost_response(
                    side, step, turn_ref, w_tile, block_ref, layout, messages, weights, wide, source, matrix
                )
                for i in range(cells - 2 * SWEEPS):
                    inner_tiles[i] = tile_in[i] + response[SWEEPS + i]
                columns = (SWEEPS, cells - 2 * SWEEPS)
                store(inner_tiles, k, columns, (side.edge_tile, TILE))
            items = []
            for d in range(1, SWEEPS + 1):
                for e in range(2):
                    first = end_columns(e, cells, SWEEPS).start

                    def take(new, e=e, k=k, i=column(e, d) - first, first=first):
                        new = new[shifted(side.own, -side.first)]
                        last[e, k, i] = new
                        if k == facing:
                            last[e, k, i, tile] = new[tile] + response[first + i]

                    items.append(own_column(SWEEPS - 1, e, k, d, take))
            relax_all(side, matrix, items)
            for e in range(2):
                first = end_columns(e, cells, SWEEPS).start
                store(last.at[e, k], k, (first, SWEEPS), (0, radial_cells))
        if not known:
            row = side.edge - OWN
            cut_out[0, :, SWEEPS : cells - SWEEPS] = cut_in[...]
            for i in range(cells - 2 * SWEEPS):
                j = SWEEPS + i
                r = row - side.edge_tile
                edge_out[j : j + 1] = inner_tiles[i, r : r + 1]
            for e in range(2):
                first = end_columns(e, cells, SWEEPS).start
                cut_out[0, :, first : first + SWEEPS] = last[e, :, :, side.sent, :]
                for i in range(SWEEPS):
                    edge_out[first + i : first + i + 1] = last[e, facing, i, row : row + 1]
        for c in copies:
            c.wait()

    on_each_side(radial_cells, body)


def ring(size, step):
    return [(i, (i + step) % size) for i in range(size)]


def facing_pairs(size, turn):
    pairs = []
    for i in range(size):
        pairs.append((2 * ((i - turn) % size) + 1, 2 * i))
        pairs.append((2 * ((i + turn) % size), 2 * i + 1))
    return pairs


def far_pairs(size, turn):
    return [(2 * i + r, 2 * ((i + (2 * r - 1) * turn) % size) + r) for i in range(size) for r in range(2)]


def facing_block(edge, offset):
    size = lax.axis_size("az")
    cells = edge.shape[0]
    turn = (offset + cells // 2) // cells % size
    near = min(size, 16)

    def far(t):
        return lambda e: lax.ppermute(e, ("az", "rad"), far_pairs(size, t * near))

    def branch(t):
        return lambda e: lax.ppermute(e, ("az", "rad"), facing_pairs(size, t))

    if size > near:
        edge = lax.switch(turn // near, [far(t) for t in range(-(-size // near))], edge)
    return lax.switch(turn % near, [branch(t) for t in range(near)], edge)


def per_device(pressure, source, diagonal, rot_offset):
    _, cells, radial_cells, lanes = pressure.shape
    size = lax.axis_size("az")
    rows, span = radial_cells + 4 * TILE, radial_cells + TILE

    def array(*shape):
        return jax.ShapeDtypeStruct(shape, jnp.float32)

    def scratch(*shape):
        return pltpu.VMEM(shape, jnp.float32)

    def pinned(x):
        return pltpu.with_memory_space_constraint(x, pltpu.HBM)

    kept = pltpu.HBM((2, cells, span, lanes), jnp.float32)
    kept_ends = array(2, 2, SWEEPS, span, lanes)
    stash = array(2, SWEEPS, 2, 2, rows, lanes)
    cells_in = cells - 2 * SWEEPS
    tiles = array(cells_in, TILE, lanes)
    vmem = pl.BlockSpec(memory_space=pltpu.VMEM)
    smem = pl.BlockSpec(memory_space=pltpu.SMEM)
    hbm = pl.BlockSpec(memory_space=pltpu.HBM)
    anywhere = pl.BlockSpec(memory_space=pl.ANY)
    columns = scratch(2, 2, SWEEPS, rows, lanes)
    three = scratch(2, 2, SWEEPS - 1, span, lanes)

    def call(kernel, out_shape, in_specs, out_specs, scratch_shapes, operands, work_columns, **more):
        work = 2 * work_columns * span * lanes
        return pl.pallas_call(
            kernel,
            out_shape=out_shape,
            in_specs=in_specs,
            out_specs=out_specs,
            scratch_shapes=scratch_shapes,
            compiler_params=pltpu.CompilerParams(vmem_limit_bytes=28 << 20),
            cost_estimate=pl.CostEstimate(
                flops=12 * work, bytes_accessed=8 * work, transcendentals=0
            ),
            **more,
        )(*operands)

    fields = tuple(pinned(x) for x in (pressure, source, diagonal))
    cut, edge, *ends = call(
        pack,
        (
            array(3, 2, cells, SWEEPS, lanes),
            array(cells, lanes),
            array(2, 2, SWEEPS, radial_cells, lanes),
            array(2, 2, SWEEPS - 1, radial_cells, lanes),
            array(2, 2, SWEEPS - 1, radial_cells, lanes),
        ),
        [hbm] * 3,
        [vmem] * 5,
        [
            scratch(3, 2, cells, TILE, lanes),
            scratch(cells, TILE, lanes),
            pltpu.SemaphoreType.DMA((10,)),
        ],
        fields,
        1,
        name="pack",
    )
    for step in range(1, STEPS + 1):
        known = step > 1
        cut = lax.ppermute(cut, "rad", [(0, 1), (1, 0)])
        offset = rot_offset[0] * step % (cells * size)
        block = facing_block(edge, offset)
        message = array(message_of(step, radial_cells, cells).rows, lanes)
        last, first = call(
            later_edges if known else first_edges,
            (message, message),
            [vmem] * 4 + [anywhere],
            [vmem] * 2,
            [scratch(cells, lanes), pltpu.SemaphoreType.DMA, columns, columns]
            + ([] if known else [three] * 2),
            (*ends, cut, block),
            12,
            name="edges",
        )
        left = lax.ppermute(last, "az", ring(size, 1))
        right = lax.ppermute(first, "az", ring(size, -1))
        result = pltpu.HBM(pressure.shape, jnp.float32)
        inner_shape = (2, cells_in, radial_cells, lanes)
        outs = (stash, tiles, array(cells, TILE, lanes))
        levels = scratch(SWEEPS, 2, cells, rows, lanes)
        whole = [scratch(*kept.shape), scratch(*kept.shape), pltpu.SemaphoreType.DMA((3,))]
        if not known:
            saved, inner_tiles, w_tile, inner_cut, b_ends, w_ends, inner, shift, weight = call(
                first_interior,
                (
                    *outs,
                    array(2, cells_in, SWEEPS, lanes),
                    *[kept_ends] * 2,
                    pltpu.HBM(inner_shape, jnp.float32),
                    *[kept] * 2,
                ),
                [hbm] * 3 + [vmem],
                [vmem] * 6 + [hbm] * 3,
                [levels, scratch(*inner_shape), *whole],
                (*fields, cut),
                44,
                name="interior",
            )
        else:
            done, saved, inner_tiles, w_tile = call(
                later_interior,
                (result, *outs),
                [hbm] + [vmem] * 2 + [hbm] * 2 + [vmem],
                [hbm] + [vmem] * 3,
                [levels, scratch(*inner_shape), *whole],
                (pinned(inner), fixed_tiles, ends[0], pinned(shift), pinned(weight), cut),
                44,
                name="interior",
            )
        operands = (
            rot_offset,
            b_ends,
            w_ends,
            w_tile,
            saved,
            block,
            inner_tiles,
            left,
            right,
        )
        last = (2, 2, SWEEPS, radial_cells, lanes)
        work = [
            scratch(2, 2, 2, rows, lanes),
            scratch(2, 2, 2, rows, lanes),
            scratch(3 * cells, lanes),
            scratch(cells + 2 * (SWEEPS - 1), TILE, lanes),
        ]
        levels = scratch(SWEEPS, 2, 2, SWEEPS, rows, lanes)
        if not known:
            operands += (inner_cut,)
            cut, edge, ends_now, fixed_tiles, beyond = call(
                functools.partial(finish, step),
                (
                    array(1, 2, cells, SWEEPS, lanes),
                    array(cells, lanes),
                    array(*last),
                    tiles,
                    array(2, 2, 2, span, lanes),
                ),
                [smem] + [vmem] * (len(operands) - 1),
                [vmem] * 5,
                [levels, *work],
                operands,
                26,
                name="finish",
            )
            ends = (ends_now, b_ends, w_ends)
        else:
            operands += (beyond,)
            pressure = call(
                functools.partial(finish, step),
                result,
                [smem] + [vmem] * (len(operands) - 1) + [hbm],
                hbm,
                [
                    levels,
                    scratch(*last),
                    scratch(*tiles.shape),
                    *work,
                    pltpu.SemaphoreType.DMA((5,)),
                ],
                (*operands, done),
                26,
                input_output_aliases={len(operands): 0},
                name="finish",
            )
    return pressure


def solution(mesh):
    placed = (
        P(None, "az", "rad", None),
        P(None, "az", "rad", None),
        P(None, "az", "rad", None),
        P(),
    )
    return jax.shard_map(
        per_device,
        mesh=mesh,
        in_specs=placed,
        out_specs=P(None, "az", "rad", None),
        check_vma=False,
    )
```
